32 devices in a mesh: page: 8 (over z, y), seq: 4 (over x, core).
Axes of the slice: x: 2, y: 2, z: 4, core: 2. Of those that a mesh axis runs over, the one named last changes fastest.
Arguments:
- tokens: bfloat16 [24, 512, 768], P('page', 'seq'), may hold values from -6 to 6
- patches: bfloat16 [24, 64, 768], P('page', 'seq'), may hold values from -6 to 6
- page_length: int32 [24], P('page'), may hold values from 64 to 512, as said below
- box_position: int32 [2, 24, 512], P(None, 'page'), may hold values from 0 to 1023
- query_weight: bfloat16 [768, 768], replicated, may hold values from -0.21875 to 0.21875
- key_weight: bfloat16 [768, 768], replicated, may hold values from -0.21875 to 0.21875
- value_weight: bfloat16 [768, 768], replicated, may hold values from -0.21875 to 0.21875
- out_weight: bfloat16 [768, 768], replicated, may hold values from -0.625 to 0.625
- up_weight: bfloat16 [768, 3072], replicated, may hold values from -0.21875 to 0.21875
- down_weight: bfloat16 [3072, 768], replicated, may hold values from -0.109375 to 0.109375
- conv_weight: bfloat16 [768, 9], replicated, may hold values from -1.796875 to 1.796875
- patch_conv_weight: bfloat16 [768, 9], replicated, may hold values from -1.796875 to 1.796875
- query_bias: bfloat16 [768], replicated, may hold values from -3 to 3
- value_bias: bfloat16 [768], replicated, may hold values from -3 to 3
- out_bias: bfloat16 [768], replicated, may hold values from -3 to 3
- up_bias: bfloat16 [3072], replicated, may hold values from -3 to 3
- down_bias: bfloat16 [768], replicated, may hold values from -3 to 3
- attention_gain: bfloat16 [768], replicated, may hold values from 0.5 to 1.5
- attention_shift: bfloat16 [768], replicated, may hold values from -1.796875 to 1.796875
- feedforward_gain: bfloat16 [768], replicated, may hold values from 0.5 to 1.5
- feedforward_shift: bfloat16 [768], replicated, may hold values from -1.796875 to 1.796875
- reading_bias_table: bfloat16 [12, 32], replicated, may hold values from -4 to 4
- horizontal_bias_table: bfloat16 [12, 64], replicated, may hold values from -4 to 4
- vertical_bias_table: bfloat16 [12, 64], replicated, may hold values from -4 to 4
- cotangent: bfloat16 [24, 512, 768], P('page', 'seq'), may hold values from -6 to 6
- patch_cotangent: bfloat16 [24, 64, 768], P('page', 'seq'), may hold values from -6 to 6
Outputs:
- output: float32 [24, 512, 768], P('page', 'seq')
- patch_output: float32 [24, 64, 768], P('page', 'seq')
- tokens_gradient: float32 [24, 512, 768], P('page', 'seq')
- patches_gradient: float32 [24, 64, 768], P('page', 'seq')
- query_weight_gradient: float32 [768, 768], P('page', 'seq')
- key_weight_gradient: float32 [768, 768], P('page', 'seq')
- value_weight_gradient: float32 [768, 768], P('page', 'seq')
- out_weight_gradient: float32 [768, 768], P('page', 'seq')
- up_weight_gradient: float32 [768, 3072], P('page', 'seq')
- down_weight_gradient: float32 [3072, 768], P('page', 'seq')
- conv_weight_gradient: float32 [768, 9], replicated
- patch_conv_weight_gradient: float32 [768, 9], replicated
- query_bias_gradient: float32 [768], replicated
- value_bias_gradient: float32 [768], replicated
- out_bias_gradient: float32 [768], replicated
- up_bias_gradient: float32 [3072], replicated
- down_bias_gradient: float32 [768], replicated
- attention_gain_gradient: float32 [768], replicated
- attention_shift_gradient: float32 [768], replicated
- feedforward_gain_gradient: float32 [768], replicated
- feedforward_shift_gradient: float32 [768], replicated
- line_table_gradient: float32 [12, 32], replicated
- across_table_gradient: float32 [12, 64], replicated
- upward_table_gradient: float32 [12, 64], replicated
The draws below stay inside these ranges and needn't reach their ends.
Inputs may be any that keep to these rules, and one draw needn't show every extreme that they name: `page_length`: in every aligned block of 3 pages (the pages of one index of page) at least one page has 512 tokens.
All inputs are finite; a program needn't handle non-finite values.
Results may differ from the reference program's by a relative error of at most 0.019.
The reference program's roundings to bfloat16 on the way count: a program that leaves them out, or rounds other values in their place, can miss the bound.
Values may be sent and summed in bfloat16 or wider, within the bound.
A program may use at most 256 MiB of HBM per device.

```python
import jax
import jax.numpy as jnp
from jax import lax

D = 768
HEADS = 12
HEAD = 64
FF = 3072
LINE_BINS = 32
PLANE_BINS = 64
SLOT = 512
GRID_SIDE = 8
PAGE_DEV = 3
PATCH_SLOT = 64
SEQ_ALL = 576
PAGES = 24
N_PAGE = 8


def draw_page_length(key, part):
    key = jax.random.fold_in(key, 11)
    first_key, second_key = jax.random.split(key)
    lengths = jax.random.randint(first_key, (PAGES,), SLOT // 8, SLOT + 1)
    groups = PAGES // PAGE_DEV
    chosen = jax.random.randint(second_key, (groups,), 0, PAGE_DEV)
    longest = jnp.arange(PAGES) % PAGE_DEV == jnp.repeat(chosen, PAGE_DEV)
    return jnp.where(longest, SLOT, lengths).astype(jnp.int32)


def set_ends(entries, own_key, smallest, largest):
    place = [jax.random.randint(jax.random.fold_in(own_key, axis), (), 0, length) for axis, length in enumerate(entries.shape)]
    main_axis = entries.shape.index(max(entries.shape))
    neighbour = place[:main_axis] + [(place[main_axis] + 1) % entries.shape[main_axis]] + place[main_axis + 1:]
    return entries.at[tuple(place)].set(smallest).at[tuple(neighbour)].set(largest)


def shard_levels(stream_key, shape, cuts, low, high):
    level, own = 1.0, jax.random.fold_in(stream_key, 6)
    for axis_at, parts in cuts:
        heights = jnp.exp(jax.random.uniform(jax.random.fold_in(own, axis_at), (parts,), jnp.float32, low / len(cuts), high / len(cuts)))
        level = level * jnp.repeat(heights, shape[axis_at] // parts).reshape([-1 if axis == axis_at else 1 for axis in range(len(shape))])
    return level


def scatter_about(rng, dims, spread, limit, cuts=(), kind=jnp.bfloat16):
    array = spread * jax.random.normal(rng, dims, jnp.float32)
    if cuts:
        array = array * shard_levels(rng, dims, cuts, -0.22, 0.18)
    return jnp.clip(array, -limit, limit).astype(kind)


def setup_inputs(seed: int = 0) -> dict:
    key_of = jax.random.split(jax.random.key(seed), 27)
    tokens = scatter_about(key_of[0], (PAGES, SLOT, D), 1.0, 6.0, ((0, 8), (1, 4)))
    patches = scatter_about(key_of[1], (PAGES, PATCH_SLOT, D), 1.0, 6.0, ((0, 8), (1, 4)))
    page_length = draw_page_length(jax.random.fold_in(key_of[26], 71), 0)
    box_position = set_ends(jax.random.randint(key_of[3], (2, PAGES, SLOT), 0, 1024), jax.random.fold_in(key_of[3], 1), 0, 1023).astype(jnp.int32)
    query_weight = scatter_about(key_of[4], (D, D), D ** -0.5, 0.21875)
    key_weight = scatter_about(key_of[5], (D, D), D ** -0.5, 0.21875)
    value_weight = scatter_about(key_of[6], (D, D), D ** -0.5, 0.21875)
    out_weight = scatter_about(key_of[7], (D, D), (D // 8) ** -0.5, 0.625)
    up_weight = scatter_about(key_of[8], (D, FF), D ** -0.5, 0.21875)
    down_weight = scatter_about(key_of[9], (FF, D), FF ** -0.5, 0.109375)
    conv_weight = scatter_about(key_of[10], (D, 9), 0.3, 1.796875)
    patch_conv_weight = scatter_about(key_of[11], (D, 9), 0.3, 1.796875)
    query_bias = scatter_about(key_of[12], (D,), 0.5, 3.0)
    value_bias = scatter_about(key_of[13], (D,), 0.5, 3.0)
    out_bias = scatter_about(key_of[14], (D,), 0.5, 3.0)
    up_bias = scatter_about(key_of[15], (FF,), 0.5, 3.0)
    down_bias = scatter_about(key_of[16], (D,), 0.5, 3.0)
    attention_gain = jnp.clip(1.0 + 0.1 * jax.random.normal(key_of[17], (D,), jnp.float32), 0.5, 1.5).astype(jnp.bfloat16)
    attention_shift = scatter_about(key_of[18], (D,), 0.3, 1.796875)
    feedforward_gain = jnp.clip(1.0 + 0.1 * jax.random.normal(key_of[19], (D,), jnp.float32), 0.5, 1.5).astype(jnp.bfloat16)
    feedforward_shift = scatter_about(key_of[20], (D,), 0.3, 1.796875)
    reading_bias_table = scatter_about(key_of[21], (HEADS, LINE_BINS), 1.0, 4.0)
    horizontal_bias_table = scatter_about(key_of[22], (HEADS, PLANE_BINS), 1.0, 4.0)
    vertical_bias_table = scatter_about(key_of[23], (HEADS, PLANE_BINS), 1.0, 4.0)
    cotangent = scatter_about(key_of[24], (PAGES, SLOT, D), 1.0, 6.0, ((0, 8), (1, 4)))
    patch_cotangent = scatter_about(key_of[25], (PAGES, PATCH_SLOT, D), 1.0, 6.0, ((0, 8), (1, 4)))
    return dict(tokens=tokens, patches=patches, page_length=page_length, box_position=box_position, query_weight=query_weight, key_weight=key_weight, value_weight=value_weight, out_weight=out_weight, up_weight=up_weight, down_weight=down_weight, conv_weight=conv_weight, patch_conv_weight=patch_conv_weight, query_bias=query_bias, value_bias=value_bias, out_bias=out_bias, up_bias=up_bias, down_bias=down_bias, attention_gain=attention_gain, attention_shift=attention_shift, feedforward_gain=feedforward_gain, feedforward_shift=feedforward_shift, reading_bias_table=reading_bias_table, horizontal_bias_table=horizontal_bias_table, vertical_bias_table=vertical_bias_table, cotangent=cotangent, patch_cotangent=patch_cotangent)


@jax.custom_vjp
def low(v):
    return lax.optimization_barrier(v.astype(jnp.bfloat16)).astype(jnp.float32)

@jax.custom_vjp
def low_back(v):
    return v

def low_keep(v):
    return (low(v), None)

def low_pass(kept, grad):
    return (grad,)

def back_keep(v):
    return (v, None)

def back_low(kept, grad):
    return (low(grad),)
low.defvjp(low_keep, low_pass)
low_back.defvjp(back_keep, back_low)
epsilon = 1e-05
coordinate_step = 16
masked_score = -1000000000.0
patch_pitch = 146
patch_centre = 73

def matmul(operand, matrix):
    return jnp.dot(operand, matrix, precision=lax.Precision.HIGHEST)

def layer_norm(values, gain_vector, shift_vector):
    row_mean = lax.optimization_barrier(jnp.mean(values, axis=-1, keepdims=True))
    centred = values - row_mean
    variance = lax.optimization_barrier(jnp.mean(centred * centred, axis=-1, keepdims=True))
    return centred * lax.rsqrt(variance + epsilon) * gain_vector + shift_vector

def position_conv(masked, conv_taps):
    length = masked.shape[1]
    padded = jnp.pad(masked, ((0, 0), (3, 3), (0, 0)))
    result = jnp.zeros_like(masked)
    for dilation in (1, 2, 3):
        for offset in (-1, 0, 1):
            column = 3 * (dilation - 1) + offset + 1
            anchor = 3 + offset * dilation
            result = result + padded[:, anchor:anchor + length, :] * conv_taps[:, column]
    return result

def patch_conv(masked, patch_taps):
    length = masked.shape[1]
    reach = GRID_SIDE + 1
    padded = jnp.pad(masked, ((0, 0), (reach, reach), (0, 0)))
    result = jnp.zeros_like(masked)
    for vertical in (-1, 0, 1):
        for horizontal in (-1, 0, 1):
            column = 3 * (vertical + 1) + horizontal + 1
            anchor = reach + vertical * GRID_SIDE + horizontal
            result = result + padded[:, anchor:anchor + length, :] * patch_taps[:, column]
    return result

def patch_live_mask():
    cells = jnp.arange(PATCH_SLOT, dtype=jnp.int32)
    return (cells // GRID_SIDE < GRID_SIDE - 1) & (cells % GRID_SIDE < GRID_SIDE - 1)

def plane_part(table_values, coordinate):
    half_plane = PLANE_BINS // 2
    bucket = jnp.clip(jnp.floor_divide(coordinate[:, None, :] - coordinate[:, :, None], coordinate_step), -half_plane, half_plane - 1) + half_plane
    return jnp.transpose(table_values.T[bucket], (0, 3, 1, 2))

def relative_bias(reading_bias_table, horizontal_bias_table, vertical_bias_table, box_block):
    places = jnp.arange(SEQ_ALL, dtype=jnp.int32)
    half_line = LINE_BINS // 2
    line_bucket = jnp.clip(places[None, :] - places[:, None], -half_line, half_line - 1) + half_line
    reading_bias_part = reading_bias_table[:, line_bucket]
    cells = jnp.arange(PATCH_SLOT, dtype=jnp.int32)
    patch_box = jnp.stack([patch_pitch * (cells % GRID_SIDE) + patch_centre, patch_pitch * (cells // GRID_SIDE) + patch_centre])
    page_count = box_block.shape[1]
    patch_boxes = jnp.broadcast_to(patch_box[:, None, :], (2, page_count, PATCH_SLOT))
    boxes = jnp.concatenate([box_block, patch_boxes], axis=2)
    return reading_bias_part[None] + plane_part(horizontal_bias_table, boxes[0]) + plane_part(vertical_bias_table, boxes[1])

def forward(params, tokens_block, patch_block, lengths_block, box_block):
    query_weight, key_weight, value_weight, out_weight, up_weight, down_weight, conv_weight, patch_conv_weight, query_bias, value_bias, out_bias, up_bias, down_bias, attention_gain, attention_shift, feedforward_gain, feedforward_shift, reading_bias_table, horizontal_bias_table, vertical_bias_table = params
    page_count = tokens_block.shape[0]
    places = jnp.arange(SLOT, dtype=jnp.int32)
    text_live = places[None, :] < lengths_block[:, None]
    patch_live = patch_live_mask()
    masked = tokens_block * text_live[:, :, None].astype(jnp.float32)
    text_hidden = tokens_block + low_back(position_conv(masked, conv_weight))
    patch_masked = patch_block * patch_live[None, :, None].astype(jnp.float32)
    patch_hidden = patch_block + low_back(patch_conv(patch_masked, patch_conv_weight))
    hidden = jnp.concatenate([text_hidden, patch_hidden], axis=1)
    key_mask = jnp.concatenate([text_live, jnp.broadcast_to(patch_live[None, :], (page_count, PATCH_SLOT))], axis=1)
    hidden_low = low(hidden)
    queries = low_back(low(matmul(hidden_low, query_weight) + query_bias)).reshape(page_count, SEQ_ALL, HEADS, HEAD)
    key_vectors = low_back(low(matmul(hidden_low, key_weight))).reshape(page_count, SEQ_ALL, HEADS, HEAD)
    value_vectors = low_back(low(matmul(hidden_low, value_weight) + value_bias)).reshape(page_count, SEQ_ALL, HEADS, HEAD)
    scores = jnp.einsum('pqhe,pkhe->phqk', queries, key_vectors, precision=lax.Precision.HIGHEST) * HEAD ** (-0.5)
    scores = scores + relative_bias(reading_bias_table, horizontal_bias_table, vertical_bias_table, box_block)
    scores = jnp.where(key_mask[:, None, None, :], scores, masked_score)
    weights = low(jax.nn.softmax(low_back(scores), axis=-1))
    mixture = jnp.einsum('phqk,pkhe->pqhe', weights, value_vectors, precision=lax.Precision.HIGHEST).reshape(page_count, SEQ_ALL, D)
    attention = low_back(matmul(low_back(low(mixture)), out_weight) + out_bias)
    normed = layer_norm(hidden + attention, attention_gain, attention_shift)
    up_branch = low_back(matmul(low(normed), up_weight) + up_bias)
    down_branch = low_back(matmul(low(jax.nn.gelu(up_branch, approximate=False)), down_weight) + down_bias)
    result = layer_norm(normed + down_branch, feedforward_gain, feedforward_shift)
    return (result[:, :SLOT], result[:, SLOT:])

def reference(tokens, patches, page_length, box_position, query_weight, key_weight, value_weight, out_weight, up_weight, down_weight, conv_weight, patch_conv_weight, query_bias, value_bias, out_bias, up_bias, down_bias, attention_gain, attention_shift, feedforward_gain, feedforward_shift, reading_bias_table, horizontal_bias_table, vertical_bias_table, cotangent, patch_cotangent):
    params = tuple((item.astype(jnp.float32) for item in (query_weight, key_weight, value_weight, out_weight, up_weight, down_weight, conv_weight, patch_conv_weight, query_bias, value_bias, out_bias, up_bias, down_bias, attention_gain, attention_shift, feedforward_gain, feedforward_shift, reading_bias_table, horizontal_bias_table, vertical_bias_table)))
    tokens_blocks = tokens.astype(jnp.float32).reshape(N_PAGE, PAGE_DEV, SLOT, D)
    patch_blocks = patches.astype(jnp.float32).reshape(N_PAGE, PAGE_DEV, PATCH_SLOT, D)
    cotangent_blocks = cotangent.astype(jnp.float32).reshape(N_PAGE, PAGE_DEV, SLOT, D)
    patch_cotangent_blocks = patch_cotangent.astype(jnp.float32).reshape(N_PAGE, PAGE_DEV, PATCH_SLOT, D)
    length_blocks = page_length.reshape(N_PAGE, PAGE_DEV)
    box_blocks = jnp.transpose(box_position.reshape(2, N_PAGE, PAGE_DEV, SLOT), (1, 0, 2, 3))

    def block_step(running, pieces):
        tokens_block, patch_block, lengths_block, box_block, cotangent_block, patch_cotangent_block = pieces

        def forward_block(param_tuple, text_inputs, patch_inputs):
            return forward(param_tuple, text_inputs, patch_inputs, lengths_block, box_block)
        result, pullback = jax.vjp(forward_block, params, tokens_block, patch_block)
        param_grads, tokens_grad, patch_grad = pullback((cotangent_block, patch_cotangent_block))
        running = jax.tree.map(jnp.add, running, param_grads)
        return (running, (result[0], result[1], tokens_grad, patch_grad))
    initial = jax.tree.map(jnp.zeros_like, params)
    totals, (results, patch_results, tokens_grads, patch_grads) = lax.scan(block_step, initial, (tokens_blocks, patch_blocks, length_blocks, box_blocks, cotangent_blocks, patch_cotangent_blocks))
    return (results.reshape(PAGES, SLOT, D), patch_results.reshape(PAGES, PATCH_SLOT, D), tokens_grads.reshape(PAGES, SLOT, D), patch_grads.reshape(PAGES, PATCH_SLOT, D), totals[0], totals[1], totals[2], totals[3], totals[4], totals[5], totals[6], totals[7], totals[8], totals[9], totals[10], totals[11], totals[12], totals[13], totals[14], totals[15], totals[16], totals[17], totals[18], totals[19])
```

```python
import jax
import jax.numpy as jnp
from jax import lax
from jax.sharding import PartitionSpec as P

GRID_SIDE = 8


epsilon = 1e-05
coordinate_step = 16
masked_score = -1000000000.0
patch_pitch = 146
patch_centre = 73


def with_halo(cells, sides, width):
    for axis, dim in sides:
        count = lax.axis_size(axis)
        ends = count - 1
        head = lax.slice_in_dim(cells, 0, width, axis=dim)
        tail = lax.slice_in_dim(cells, cells.shape[dim] - width, cells.shape[dim], axis=dim)
        cells = jnp.concatenate(
            [
                lax.ppermute(tail, axis, [(i, (i + 1) % count) for i in range(ends)]),
                cells,
                lax.ppermute(head, axis, [((i + 1) % count, i) for i in range(ends)]),
            ],
            axis=dim,
        )
    return cells


def layer_norm(values, gain_vector, shift_vector):
    row_mean = jnp.mean(values, axis=-1, keepdims=True)
    centred = values - row_mean
    variance = jnp.mean(centred * centred, axis=-1, keepdims=True)
    return centred * lax.rsqrt(variance + epsilon) * gain_vector + shift_vector


def gelu_exact(values):
    return jax.nn.gelu(values, approximate=False)


def flat_dot(operand, matrix):
    front = operand.shape[:-1]
    result = jnp.dot(
        operand.reshape(-1, operand.shape[-1]), matrix, preferred_element_type=jnp.float32
    )
    return result.reshape(front + (matrix.shape[-1],))


def back_dot(operand, matrix):
    front = operand.shape[:-1]
    result = lax.dot_general(
        operand.reshape(-1, operand.shape[-1]),
        matrix,
        (((1,), (1,)), ((), ())),
        preferred_element_type=jnp.float32,
    )
    return result.reshape(front + (matrix.shape[0],))


def outer_dot(operand, gradient):
    return lax.dot_general(
        operand.reshape(-1, operand.shape[-1]),
        gradient.reshape(-1, gradient.shape[-1]),
        (((0,), (0,)), ((), ())),
        preferred_element_type=jnp.float32,
    )


def row_sum(gradient):
    return jnp.sum(gradient.astype(jnp.float32).reshape(-1, gradient.shape[-1]), axis=0)


def swap(value, axis, bit):
    count = lax.axis_size(axis)
    return lax.ppermute(value, axis, [(i, i ^ bit) for i in range(count)])


def halve(state, dim, axis, bit):
    index = lax.axis_index(axis)
    mine = (index // bit) % 2
    keep = lax.dynamic_index_in_dim(state, mine, dim, keepdims=False)
    send = lax.dynamic_index_in_dim(state, 1 - mine, dim, keepdims=False)
    got = swap(send, axis, bit)
    return (keep.astype(jnp.float32) + got.astype(jnp.float32)).astype(jnp.bfloat16)


def scatter_sum(matrix, x_first):
    pages = lax.axis_size("page")
    rows, columns = matrix.shape
    part = rows // pages
    levels = pages.bit_length() - 1
    state = matrix.reshape([2] * levels + [2, part // 2, 2, columns // 2])
    state = halve(state, levels, "seq", 1)

    def halve_x(value):
        return halve(value, value.ndim - 2, "seq", 2)

    if x_first:
        state = halve_x(state)
    for level in range(levels):
        state = halve(state, levels - 1 - level, "page", 2**level)
        if level == 0 and not x_first:
            state = halve_x(state)
    core = lax.axis_index("seq") % 2
    state = state.reshape(part // 2, 2, columns // 4)
    keep = lax.dynamic_index_in_dim(state, core, 1, keepdims=False)
    got = swap(lax.dynamic_index_in_dim(state, 1 - core, 1, keepdims=False), "seq", 1)
    first = jnp.where(core == 0, keep, got)
    second = jnp.where(core == 0, got, keep)
    return jnp.concatenate([first, second], axis=0).astype(jnp.float32)


def total_sum(vectors):
    flat = jnp.concatenate([vector.reshape(-1) for vector in vectors])
    flat = jnp.pad(flat, (0, -flat.size % 1024)).reshape(-1, 128)
    for bit in (1, 2):
        flat = flat + swap(flat, "seq", bit)
    bit = 1
    while bit < lax.axis_size("page"):
        flat = flat + swap(flat, "page", bit)
        bit *= 2
    flat = flat.reshape(-1)
    result, start = [], 0
    for vector in vectors:
        result.append(flat[start : start + vector.size].reshape(vector.shape))
        start += vector.size
    return result


def plane_hots(query_coord, key_coord, bins):
    half_bins = bins // 2
    bucket = (
        jnp.clip(
            jnp.floor_divide(key_coord[None, :] - query_coord[:, None], coordinate_step),
            -half_bins,
            half_bins - 1,
        )
        + half_bins
    )
    return (bucket[None, :, :] == jnp.arange(bins, dtype=jnp.int32)[:, None, None]).astype(
        jnp.bfloat16
    )


def grid_live(cells):
    return (cells // GRID_SIDE < GRID_SIDE - 1) & (cells % GRID_SIDE < GRID_SIDE - 1)


def grid_boxes(cells):
    return jnp.stack(
        [
            patch_pitch * (cells % GRID_SIDE) + patch_centre,
            patch_pitch * (cells // GRID_SIDE) + patch_centre,
        ]
    )


def shards(
    tokens,
    patches,
    page_length,
    box_position,
    query_weight,
    key_weight,
    value_weight,
    out_weight,
    up_weight,
    down_weight,
    conv_weight,
    patch_conv_weight,
    query_bias,
    value_bias,
    out_bias,
    up_bias,
    down_bias,
    attention_gain,
    attention_shift,
    feedforward_gain,
    feedforward_shift,
    reading_bias_table,
    horizontal_bias_table,
    vertical_bias_table,
    cotangent,
    patch_cotangent,
):
    conv_taps = conv_weight.astype(jnp.float32)
    patch_taps = patch_conv_weight.astype(jnp.float32)
    query_offset = query_bias.astype(jnp.float32)
    value_offset = value_bias.astype(jnp.float32)
    out_offset = out_bias.astype(jnp.float32)
    up_offset = up_bias.astype(jnp.float32)
    down_offset = down_bias.astype(jnp.float32)
    first_gain = attention_gain.astype(jnp.float32)
    first_shift = attention_shift.astype(jnp.float32)
    second_gain = feedforward_gain.astype(jnp.float32)
    second_shift = feedforward_shift.astype(jnp.float32)
    page_count, span_size, model_width = tokens.shape
    patch_span = patches.shape[1]
    seq_count = lax.axis_size("seq")
    slot_size = span_size * seq_count
    patch_slots = patch_span * seq_count
    row_count = span_size + patch_span
    key_count = row_count * seq_count
    head_count = reading_bias_table.shape[0]
    head_size = model_width // head_count
    line_bins = reading_bias_table.shape[1]
    plane_bins = horizontal_bias_table.shape[1]
    score_scale = head_size ** (-0.5)
    seq_index = lax.axis_index("seq")
    text_places = seq_index * span_size + jnp.arange(span_size, dtype=jnp.int32)
    local_cells = seq_index * patch_span + jnp.arange(patch_span, dtype=jnp.int32)
    query_places = jnp.concatenate([text_places, slot_size + local_cells])
    all_cells = jnp.arange(patch_slots, dtype=jnp.int32)
    key_places = jnp.concatenate(
        [
            jnp.arange(slot_size, dtype=jnp.int32).reshape(seq_count, span_size),
            (slot_size + all_cells).reshape(seq_count, patch_span),
        ],
        axis=1,
    ).reshape(key_count)
    text_live = text_places[None, :] < page_length[:, None]
    patch_live = grid_live(local_cells)
    all_text_live = (
        jnp.arange(slot_size, dtype=jnp.int32)[None, :] < page_length[:, None]
    ).reshape(page_count, seq_count, span_size)
    all_patch_live = jnp.broadcast_to(
        grid_live(all_cells).reshape(1, seq_count, patch_span), (page_count, seq_count, patch_span)
    )
    key_mask = jnp.concatenate([all_text_live, all_patch_live], axis=2).reshape(
        page_count, key_count
    )
    text_box_all = box_position.reshape(2, page_count, seq_count, span_size)
    patch_box_all = jnp.broadcast_to(
        grid_boxes(all_cells).reshape(2, 1, seq_count, patch_span),
        (2, page_count, seq_count, patch_span),
    )
    key_box = jnp.concatenate([text_box_all, patch_box_all], axis=3).reshape(
        2, page_count, key_count
    )
    local_patch_box = jnp.broadcast_to(
        grid_boxes(local_cells)[:, None, :], (2, page_count, patch_span)
    )
    query_box = jnp.concatenate(
        [
            lax.dynamic_slice_in_dim(box_position, seq_index * span_size, span_size, 2),
            local_patch_box,
        ],
        axis=2,
    )
    text_factor = text_live[:, :, None]
    patch_factor = patch_live[None, :, None]
    masked = tokens * text_factor.astype(jnp.bfloat16)
    rimmed = with_halo(masked, (("seq", 1),), 3)
    convolved = jnp.zeros((page_count, span_size, model_width), jnp.float32)
    for dilation in (1, 2, 3):
        for offset in (-1, 0, 1):
            column = 3 * (dilation - 1) + offset + 1
            anchor = 3 + offset * dilation
            convolved = convolved + rimmed[:, anchor : anchor + span_size, :] * conv_taps[:, column]
    reach = GRID_SIDE + 1
    patch_masked = patches * patch_factor.astype(jnp.bfloat16)
    patch_rimmed = with_halo(patch_masked, (("seq", 1),), reach)
    patch_convolved = jnp.zeros((page_count, patch_span, model_width), jnp.float32)
    for vertical in (-1, 0, 1):
        for horizontal in (-1, 0, 1):
            column = 3 * (vertical + 1) + horizontal + 1
            anchor = reach + vertical * GRID_SIDE + horizontal
            patch_convolved = (
                patch_convolved
                + patch_rimmed[:, anchor : anchor + patch_span, :] * patch_taps[:, column]
            )
    hidden = jnp.concatenate(
        [tokens.astype(jnp.float32) + convolved, patches.astype(jnp.float32) + patch_convolved],
        axis=1,
    )
    hidden_low = hidden.astype(jnp.bfloat16)
    queries = (flat_dot(hidden_low, query_weight) + query_offset).astype(jnp.bfloat16)
    key_rows = flat_dot(hidden_low, key_weight).astype(jnp.bfloat16)
    value_rows = (flat_dot(hidden_low, value_weight) + value_offset).astype(jnp.bfloat16)
    key_all, value_all = (
        lax.all_gather(key_rows, "seq", axis=1, tiled=True),
        lax.all_gather(value_rows, "seq", axis=1, tiled=True),
    )
    half_line = line_bins // 2
    line_bucket = (
        jnp.clip(key_places[None, :] - query_places[:, None], -half_line, half_line - 1) + half_line
    )
    reading_onehot = (
        line_bucket[None, :, :] == jnp.arange(line_bins, dtype=jnp.int32)[:, None, None]
    ).astype(jnp.bfloat16)
    reading_bias_part = jnp.einsum(
        "cd,dof->cof", reading_bias_table, reading_onehot, preferred_element_type=jnp.float32
    )
    query_pages = jnp.moveaxis(query_box, 1, 0)
    key_pages = jnp.moveaxis(key_box, 1, 0)

    def page_bias(page_inputs):
        query_page, key_page = page_inputs
        horizontal_onehot = plane_hots(query_page[0], key_page[0], plane_bins)
        vertical_onehot = plane_hots(query_page[1], key_page[1], plane_bins)
        across_part = jnp.einsum(
            "cd,dof->cof",
            horizontal_bias_table,
            horizontal_onehot,
            preferred_element_type=jnp.float32,
        )
        upward_part = jnp.einsum(
            "cd,dof->cof", vertical_bias_table, vertical_onehot, preferred_element_type=jnp.float32
        )
        return across_part + upward_part

    bias = reading_bias_part[None] + lax.map(page_bias, (query_pages, key_pages))
    query_heads = queries.reshape(page_count, row_count, head_count, head_size)

    def attention_scores(key_source):
        key_heads = key_source.reshape(page_count, key_count, head_count, head_size)
        scores = (
            jnp.einsum(
                "pqhe,pkhe->phqk", query_heads, key_heads, preferred_element_type=jnp.float32
            )
            * score_scale
            + bias
        )
        return jnp.where(key_mask[:, None, None, :], scores, masked_score)

    scores = attention_scores(key_all)
    row_max = jnp.max(scores, axis=-1, keepdims=True)
    shifted_exp = jnp.exp(scores - row_max)
    row_total = jnp.sum(shifted_exp, axis=-1, keepdims=True)
    log_total = row_max + jnp.log(row_total)
    weights_low = (shifted_exp / row_total).astype(jnp.bfloat16)
    value_heads = value_all.reshape(page_count, key_count, head_count, head_size)
    mixture = jnp.einsum(
        "phqk,pkhe->pqhe", weights_low, value_heads, preferred_element_type=jnp.float32
    )
    mixture_low = mixture.reshape(page_count, row_count, model_width).astype(jnp.bfloat16)
    attention = flat_dot(mixture_low, out_weight) + out_offset
    first_input = hidden + attention
    normed = layer_norm(first_input, first_gain, first_shift)
    normed_low = normed.astype(jnp.bfloat16)
    up_branch = flat_dot(normed_low, up_weight) + up_offset
    activated_low = gelu_exact(up_branch).astype(jnp.bfloat16)
    down_branch = flat_dot(activated_low, down_weight) + down_offset
    second_input = normed + down_branch
    output = layer_norm(second_input, second_gain, second_shift)
    delta_output = jnp.concatenate([cotangent, patch_cotangent], axis=1).astype(jnp.float32)
    second_pullback = jax.vjp(layer_norm, second_input, second_gain, second_shift)[1]
    delta_second, delta_second_gain, delta_second_shift = second_pullback(delta_output)
    delta_down = delta_second.astype(jnp.bfloat16)
    delta_down_offset = row_sum(delta_down)
    delta_down_matrix = outer_dot(activated_low, delta_down)
    delta_activated = back_dot(delta_down, down_weight)
    delta_up = jax.vjp(gelu_exact, up_branch)[1](delta_activated)[0].astype(jnp.bfloat16)
    delta_up_offset = row_sum(delta_up)
    delta_up_matrix = outer_dot(normed_low, delta_up)
    delta_normed = delta_second + back_dot(delta_up, up_weight)
    first_pullback = jax.vjp(layer_norm, first_input, first_gain, first_shift)[1]
    delta_first, delta_first_gain, delta_first_shift = first_pullback(delta_normed)
    delta_attention = delta_first.astype(jnp.bfloat16)
    delta_out_offset = row_sum(delta_attention)
    delta_out_matrix = outer_dot(mixture_low, delta_attention)
    delta_mixture = back_dot(delta_attention, out_weight).astype(jnp.bfloat16)
    key_back, value_back = key_all, value_all
    key_back_heads = key_back.reshape(page_count, key_count, head_count, head_size)
    value_back_heads = value_back.reshape(page_count, key_count, head_count, head_size)
    weights_again = jnp.exp(attention_scores(key_back) - log_total)
    weights_again_low = weights_again.astype(jnp.bfloat16)
    delta_heads = delta_mixture.reshape(page_count, row_count, head_count, head_size)
    delta_weights = jnp.einsum(
        "pqhe,pkhe->phqk", delta_heads, value_back_heads, preferred_element_type=jnp.float32
    )
    scores_gradient = (
        weights_again
        * (delta_weights - jnp.sum(weights_again * delta_weights, axis=-1, keepdims=True))
    ).astype(jnp.bfloat16)
    delta_queries = (
        (
            jnp.einsum(
                "phqk,pkhe->pqhe",
                scores_gradient,
                key_back_heads,
                preferred_element_type=jnp.float32,
            )
            * score_scale
        )
        .reshape(page_count, row_count, model_width)
        .astype(jnp.bfloat16)
    )
    delta_key_all = (
        jnp.einsum(
            "phqk,pqhe->pkhe", scores_gradient, query_heads, preferred_element_type=jnp.float32
        )
        * score_scale
    ).reshape(page_count, key_count, model_width)
    delta_value_all = jnp.einsum(
        "phqk,pqhe->pkhe", weights_again_low, delta_heads, preferred_element_type=jnp.float32
    ).reshape(page_count, key_count, model_width)
    delta_key_sum, delta_value_sum = (
        lax.psum_scatter(
            delta_key_all.astype(jnp.bfloat16), "seq", scatter_dimension=1, tiled=True
        ).astype(jnp.float32),
        lax.psum_scatter(
            delta_value_all.astype(jnp.bfloat16), "seq", scatter_dimension=1, tiled=True
        ).astype(jnp.float32),
    )
    delta_keys = delta_key_sum.astype(jnp.bfloat16)
    delta_values = delta_value_sum.astype(jnp.bfloat16)
    delta_line = jnp.einsum(
        "aiey,jey->ij", scores_gradient, reading_onehot, preferred_element_type=jnp.float32
    )

    def page_delta(page_inputs):
        page_gradient_rows, query_page, key_page = page_inputs
        horizontal_onehot = plane_hots(query_page[0], key_page[0], plane_bins)
        vertical_onehot = plane_hots(query_page[1], key_page[1], plane_bins)
        across_sum = jnp.einsum(
            "iwu,twu->it", page_gradient_rows, horizontal_onehot, preferred_element_type=jnp.float32
        )
        upward_sum = jnp.einsum(
            "iwu,twu->it", page_gradient_rows, vertical_onehot, preferred_element_type=jnp.float32
        )
        return (across_sum, upward_sum)

    across_parts, upward_parts = lax.map(page_delta, (scores_gradient, query_pages, key_pages))
    delta_across = jnp.sum(across_parts, axis=0)
    delta_upward = jnp.sum(upward_parts, axis=0)
    delta_query_offset = row_sum(delta_queries)
    delta_value_offset = row_sum(delta_values)
    delta_query_matrix = outer_dot(hidden_low, delta_queries)
    delta_key_matrix = outer_dot(hidden_low, delta_keys)
    delta_value_matrix = outer_dot(hidden_low, delta_values)
    delta_hidden = (
        delta_first
        + back_dot(delta_queries, query_weight)
        + back_dot(delta_keys, key_weight)
        + back_dot(delta_values, value_weight)
    )
    delta_position = delta_hidden[:, :span_size].astype(jnp.bfloat16)
    delta_rim = with_halo(delta_position, (("seq", 1),), 3)
    delta_masked = jnp.zeros((page_count, span_size, model_width), jnp.float32)
    tap_columns = []
    for dilation in (1, 2, 3):
        for offset in (-1, 0, 1):
            column = 3 * (dilation - 1) + offset + 1
            anchor = 3 + offset * dilation
            anchor_back = 3 - offset * dilation
            delta_masked = (
                delta_masked
                + delta_rim[:, anchor_back : anchor_back + span_size, :] * conv_taps[:, column]
            )
            tap_columns.append(
                jnp.einsum(
                    "ptd,ptd->d",
                    delta_position,
                    rimmed[:, anchor : anchor + span_size, :],
                    preferred_element_type=jnp.float32,
                )
            )
    delta_taps = jnp.stack(tap_columns, axis=1)
    tokens_gradient = delta_hidden[:, :span_size] + delta_masked * text_factor.astype(jnp.float32)
    delta_patch_position = delta_hidden[:, span_size:].astype(jnp.bfloat16)
    delta_patch_rim = with_halo(delta_patch_position, (("seq", 1),), reach)
    delta_patch_masked = jnp.zeros((page_count, patch_span, model_width), jnp.float32)
    patch_columns = []
    for vertical in (-1, 0, 1):
        for horizontal in (-1, 0, 1):
            column = 3 * (vertical + 1) + horizontal + 1
            anchor = reach + vertical * GRID_SIDE + horizontal
            anchor_back = reach - vertical * GRID_SIDE - horizontal
            delta_patch_masked = (
                delta_patch_masked
                + delta_patch_rim[:, anchor_back : anchor_back + patch_span, :]
                * patch_taps[:, column]
            )
            patch_columns.append(
                jnp.einsum(
                    "ptd,ptd->d",
                    delta_patch_position,
                    patch_rimmed[:, anchor : anchor + patch_span, :],
                    preferred_element_type=jnp.float32,
                )
            )
    delta_patch_taps = jnp.stack(patch_columns, axis=1)
    patches_gradient = delta_hidden[:, span_size:] + delta_patch_masked * patch_factor.astype(
        jnp.float32
    )
    matrix_parts = [
        scatter_sum(matrix.astype(jnp.bfloat16), x_first)
        for matrix, x_first in (
            (delta_query_matrix, True),
            (delta_key_matrix, True),
            (delta_value_matrix, False),
            (delta_out_matrix, False),
            (delta_up_matrix, True),
            (delta_down_matrix, False),
        )
    ]
    vector_parts = total_sum(
        (
            delta_taps,
            delta_patch_taps,
            delta_query_offset,
            delta_value_offset,
            delta_out_offset,
            delta_up_offset,
            delta_down_offset,
            delta_first_gain,
            delta_first_shift,
            delta_second_gain,
            delta_second_shift,
            delta_line,
            delta_across,
            delta_upward,
        )
    )
    return (
        output[:, :span_size],
        output[:, span_size:],
        tokens_gradient,
        patches_gradient,
        matrix_parts[0],
        matrix_parts[1],
        matrix_parts[2],
        matrix_parts[3],
        matrix_parts[4],
        matrix_parts[5],
        vector_parts[0],
        vector_parts[1],
        vector_parts[2],
        vector_parts[3],
        vector_parts[4],
        vector_parts[5],
        vector_parts[6],
        vector_parts[7],
        vector_parts[8],
        vector_parts[9],
        vector_parts[10],
        vector_parts[11],
        vector_parts[12],
        vector_parts[13],
    )


def solution(mesh):
    in_specs = (
        P("page", "seq", None),
        P("page", "seq", None),
        P("page"),
        P(None, "page", None),
        P(),
        P(),
        P(),
        P(),
        P(),
        P(),
        P(),
        P(),
        P(),
        P(),
        P(),
        P(),
        P(),
        P(),
        P(),
        P(),
        P(),
        P(),
        P(),
        P(),
        P("page", "seq", None),
        P("page", "seq", None),
    )
    out_specs = (
        P("page", "seq", None),
        P("page", "seq", None),
        P("page", "seq", None),
        P("page", "seq", None),
        P("page", "seq"),
        P("page", "seq"),
        P("page", "seq"),
        P("page", "seq"),
        P("page", "seq"),
        P("page", "seq"),
        P(),
        P(),
        P(),
        P(),
        P(),
        P(),
        P(),
        P(),
        P(),
        P(),
        P(),
        P(),
        P(),
        P(),
    )
    return jax.shard_map(shards, mesh=mesh, in_specs=in_specs, out_specs=out_specs, check_vma=False)
```

```python
import functools

import jax
import jax.numpy as jnp
from jax import lax
from jax.experimental import pallas as pl
from jax.experimental.pallas import tpu as pltpu
from jax.sharding import PartitionSpec as P

GRID_SIDE = 8


epsilon = 1e-05
coordinate_step = 16
masked_score = -1000000000.0
patch_pitch = 146
patch_centre = 73


def with_halo(cells, sides, width):
    for axis, dim in sides:
        count = lax.axis_size(axis)
        ends = count - 1
        head = lax.slice_in_dim(cells, 0, width, axis=dim)
        tail = lax.slice_in_dim(cells, cells.shape[dim] - width, cells.shape[dim], axis=dim)
        cells = jnp.concatenate(
            [
                lax.ppermute(tail, axis, [(i, (i + 1) % count) for i in range(ends)]),
                cells,
                lax.ppermute(head, axis, [((i + 1) % count, i) for i in range(ends)]),
            ],
            axis=dim,
        )
    return cells


def layer_norm(values, gain_vector, shift_vector):
    row_mean = jnp.mean(values, axis=-1, keepdims=True)
    centred = values - row_mean
    variance = jnp.mean(centred * centred, axis=-1, keepdims=True)
    return centred * lax.rsqrt(variance + epsilon) * gain_vector + shift_vector


def gelu_exact(values):
    return jax.nn.gelu(values, approximate=False)


def flat_dot(operand, matrix):
    front = operand.shape[:-1]
    result = jnp.dot(
        operand.reshape(-1, operand.shape[-1]), matrix, preferred_element_type=jnp.float32
    )
    return result.reshape(front + (matrix.shape[-1],))


def back_dot(operand, matrix):
    front = operand.shape[:-1]
    result = lax.dot_general(
        operand.reshape(-1, operand.shape[-1]),
        matrix,
        (((1,), (1,)), ((), ())),
        preferred_element_type=jnp.float32,
    )
    return result.reshape(front + (matrix.shape[0],))


def outer_dot(operand, gradient):
    return lax.dot_general(
        operand.reshape(-1, operand.shape[-1]),
        gradient.reshape(-1, gradient.shape[-1]),
        (((0,), (0,)), ((), ())),
        preferred_element_type=jnp.float32,
    )


def row_sum(gradient):
    return jnp.sum(gradient.astype(jnp.float32).reshape(-1, gradient.shape[-1]), axis=0)


def swap(value, axis, bit):
    count = lax.axis_size(axis)
    return lax.ppermute(value, axis, [(i, i ^ bit) for i in range(count)])


def total_sum(vectors):
    flat = jnp.concatenate([vector.reshape(-1) for vector in vectors])
    flat = jnp.pad(flat, (0, -flat.size % 1024)).reshape(-1, 128)
    for bit in (1, 2):
        flat = flat + swap(flat, "seq", bit)
    bit = 1
    while bit < lax.axis_size("page"):
        flat = flat + swap(flat, "page", bit)
        bit *= 2
    flat = flat.reshape(-1)
    result, start = [], 0
    for vector in vectors:
        result.append(flat[start : start + vector.size].reshape(vector.shape))
        start += vector.size
    return result


def query_places(seq_index, shape, span, patch_span, text_slots):
    row = lax.broadcasted_iota(jnp.int32, shape, 0)
    return jnp.where(
        row < span, seq_index * span + row, text_slots + seq_index * patch_span + row - span
    )


FIXED = 2048.0


def lookup(table_row, lanes):
    return jnp.take_along_axis(jnp.broadcast_to(table_row, lanes.shape), lanes, axis=1)


def pair_masked(pair):
    lane = lax.broadcasted_iota(jnp.int32, pair.shape, 1)
    half = pair.shape[1] // 2
    zero = jnp.zeros_like(pair)
    return jnp.concatenate(
        [jnp.where(lane < half, pair, zero), jnp.where(lane < half, zero, pair)], axis=0
    )


def pair_merged(both):
    rows, width = both.shape[0] // 2, both.shape[1]
    lane = lax.broadcasted_iota(jnp.int32, (rows, width), 1)
    return jnp.where(lane < width // 2, both[:rows], both[rows:])


def dot_nt(left, right):
    return lax.dot_general(left, right, (((1,), (1,)), ((), ())), preferred_element_type=jnp.float32)


def dot_nn(left, right):
    return lax.dot_general(left, right, (((1,), (0,)), ((), ())), preferred_element_type=jnp.float32)


def dot_tn(left, right):
    return lax.dot_general(left, right, (((0,), (0,)), ((), ())), preferred_element_type=jnp.float32)


CHUNK = 16


def line_kernel(scalar_ref, table_ref, bias_ref, lane_ref):
    pairs, row_count, key_pad = bias_ref.shape
    patch_span = GRID_SIDE * GRID_SIDE // 4
    span = row_count - patch_span
    key = lax.broadcasted_iota(jnp.int32, (row_count, key_pad), 1)
    place = query_places(scalar_ref[0], (row_count, key_pad), span, patch_span, 4 * span)
    lane_ref[...] = jnp.clip(key - place, -16, 15) + 16

    def fill(pair, carry):
        row = table_ref[pl.ds(pair, 1), :]
        for at in range(0, key_pad, 128):
            bias_ref[pair, :, at : at + 128] = lookup(row, lane_ref[:, at : at + 128])
        return carry

    lax.fori_loop(0, pairs, fill, 0)


def line_bias(scalars, table, pairs, row_count, key_pad):
    return pl.pallas_call(
        line_kernel,
        out_shape=jax.ShapeDtypeStruct((pairs, row_count, key_pad), jnp.int32),
        in_specs=[pl.BlockSpec(memory_space=pltpu.SMEM)] + in_vmem(1),
        out_specs=in_vmem(1)[0],
        scratch_shapes=[pltpu.VMEM((row_count, key_pad), jnp.int32)],
        compiler_params=pltpu.CompilerParams(vmem_limit_bytes=KERNEL_VMEM),
        cost_estimate=pl.CostEstimate(flops=2_000_000, bytes_accessed=2_300_000, transcendentals=0),
        name="line_bias",
    )(scalars, table)


def forward_kernel(
    scalar_ref, columns_ref, rows_ref, block0, block1, block2, block3, taps_ref, patch_taps_ref,
    query_weight_ref, key_weight_ref, value_weight_ref, query_bias_ref, value_bias_ref,
    plane_table_ref, line_ref,
    hidden_ref, hidden_low_ref, query_ref, key_ref, value_ref, mixture_ref, weights_ref,
    text, grid, low, scores, across_ref, upward_ref, live_ref,
):
    seq_index, length = scalar_ref[0], scalar_ref[1]
    row_count, width = hidden_ref.shape
    key_pad = key_ref.shape[0]
    blocks = (block0, block1, block2, block3)
    count = len(blocks)
    patch_span = grid.shape[0] // (count + 2)
    span = row_count - patch_span
    text_slots = span * count
    rim = 8
    text[0:rim, :] = jnp.zeros((rim, width), jnp.float32)
    text[rim + text_slots :, :] = jnp.zeros((rim, width), jnp.float32)
    grid[0:patch_span, :] = jnp.zeros((patch_span, width), jnp.float32)
    grid[patch_span * (count + 1) :, :] = jnp.zeros((patch_span, width), jnp.float32)
    for step, block in enumerate(blocks):
        where = seq_index ^ step
        place = where * span + lax.broadcasted_iota(jnp.int32, (span, 1), 0)
        text[pl.ds(pl.multiple_of(rim + where * span, 8), span), :] = jnp.where(
            place < length, block[0:span, :].astype(jnp.float32), 0.0
        )
        cell = where * patch_span + lax.broadcasted_iota(jnp.int32, (patch_span, 1), 0)
        live = ((cell >> 3) < GRID_SIDE - 1) & ((cell & 7) < GRID_SIDE - 1)
        grid[pl.ds(pl.multiple_of(patch_span + where * patch_span, 8), patch_span), :] = jnp.where(
            live, block[span:row_count, :].astype(jnp.float32), 0.0
        )
    low[row_count * count :, :] = jnp.zeros((key_pad - row_count * count, width), jnp.bfloat16)
    lanes = 256
    for step, block in enumerate(blocks):
        where = seq_index ^ step

        def convolve(tile, carry):
            at = pl.ds(pl.multiple_of(tile * lanes, lanes), lanes)
            window = text[pl.ds(pl.multiple_of(where * span, 8), span + 2 * rim), at]
            centre = taps_ref[1:2, at] + taps_ref[4:5, at] + taps_ref[7:8, at]
            total = block[0:span, at].astype(jnp.float32) + window[rim : rim + span] * centre
            for dilation in (1, 2, 3):
                for offset in (-1, 1):
                    column = 3 * (dilation - 1) + offset + 1
                    anchor = rim + offset * dilation
                    total = total + window[anchor : anchor + span] * taps_ref[column : column + 1, at]
            low[pl.ds(pl.multiple_of(where * span, 16), span), at] = total.astype(jnp.bfloat16)
            window = grid[pl.ds(pl.multiple_of(where * patch_span, 8), 3 * patch_span), at]
            patch_total = block[span:row_count, at].astype(jnp.float32)
            for vertical in (-1, 0, 1):
                for horizontal in (-1, 0, 1):
                    column = 3 * (vertical + 1) + horizontal + 1
                    anchor = patch_span + vertical * GRID_SIDE + horizontal
                    patch_total = (
                        patch_total
                        + window[anchor : anchor + patch_span]
                        * patch_taps_ref[column : column + 1, at]
                    )
            low[pl.ds(pl.multiple_of(text_slots + where * patch_span, 16), patch_span), at] = (
                patch_total.astype(jnp.bfloat16)
            )
            if step == 0:
                hidden_ref[0:span, at] = total
                hidden_ref[span:row_count, at] = patch_total
                hidden_low_ref[0:span, at] = total.astype(jnp.bfloat16)
                hidden_low_ref[span:row_count, at] = patch_total.astype(jnp.bfloat16)
            return carry

        lax.fori_loop(0, width // lanes, convolve, 0)

    def project(tile, carry):
        at = pl.ds(pl.multiple_of(tile * lanes, lanes), lanes)
        key_ref[:, at] = dot_nn(low[...], key_weight_ref[:, at]).astype(jnp.bfloat16)
        value_ref[:, at] = (dot_nn(low[...], value_weight_ref[:, at]) + value_bias_ref[:, at]).astype(
            jnp.bfloat16
        )
        query_ref[:, at] = (
            (dot_nn(hidden_low_ref[...], query_weight_ref[:, at]) + query_bias_ref[:, at])
            .astype(jnp.bfloat16)
            * jnp.bfloat16(0.125)
        )
        return carry

    lax.fori_loop(0, width // lanes, project, 0)
    columns, rows = columns_ref[...], rows_ref[...]
    across_ref[...] = jnp.clip((rows[0:1, :] - columns[:, 0:1]) >> 4, -32, 31) + 32
    upward_ref[...] = jnp.clip((rows[1:2, :] - columns[:, 1:2]) >> 4, -32, 31) + 96
    key = lax.broadcasted_iota(jnp.int32, live_ref.shape, 1)
    cell = key - text_slots
    live = (key < length) | (
        (cell >= 0) & ((cell >> 3) < GRID_SIDE - 1) & ((cell & 7) < GRID_SIDE - 1)
    )
    live_ref[...] = jnp.where(live, 0.0, masked_score * FIXED)
    pair_width = 128
    power = 1.4426950408889634 / FIXED

    def attend(pair, carry):
        at = pl.ds(pl.multiple_of(pair * pair_width, pair_width), pair_width)
        scores[...] = dot_nt(pair_masked(query_ref[:, at] * jnp.bfloat16(FIXED)), key_ref[:, at])
        plane_row = plane_table_ref[pl.ds(pair, 1), :]
        for start in range(0, row_count, CHUNK):
            here = slice(start, start + CHUNK)
            packed = []
            for block_at in range(0, key_pad, 128):
                lane = slice(block_at, block_at + 128)
                packed.append(
                    line_ref[pair, here, lane]
                    + lookup(plane_row, across_ref[here, lane])
                    + lookup(plane_row, upward_ref[here, lane])
                )
            for side in range(2):
                there = slice(side * row_count + start, side * row_count + start + CHUNK)
                parts, top = [], None
                for index, word in enumerate(packed):
                    lane = slice(128 * index, 128 * (index + 1))
                    field = (word >> 16) if side else (word & 0xFFFF)
                    part = (scores[there, lane] + field.astype(jnp.float32)) + live_ref[0:1, lane]
                    top = part if top is None else jnp.maximum(top, part)
                    parts.append(part)
                top = jnp.max(top, axis=1, keepdims=True)
                parts = [jnp.exp2((part - top) * power) for part in parts]
                total = parts[0]
                for part in parts[1:]:
                    total = total + part
                inverse = 1.0 / jnp.sum(total, axis=1, keepdims=True)
                for index, part in enumerate(parts):
                    weights_ref[pair, there, 128 * index : 128 * (index + 1)] = (part * inverse).astype(
                        jnp.bfloat16
                    )
        mixture_ref[:, at] = pair_merged(dot_nn(weights_ref[pair], value_ref[:, at])).astype(jnp.bfloat16)
        return carry

    lax.fori_loop(0, width // pair_width, attend, 0)


VMEM = pltpu.VMEM
KERNEL_VMEM = 48 * 1024 * 1024


def in_vmem(count):
    return [pl.BlockSpec(memory_space=VMEM)] * count


def forward_page(scalars, columns, rows, blocks, taps, patch_taps, matrices, offsets, tables):
    row_count, width = blocks[0].shape
    key_pad = rows.shape[1]
    patch_span = GRID_SIDE * GRID_SIDE // 4
    text_slots = 4 * (row_count - patch_span)
    own = jax.ShapeDtypeStruct((row_count, width), jnp.bfloat16)
    every = jax.ShapeDtypeStruct((key_pad, width), jnp.bfloat16)
    lanes = pltpu.VMEM((row_count, key_pad), jnp.int32)
    return pl.pallas_call(
        forward_kernel,
        out_shape=(
            jax.ShapeDtypeStruct((row_count, width), jnp.float32), own, own, every, every, own,
            jax.ShapeDtypeStruct((width // 128, 2 * row_count, key_pad), jnp.bfloat16),
        ),
        in_specs=[pl.BlockSpec(memory_space=pltpu.SMEM)] + in_vmem(15),
        out_specs=tuple(in_vmem(7)),
        scratch_shapes=[
            pltpu.VMEM((text_slots + 16, width), jnp.float32),
            pltpu.VMEM((6 * patch_span, width), jnp.float32),
            pltpu.VMEM((key_pad, width), jnp.bfloat16),
            pltpu.VMEM((2 * row_count, key_pad), jnp.float32),
            lanes, lanes,
            pltpu.VMEM((8, key_pad), jnp.float32),
        ],
        compiler_params=pltpu.CompilerParams(vmem_limit_bytes=KERNEL_VMEM),
        cost_estimate=pl.CostEstimate(flops=2_600_000_000, bytes_accessed=9_000_000, transcendentals=1_000_000),
        name="forward_page",
    )(scalars, columns, rows, *blocks, taps, patch_taps, *matrices, *offsets, *tables)


def backward_kernel(
    scalar_ref, columns_ref, rows_ref, query_rows_ref, query_ref, key_ref, value_ref, mixture_back_ref, weights_ref,
    query_back_ref, block_back_ref, plane_back_ref, line_back_ref,
    back, steps, mask_ref, hot_ref, query_hot_ref, band_ref,
):
    seq_index = scalar_ref[0]
    row_count, width = query_ref.shape
    key_pad = key_ref.shape[0]
    count = 4
    patch_span = GRID_SIDE * GRID_SIDE // count
    span = row_count - patch_span
    text_slots = span * count
    columns, rows = columns_ref[...], rows_ref[...]
    mask_ref[:, 0:key_pad] = ((rows[0:1, :] & 15) < (columns[:, 0:1] & 15)).astype(jnp.float32).astype(jnp.bfloat16)
    mask_ref[:, key_pad:] = ((rows[1:2, :] & 15) < (columns[:, 1:2] & 15)).astype(jnp.float32).astype(jnp.bfloat16)
    bin_at = lax.broadcasted_iota(jnp.int32, (128, key_pad), 0) - 1
    key_block = lax.broadcasted_iota(jnp.int32, (128, key_pad), 1) >> 4
    for side in range(2):
        key_bin = rows[side : side + 1, :] >> 4
        plain = (key_bin == bin_at).astype(jnp.float32)
        lower = (key_bin - 1 == bin_at).astype(jnp.float32)
        plain, lower = jnp.where(bin_at < 64, plain, 0.0), jnp.where(bin_at < 64, lower, 0.0)
        mine = slice(128 * side, 128 * (side + 1))
        other = slice(128 * (1 - side), 128 * (2 - side))
        change = lower - plain
        if side == 0:
            plain = jnp.where(bin_at - 71 == key_block, 1.0, plain)
        hot_ref[mine, 0:key_pad] = plain.astype(jnp.bfloat16)
        hot_ref[mine, (1 + side) * key_pad : (2 + side) * key_pad] = change.astype(jnp.bfloat16)
        hot_ref[other, (1 + side) * key_pad : (2 + side) * key_pad] = jnp.zeros((128, key_pad), jnp.bfloat16)
    half_bin = lax.broadcasted_iota(jnp.int32, (72, row_count), 0)
    for side in range(2):
        query_hot_ref[72 * side : 72 * (side + 1), :] = (
            (71 - (query_rows_ref[side : side + 1, :] >> 4) == half_bin).astype(jnp.float32).astype(jnp.bfloat16)
        )
    lane128 = lax.broadcasted_iota(jnp.int32, (row_count, 128), 1)
    place = query_places(seq_index, (row_count, 128), span, patch_span, text_slots)
    aim = place + lane128 - 32
    near = (lane128 < 64) & (aim >= 0) & (aim < text_slots + patch_span * count)
    apart = (aim >> 4) - (place >> 4)
    near = near & (apart >= -1) & (apart <= 1)
    band_ref[...] = jnp.where(near, aim, -1)
    pair_width = 128
    line_back_ref[...] = jnp.zeros_like(line_back_ref)
    plane_back_ref[...] = jnp.zeros_like(plane_back_ref)

    def attend(pair, carry):
        at = pl.ds(pl.multiple_of(pair * pair_width, pair_width), pair_width)
        both_query = pair_masked(query_ref[:, at])
        both_back = pair_masked(mixture_back_ref[:, at])
        back[...] = dot_nt(both_back, value_ref[:, at])
        for start in range(0, 2 * row_count, CHUNK):
            there = slice(start, start + CHUNK)
            here = slice(start % row_count, start % row_count + CHUNK)
            parts, total = [], None
            for block_at in range(0, key_pad, 128):
                lane = slice(block_at, block_at + 128)
                part = weights_ref[pair, there, lane].astype(jnp.float32)
                product = part * back[there, lane]
                total = product if total is None else total + product
                parts.append(part)
            mean = jnp.sum(total, axis=1, keepdims=True)
            for index, part in enumerate(parts):
                lane = slice(128 * index, 128 * (index + 1))
                step = (part * (back[there, lane] - mean)).astype(jnp.bfloat16)
                steps[there, lane] = step
                steps[there, key_pad + 128 * index : key_pad + 128 * (index + 1)] = step * mask_ref[here, lane]
                steps[there, 2 * key_pad + 128 * index : 2 * key_pad + 128 * (index + 1)] = (
                    step * mask_ref[here, key_pad + 128 * index : key_pad + 128 * (index + 1)]
                )
        query_back_ref[:, at] = (pair_merged(dot_nn(steps[:, 0:key_pad], key_ref[:, at])) * 0.125).astype(
            jnp.bfloat16
        )
        for kind, value in enumerate(
            (dot_tn(steps[:, 0:key_pad], both_query), dot_tn(weights_ref[pair], both_back))
        ):
            value = value.astype(jnp.bfloat16)
            for where in range(count):
                step_at = seq_index ^ where
                slot = (step_at & 1) * 2 + (step_at >> 1)
                block_back_ref[slot, kind, 0:span, at] = value[where * span : (where + 1) * span]
                block_back_ref[slot, kind, span:row_count, at] = value[
                    text_slots + where * patch_span : text_slots + (where + 1) * patch_span
                ]
        bins = dot_nt(steps[...], hot_ref[...])
        low_bins = bins.astype(jnp.bfloat16)
        lane_one = lax.broadcasted_iota(jnp.int32, (1, 128), 1)
        far = lane128 - 72 - (place >> 4)
        in_line = (lane128 >= 72) & (lane128 < 72 + key_pad // 16)
        for side in range(2):
            head = pl.ds(2 * pair + side, 1)
            own = slice(side * row_count, (side + 1) * row_count)
            both = dot_nn(query_hot_ref[...], low_bins[own])
            for plane in range(2):
                table = both[72 * plane : 72 * (plane + 1), 128 * plane : 128 * (plane + 1)]
                wide_lane = lax.broadcasted_iota(jnp.int32, table.shape, 1)
                table = jnp.where(wide_lane < 72, table, 0.0)
                table = jnp.concatenate([table, jnp.zeros_like(table)], axis=1)
                sheared = pltpu.roll(table, 0, 1, stride=1, stride_axis=0)
                plane_back_ref[plane, head, :] = jnp.sum(sheared, axis=0, keepdims=True)
            line_bins = bins[own, 0:128]
            low_tail = jnp.sum(jnp.where(in_line & (far <= -2), line_bins, 0.0), axis=(0, 1), keepdims=True)
            high_tail = jnp.sum(jnp.where(in_line & (far >= 2), line_bins, 0.0), axis=(0, 1), keepdims=True)
            band = jnp.zeros((1, 128), jnp.float32)
            base = side * row_count
            for first, rows_here, block in (
                (0, span, seq_index),
                (0, 32, jnp.maximum(seq_index - 1, 0)),
                (span - 32, 32, seq_index + 1),
                (span, patch_span, count - 1),
                (span, patch_span, count),
            ):
                aims = band_ref[first : first + rows_here, :]
                source = steps[
                    base + first : base + first + rows_here, pl.ds(pl.multiple_of(block * 128, 128), 128)
                ].astype(jnp.float32)
                taken = jnp.take_along_axis(source, aims & 127, axis=1)
                right = (aims >> 7) == block
                if first == 0 and rows_here == 32:
                    right = right & (seq_index > 0)
                band = band + jnp.sum(jnp.where(right, taken, 0.0), axis=0, keepdims=True)
            line_back_ref[head, :] = (
                band + jnp.where(lane_one == 0, low_tail, 0.0) + jnp.where(lane_one == 63, high_tail, 0.0)
            )
        return carry

    lax.fori_loop(0, width // pair_width, attend, 0)


def backward_page(scalars, columns, rows, query_rows, queries, keys, values, mixture_back, weights):
    row_count, width = queries.shape
    key_pad = keys.shape[0]
    heads = 2 * weights.shape[0]
    return pl.pallas_call(
        backward_kernel,
        out_shape=(
            jax.ShapeDtypeStruct((row_count, width), jnp.bfloat16),
            jax.ShapeDtypeStruct((4, 2, row_count, width), jnp.bfloat16),
            jax.ShapeDtypeStruct((2, heads, 256), jnp.float32),
            jax.ShapeDtypeStruct((heads, 128), jnp.float32),
        ),
        in_specs=[pl.BlockSpec(memory_space=pltpu.SMEM)] + in_vmem(8),
        out_specs=tuple(in_vmem(4)),
        scratch_shapes=[
            pltpu.VMEM((2 * row_count, key_pad), jnp.float32),
            pltpu.VMEM((2 * row_count, 3 * key_pad), jnp.bfloat16),
            pltpu.VMEM((row_count, 2 * key_pad), jnp.bfloat16),
            pltpu.VMEM((256, 3 * key_pad), jnp.bfloat16),
            pltpu.VMEM((144, row_count), jnp.bfloat16),
            pltpu.VMEM((row_count, 128), jnp.int32),
        ],
        compiler_params=pltpu.CompilerParams(vmem_limit_bytes=KERNEL_VMEM),
        cost_estimate=pl.CostEstimate(flops=3_000_000_000, bytes_accessed=6_000_000, transcendentals=1_000_000),
        name="backward_page",
    )(scalars, columns, rows, query_rows, queries, keys, values, mixture_back, weights)


def block_slots(scalar_ref, page, column, levels):
    far = page ^ scalar_ref[2]
    side = column ^ scalar_ref[3]
    rest = 0
    for level in range(1, levels):
        rest = rest + (((far >> level) & 1) << (levels - 1 - level))
    near = far & 1
    return (side << levels) + (near << (levels - 1)) + rest, (near << levels) + (side << (levels - 1)) + rest


NORM_CHUNK = 48


def norm_rows(values):
    mean = jnp.mean(values, axis=-1, keepdims=True)
    centred = values - mean
    scale = lax.rsqrt(jnp.mean(centred * centred, axis=-1, keepdims=True) + epsilon)
    return centred * scale, scale


def norm_back(delta, unit, scale):
    return scale * (
        delta
        - jnp.mean(delta, axis=-1, keepdims=True)
        - unit * jnp.mean(delta * unit, axis=-1, keepdims=True)
    )


def column_sum(values):
    return jnp.sum(values, axis=0, keepdims=True)


OUT_BIAS, DOWN_BIAS, FIRST_GAIN, FIRST_SHIFT, SECOND_GAIN, SECOND_SHIFT = range(6)
UP_BIAS = 6


def middle_kernel(
    pages, direct,
    scalar_ref, hidden_ref, mixture_ref, cotangent_ref, patch_cotangent_ref, out_weight_ref, up_weight_ref,
    down_weight_ref, vector_ref,
    output_ref, patch_output_ref, first_back_ref, mixture_back_ref, sums_ref, *rest,
):
    if direct:
        bundle_ref, *rest = rest
    else:
        normed_out_ref, up_out_ref, activated_out_ref, down_out_ref, attention_out_ref, *rest = rest
    state, unit, scale_ref, normed, activated, slope, up_back, down_back, attention_back, flipped = rest
    count, span, width = output_ref.shape
    patch_span = patch_output_ref.shape[1]
    row_count = span + patch_span
    total_rows = count * row_count
    wide = up_weight_ref.shape[1]
    lanes = 256
    sums_ref[...] = jnp.zeros_like(sums_ref)

    def tile_at(tile):
        return pl.ds(pl.multiple_of(tile * lanes, lanes), lanes)

    def attention_tile(tile, carry):
        at = tile_at(tile)
        state[:, at] = hidden_ref[:, at] + (dot_nn(mixture_ref[...], out_weight_ref[:, at]) + vector_ref[2:3, at])
        return carry

    lax.fori_loop(0, width // lanes, attention_tile, 0)

    def first_norm(chunk, carry):
        here = pl.ds(pl.multiple_of(chunk * NORM_CHUNK, 16), NORM_CHUNK)
        rows, scale = norm_rows(state[here, :])
        unit[here, :] = rows
        scale_ref[here, :] = jnp.broadcast_to(scale, (NORM_CHUNK, 128))
        rows = rows * vector_ref[4:5, :] + vector_ref[5:6, :]
        state[here, :] = rows
        normed[here, :] = rows.astype(jnp.bfloat16)
        return carry

    lax.fori_loop(0, total_rows // NORM_CHUNK, first_norm, 0)

    def up_tile(tile, carry):
        at = tile_at(tile)
        branch = dot_nn(normed[...], up_weight_ref[:, at]) + vector_ref[pl.ds(8 + tile // 3, 1), tile_at(tile % 3)]
        chance = 0.5 * (1.0 + lax.erf(branch * 0.7071067811865476))
        activated[:, at] = (branch * chance).astype(jnp.bfloat16)
        slope[:, at] = chance + branch * (jnp.exp(branch * branch * -0.5) * 0.3989422804014327)
        return carry

    lax.fori_loop(0, wide // lanes, up_tile, 0)

    def down_tile(tile, carry):
        at = tile_at(tile)
        state[:, at] = state[:, at] + (dot_nn(activated[...], down_weight_ref[:, at]) + vector_ref[3:4, at])
        return carry

    lax.fori_loop(0, width // lanes, down_tile, 0)

    def second_norm(start, rows_here, page, out_ref, delta_ref):
        here = pl.ds(pl.multiple_of(page * row_count + start, 16), rows_here)
        there = pl.ds(0 if start == span else start, rows_here)
        rows, scale = norm_rows(state[here, :])
        out_ref[page, there, :] = rows * vector_ref[6:7, :] + vector_ref[7:8, :]
        delta = delta_ref[page, there, :].astype(jnp.float32)
        back = norm_back(delta * vector_ref[6:7, :], rows, scale)
        state[here, :] = back
        low = back.astype(jnp.bfloat16)
        down_back[here, :] = low
        for index, value in (
            (SECOND_GAIN, delta * rows), (SECOND_SHIFT, delta), (DOWN_BIAS, low.astype(jnp.float32))
        ):
            sums_ref[index : index + 1, :] += column_sum(value)

    def second_page(page, carry):
        for start in range(0, span, 32):
            second_norm(start, 32, page, output_ref, cotangent_ref)
        second_norm(span, patch_span, page, patch_output_ref, patch_cotangent_ref)
        return carry

    lax.fori_loop(0, count, second_page, 0)

    def up_back_tile(tile, carry):
        at = tile_at(tile)
        low = (dot_nt(down_back[...], down_weight_ref[at, :]) * slope[:, at]).astype(jnp.bfloat16)
        up_back[:, at] = low
        sums_ref[pl.ds(UP_BIAS + tile // 3, 1), tile_at(tile % 3)] = column_sum(low.astype(jnp.float32))
        return carry

    lax.fori_loop(0, wide // lanes, up_back_tile, 0)

    def normed_back_tile(tile, carry):
        at = tile_at(tile)
        state[:, at] = state[:, at] + dot_nt(up_back[...], up_weight_ref[at, :])
        return carry

    lax.fori_loop(0, width // lanes, normed_back_tile, 0)

    def first_back(chunk, carry):
        here = pl.ds(pl.multiple_of(chunk * NORM_CHUNK, 16), NORM_CHUNK)
        delta, rows = state[here, :], unit[here, :]
        back = norm_back(delta * vector_ref[4:5, :], rows, scale_ref[here, 0:1])
        first_back_ref[here, :] = back
        low = back.astype(jnp.bfloat16)
        attention_back[here, :] = low
        for index, value in (
            (FIRST_GAIN, delta * rows), (FIRST_SHIFT, delta), (OUT_BIAS, low.astype(jnp.float32))
        ):
            sums_ref[index : index + 1, :] += column_sum(value)
        return carry

    lax.fori_loop(0, total_rows // NORM_CHUNK, first_back, 0)

    def mixture_tile(tile, carry):
        at = tile_at(tile)
        mixture_back_ref[:, at] = dot_nt(attention_back[...], out_weight_ref[at, :]).astype(jnp.bfloat16)
        return carry

    lax.fori_loop(0, width // lanes, mixture_tile, 0)
    if not direct:
        normed_out_ref[...] = normed[...]
        up_out_ref[...] = up_back[...]
        activated_out_ref[...] = activated[...]
        down_out_ref[...] = down_back[...]
        attention_out_ref[...] = attention_back[...]
        return
    levels = pages.bit_length() - 1
    core = scalar_ref[1]
    rows = width // pages
    tall = wide // pages
    block = 384
    groups = wide // (2 * block)
    flipped[...] = normed[...].T

    def up_weight_tile(tile, carry):
        column, group = tile // groups, tile % groups
        at = pl.ds(pl.multiple_of(tile * block, block), block)
        result = dot_nn(flipped[...], up_back[:, at]).astype(jnp.bfloat16)
        for page in range(pages):
            slot = block_slots(scalar_ref, page, column, levels)[0]
            bundle_ref[core, slot, pl.ds(pl.multiple_of(group * rows, 16), rows), :] = result[
                page * rows : (page + 1) * rows
            ]
        return carry

    lax.fori_loop(0, 2 * groups, up_weight_tile, 0)

    def down_weight_tile(page, carry):
        at = pl.ds(pl.multiple_of(page * tall, 128), tall)
        result = dot_tn(activated[:, at], down_back[...]).astype(jnp.bfloat16)
        for column in range(2):
            slot = block_slots(scalar_ref, page, column, levels)[1]
            bundle_ref[1 - core, slot, 0:tall, :] = result[:, column * block : (column + 1) * block]
        return carry

    lax.fori_loop(0, pages, down_weight_tile, 0)
    flipped[...] = mixture_ref[...].T
    half = rows // 2

    def out_weight_tile(column, carry):
        at = pl.ds(pl.multiple_of(column * block, block), block)
        result = dot_nn(flipped[...], attention_back[:, at]).astype(jnp.bfloat16)
        for page in range(pages):
            slots = block_slots(scalar_ref, page, column, levels)
            for order in range(2):
                first = page * rows + order * half
                bundle_ref[core if order == 0 else 1 - core, slots[order], tall : tall + half, :] = result[
                    first : first + half
                ]
        return carry

    lax.fori_loop(0, 2, out_weight_tile, 0)


def middle(places, hidden, mixture, cotangent, patch_cotangent, matrices, vectors, pages):
    count, span, width = cotangent.shape
    patch_span = patch_cotangent.shape[1]
    total_rows = hidden.shape[0]
    wide = matrices[1].shape[1]
    direct = (width // pages) % 32 == 0
    bf16, f32 = jnp.bfloat16, jnp.float32
    if direct:
        extra = (jax.ShapeDtypeStruct((2, 2 * pages, (wide + width // 2) // pages, 384), bf16),)
    else:
        extra = tuple(
            jax.ShapeDtypeStruct((total_rows, size), bf16) for size in (width, wide, wide, width, width)
        )
    result = pl.pallas_call(
        functools.partial(middle_kernel, pages, direct),
        out_shape=(
            jax.ShapeDtypeStruct(cotangent.shape, f32),
            jax.ShapeDtypeStruct(patch_cotangent.shape, f32),
            jax.ShapeDtypeStruct((total_rows, width), f32),
            jax.ShapeDtypeStruct((total_rows, width), bf16),
            jax.ShapeDtypeStruct((16, width), f32),
        )
        + extra,
        in_specs=[pl.BlockSpec(memory_space=pltpu.SMEM)] + in_vmem(8),
        out_specs=tuple(in_vmem(5 + len(extra))),
        scratch_shapes=[
            pltpu.VMEM((total_rows, width), f32),
            pltpu.VMEM((total_rows, width), f32),
            pltpu.VMEM((total_rows, 128), f32),
            pltpu.VMEM((total_rows, width), bf16),
            pltpu.VMEM((total_rows, wide), bf16),
            pltpu.VMEM((total_rows, wide), f32),
            pltpu.VMEM((total_rows, wide), bf16),
            pltpu.VMEM((total_rows, width), bf16),
            pltpu.VMEM((total_rows, width), bf16),
            pltpu.VMEM((width, total_rows), bf16),
        ],
        compiler_params=pltpu.CompilerParams(vmem_limit_bytes=56 * 1024 * 1024),
        cost_estimate=pl.CostEstimate(flops=14_000_000_000, bytes_accessed=30_000_000, transcendentals=2_600_000),
        name="middle",
    )(places, hidden, mixture, cotangent, patch_cotangent, *matrices, vectors)
    first, rest = result[:5], result[5:]
    if direct:
        return first + rest
    normed, up_back, activated, down_back, attention_back = rest
    return first + (
        indexed_bundle(
            (
                ((normed, up_back, None), (mixture, attention_back, 0)),
                ((activated, down_back, None), (mixture, attention_back, 1)),
            ),
            places,
            pages,
        ),
    )


def indexed_bundle(matrices, scalars, pages):
    levels = pages.bit_length() - 1
    place = jnp.arange(2 * pages, dtype=jnp.int32)
    bits = [(place >> (levels - k)) & 1 for k in range(levels + 1)]
    halves = []
    for order, group in enumerate(matrices):
        side, near = (bits[0], bits[1]) if order == 0 else (bits[1], bits[0])
        far = near
        for level in range(1, levels):
            far = far + (bits[level + 1] << level)
        index = (far ^ scalars[2]) * 2 + (side ^ scalars[3])
        blocks = []
        for operand, gradient, part in group:
            rows = in_blocks(outer_dot(operand, gradient).astype(jnp.bfloat16), pages)
            if part is not None:
                half = rows.shape[1] // 2
                rows = rows[:, part * half : (part + 1) * half]
            blocks.append(rows)
        halves.append(jnp.concatenate(blocks, axis=1)[index])
    first, second = halves
    mine = scalars[1] == 0
    return jnp.stack([jnp.where(mine, first, second), jnp.where(mine, second, first)])


def attention_weight_kernel(
    pages, scalar_ref, hidden_ref, query_back_ref, key_back_ref, value_back_ref, out_ref, flipped
):
    levels = pages.bit_length() - 1
    core = scalar_ref[1]
    rows = hidden_ref.shape[1] // pages
    half = rows // 2
    lanes = out_ref.shape[3]
    flipped[...] = hidden_ref[...].T

    def tile(column, carry):
        at = pl.ds(pl.multiple_of(column * lanes, lanes), lanes)
        for index, back_ref in enumerate((query_back_ref, key_back_ref, value_back_ref)):
            result = dot_nn(flipped[...], back_ref[:, at]).astype(jnp.bfloat16)
            for page in range(pages):
                slots = block_slots(scalar_ref, page, column, levels)
                first = page * rows
                if index < 2:
                    where = core if index == 0 else 1 - core
                    out_ref[where, slots[index], 0:rows, :] = result[first : first + rows]
                else:
                    out_ref[core, slots[0], rows : rows + half, :] = result[first : first + half]
                    out_ref[1 - core, slots[1], rows : rows + half, :] = result[first + half : first + rows]
        return carry

    lax.fori_loop(0, 2, tile, 0)


def in_blocks(matrix, pages):
    rows, columns = matrix.shape[0] // pages, matrix.shape[1] // 2
    lanes = min(columns, 384)
    blocks = matrix.reshape(pages, rows, 2, columns // lanes, lanes)
    return blocks.transpose(0, 2, 3, 1, 4).reshape(pages * 2, rows * columns // lanes, lanes)


def attention_bundle(places, operands, pages):
    hidden, query_back, key_back, value_back = operands
    width = hidden.shape[1]
    if (width // pages) % 32:
        return indexed_bundle(
            (
                ((hidden, query_back, None), (hidden, value_back, 0)),
                ((hidden, key_back, None), (hidden, value_back, 1)),
            ),
            places,
            pages,
        )
    return pl.pallas_call(
        functools.partial(attention_weight_kernel, pages),
        out_shape=jax.ShapeDtypeStruct((2, 2 * pages, 3 * width // (2 * pages), 384), jnp.bfloat16),
        in_specs=[pl.BlockSpec(memory_space=pltpu.SMEM)] + in_vmem(4),
        out_specs=in_vmem(1)[0],
        scratch_shapes=[pltpu.VMEM(hidden.shape[::-1], jnp.bfloat16)],
        compiler_params=pltpu.CompilerParams(vmem_limit_bytes=KERNEL_VMEM),
        cost_estimate=pl.CostEstimate(flops=1_600_000_000, bytes_accessed=10_000_000, transcendentals=0),
        name="attention_weights",
    )(places, *operands)


def exchange(value, pages, step):
    moves = []
    for page in range(pages):
        for seq in range(4):
            on_page, on_seq = page, seq
            if (seq % 2 == step) if step < 2 else False:
                on_seq = seq ^ 2
            else:
                on_page = page ^ (1 if step < 2 else 1 << (step - 1))
            moves.append((page * 4 + seq, on_page * 4 + on_seq))
    return lax.ppermute(value, ("page", "seq"), moves)


def added(kept, got):
    return (kept.astype(jnp.float32) + got.astype(jnp.float32)).astype(jnp.bfloat16)


def bundle_sum(state, pages):
    for step in range(pages.bit_length()):
        half = state.shape[0] // 2
        state = added(state[:half], exchange(state[half:], pages, step))
    return state[0]


def bundle_parts(state, wide_rows, core):
    lanes = state.shape[1] // 2
    first = core == 0
    tail = state[wide_rows:]
    if wide_rows > 2 * tail.shape[0]:
        group = state[:wide_rows].reshape(4, wide_rows // 4, 2 * lanes)
        low = group[:2].transpose(1, 0, 2).reshape(-1, lanes)
        high = group[2:].transpose(1, 0, 2).reshape(-1, lanes)
    else:
        low, high = state[:wide_rows, :lanes], state[:wide_rows, lanes:]
    left, right = state[:wide_rows, :lanes], state[:wide_rows, lanes:]
    sent = jnp.concatenate(
        [jnp.where(first, high, left), jnp.where(first, tail[:, lanes:], tail[:, :lanes])], axis=0
    )
    got = swap(sent, "seq", 1)
    kept_tail = jnp.where(first, tail[:, :lanes], tail[:, lanes:])
    one = jnp.where(first, low, got[:wide_rows])
    two = jnp.where(first, got[:wide_rows], right)
    three = jnp.concatenate(
        [jnp.where(first, kept_tail, got[wide_rows:]), jnp.where(first, got[wide_rows:], kept_tail)], axis=0
    )
    return [value.astype(jnp.float32) for value in (one, two, three)]


def grid_live(cells):
    return (cells // GRID_SIDE < GRID_SIDE - 1) & (cells % GRID_SIDE < GRID_SIDE - 1)


def grid_boxes(cells):
    return jnp.stack(
        [
            patch_pitch * (cells % GRID_SIDE) + patch_centre,
            patch_pitch * (cells // GRID_SIDE) + patch_centre,
        ]
    )


def shards(
    tokens,
    patches,
    page_length,
    box_position,
    query_weight,
    key_weight,
    value_weight,
    out_weight,
    up_weight,
    down_weight,
    conv_weight,
    patch_conv_weight,
    query_bias,
    value_bias,
    out_bias,
    up_bias,
    down_bias,
    attention_gain,
    attention_shift,
    feedforward_gain,
    feedforward_shift,
    reading_bias_table,
    horizontal_bias_table,
    vertical_bias_table,
    cotangent,
    patch_cotangent,
):
    conv_taps = conv_weight.astype(jnp.float32)
    patch_taps = patch_conv_weight.astype(jnp.float32)
    query_offset = query_bias.astype(jnp.float32)
    value_offset = value_bias.astype(jnp.float32)
    out_offset = out_bias.astype(jnp.float32)
    up_offset = up_bias.astype(jnp.float32)
    down_offset = down_bias.astype(jnp.float32)
    first_gain = attention_gain.astype(jnp.float32)
    first_shift = attention_shift.astype(jnp.float32)
    second_gain = feedforward_gain.astype(jnp.float32)
    second_shift = feedforward_shift.astype(jnp.float32)
    page_count, span_size, model_width = tokens.shape
    patch_span = patches.shape[1]
    seq_count = lax.axis_size("seq")
    slot_size = span_size * seq_count
    patch_slots = patch_span * seq_count
    row_count = span_size + patch_span
    key_count = row_count * seq_count
    head_count = reading_bias_table.shape[0]
    head_size = model_width // head_count
    line_bins = reading_bias_table.shape[1]
    plane_bins = horizontal_bias_table.shape[1]
    score_scale = head_size ** (-0.5)
    seq_index = lax.axis_index("seq")
    text_places = seq_index * span_size + jnp.arange(span_size, dtype=jnp.int32)
    local_cells = seq_index * patch_span + jnp.arange(patch_span, dtype=jnp.int32)
    all_cells = jnp.arange(patch_slots, dtype=jnp.int32)
    text_live = text_places[None, :] < page_length[:, None]
    patch_live = grid_live(local_cells)
    key_pad = -(-key_count // 128) * 128
    patch_box_all = jnp.broadcast_to(
        grid_boxes(all_cells)[:, None, :], (2, page_count, patch_slots)
    )
    key_box = jnp.pad(
        jnp.concatenate([box_position, patch_box_all], axis=2),
        ((0, 6), (0, 0), (0, key_pad - key_count)),
    )
    local_patch_box = jnp.broadcast_to(
        grid_boxes(local_cells)[:, None, :], (2, page_count, patch_span)
    )
    query_box = jnp.concatenate(
        [
            lax.dynamic_slice_in_dim(box_position, seq_index * span_size, span_size, 2),
            local_patch_box,
        ],
        axis=2,
    )
    text_factor = text_live[:, :, None]
    patch_factor = patch_live[None, :, None]
    masked = tokens * text_factor.astype(jnp.bfloat16)
    rimmed = with_halo(masked, (("seq", 1),), 3)
    reach = GRID_SIDE + 1
    patch_masked = patches * patch_factor.astype(jnp.bfloat16)
    patch_rimmed = with_halo(patch_masked, (("seq", 1),), reach)
    def packed_table(table):
        steps = jnp.round(table.astype(jnp.float32) * FIXED).astype(jnp.int32)
        return (steps[0::2] + 8192) + steps[1::2] * 65536

    plane_table = packed_table(
        jnp.concatenate([horizontal_bias_table, vertical_bias_table], axis=1)
    )
    line_table = jnp.pad(packed_table(reading_bias_table), ((0, 0), (0, 128 - line_bins)))
    line_values = line_bias(
        jnp.stack([seq_index.astype(jnp.int32)]), line_table, head_count // 2, row_count, key_pad
    )
    tables = (plane_table, line_values)
    rows_in = jnp.concatenate([tokens, patches], axis=1)
    tap_rows = jnp.pad(conv_taps.T, ((0, 7), (0, 0)))
    patch_tap_rows = jnp.pad(patch_taps.T, ((0, 7), (0, 0)))
    page_state = []
    for page in range(page_count):
        own = rows_in[page]
        far = swap(own, "seq", 2)
        blocks = (own, swap(own, "seq", 1), far, swap(far, "seq", 1))
        scalars = jnp.stack([seq_index.astype(jnp.int32), page_length[page]])
        columns = query_box[:, page].T
        page_state.append(
            (scalars, columns, key_box[:, page])
            + tuple(
                forward_page(
                    scalars,
                    columns,
                    key_box[:, page],
                    blocks,
                    tap_rows,
                    patch_tap_rows,
                    (query_weight, key_weight, value_weight),
                    (query_offset[None], value_offset[None]),
                    tables,
                )
            )
        )
    hidden = jnp.stack([state[3] for state in page_state])
    hidden_low = jnp.stack([state[4] for state in page_state])
    mixture_low = jnp.stack([state[8] for state in page_state])
    pages = lax.axis_size("page")
    places = jnp.stack(
        [seq_index, seq_index % 2, lax.axis_index("page"), seq_index // 2]
    ).astype(jnp.int32)
    vectors = jnp.concatenate(
        [
            jnp.stack(
                [
                    query_bias, value_bias, out_bias, down_bias,
                    attention_gain, attention_shift, feedforward_gain, feedforward_shift,
                ]
            ),
            up_bias.reshape(-1, model_width),
        ]
    ).astype(jnp.float32)

    def flat(value):
        return value.reshape(-1, value.shape[-1])

    output, patch_output, delta_first, delta_mixture, middle_sums, feedforward_bundle = middle(
        places, flat(hidden), flat(mixture_low), cotangent, patch_cotangent,
        (out_weight, up_weight, down_weight), vectors, pages,
    )
    delta_first = delta_first.reshape(page_count, row_count, model_width)
    delta_mixture = delta_mixture.reshape(page_count, row_count, model_width)
    early_state = added(feedforward_bundle[0], swap(feedforward_bundle[1], "seq", 1))
    delta_mixture, early_state = lax.optimization_barrier((delta_mixture, early_state))
    delta_query_pages, delta_key_pages, delta_value_pages = [], [], []
    delta_plane, delta_line = 0.0, 0.0
    for page, state in enumerate(page_state):
        scalars, columns, key_rows, _, _, queries, keys, values, _, weights = state
        query_rows = jnp.pad(query_box[:, page], ((0, 6), (0, 0)))
        delta_page_queries, delta_blocks, plane_part, line_part = backward_page(
            scalars,
            columns,
            key_rows,
            query_rows,
            queries,
            keys,
            values,
            delta_mixture[page],
            weights,
        )
        got = swap(delta_blocks[2:], "seq", 1)
        chip_sum = delta_blocks[:2].astype(jnp.float32) + got.astype(jnp.float32)
        got = swap(chip_sum[1].astype(jnp.bfloat16), "seq", 2)
        whole = (chip_sum[0] + got.astype(jnp.float32)).astype(jnp.bfloat16)
        delta_query_pages.append(delta_page_queries)
        delta_key_pages.append(whole[0])
        delta_value_pages.append(whole[1])
        delta_plane = delta_plane + plane_part
        delta_line = delta_line + line_part
    delta_queries = jnp.stack(delta_query_pages)
    delta_keys = jnp.stack(delta_key_pages)
    delta_values = jnp.stack(delta_value_pages)
    def clipped(sums, centre, bins):
        first, last = centre + 1 - bins // 2, centre - 1 + bins // 2
        return jnp.concatenate(
            [
                jnp.sum(sums[..., :first], axis=-1, keepdims=True),
                sums[..., first:last],
                jnp.sum(sums[..., last:], axis=-1, keepdims=True),
            ],
            axis=-1,
        )

    delta_plane = clipped(delta_plane, 72, plane_bins)
    delta_line = clipped(delta_line, 32, line_bins)
    delta_across, delta_upward = delta_plane[0], delta_plane[1]
    delta_query_offset = row_sum(delta_queries)
    delta_value_offset = row_sum(delta_values)
    delta_hidden = (
        delta_first
        + back_dot(delta_queries, query_weight)
        + back_dot(delta_keys, key_weight)
        + back_dot(delta_values, value_weight)
    )
    delta_position = delta_hidden[:, :span_size].astype(jnp.bfloat16)
    delta_rim = with_halo(delta_position, (("seq", 1),), 3)
    delta_masked = jnp.zeros((page_count, span_size, model_width), jnp.float32)
    tap_columns = []
    for dilation in (1, 2, 3):
        for offset in (-1, 0, 1):
            column = 3 * (dilation - 1) + offset + 1
            anchor = 3 + offset * dilation
            anchor_back = 3 - offset * dilation
            delta_masked = (
                delta_masked
                + delta_rim[:, anchor_back : anchor_back + span_size, :] * conv_taps[:, column]
            )
            tap_columns.append(
                jnp.einsum(
                    "ptd,ptd->d",
                    delta_position,
                    rimmed[:, anchor : anchor + span_size, :],
                    preferred_element_type=jnp.float32,
                )
            )
    delta_taps = jnp.stack(tap_columns, axis=1)
    tokens_gradient = delta_hidden[:, :span_size] + delta_masked * text_factor.astype(jnp.float32)
    delta_patch_position = delta_hidden[:, span_size:].astype(jnp.bfloat16)
    delta_patch_rim = with_halo(delta_patch_position, (("seq", 1),), reach)
    delta_patch_masked = jnp.zeros((page_count, patch_span, model_width), jnp.float32)
    patch_columns = []
    for vertical in (-1, 0, 1):
        for horizontal in (-1, 0, 1):
            column = 3 * (vertical + 1) + horizontal + 1
            anchor = reach + vertical * GRID_SIDE + horizontal
            anchor_back = reach - vertical * GRID_SIDE - horizontal
            delta_patch_masked = (
                delta_patch_masked
                + delta_patch_rim[:, anchor_back : anchor_back + patch_span, :]
                * patch_taps[:, column]
            )
            patch_columns.append(
                jnp.einsum(
                    "ptd,ptd->d",
                    delta_patch_position,
                    patch_rimmed[:, anchor : anchor + patch_span, :],
                    preferred_element_type=jnp.float32,
                )
            )
    delta_patch_taps = jnp.stack(patch_columns, axis=1)
    patches_gradient = delta_hidden[:, span_size:] + delta_patch_masked * patch_factor.astype(
        jnp.float32
    )
    tail_bundle = attention_bundle(
        places, [flat(value) for value in (hidden_low, delta_queries, delta_keys, delta_values)], pages
    )
    tail_state = added(tail_bundle[0], swap(tail_bundle[1], "seq", 1))
    query_part, key_part, value_part = bundle_parts(
        bundle_sum(tail_state, pages), model_width // pages, places[1]
    )
    up_part, down_part, out_part = bundle_parts(
        bundle_sum(early_state, pages), up_weight.shape[1] // pages, places[1]
    )
    up_part = up_part.reshape(model_width // pages, -1)
    matrix_parts = (query_part, key_part, value_part, out_part, up_part, down_part)
    vector_parts = total_sum(
        (
            delta_taps,
            delta_patch_taps,
            delta_query_offset,
            delta_value_offset,
            middle_sums[OUT_BIAS],
            middle_sums[UP_BIAS : UP_BIAS + 4].reshape(-1),
            middle_sums[DOWN_BIAS],
            middle_sums[FIRST_GAIN],
            middle_sums[FIRST_SHIFT],
            middle_sums[SECOND_GAIN],
            middle_sums[SECOND_SHIFT],
            delta_line,
            delta_across,
            delta_upward,
        )
    )
    return (
        output,
        patch_output,
        tokens_gradient,
        patches_gradient,
        matrix_parts[0],
        matrix_parts[1],
        matrix_parts[2],
        matrix_parts[3],
        matrix_parts[4],
        matrix_parts[5],
        vector_parts[0],
        vector_parts[1],
        vector_parts[2],
        vector_parts[3],
        vector_parts[4],
        vector_parts[5],
        vector_parts[6],
        vector_parts[7],
        vector_parts[8],
        vector_parts[9],
        vector_parts[10],
        vector_parts[11],
        vector_parts[12],
        vector_parts[13],
    )


def solution(mesh):
    in_specs = (
        P("page", "seq", None),
        P("page", "seq", None),
        P("page"),
        P(None, "page", None),
        P(),
        P(),
        P(),
        P(),
        P(),
        P(),
        P(),
        P(),
        P(),
        P(),
        P(),
        P(),
        P(),
        P(),
        P(),
        P(),
        P(),
        P(),
        P(),
        P(),
        P("page", "seq", None),
        P("page", "seq", None),
    )
    out_specs = (
        P("page", "seq", None),
        P("page", "seq", None),
        P("page", "seq", None),
        P("page", "seq", None),
        P("page", "seq"),
        P("page", "seq"),
        P("page", "seq"),
        P("page", "seq"),
        P("page", "seq"),
        P("page", "seq"),
        P(),
        P(),
        P(),
        P(),
        P(),
        P(),
        P(),
        P(),
        P(),
        P(),
        P(),
        P(),
        P(),
        P(),
    )
    return jax.shard_map(shards, mesh=mesh, in_specs=in_specs, out_specs=out_specs, check_vma=False)
```

```python
import functools

import jax
import jax.numpy as jnp
from jax import lax
from jax.experimental import pallas as pl
from jax.experimental.pallas import tpu as pltpu
from jax.sharding import PartitionSpec as P

GRID_SIDE = 8


epsilon = 1e-05
coordinate_step = 16
masked_score = -1000000000.0
patch_pitch = 146
patch_centre = 73


def with_halo(cells, sides, width):
    for axis, dim in sides:
        count = lax.axis_size(axis)
        ends = count - 1
        head = lax.slice_in_dim(cells, 0, width, axis=dim)
        tail = lax.slice_in_dim(cells, cells.shape[dim] - width, cells.shape[dim], axis=dim)
        cells = jnp.concatenate(
            [
                lax.ppermute(tail, axis, [(i, (i + 1) % count) for i in range(ends)]),
                cells,
                lax.ppermute(head, axis, [((i + 1) % count, i) for i in range(ends)]),
            ],
            axis=dim,
        )
    return cells


def layer_norm(values, gain_vector, shift_vector):
    row_mean = jnp.mean(values, axis=-1, keepdims=True)
    centred = values - row_mean
    variance = jnp.mean(centred * centred, axis=-1, keepdims=True)
    return centred * lax.rsqrt(variance + epsilon) * gain_vector + shift_vector


def gelu_exact(values):
    return jax.nn.gelu(values, approximate=False)


def flat_dot(operand, matrix):
    front = operand.shape[:-1]
    result = jnp.dot(
        operand.reshape(-1, operand.shape[-1]), matrix, preferred_element_type=jnp.float32
    )
    return result.reshape(front + (matrix.shape[-1],))


def back_dot(operand, matrix):
    front = operand.shape[:-1]
    result = lax.dot_general(
        operand.reshape(-1, operand.shape[-1]),
        matrix,
        (((1,), (1,)), ((), ())),
        preferred_element_type=jnp.float32,
    )
    return result.reshape(front + (matrix.shape[0],))


def outer_dot(operand, gradient):
    return lax.dot_general(
        operand.reshape(-1, operand.shape[-1]),
        gradient.reshape(-1, gradient.shape[-1]),
        (((0,), (0,)), ((), ())),
        preferred_element_type=jnp.float32,
    )


def row_sum(gradient):
    return jnp.sum(gradient.astype(jnp.float32).reshape(-1, gradient.shape[-1]), axis=0)


def swap(value, axis, bit):
    count = lax.axis_size(axis)
    return lax.ppermute(value, axis, [(i, i ^ bit) for i in range(count)])


def total_sum(vectors):
    flat = jnp.concatenate([vector.reshape(-1) for vector in vectors])
    flat = jnp.pad(flat, (0, -flat.size % 1024)).reshape(-1, 128)
    for bit in (1, 2):
        flat = flat + swap(flat, "seq", bit)
    bit = 1
    while bit < lax.axis_size("page"):
        flat = flat + swap(flat, "page", bit)
        bit *= 2
    flat = flat.reshape(-1)
    result, start = [], 0
    for vector in vectors:
        result.append(flat[start : start + vector.size].reshape(vector.shape))
        start += vector.size
    return result


def query_places(seq_index, shape, span, patch_span, text_slots):
    row = lax.broadcasted_iota(jnp.int32, shape, 0)
    return jnp.where(
        row < span, seq_index * span + row, text_slots + seq_index * patch_span + row - span
    )


FIXED = 2048.0


def lookup(table_row, lanes):
    return jnp.take_along_axis(jnp.broadcast_to(table_row, lanes.shape), lanes, axis=1)


def pair_masked(pair):
    lane = lax.broadcasted_iota(jnp.int32, pair.shape, 1)
    half = pair.shape[1] // 2
    zero = jnp.zeros_like(pair)
    return jnp.concatenate(
        [jnp.where(lane < half, pair, zero), jnp.where(lane < half, zero, pair)], axis=0
    )


def pair_merged(both):
    rows, width = both.shape[0] // 2, both.shape[1]
    lane = lax.broadcasted_iota(jnp.int32, (rows, width), 1)
    return jnp.where(lane < width // 2, both[:rows], both[rows:])


def dot_nt(left, right):
    return lax.dot_general(left, right, (((1,), (1,)), ((), ())), preferred_element_type=jnp.float32)


def dot_nn(left, right):
    return lax.dot_general(left, right, (((1,), (0,)), ((), ())), preferred_element_type=jnp.float32)


def dot_tn(left, right):
    return lax.dot_general(left, right, (((0,), (0,)), ((), ())), preferred_element_type=jnp.float32)


CHUNK = 16


MESH = pl.DeviceIdType.MESH


def places_of(pages):
    page = lax.axis_index("page")
    seq = lax.axis_index("seq")
    bits = []
    rest = page
    for _ in range(pages.bit_length() - 1):
        bits.append(rest % 2)
        rest = rest // 2
    return page, bits, seq, seq // 2, seq % 2


def sibling_of(seq):
    return seq + 1 - 2 * (seq % 2)


def across_of(seq):
    return seq + 2 - 4 * (seq // 2)


def remote(source, target, send, receive, page, seq):
    return pltpu.make_async_remote_copy(
        src_ref=source, dst_ref=target, send_sem=send, recv_sem=receive, device_id=(page, seq), device_id_type=MESH
    )


def column_of(row):
    square = jnp.broadcast_to(row.astype(jnp.float32), (128, 128)).T
    return square[:, 0:1].astype(jnp.int32)


def forward_kernel(
    pages,
    length_ref, tokens_ref, patches_ref, box_ref, taps_ref, query_weight_ref, key_weight_ref, value_weight_ref,
    vector_ref, table_ref,
    hidden_ref, hidden_low_ref, query_ref, key_ref, value_ref, mixture_ref, weights_ref, columns_ref, rows_ref,
    query_rows_ref,
    arrived, text, grid, low, scores, across_ref, upward_ref, live_ref, line_ref, packed_ref,
    send_sem, recv_sem,
):
    page_at, _, seq, _, _ = places_of(pages)
    count, span, width = tokens_ref.shape
    patch_span = patches_ref.shape[1]
    row_count = span + patch_span
    key_pad = key_ref.shape[1]
    text_slots = 4 * span
    rim = 8
    pairs = weights_ref.shape[1]
    peers = (sibling_of(seq), across_of(seq))
    barrier = pltpu.get_barrier_semaphore()
    for peer in peers:
        pl.semaphore_signal(barrier, inc=1, device_id=(page_at, peer), device_id_type=MESH)
    pl.semaphore_wait(barrier, 2)

    def first_copies(page, side):
        return (
            remote(
                tokens_ref.at[page], arrived.at[side, page, 0:span], send_sem.at[2 * side, page],
                recv_sem.at[2 * side, page], page_at, peers[side],
            ),
            remote(
                patches_ref.at[page], arrived.at[side, page, span:row_count], send_sem.at[2 * side + 1, page],
                recv_sem.at[2 * side + 1, page], page_at, peers[side],
            ),
        )

    def onward_copy(page):
        return remote(
            arrived.at[1, page], arrived.at[2, page], send_sem.at[4, page], recv_sem.at[4, page], page_at, peers[0]
        )

    for page in range(count):
        for side in range(2):
            for copy in first_copies(page, side):
                copy.start()

    steps = jnp.floor(table_ref[...].astype(jnp.float32) * FIXED + 0.5).astype(jnp.int32)
    for pair in range(pairs):
        words = (steps[2 * pair : 2 * pair + 1] + 8192) + steps[2 * pair + 1 : 2 * pair + 2] * 65536
        packed_ref[0, pair : pair + 1, :] = words[:, 0:128]
        packed_ref[1, pair : pair + 1, :] = words[:, 128:256]
    key = lax.broadcasted_iota(jnp.int32, (row_count, key_pad), 1)
    place = query_places(seq, (row_count, key_pad), span, patch_span, text_slots)
    across_ref[...] = jnp.clip(key - place, -16, 15) + 16

    def fill(pair, carry):
        row = packed_ref[1, pl.ds(pair, 1), :]
        for at in range(0, key_pad, 128):
            line_ref[pair, :, at : at + 128] = lookup(row, across_ref[:, at : at + 128])
        return carry

    lax.fori_loop(0, pairs, fill, 0)
    text[0:rim, :] = jnp.zeros((rim, width), jnp.float32)
    text[rim + text_slots :, :] = jnp.zeros((rim, width), jnp.float32)
    grid[0:patch_span, :] = jnp.zeros((patch_span, width), jnp.float32)
    grid[patch_span * 5 :, :] = jnp.zeros((patch_span, width), jnp.float32)
    low[row_count * 4 :, :] = jnp.zeros((key_pad - row_count * 4, width), jnp.bfloat16)
    lanes = 256
    pair_width = 128
    power = 1.4426950408889634 / FIXED
    for copy in first_copies(0, 1):
        copy.wait_recv()
    onward_copy(0).start()

    def page_step(page, carry):
        length = length_ref[page]
        base = page * row_count
        cell = lax.broadcasted_iota(jnp.int32, (1, 128), 1)
        query_cell = seq * patch_span + cell
        row_cell = seq * patch_span + lax.broadcasted_iota(jnp.int32, (patch_span, 1), 0)
        for plane in range(2):
            boxes = box_ref[plane]
            of_page = lax.broadcasted_iota(jnp.int32, boxes.shape, 0) == page
            box = jnp.sum(jnp.where(of_page, boxes, 0), axis=0, keepdims=True)
            patch = 146 * ((cell % GRID_SIDE) if plane == 0 else (cell // GRID_SIDE)) + 73
            own_patch = 146 * ((query_cell % GRID_SIDE) if plane == 0 else (query_cell // GRID_SIDE)) + 73
            column_patch = 146 * ((row_cell % GRID_SIDE) if plane == 0 else (row_cell // GRID_SIDE)) + 73
            rows_ref[page, plane : plane + 1, 0:text_slots] = box
            rows_ref[page, plane : plane + 1, text_slots:key_pad] = patch
            own = rows_ref[page, plane : plane + 1, pl.ds(pl.multiple_of(seq * span, 128), span)]
            query_rows_ref[page, plane : plane + 1, 0:span] = own
            query_rows_ref[page, plane : plane + 1, span:256] = own_patch
            columns_ref[page, 0:span, plane * 128 : (plane + 1) * 128] = jnp.broadcast_to(column_of(own), (span, 128))
            columns_ref[page, span:row_count, plane * 128 : (plane + 1) * 128] = jnp.broadcast_to(
                column_patch, (patch_span, 128)
            )
        for plane, lanes_ref in enumerate((across_ref, upward_ref)):
            difference = rows_ref[page, plane : plane + 1, :] - columns_ref[page, :, plane * 128 : plane * 128 + 1]
            lanes_ref[...] = jnp.clip(difference >> 4, -32, 31) + (32 + 64 * plane)
        key_at = lax.broadcasted_iota(jnp.int32, live_ref.shape, 1)
        key_cell = key_at - text_slots
        live = (key_at < length) | (
            (key_cell >= 0) & ((key_cell >> 3) < GRID_SIDE - 1) & ((key_cell & 7) < GRID_SIDE - 1)
        )
        live_ref[...] = jnp.where(live, 0.0, masked_score * FIXED)
        for copy in first_copies(page, 0):
            copy.wait_recv()
        onward_copy(page).wait_recv()

        def block_of(step, start, stop, at):
            if step:
                return arrived[step - 1, page, start:stop, at].astype(jnp.float32)
            if start:
                return patches_ref[page, :, at].astype(jnp.float32)
            return tokens_ref[page, :, at].astype(jnp.float32)

        def slot_of(step):
            return (seq, peers[0], peers[1], sibling_of(peers[1]))[step]

        everything = slice(0, width)
        for step in range(4):
            where = slot_of(step)
            at_place = where * span + lax.broadcasted_iota(jnp.int32, (span, 1), 0)
            text[pl.ds(pl.multiple_of(rim + where * span, 8), span), :] = jnp.where(
                at_place < length, block_of(step, 0, span, everything), 0.0
            )
            at_cell = where * patch_span + lax.broadcasted_iota(jnp.int32, (patch_span, 1), 0)
            cell_live = ((at_cell >> 3) < GRID_SIDE - 1) & ((at_cell & 7) < GRID_SIDE - 1)
            grid[pl.ds(pl.multiple_of(patch_span + where * patch_span, 8), patch_span), :] = jnp.where(
                cell_live, block_of(step, span, row_count, everything), 0.0
            )
        for step in range(4):
            where = slot_of(step)

            def convolve(tile, carry):
                at = pl.ds(pl.multiple_of(tile * lanes, lanes), lanes)
                window = text[pl.ds(pl.multiple_of(where * span, 8), span + 2 * rim), at]
                centre = taps_ref[1:2, at] + taps_ref[4:5, at] + taps_ref[7:8, at]
                total = block_of(step, 0, span, at) + window[rim : rim + span] * centre
                for dilation in (1, 2, 3):
                    for offset in (-1, 1):
                        tap = 3 * (dilation - 1) + offset + 1
                        anchor = rim + offset * dilation
                        total = total + window[anchor : anchor + span] * taps_ref[tap : tap + 1, at]
                low[pl.ds(pl.multiple_of(where * span, 16), span), at] = total.astype(jnp.bfloat16)
                window = grid[pl.ds(pl.multiple_of(where * patch_span, 8), 3 * patch_span), at]
                patch_total = block_of(step, span, row_count, at)
                for vertical in (-1, 0, 1):
                    for horizontal in (-1, 0, 1):
                        tap = 9 + 3 * (vertical + 1) + horizontal + 1
                        anchor = patch_span + vertical * GRID_SIDE + horizontal
                        patch_total = patch_total + window[anchor : anchor + patch_span] * taps_ref[tap : tap + 1, at]
                low[pl.ds(pl.multiple_of(text_slots + where * patch_span, 16), patch_span), at] = (
                    patch_total.astype(jnp.bfloat16)
                )
                if step == 0:
                    for first, rows_here, value in ((0, span, total), (span, patch_span, patch_total)):
                        here = pl.ds(pl.multiple_of(base + first, 16), rows_here)
                        hidden_ref[here, at] = value
                        hidden_low_ref[here, at] = value.astype(jnp.bfloat16)
                return carry

            lax.fori_loop(0, width // lanes, convolve, 0)
        own_rows = pl.ds(pl.multiple_of(base, 16), row_count)

        def project(tile, carry):
            at = pl.ds(pl.multiple_of(tile * lanes, lanes), lanes)
            key_ref[page, :, at] = dot_nn(low[...], key_weight_ref[:, at]).astype(jnp.bfloat16)
            value_ref[page, :, at] = (dot_nn(low[...], value_weight_ref[:, at]) + vector_ref[1:2, at]).astype(
                jnp.bfloat16
            )
            query_ref[own_rows, at] = (
                (dot_nn(hidden_low_ref[own_rows, :], query_weight_ref[:, at]) + vector_ref[0:1, at])
                .astype(jnp.bfloat16)
                * jnp.bfloat16(0.125)
            )
            return carry

        lax.fori_loop(0, width // lanes, project, 0)

        @pl.when(page < count - 1)
        def _():
            for copy in first_copies(page + 1, 1):
                copy.wait_recv()
            onward_copy(page + 1).start()

        def attend(pair, carry):
            at = pl.ds(pl.multiple_of(pair * pair_width, pair_width), pair_width)
            scores[...] = dot_nt(pair_masked(query_ref[own_rows, at] * jnp.bfloat16(FIXED)), key_ref[page, :, at])
            plane_row = packed_ref[0, pl.ds(pair, 1), :]
            for start in range(0, row_count, CHUNK):
                here = slice(start, start + CHUNK)
                packed = []
                for block_at in range(0, key_pad, 128):
                    lane = slice(block_at, block_at + 128)
                    packed.append(
                        line_ref[pair, here, lane]
                        + lookup(plane_row, across_ref[here, lane])
                        + lookup(plane_row, upward_ref[here, lane])
                    )
                for side in range(2):
                    there = slice(side * row_count + start, side * row_count + start + CHUNK)
                    parts, top = [], None
                    for index, word in enumerate(packed):
                        lane = slice(128 * index, 128 * (index + 1))
                        field = (word >> 16) if side else (word & 0xFFFF)
                        part = (scores[there, lane] + field.astype(jnp.float32)) + live_ref[0:1, lane]
                        top = part if top is None else jnp.maximum(top, part)
                        parts.append(part)
                    top = jnp.max(top, axis=1, keepdims=True)
                    parts = [jnp.exp2((part - top) * power) for part in parts]
                    total = parts[0]
                    for part in parts[1:]:
                        total = total + part
                    inverse = 1.0 / jnp.sum(total, axis=1, keepdims=True)
                    for index, part in enumerate(parts):
                        weights_ref[page, pair, there, 128 * index : 128 * (index + 1)] = (part * inverse).astype(
                            jnp.bfloat16
                        )
            mixture_ref[own_rows, at] = pair_merged(
                dot_nn(weights_ref[page, pair], value_ref[page, :, at])
            ).astype(jnp.bfloat16)
            return carry

        lax.fori_loop(0, pairs, attend, 0)
        return carry

    lax.fori_loop(0, count, page_step, 0)
    for page in range(count):
        for side in range(2):
            for copy in first_copies(page, side):
                copy.wait_send()
        onward_copy(page).wait_send()


VMEM = pltpu.VMEM
KERNEL_VMEM = 48 * 1024 * 1024


def in_vmem(count):
    return [pl.BlockSpec(memory_space=VMEM)] * count


def forward(pages, lengths, tokens, patches, box, taps, matrices, vectors, table):
    count, span, width = tokens.shape
    patch_span = patches.shape[1]
    row_count = span + patch_span
    total_rows = count * row_count
    key_pad = -(-4 * row_count // 128) * 128
    pairs = table.shape[0] // 2
    bf16, f32, i32 = jnp.bfloat16, jnp.float32, jnp.int32
    own = jax.ShapeDtypeStruct((total_rows, width), bf16)
    every = jax.ShapeDtypeStruct((count, key_pad, width), bf16)
    return pl.pallas_call(
        functools.partial(forward_kernel, pages),
        out_shape=(
            jax.ShapeDtypeStruct((total_rows, width), f32), own, own, every, every, own,
            jax.ShapeDtypeStruct((count, pairs, 2 * row_count, key_pad), bf16),
            jax.ShapeDtypeStruct((count, row_count, 256), i32),
            jax.ShapeDtypeStruct((count, 8, key_pad), i32),
            jax.ShapeDtypeStruct((count, 8, 256), i32),
        ),
        in_specs=[pl.BlockSpec(memory_space=pltpu.SMEM)] + in_vmem(9),
        out_specs=tuple(in_vmem(10)),
        scratch_shapes=[
            VMEM((3, count, row_count, width), bf16),
            VMEM((4 * span + 16, width), f32),
            VMEM((6 * patch_span, width), f32),
            VMEM((key_pad, width), bf16),
            VMEM((2 * row_count, key_pad), f32),
            VMEM((row_count, key_pad), i32),
            VMEM((row_count, key_pad), i32),
            VMEM((8, key_pad), f32),
            VMEM((pairs, row_count, key_pad), i32),
            VMEM((2, 8, 128), i32),
            pltpu.SemaphoreType.DMA((5, count)),
            pltpu.SemaphoreType.DMA((5, count)),
        ],
        compiler_params=pltpu.CompilerParams(
            collective_id=0, has_side_effects=True, vmem_limit_bytes=KERNEL_VMEM
        ),
        cost_estimate=pl.CostEstimate(flops=8_000_000_000, bytes_accessed=25_000_000, transcendentals=3_000_000),
        name="forward",
    )(lengths, tokens, patches, box, taps, *matrices, vectors, table)


def backward_kernel(
    scalar_ref, columns_ref, rows_ref, query_rows_ref, query_ref, key_ref, value_ref, mixture_back_ref, weights_ref,
    query_back_ref, block_back_ref, plane_back_ref, line_back_ref,
    back, steps, mask_ref, hot_ref, query_hot_ref, band_ref,
):
    seq_index = scalar_ref[0]
    row_count, width = query_ref.shape
    key_pad = key_ref.shape[0]
    count = 4
    patch_span = GRID_SIDE * GRID_SIDE // count
    span = row_count - patch_span
    text_slots = span * count
    columns, rows = columns_ref[...], rows_ref[...]
    mask_ref[:, 0:key_pad] = ((rows[0:1, :] & 15) < (columns[:, 0:1] & 15)).astype(jnp.float32).astype(jnp.bfloat16)
    mask_ref[:, key_pad:] = ((rows[1:2, :] & 15) < (columns[:, 1:2] & 15)).astype(jnp.float32).astype(jnp.bfloat16)
    bin_at = lax.broadcasted_iota(jnp.int32, (128, key_pad), 0) - 1
    key_block = lax.broadcasted_iota(jnp.int32, (128, key_pad), 1) >> 4
    for side in range(2):
        key_bin = rows[side : side + 1, :] >> 4
        plain = (key_bin == bin_at).astype(jnp.float32)
        lower = (key_bin - 1 == bin_at).astype(jnp.float32)
        plain, lower = jnp.where(bin_at < 64, plain, 0.0), jnp.where(bin_at < 64, lower, 0.0)
        mine = slice(128 * side, 128 * (side + 1))
        other = slice(128 * (1 - side), 128 * (2 - side))
        change = lower - plain
        if side == 0:
            plain = jnp.where(bin_at - 71 == key_block, 1.0, plain)
        hot_ref[mine, 0:key_pad] = plain.astype(jnp.bfloat16)
        hot_ref[mine, (1 + side) * key_pad : (2 + side) * key_pad] = change.astype(jnp.bfloat16)
        hot_ref[other, (1 + side) * key_pad : (2 + side) * key_pad] = jnp.zeros((128, key_pad), jnp.bfloat16)
    half_bin = lax.broadcasted_iota(jnp.int32, (72, row_count), 0)
    for side in range(2):
        query_hot_ref[72 * side : 72 * (side + 1), :] = (
            (71 - (query_rows_ref[side : side + 1, :] >> 4) == half_bin).astype(jnp.float32).astype(jnp.bfloat16)
        )
    lane128 = lax.broadcasted_iota(jnp.int32, (row_count, 128), 1)
    place = query_places(seq_index, (row_count, 128), span, patch_span, text_slots)
    aim = place + lane128 - 32
    near = (lane128 < 64) & (aim >= 0) & (aim < text_slots + patch_span * count)
    apart = (aim >> 4) - (place >> 4)
    near = near & (apart >= -1) & (apart <= 1)
    band_ref[...] = jnp.where(near, aim, -1)
    pair_width = 128
    line_back_ref[...] = jnp.zeros_like(line_back_ref)
    plane_back_ref[...] = jnp.zeros_like(plane_back_ref)

    def attend(pair, carry):
        at = pl.ds(pl.multiple_of(pair * pair_width, pair_width), pair_width)
        both_query = pair_masked(query_ref[:, at])
        both_back = pair_masked(mixture_back_ref[:, at])
        back[...] = dot_nt(both_back, value_ref[:, at])
        for start in range(0, 2 * row_count, CHUNK):
            there = slice(start, start + CHUNK)
            here = slice(start % row_count, start % row_count + CHUNK)
            parts, total = [], None
            for block_at in range(0, key_pad, 128):
                lane = slice(block_at, block_at + 128)
                part = weights_ref[pair, there, lane].astype(jnp.float32)
                product = part * back[there, lane]
                total = product if total is None else total + product
                parts.append(part)
            mean = jnp.sum(total, axis=1, keepdims=True)
            for index, part in enumerate(parts):
                lane = slice(128 * index, 128 * (index + 1))
                step = (part * (back[there, lane] - mean)).astype(jnp.bfloat16)
                steps[there, lane] = step
                steps[there, key_pad + 128 * index : key_pad + 128 * (index + 1)] = step * mask_ref[here, lane]
                steps[there, 2 * key_pad + 128 * index : 2 * key_pad + 128 * (index + 1)] = (
                    step * mask_ref[here, key_pad + 128 * index : key_pad + 128 * (index + 1)]
                )
        query_back_ref[:, at] = (pair_merged(dot_nn(steps[:, 0:key_pad], key_ref[:, at])) * 0.125).astype(
            jnp.bfloat16
        )
        for kind, value in enumerate(
            (dot_tn(steps[:, 0:key_pad], both_query), dot_tn(weights_ref[pair], both_back))
        ):
            value = value.astype(jnp.bfloat16)
            for where in range(count):
                step_at = seq_index ^ where
                slot = (step_at & 1) * 2 + (step_at >> 1)
                block_back_ref[slot, kind, 0:span, at] = value[where * span : (where + 1) * span]
                block_back_ref[slot, kind, span:row_count, at] = value[
                    text_slots + where * patch_span : text_slots + (where + 1) * patch_span
                ]
        bins = dot_nt(steps[...], hot_ref[...])
        low_bins = bins.astype(jnp.bfloat16)
        lane_one = lax.broadcasted_iota(jnp.int32, (1, 128), 1)
        far = lane128 - 72 - (place >> 4)
        in_line = (lane128 >= 72) & (lane128 < 72 + key_pad // 16)
        for side in range(2):
            head = pl.ds(2 * pair + side, 1)
            own = slice(side * row_count, (side + 1) * row_count)
            both = dot_nn(query_hot_ref[...], low_bins[own])
            for plane in range(2):
                table = both[72 * plane : 72 * (plane + 1), 128 * plane : 128 * (plane + 1)]
                wide_lane = lax.broadcasted_iota(jnp.int32, table.shape, 1)
                table = jnp.where(wide_lane < 72, table, 0.0)
                table = jnp.concatenate([table, jnp.zeros_like(table)], axis=1)
                sheared = pltpu.roll(table, 0, 1, stride=1, stride_axis=0)
                plane_back_ref[plane, head, :] = jnp.sum(sheared, axis=0, keepdims=True)
            line_bins = bins[own, 0:128]
            low_tail = jnp.sum(jnp.where(in_line & (far <= -2), line_bins, 0.0), axis=(0, 1), keepdims=True)
            high_tail = jnp.sum(jnp.where(in_line & (far >= 2), line_bins, 0.0), axis=(0, 1), keepdims=True)
            band = jnp.zeros((1, 128), jnp.float32)
            base = side * row_count
            for first, rows_here, block in (
                (0, span, seq_index),
                (0, 32, jnp.maximum(seq_index - 1, 0)),
                (span - 32, 32, seq_index + 1),
                (span, patch_span, count - 1),
                (span, patch_span, count),
            ):
                aims = band_ref[first : first + rows_here, :]
                source = steps[
                    base + first : base + first + rows_here, pl.ds(pl.multiple_of(block * 128, 128), 128)
                ].astype(jnp.float32)
                taken = jnp.take_along_axis(source, aims & 127, axis=1)
                right = (aims >> 7) == block
                if first == 0 and rows_here == 32:
                    right = right & (seq_index > 0)
                band = band + jnp.sum(jnp.where(right, taken, 0.0), axis=0, keepdims=True)
            line_back_ref[head, :] = (
                band + jnp.where(lane_one == 0, low_tail, 0.0) + jnp.where(lane_one == 63, high_tail, 0.0)
            )
        return carry

    lax.fori_loop(0, width // pair_width, attend, 0)


def backward_page(scalars, columns, rows, query_rows, queries, keys, values, mixture_back, weights):
    row_count, width = queries.shape
    key_pad = keys.shape[0]
    heads = 2 * weights.shape[0]
    return pl.pallas_call(
        backward_kernel,
        out_shape=(
            jax.ShapeDtypeStruct((row_count, width), jnp.bfloat16),
            jax.ShapeDtypeStruct((4, 2, row_count, width), jnp.bfloat16),
            jax.ShapeDtypeStruct((2, heads, 256), jnp.float32),
            jax.ShapeDtypeStruct((heads, 128), jnp.float32),
        ),
        in_specs=[pl.BlockSpec(memory_space=pltpu.SMEM)] + in_vmem(8),
        out_specs=tuple(in_vmem(4)),
        scratch_shapes=[
            pltpu.VMEM((2 * row_count, key_pad), jnp.float32),
            pltpu.VMEM((2 * row_count, 3 * key_pad), jnp.bfloat16),
            pltpu.VMEM((row_count, 2 * key_pad), jnp.bfloat16),
            pltpu.VMEM((256, 3 * key_pad), jnp.bfloat16),
            pltpu.VMEM((144, row_count), jnp.bfloat16),
            pltpu.VMEM((row_count, 128), jnp.int32),
        ],
        compiler_params=pltpu.CompilerParams(vmem_limit_bytes=KERNEL_VMEM),
        cost_estimate=pl.CostEstimate(flops=3_000_000_000, bytes_accessed=6_000_000, transcendentals=1_000_000),
        name="backward_page",
    )(scalars, columns, rows, query_rows, queries, keys, values, mixture_back, weights)


def block_slots(scalar_ref, page, column, levels):
    far = page ^ scalar_ref[2]
    side = column ^ scalar_ref[3]
    rest = 0
    for level in range(1, levels):
        rest = rest + (((far >> level) & 1) << (levels - 1 - level))
    near = far & 1
    return (side << levels) + (near << (levels - 1)) + rest, (near << levels) + (side << (levels - 1)) + rest


NORM_CHUNK = 48


def norm_rows(values):
    mean = jnp.mean(values, axis=-1, keepdims=True)
    centred = values - mean
    scale = lax.rsqrt(jnp.mean(centred * centred, axis=-1, keepdims=True) + epsilon)
    return centred * scale, scale


def norm_back(delta, unit, scale):
    return scale * (
        delta
        - jnp.mean(delta, axis=-1, keepdims=True)
        - unit * jnp.mean(delta * unit, axis=-1, keepdims=True)
    )


def column_sum(values):
    return jnp.sum(values, axis=0, keepdims=True)


OUT_BIAS, DOWN_BIAS, FIRST_GAIN, FIRST_SHIFT, SECOND_GAIN, SECOND_SHIFT = range(6)
UP_BIAS = 6


def middle_kernel(
    pages, direct,
    scalar_ref, hidden_ref, mixture_ref, cotangent_ref, patch_cotangent_ref, out_weight_ref, up_weight_ref,
    down_weight_ref, vector_ref,
    output_ref, patch_output_ref, first_back_ref, mixture_back_ref, sums_ref, *rest,
):
    if direct:
        bundle_ref, *rest = rest
    else:
        normed_out_ref, up_out_ref, activated_out_ref, down_out_ref, attention_out_ref, *rest = rest
    state, unit, scale_ref, normed, activated, slope, up_back, down_back, attention_back, flipped = rest
    count, span, width = output_ref.shape
    patch_span = patch_output_ref.shape[1]
    row_count = span + patch_span
    total_rows = count * row_count
    wide = up_weight_ref.shape[1]
    lanes = 256
    sums_ref[...] = jnp.zeros_like(sums_ref)

    def tile_at(tile):
        return pl.ds(pl.multiple_of(tile * lanes, lanes), lanes)

    def attention_tile(tile, carry):
        at = tile_at(tile)
        state[:, at] = hidden_ref[:, at] + (dot_nn(mixture_ref[...], out_weight_ref[:, at]) + vector_ref[2:3, at])
        return carry

    lax.fori_loop(0, width // lanes, attention_tile, 0)

    def first_norm(chunk, carry):
        here = pl.ds(pl.multiple_of(chunk * NORM_CHUNK, 16), NORM_CHUNK)
        rows, scale = norm_rows(state[here, :])
        unit[here, :] = rows
        scale_ref[here, :] = jnp.broadcast_to(scale, (NORM_CHUNK, 128))
        rows = rows * vector_ref[4:5, :] + vector_ref[5:6, :]
        state[here, :] = rows
        normed[here, :] = rows.astype(jnp.bfloat16)
        return carry

    lax.fori_loop(0, total_rows // NORM_CHUNK, first_norm, 0)

    def up_tile(tile, carry):
        at = tile_at(tile)
        branch = dot_nn(normed[...], up_weight_ref[:, at]) + vector_ref[pl.ds(8 + tile // 3, 1), tile_at(tile % 3)]
        chance = 0.5 * (1.0 + lax.erf(branch * 0.7071067811865476))
        activated[:, at] = (branch * chance).astype(jnp.bfloat16)
        slope[:, at] = chance + branch * (jnp.exp(branch * branch * -0.5) * 0.3989422804014327)
        return carry

    lax.fori_loop(0, wide // lanes, up_tile, 0)

    def down_tile(tile, carry):
        at = tile_at(tile)
        state[:, at] = state[:, at] + (dot_nn(activated[...], down_weight_ref[:, at]) + vector_ref[3:4, at])
        return carry

    lax.fori_loop(0, width // lanes, down_tile, 0)

    def second_norm(start, rows_here, page, out_ref, delta_ref):
        here = pl.ds(pl.multiple_of(page * row_count + start, 16), rows_here)
        there = pl.ds(0 if start == span else start, rows_here)
        rows, scale = norm_rows(state[here, :])
        out_ref[page, there, :] = rows * vector_ref[6:7, :] + vector_ref[7:8, :]
        delta = delta_ref[page, there, :].astype(jnp.float32)
        back = norm_back(delta * vector_ref[6:7, :], rows, scale)
        state[here, :] = back
        low = back.astype(jnp.bfloat16)
        down_back[here, :] = low
        for index, value in (
            (SECOND_GAIN, delta * rows), (SECOND_SHIFT, delta), (DOWN_BIAS, low.astype(jnp.float32))
        ):
            sums_ref[index : index + 1, :] += column_sum(value)

    def second_page(page, carry):
        for start in range(0, span, 32):
            second_norm(start, 32, page, output_ref, cotangent_ref)
        second_norm(span, patch_span, page, patch_output_ref, patch_cotangent_ref)
        return carry

    lax.fori_loop(0, count, second_page, 0)

    def up_back_tile(tile, carry):
        at = tile_at(tile)
        low = (dot_nt(down_back[...], down_weight_ref[at, :]) * slope[:, at]).astype(jnp.bfloat16)
        up_back[:, at] = low
        sums_ref[pl.ds(UP_BIAS + tile // 3, 1), tile_at(tile % 3)] = column_sum(low.astype(jnp.float32))
        return carry

    lax.fori_loop(0, wide // lanes, up_back_tile, 0)

    def normed_back_tile(tile, carry):
        at = tile_at(tile)
        state[:, at] = state[:, at] + dot_nt(up_back[...], up_weight_ref[at, :])
        return carry

    lax.fori_loop(0, width // lanes, normed_back_tile, 0)

    def first_back(chunk, carry):
        here = pl.ds(pl.multiple_of(chunk * NORM_CHUNK, 16), NORM_CHUNK)
        delta, rows = state[here, :], unit[here, :]
        back = norm_back(delta * vector_ref[4:5, :], rows, scale_ref[here, 0:1])
        first_back_ref[here, :] = back
        low = back.astype(jnp.bfloat16)
        attention_back[here, :] = low
        for index, value in (
            (FIRST_GAIN, delta * rows), (FIRST_SHIFT, delta), (OUT_BIAS, low.astype(jnp.float32))
        ):
            sums_ref[index : index + 1, :] += column_sum(value)
        return carry

    lax.fori_loop(0, total_rows // NORM_CHUNK, first_back, 0)

    def mixture_tile(tile, carry):
        at = tile_at(tile)
        mixture_back_ref[:, at] = dot_nt(attention_back[...], out_weight_ref[at, :]).astype(jnp.bfloat16)
        return carry

    lax.fori_loop(0, width // lanes, mixture_tile, 0)
    if not direct:
        normed_out_ref[...] = normed[...]
        up_out_ref[...] = up_back[...]
        activated_out_ref[...] = activated[...]
        down_out_ref[...] = down_back[...]
        attention_out_ref[...] = attention_back[...]
        return
    levels = pages.bit_length() - 1
    core = scalar_ref[1]
    rows = width // pages
    tall = wide // pages
    block = 384
    groups = wide // (2 * block)
    flipped[...] = normed[...].T

    def up_weight_tile(tile, carry):
        column, group = tile // groups, tile % groups
        at = pl.ds(pl.multiple_of(tile * block, block), block)
        result = dot_nn(flipped[...], up_back[:, at]).astype(jnp.bfloat16)
        for page in range(pages):
            slot = block_slots(scalar_ref, page, column, levels)[0]
            bundle_ref[core, slot, pl.ds(pl.multiple_of(group * rows, 16), rows), :] = result[
                page * rows : (page + 1) * rows
            ]
        return carry

    lax.fori_loop(0, 2 * groups, up_weight_tile, 0)

    def down_weight_tile(page, carry):
        at = pl.ds(pl.multiple_of(page * tall, 128), tall)
        result = dot_tn(activated[:, at], down_back[...]).astype(jnp.bfloat16)
        for column in range(2):
            slot = block_slots(scalar_ref, page, column, levels)[1]
            bundle_ref[1 - core, slot, 0:tall, :] = result[:, column * block : (column + 1) * block]
        return carry

    lax.fori_loop(0, pages, down_weight_tile, 0)
    flipped[...] = mixture_ref[...].T
    half = rows // 2

    def out_weight_tile(column, carry):
        at = pl.ds(pl.multiple_of(column * block, block), block)
        result = dot_nn(flipped[...], attention_back[:, at]).astype(jnp.bfloat16)
        for page in range(pages):
            slots = block_slots(scalar_ref, page, column, levels)
            for order in range(2):
                first = page * rows + order * half
                bundle_ref[core if order == 0 else 1 - core, slots[order], tall : tall + half, :] = result[
                    first : first + half
                ]
        return carry

    lax.fori_loop(0, 2, out_weight_tile, 0)


def middle(places, hidden, mixture, cotangent, patch_cotangent, matrices, vectors, pages):
    count, span, width = cotangent.shape
    patch_span = patch_cotangent.shape[1]
    total_rows = hidden.shape[0]
    wide = matrices[1].shape[1]
    direct = (width // pages) % 32 == 0
    bf16, f32 = jnp.bfloat16, jnp.float32
    if direct:
        extra = (jax.ShapeDtypeStruct((2, 2 * pages, (wide + width // 2) // pages, 384), bf16),)
    else:
        extra = tuple(
            jax.ShapeDtypeStruct((total_rows, size), bf16) for size in (width, wide, wide, width, width)
        )
    result = pl.pallas_call(
        functools.partial(middle_kernel, pages, direct),
        out_shape=(
            jax.ShapeDtypeStruct(cotangent.shape, f32),
            jax.ShapeDtypeStruct(patch_cotangent.shape, f32),
            jax.ShapeDtypeStruct((total_rows, width), f32),
            jax.ShapeDtypeStruct((total_rows, width), bf16),
            jax.ShapeDtypeStruct((16, width), f32),
        )
        + extra,
        in_specs=[pl.BlockSpec(memory_space=pltpu.SMEM)] + in_vmem(8),
        out_specs=tuple(in_vmem(5 + len(extra))),
        scratch_shapes=[
            pltpu.VMEM((total_rows, width), f32),
            pltpu.VMEM((total_rows, width), f32),
            pltpu.VMEM((total_rows, 128), f32),
            pltpu.VMEM((total_rows, width), bf16),
            pltpu.VMEM((total_rows, wide), bf16),
            pltpu.VMEM((total_rows, wide), f32),
            pltpu.VMEM((total_rows, wide), bf16),
            pltpu.VMEM((total_rows, width), bf16),
            pltpu.VMEM((total_rows, width), bf16),
            pltpu.VMEM((width, total_rows), bf16),
        ],
        compiler_params=pltpu.CompilerParams(vmem_limit_bytes=56 * 1024 * 1024),
        cost_estimate=pl.CostEstimate(flops=14_000_000_000, bytes_accessed=30_000_000, transcendentals=2_600_000),
        name="middle",
    )(places, hidden, mixture, cotangent, patch_cotangent, *matrices, vectors)
    first, rest = result[:5], result[5:]
    if direct:
        return first + rest
    normed, up_back, activated, down_back, attention_back = rest
    return first + (
        indexed_bundle(
            (
                ((normed, up_back, None), (mixture, attention_back, 0)),
                ((activated, down_back, None), (mixture, attention_back, 1)),
            ),
            places,
            pages,
        ),
    )


def indexed_bundle(matrices, scalars, pages):
    levels = pages.bit_length() - 1
    place = jnp.arange(2 * pages, dtype=jnp.int32)
    bits = [(place >> (levels - k)) & 1 for k in range(levels + 1)]
    halves = []
    for order, group in enumerate(matrices):
        side, near = (bits[0], bits[1]) if order == 0 else (bits[1], bits[0])
        far = near
        for level in range(1, levels):
            far = far + (bits[level + 1] << level)
        index = (far ^ scalars[2]) * 2 + (side ^ scalars[3])
        blocks = []
        for operand, gradient, part in group:
            rows = in_blocks(outer_dot(operand, gradient).astype(jnp.bfloat16), pages)
            if part is not None:
                half = rows.shape[1] // 2
                rows = rows[:, part * half : (part + 1) * half]
            blocks.append(rows)
        halves.append(jnp.concatenate(blocks, axis=1)[index])
    first, second = halves
    mine = scalars[1] == 0
    return jnp.stack([jnp.where(mine, first, second), jnp.where(mine, second, first)])


def attention_weight_kernel(
    pages, scalar_ref, hidden_ref, query_back_ref, key_back_ref, value_back_ref, out_ref, flipped
):
    levels = pages.bit_length() - 1
    core = scalar_ref[1]
    rows = hidden_ref.shape[1] // pages
    half = rows // 2
    lanes = out_ref.shape[3]
    flipped[...] = hidden_ref[...].T

    def tile(column, carry):
        at = pl.ds(pl.multiple_of(column * lanes, lanes), lanes)
        for index, back_ref in enumerate((query_back_ref, key_back_ref, value_back_ref)):
            result = dot_nn(flipped[...], back_ref[:, at]).astype(jnp.bfloat16)
            for page in range(pages):
                slots = block_slots(scalar_ref, page, column, levels)
                first = page * rows
                if index < 2:
                    where = core if index == 0 else 1 - core
                    out_ref[where, slots[index], 0:rows, :] = result[first : first + rows]
                else:
                    out_ref[core, slots[0], rows : rows + half, :] = result[first : first + half]
                    out_ref[1 - core, slots[1], rows : rows + half, :] = result[first + half : first + rows]
        return carry

    lax.fori_loop(0, 2, tile, 0)


def in_blocks(matrix, pages):
    rows, columns = matrix.shape[0] // pages, matrix.shape[1] // 2
    lanes = min(columns, 384)
    blocks = matrix.reshape(pages, rows, 2, columns // lanes, lanes)
    return blocks.transpose(0, 2, 3, 1, 4).reshape(pages * 2, rows * columns // lanes, lanes)


def attention_bundle(places, operands, pages):
    hidden, query_back, key_back, value_back = operands
    width = hidden.shape[1]
    if (width // pages) % 32:
        return indexed_bundle(
            (
                ((hidden, query_back, None), (hidden, value_back, 0)),
                ((hidden, key_back, None), (hidden, value_back, 1)),
            ),
            places,
            pages,
        )
    return pl.pallas_call(
        functools.partial(attention_weight_kernel, pages),
        out_shape=jax.ShapeDtypeStruct((2, 2 * pages, 3 * width // (2 * pages), 384), jnp.bfloat16),
        in_specs=[pl.BlockSpec(memory_space=pltpu.SMEM)] + in_vmem(4),
        out_specs=in_vmem(1)[0],
        scratch_shapes=[pltpu.VMEM(hidden.shape[::-1], jnp.bfloat16)],
        compiler_params=pltpu.CompilerParams(vmem_limit_bytes=KERNEL_VMEM),
        cost_estimate=pl.CostEstimate(flops=1_600_000_000, bytes_accessed=10_000_000, transcendentals=0),
        name="attention_weights",
    )(places, *operands)


def exchange(value, pages, step):
    moves = []
    for page in range(pages):
        for seq in range(4):
            on_page, on_seq = page, seq
            if (seq % 2 == step) if step < 2 else False:
                on_seq = seq ^ 2
            else:
                on_page = page ^ (1 if step < 2 else 1 << (step - 1))
            moves.append((page * 4 + seq, on_page * 4 + on_seq))
    return lax.ppermute(value, ("page", "seq"), moves)


def added(kept, got):
    return (kept.astype(jnp.float32) + got.astype(jnp.float32)).astype(jnp.bfloat16)


def bundle_sum(state, pages):
    for step in range(pages.bit_length()):
        half = state.shape[0] // 2
        state = added(state[:half], exchange(state[half:], pages, step))
    return state[0]


def bundle_parts(state, wide_rows, core):
    lanes = state.shape[1] // 2
    first = core == 0
    tail = state[wide_rows:]
    if wide_rows > 2 * tail.shape[0]:
        group = state[:wide_rows].reshape(4, wide_rows // 4, 2 * lanes)
        low = group[:2].transpose(1, 0, 2).reshape(-1, lanes)
        high = group[2:].transpose(1, 0, 2).reshape(-1, lanes)
    else:
        low, high = state[:wide_rows, :lanes], state[:wide_rows, lanes:]
    left, right = state[:wide_rows, :lanes], state[:wide_rows, lanes:]
    sent = jnp.concatenate(
        [jnp.where(first, high, left), jnp.where(first, tail[:, lanes:], tail[:, :lanes])], axis=0
    )
    got = swap(sent, "seq", 1)
    kept_tail = jnp.where(first, tail[:, :lanes], tail[:, lanes:])
    one = jnp.where(first, low, got[:wide_rows])
    two = jnp.where(first, got[:wide_rows], right)
    three = jnp.concatenate(
        [jnp.where(first, kept_tail, got[wide_rows:]), jnp.where(first, got[wide_rows:], kept_tail)], axis=0
    )
    return [value.astype(jnp.float32) for value in (one, two, three)]


def grid_live(cells):
    return (cells // GRID_SIDE < GRID_SIDE - 1) & (cells % GRID_SIDE < GRID_SIDE - 1)


def grid_boxes(cells):
    return jnp.stack(
        [
            patch_pitch * (cells % GRID_SIDE) + patch_centre,
            patch_pitch * (cells // GRID_SIDE) + patch_centre,
        ]
    )


def shards(
    tokens,
    patches,
    page_length,
    box_position,
    query_weight,
    key_weight,
    value_weight,
    out_weight,
    up_weight,
    down_weight,
    conv_weight,
    patch_conv_weight,
    query_bias,
    value_bias,
    out_bias,
    up_bias,
    down_bias,
    attention_gain,
    attention_shift,
    feedforward_gain,
    feedforward_shift,
    reading_bias_table,
    horizontal_bias_table,
    vertical_bias_table,
    cotangent,
    patch_cotangent,
):
    conv_taps = conv_weight.astype(jnp.float32)
    patch_taps = patch_conv_weight.astype(jnp.float32)
    query_offset = query_bias.astype(jnp.float32)
    value_offset = value_bias.astype(jnp.float32)
    out_offset = out_bias.astype(jnp.float32)
    up_offset = up_bias.astype(jnp.float32)
    down_offset = down_bias.astype(jnp.float32)
    first_gain = attention_gain.astype(jnp.float32)
    first_shift = attention_shift.astype(jnp.float32)
    second_gain = feedforward_gain.astype(jnp.float32)
    second_shift = feedforward_shift.astype(jnp.float32)
    page_count, span_size, model_width = tokens.shape
    patch_span = patches.shape[1]
    seq_count = lax.axis_size("seq")
    slot_size = span_size * seq_count
    patch_slots = patch_span * seq_count
    row_count = span_size + patch_span
    key_count = row_count * seq_count
    head_count = reading_bias_table.shape[0]
    head_size = model_width // head_count
    line_bins = reading_bias_table.shape[1]
    plane_bins = horizontal_bias_table.shape[1]
    score_scale = head_size ** (-0.5)
    seq_index = lax.axis_index("seq")
    text_places = seq_index * span_size + jnp.arange(span_size, dtype=jnp.int32)
    local_cells = seq_index * patch_span + jnp.arange(patch_span, dtype=jnp.int32)
    text_live = text_places[None, :] < page_length[:, None]
    patch_live = grid_live(local_cells)
    text_factor = text_live[:, :, None]
    patch_factor = patch_live[None, :, None]
    masked = tokens * text_factor.astype(jnp.bfloat16)
    rimmed = with_halo(masked, (("seq", 1),), 3)
    reach = GRID_SIDE + 1
    patch_masked = patches * patch_factor.astype(jnp.bfloat16)
    patch_rimmed = with_halo(patch_masked, (("seq", 1),), reach)
    pages = lax.axis_size("page")
    table = jnp.concatenate(
        [
            horizontal_bias_table,
            vertical_bias_table,
            reading_bias_table,
            jnp.zeros((head_count, 256 - 2 * plane_bins - line_bins), jnp.bfloat16),
        ],
        axis=1,
    ).astype(jnp.float32)
    taps = jnp.pad(
        jnp.concatenate([conv_weight, patch_conv_weight], axis=1).astype(jnp.float32).T, ((0, 6), (0, 0))
    )
    vectors = jnp.concatenate(
        [
            jnp.stack(
                [
                    query_bias, value_bias, out_bias, down_bias,
                    attention_gain, attention_shift, feedforward_gain, feedforward_shift,
                ]
            ),
            up_bias.reshape(-1, model_width),
        ]
    ).astype(jnp.float32)
    (
        hidden, hidden_low, queries, keys, values, mixture_low, weights, columns, key_rows, query_rows,
    ) = forward(
        pages, page_length, tokens, patches, box_position, taps, (query_weight, key_weight, value_weight),
        vectors, table,
    )
    places = jnp.stack(
        [seq_index, seq_index % 2, lax.axis_index("page"), seq_index // 2]
    ).astype(jnp.int32)
    def flat(value):
        return value.reshape(-1, value.shape[-1])

    output, patch_output, delta_first, delta_mixture, middle_sums, feedforward_bundle = middle(
        places, hidden, mixture_low, cotangent, patch_cotangent,
        (out_weight, up_weight, down_weight), vectors, pages,
    )
    delta_first = delta_first.reshape(page_count, row_count, model_width)
    delta_mixture = delta_mixture.reshape(page_count, row_count, model_width)
    early_state = added(feedforward_bundle[0], swap(feedforward_bundle[1], "seq", 1))
    delta_mixture, early_state = lax.optimization_barrier((delta_mixture, early_state))
    delta_query_pages, delta_key_pages, delta_value_pages = [], [], []
    delta_plane, delta_line = 0.0, 0.0
    for page in range(page_count):
        delta_page_queries, delta_blocks, plane_part, line_part = backward_page(
            places,
            columns[page][:, ::128],
            key_rows[page],
            query_rows[page][:, :row_count],
            queries[page * row_count : (page + 1) * row_count],
            keys[page],
            values[page],
            delta_mixture[page],
            weights[page],
        )
        got = swap(delta_blocks[2:], "seq", 1)
        chip_sum = delta_blocks[:2].astype(jnp.float32) + got.astype(jnp.float32)
        got = swap(chip_sum[1].astype(jnp.bfloat16), "seq", 2)
        whole = (chip_sum[0] + got.astype(jnp.float32)).astype(jnp.bfloat16)
        delta_query_pages.append(delta_page_queries)
        delta_key_pages.append(whole[0])
        delta_value_pages.append(whole[1])
        delta_plane = delta_plane + plane_part
        delta_line = delta_line + line_part
    delta_queries = jnp.stack(delta_query_pages)
    delta_keys = jnp.stack(delta_key_pages)
    delta_values = jnp.stack(delta_value_pages)
    def clipped(sums, centre, bins):
        first, last = centre + 1 - bins // 2, centre - 1 + bins // 2
        return jnp.concatenate(
            [
                jnp.sum(sums[..., :first], axis=-1, keepdims=True),
                sums[..., first:last],
                jnp.sum(sums[..., last:], axis=-1, keepdims=True),
            ],
            axis=-1,
        )

    delta_plane = clipped(delta_plane, 72, plane_bins)
    delta_line = clipped(delta_line, 32, line_bins)
    delta_across, delta_upward = delta_plane[0], delta_plane[1]
    delta_query_offset = row_sum(delta_queries)
    delta_value_offset = row_sum(delta_values)
    delta_hidden = (
        delta_first
        + back_dot(delta_queries, query_weight)
        + back_dot(delta_keys, key_weight)
        + back_dot(delta_values, value_weight)
    )
    delta_position = delta_hidden[:, :span_size].astype(jnp.bfloat16)
    delta_rim = with_halo(delta_position, (("seq", 1),), 3)
    delta_masked = jnp.zeros((page_count, span_size, model_width), jnp.float32)
    tap_columns = []
    for dilation in (1, 2, 3):
        for offset in (-1, 0, 1):
            column = 3 * (dilation - 1) + offset + 1
            anchor = 3 + offset * dilation
            anchor_back = 3 - offset * dilation
            delta_masked = (
                delta_masked
                + delta_rim[:, anchor_back : anchor_back + span_size, :] * conv_taps[:, column]
            )
            tap_columns.append(
                jnp.einsum(
                    "ptd,ptd->d",
                    delta_position,
                    rimmed[:, anchor : anchor + span_size, :],
                    preferred_element_type=jnp.float32,
                )
            )
    delta_taps = jnp.stack(tap_columns, axis=1)
    tokens_gradient = delta_hidden[:, :span_size] + delta_masked * text_factor.astype(jnp.float32)
    delta_patch_position = delta_hidden[:, span_size:].astype(jnp.bfloat16)
    delta_patch_rim = with_halo(delta_patch_position, (("seq", 1),), reach)
    delta_patch_masked = jnp.zeros((page_count, patch_span, model_width), jnp.float32)
    patch_columns = []
    for vertical in (-1, 0, 1):
        for horizontal in (-1, 0, 1):
            column = 3 * (vertical + 1) + horizontal + 1
            anchor = reach + vertical * GRID_SIDE + horizontal
            anchor_back = reach - vertical * GRID_SIDE - horizontal
            delta_patch_masked = (
                delta_patch_masked
                + delta_patch_rim[:, anchor_back : anchor_back + patch_span, :]
                * patch_taps[:, column]
            )
            patch_columns.append(
                jnp.einsum(
                    "ptd,ptd->d",
                    delta_patch_position,
                    patch_rimmed[:, anchor : anchor + patch_span, :],
                    preferred_element_type=jnp.float32,
                )
            )
    delta_patch_taps = jnp.stack(patch_columns, axis=1)
    patches_gradient = delta_hidden[:, span_size:] + delta_patch_masked * patch_factor.astype(
        jnp.float32
    )
    tail_bundle = attention_bundle(
        places, [flat(value) for value in (hidden_low, delta_queries, delta_keys, delta_values)], pages
    )
    tail_state = added(tail_bundle[0], swap(tail_bundle[1], "seq", 1))
    query_part, key_part, value_part = bundle_parts(
        bundle_sum(tail_state, pages), model_width // pages, places[1]
    )
    up_part, down_part, out_part = bundle_parts(
        bundle_sum(early_state, pages), up_weight.shape[1] // pages, places[1]
    )
    up_part = up_part.reshape(model_width // pages, -1)
    matrix_parts = (query_part, key_part, value_part, out_part, up_part, down_part)
    vector_parts = total_sum(
        (
            delta_taps,
            delta_patch_taps,
            delta_query_offset,
            delta_value_offset,
            middle_sums[OUT_BIAS],
            middle_sums[UP_BIAS : UP_BIAS + 4].reshape(-1),
            middle_sums[DOWN_BIAS],
            middle_sums[FIRST_GAIN],
            middle_sums[FIRST_SHIFT],
            middle_sums[SECOND_GAIN],
            middle_sums[SECOND_SHIFT],
            delta_line,
            delta_across,
            delta_upward,
        )
    )
    return (
        output,
        patch_output,
        tokens_gradient,
        patches_gradient,
        matrix_parts[0],
        matrix_parts[1],
        matrix_parts[2],
        matrix_parts[3],
        matrix_parts[4],
        matrix_parts[5],
        vector_parts[0],
        vector_parts[1],
        vector_parts[2],
        vector_parts[3],
        vector_parts[4],
        vector_parts[5],
        vector_parts[6],
        vector_parts[7],
        vector_parts[8],
        vector_parts[9],
        vector_parts[10],
        vector_parts[11],
        vector_parts[12],
        vector_parts[13],
    )


def solution(mesh):
    in_specs = (
        P("page", "seq", None),
        P("page", "seq", None),
        P("page"),
        P(None, "page", None),
        P(),
        P(),
        P(),
        P(),
        P(),
        P(),
        P(),
        P(),
        P(),
        P(),
        P(),
        P(),
        P(),
        P(),
        P(),
        P(),
        P(),
        P(),
        P(),
        P(),
        P("page", "seq", None),
        P("page", "seq", None),
    )
    out_specs = (
        P("page", "seq", None),
        P("page", "seq", None),
        P("page", "seq", None),
        P("page", "seq", None),
        P("page", "seq"),
        P("page", "seq"),
        P("page", "seq"),
        P("page", "seq"),
        P("page", "seq"),
        P("page", "seq"),
        P(),
        P(),
        P(),
        P(),
        P(),
        P(),
        P(),
        P(),
        P(),
        P(),
        P(),
        P(),
        P(),
        P(),
    )
    return jax.shard_map(shards, mesh=mesh, in_specs=in_specs, out_specs=out_specs, check_vma=False)
```

```python
import functools

import jax
import jax.numpy as jnp
from jax import lax
from jax.experimental import pallas as pl
from jax.experimental.pallas import tpu as pltpu
from jax.sharding import PartitionSpec as P

GRID_SIDE = 8


epsilon = 1e-05
coordinate_step = 16
masked_score = -1000000000.0
patch_pitch = 146
patch_centre = 73


def with_halo(cells, sides, width):
    for axis, dim in sides:
        count = lax.axis_size(axis)
        ends = count - 1
        head = lax.slice_in_dim(cells, 0, width, axis=dim)
        tail = lax.slice_in_dim(cells, cells.shape[dim] - width, cells.shape[dim], axis=dim)
        cells = jnp.concatenate(
            [
                lax.ppermute(tail, axis, [(i, (i + 1) % count) for i in range(ends)]),
                cells,
                lax.ppermute(head, axis, [((i + 1) % count, i) for i in range(ends)]),
            ],
            axis=dim,
        )
    return cells


def layer_norm(values, gain_vector, shift_vector):
    row_mean = jnp.mean(values, axis=-1, keepdims=True)
    centred = values - row_mean
    variance = jnp.mean(centred * centred, axis=-1, keepdims=True)
    return centred * lax.rsqrt(variance + epsilon) * gain_vector + shift_vector


def gelu_exact(values):
    return jax.nn.gelu(values, approximate=False)


def flat_dot(operand, matrix):
    front = operand.shape[:-1]
    result = jnp.dot(
        operand.reshape(-1, operand.shape[-1]), matrix, preferred_element_type=jnp.float32
    )
    return result.reshape(front + (matrix.shape[-1],))


def back_dot(operand, matrix):
    front = operand.shape[:-1]
    result = lax.dot_general(
        operand.reshape(-1, operand.shape[-1]),
        matrix,
        (((1,), (1,)), ((), ())),
        preferred_element_type=jnp.float32,
    )
    return result.reshape(front + (matrix.shape[0],))


def outer_dot(operand, gradient):
    return lax.dot_general(
        operand.reshape(-1, operand.shape[-1]),
        gradient.reshape(-1, gradient.shape[-1]),
        (((0,), (0,)), ((), ())),
        preferred_element_type=jnp.float32,
    )


def row_sum(gradient):
    return jnp.sum(gradient.astype(jnp.float32).reshape(-1, gradient.shape[-1]), axis=0)


def swap(value, axis, bit):
    count = lax.axis_size(axis)
    return lax.ppermute(value, axis, [(i, i ^ bit) for i in range(count)])


def total_sum(vectors):
    flat = jnp.concatenate([vector.reshape(-1) for vector in vectors])
    flat = jnp.pad(flat, (0, -flat.size % 1024)).reshape(-1, 128)
    for bit in (1, 2):
        flat = flat + swap(flat, "seq", bit)
    bit = 1
    while bit < lax.axis_size("page"):
        flat = flat + swap(flat, "page", bit)
        bit *= 2
    flat = flat.reshape(-1)
    result, start = [], 0
    for vector in vectors:
        result.append(flat[start : start + vector.size].reshape(vector.shape))
        start += vector.size
    return result


def query_places(seq_index, shape, span, patch_span, text_slots):
    row = lax.broadcasted_iota(jnp.int32, shape, 0)
    return jnp.where(
        row < span, seq_index * span + row, text_slots + seq_index * patch_span + row - span
    )


FIXED = 2048.0


def lookup(table_row, lanes):
    return jnp.take_along_axis(jnp.broadcast_to(table_row, lanes.shape), lanes, axis=1)


def pair_masked(pair):
    lane = lax.broadcasted_iota(jnp.int32, pair.shape, 1)
    half = pair.shape[1] // 2
    zero = jnp.zeros_like(pair)
    return jnp.concatenate(
        [jnp.where(lane < half, pair, zero), jnp.where(lane < half, zero, pair)], axis=0
    )


def pair_merged(both):
    rows, width = both.shape[0] // 2, both.shape[1]
    lane = lax.broadcasted_iota(jnp.int32, (rows, width), 1)
    return jnp.where(lane < width // 2, both[:rows], both[rows:])


def dot_nt(left, right):
    return lax.dot_general(left, right, (((1,), (1,)), ((), ())), preferred_element_type=jnp.float32)


def dot_nn(left, right):
    return lax.dot_general(left, right, (((1,), (0,)), ((), ())), preferred_element_type=jnp.float32)


def dot_tn(left, right):
    return lax.dot_general(left, right, (((0,), (0,)), ((), ())), preferred_element_type=jnp.float32)


CHUNK = 16


MESH = pl.DeviceIdType.MESH


def places_of(pages):
    page = lax.axis_index("page")
    seq = lax.axis_index("seq")
    bits = []
    rest = page
    for _ in range(pages.bit_length() - 1):
        bits.append(rest % 2)
        rest = rest // 2
    return page, bits, seq, seq // 2, seq % 2


def sibling_of(seq):
    return seq + 1 - 2 * (seq % 2)


def across_of(seq):
    return seq + 2 - 4 * (seq // 2)


def remote(source, target, send, receive, page, seq):
    return pltpu.make_async_remote_copy(
        src_ref=source, dst_ref=target, send_sem=send, recv_sem=receive, device_id=(page, seq), device_id_type=MESH
    )


def column_of(row):
    square = jnp.broadcast_to(row.astype(jnp.float32), (128, 128)).T
    return square[:, 0:1].astype(jnp.int32)


def forward_kernel(
    pages,
    length_ref, tokens_ref, patches_ref, box_ref, taps_ref, query_weight_ref, key_weight_ref, value_weight_ref,
    vector_ref, table_ref,
    hidden_ref, hidden_low_ref, query_ref, key_ref, value_ref, mixture_ref, weights_ref, columns_ref, rows_ref,
    query_rows_ref,
    arrived, text, grid, low, scores, across_ref, upward_ref, live_ref, line_ref, packed_ref,
    send_sem, recv_sem,
):
    page_at, _, seq, _, _ = places_of(pages)
    count, span, width = tokens_ref.shape
    patch_span = patches_ref.shape[1]
    row_count = span + patch_span
    key_pad = key_ref.shape[1]
    text_slots = 4 * span
    rim = 8
    pairs = weights_ref.shape[1]
    peers = (sibling_of(seq), across_of(seq))
    barrier = pltpu.get_barrier_semaphore()
    for peer in peers:
        pl.semaphore_signal(barrier, inc=1, device_id=(page_at, peer), device_id_type=MESH)
    pl.semaphore_wait(barrier, 2)

    def first_copies(page, side):
        return (
            remote(
                tokens_ref.at[page], arrived.at[side, page, 0:span], send_sem.at[2 * side, page],
                recv_sem.at[2 * side, page], page_at, peers[side],
            ),
            remote(
                patches_ref.at[page], arrived.at[side, page, span:row_count], send_sem.at[2 * side + 1, page],
                recv_sem.at[2 * side + 1, page], page_at, peers[side],
            ),
        )

    def onward_copy(page):
        return remote(
            arrived.at[1, page], arrived.at[2, page], send_sem.at[4, page], recv_sem.at[4, page], page_at, peers[0]
        )

    for page in range(count):
        for side in range(2):
            for copy in first_copies(page, side):
                copy.start()

    steps = jnp.floor(table_ref[...].astype(jnp.float32) * FIXED + 0.5).astype(jnp.int32)
    for pair in range(pairs):
        words = (steps[2 * pair : 2 * pair + 1] + 8192) + steps[2 * pair + 1 : 2 * pair + 2] * 65536
        packed_ref[0, pair : pair + 1, :] = words[:, 0:128]
        packed_ref[1, pair : pair + 1, :] = words[:, 128:256]
    key = lax.broadcasted_iota(jnp.int32, (row_count, key_pad), 1)
    place = query_places(seq, (row_count, key_pad), span, patch_span, text_slots)
    across_ref[...] = jnp.clip(key - place, -16, 15) + 16

    def fill(pair, carry):
        row = packed_ref[1, pl.ds(pair, 1), :]
        for at in range(0, key_pad, 128):
            line_ref[pair, :, at : at + 128] = lookup(row, across_ref[:, at : at + 128])
        return carry

    lax.fori_loop(0, pairs, fill, 0)
    text[0:rim, :] = jnp.zeros((rim, width), jnp.float32)
    text[rim + text_slots :, :] = jnp.zeros((rim, width), jnp.float32)
    grid[0:patch_span, :] = jnp.zeros((patch_span, width), jnp.float32)
    grid[patch_span * 5 :, :] = jnp.zeros((patch_span, width), jnp.float32)
    low[row_count * 4 :, :] = jnp.zeros((key_pad - row_count * 4, width), jnp.bfloat16)
    lanes = 256
    pair_width = 128
    power = 1.4426950408889634 / FIXED
    for copy in first_copies(0, 1):
        copy.wait_recv()
    onward_copy(0).start()

    def page_step(page, carry):
        length = length_ref[page]
        base = page * row_count
        cell = lax.broadcasted_iota(jnp.int32, (1, 128), 1)
        query_cell = seq * patch_span + cell
        row_cell = seq * patch_span + lax.broadcasted_iota(jnp.int32, (patch_span, 1), 0)
        for plane in range(2):
            boxes = box_ref[plane]
            of_page = lax.broadcasted_iota(jnp.int32, boxes.shape, 0) == page
            box = jnp.sum(jnp.where(of_page, boxes, 0), axis=0, keepdims=True)
            patch = 146 * ((cell % GRID_SIDE) if plane == 0 else (cell // GRID_SIDE)) + 73
            own_patch = 146 * ((query_cell % GRID_SIDE) if plane == 0 else (query_cell // GRID_SIDE)) + 73
            column_patch = 146 * ((row_cell % GRID_SIDE) if plane == 0 else (row_cell // GRID_SIDE)) + 73
            rows_ref[page, plane : plane + 1, 0:text_slots] = box
            rows_ref[page, plane : plane + 1, text_slots:key_pad] = patch
            own = rows_ref[page, plane : plane + 1, pl.ds(pl.multiple_of(seq * span, 128), span)]
            query_rows_ref[page, plane : plane + 1, 0:span] = own
            query_rows_ref[page, plane : plane + 1, span:256] = own_patch
            columns_ref[page, 0:span, plane * 128 : (plane + 1) * 128] = jnp.broadcast_to(column_of(own), (span, 128))
            columns_ref[page, span:row_count, plane * 128 : (plane + 1) * 128] = jnp.broadcast_to(
                column_patch, (patch_span, 128)
            )
        for plane, lanes_ref in enumerate((across_ref, upward_ref)):
            difference = rows_ref[page, plane : plane + 1, :] - columns_ref[page, :, plane * 128 : plane * 128 + 1]
            lanes_ref[...] = jnp.clip(difference >> 4, -32, 31) + (32 + 64 * plane)
        key_at = lax.broadcasted_iota(jnp.int32, live_ref.shape, 1)
        key_cell = key_at - text_slots
        live = (key_at < length) | (
            (key_cell >= 0) & ((key_cell >> 3) < GRID_SIDE - 1) & ((key_cell & 7) < GRID_SIDE - 1)
        )
        live_ref[...] = jnp.where(live, 0.0, masked_score * FIXED)
        for copy in first_copies(page, 0):
            copy.wait_recv()
        onward_copy(page).wait_recv()

        def block_of(step, start, stop, at):
            if step:
                return arrived[step - 1, page, start:stop, at].astype(jnp.float32)
            if start:
                return patches_ref[page, :, at].astype(jnp.float32)
            return tokens_ref[page, :, at].astype(jnp.float32)

        def slot_of(step):
            return (seq, peers[0], peers[1], sibling_of(peers[1]))[step]

        everything = slice(0, width)
        for step in range(4):
            where = slot_of(step)
            at_place = where * span + lax.broadcasted_iota(jnp.int32, (span, 1), 0)
            text[pl.ds(pl.multiple_of(rim + where * span, 8), span), :] = jnp.where(
                at_place < length, block_of(step, 0, span, everything), 0.0
            )
            at_cell = where * patch_span + lax.broadcasted_iota(jnp.int32, (patch_span, 1), 0)
            cell_live = ((at_cell >> 3) < GRID_SIDE - 1) & ((at_cell & 7) < GRID_SIDE - 1)
            grid[pl.ds(pl.multiple_of(patch_span + where * patch_span, 8), patch_span), :] = jnp.where(
                cell_live, block_of(step, span, row_count, everything), 0.0
            )
        for step in range(4):
            where = slot_of(step)

            def convolve(tile, carry):
                at = pl.ds(pl.multiple_of(tile * lanes, lanes), lanes)
                window = text[pl.ds(pl.multiple_of(where * span, 8), span + 2 * rim), at]
                centre = taps_ref[1:2, at] + taps_ref[4:5, at] + taps_ref[7:8, at]
                total = block_of(step, 0, span, at) + window[rim : rim + span] * centre
                for dilation in (1, 2, 3):
                    for offset in (-1, 1):
                        tap = 3 * (dilation - 1) + offset + 1
                        anchor = rim + offset * dilation
                        total = total + window[anchor : anchor + span] * taps_ref[tap : tap + 1, at]
                low[pl.ds(pl.multiple_of(where * span, 16), span), at] = total.astype(jnp.bfloat16)
                window = grid[pl.ds(pl.multiple_of(where * patch_span, 8), 3 * patch_span), at]
                patch_total = block_of(step, span, row_count, at)
                for vertical in (-1, 0, 1):
                    for horizontal in (-1, 0, 1):
                        tap = 9 + 3 * (vertical + 1) + horizontal + 1
                        anchor = patch_span + vertical * GRID_SIDE + horizontal
                        patch_total = patch_total + window[anchor : anchor + patch_span] * taps_ref[tap : tap + 1, at]
                low[pl.ds(pl.multiple_of(text_slots + where * patch_span, 16), patch_span), at] = (
                    patch_total.astype(jnp.bfloat16)
                )
                if step == 0:
                    for first, rows_here, value in ((0, span, total), (span, patch_span, patch_total)):
                        here = pl.ds(pl.multiple_of(base + first, 16), rows_here)
                        hidden_ref[here, at] = value
                        hidden_low_ref[here, at] = value.astype(jnp.bfloat16)
                return carry

            lax.fori_loop(0, width // lanes, convolve, 0)
        own_rows = pl.ds(pl.multiple_of(base, 16), row_count)

        def project(tile, carry):
            at = pl.ds(pl.multiple_of(tile * lanes, lanes), lanes)
            key_ref[page, :, at] = dot_nn(low[...], key_weight_ref[:, at]).astype(jnp.bfloat16)
            value_ref[page, :, at] = (dot_nn(low[...], value_weight_ref[:, at]) + vector_ref[1:2, at]).astype(
                jnp.bfloat16
            )
            query_ref[own_rows, at] = (
                (dot_nn(hidden_low_ref[own_rows, :], query_weight_ref[:, at]) + vector_ref[0:1, at])
                .astype(jnp.bfloat16)
                * jnp.bfloat16(0.125)
            )
            return carry

        lax.fori_loop(0, width // lanes, project, 0)

        @pl.when(page < count - 1)
        def _():
            for copy in first_copies(page + 1, 1):
                copy.wait_recv()
            onward_copy(page + 1).start()

        def attend(pair, carry):
            at = pl.ds(pl.multiple_of(pair * pair_width, pair_width), pair_width)
            scores[...] = dot_nt(pair_masked(query_ref[own_rows, at] * jnp.bfloat16(FIXED)), key_ref[page, :, at])
            plane_row = packed_ref[0, pl.ds(pair, 1), :]
            for start in range(0, row_count, CHUNK):
                here = slice(start, start + CHUNK)
                packed = []
                for block_at in range(0, key_pad, 128):
                    lane = slice(block_at, block_at + 128)
                    packed.append(
                        line_ref[pair, here, lane]
                        + lookup(plane_row, across_ref[here, lane])
                        + lookup(plane_row, upward_ref[here, lane])
                    )
                for side in range(2):
                    there = slice(side * row_count + start, side * row_count + start + CHUNK)
                    parts, top = [], None
                    for index, word in enumerate(packed):
                        lane = slice(128 * index, 128 * (index + 1))
                        field = (word >> 16) if side else (word & 0xFFFF)
                        part = (scores[there, lane] + field.astype(jnp.float32)) + live_ref[0:1, lane]
                        top = part if top is None else jnp.maximum(top, part)
                        parts.append(part)
                    top = jnp.max(top, axis=1, keepdims=True)
                    parts = [jnp.exp2((part - top) * power) for part in parts]
                    total = parts[0]
                    for part in parts[1:]:
                        total = total + part
                    inverse = 1.0 / jnp.sum(total, axis=1, keepdims=True)
                    for index, part in enumerate(parts):
                        weights_ref[page, pair, there, 128 * index : 128 * (index + 1)] = (part * inverse).astype(
                            jnp.bfloat16
                        )
            mixture_ref[own_rows, at] = pair_merged(
                dot_nn(weights_ref[page, pair], value_ref[page, :, at])
            ).astype(jnp.bfloat16)
            return carry

        lax.fori_loop(0, pairs, attend, 0)
        return carry

    lax.fori_loop(0, count, page_step, 0)
    for page in range(count):
        for side in range(2):
            for copy in first_copies(page, side):
                copy.wait_send()
        onward_copy(page).wait_send()


VMEM = pltpu.VMEM
KERNEL_VMEM = 48 * 1024 * 1024


def in_vmem(count):
    return [pl.BlockSpec(memory_space=VMEM)] * count


def forward(pages, lengths, tokens, patches, box, taps, matrices, vectors, table):
    count, span, width = tokens.shape
    patch_span = patches.shape[1]
    row_count = span + patch_span
    total_rows = count * row_count
    key_pad = -(-4 * row_count // 128) * 128
    pairs = table.shape[0] // 2
    bf16, f32, i32 = jnp.bfloat16, jnp.float32, jnp.int32
    own = jax.ShapeDtypeStruct((total_rows, width), bf16)
    every = jax.ShapeDtypeStruct((count, key_pad, width), bf16)
    return pl.pallas_call(
        functools.partial(forward_kernel, pages),
        out_shape=(
            jax.ShapeDtypeStruct((total_rows, width), f32), own, own, every, every, own,
            jax.ShapeDtypeStruct((count, pairs, 2 * row_count, key_pad), bf16),
            jax.ShapeDtypeStruct((count, row_count, 256), i32),
            jax.ShapeDtypeStruct((count, 8, key_pad), i32),
            jax.ShapeDtypeStruct((count, 8, 256), i32),
        ),
        in_specs=[pl.BlockSpec(memory_space=pltpu.SMEM)] + in_vmem(9),
        out_specs=tuple(in_vmem(10)),
        scratch_shapes=[
            VMEM((3, count, row_count, width), bf16),
            VMEM((4 * span + 16, width), f32),
            VMEM((6 * patch_span, width), f32),
            VMEM((key_pad, width), bf16),
            VMEM((2 * row_count, key_pad), f32),
            VMEM((row_count, key_pad), i32),
            VMEM((row_count, key_pad), i32),
            VMEM((8, key_pad), f32),
            VMEM((pairs, row_count, key_pad), i32),
            VMEM((2, 8, 128), i32),
            pltpu.SemaphoreType.DMA((5, count)),
            pltpu.SemaphoreType.DMA((5, count)),
        ],
        compiler_params=pltpu.CompilerParams(
            collective_id=0, has_side_effects=True, vmem_limit_bytes=KERNEL_VMEM
        ),
        cost_estimate=pl.CostEstimate(flops=8_000_000_000, bytes_accessed=25_000_000, transcendentals=3_000_000),
        name="forward",
    )(lengths, tokens, patches, box, taps, *matrices, vectors, table)


def backward_page_kernel(
    scalar_ref, columns_ref, rows_ref, query_rows_ref, query_ref, key_ref, value_ref, mixture_back_ref, weights_ref,
    query_back_ref, block_back_ref, plane_back_ref, line_back_ref,
    back, steps, mask_ref, hot_ref, query_hot_ref, band_ref,
):
    seq_index = scalar_ref[0]
    row_count, width = query_ref.shape
    key_pad = key_ref.shape[0]
    count = 4
    patch_span = GRID_SIDE * GRID_SIDE // count
    span = row_count - patch_span
    text_slots = span * count
    columns, rows = columns_ref[...], rows_ref[...]
    mask_ref[:, 0:key_pad] = ((rows[0:1, :] & 15) < (columns[:, 0:1] & 15)).astype(jnp.float32).astype(jnp.bfloat16)
    mask_ref[:, key_pad:] = ((rows[1:2, :] & 15) < (columns[:, 1:2] & 15)).astype(jnp.float32).astype(jnp.bfloat16)
    bin_at = lax.broadcasted_iota(jnp.int32, (128, key_pad), 0) - 1
    key_block = lax.broadcasted_iota(jnp.int32, (128, key_pad), 1) >> 4
    for side in range(2):
        key_bin = rows[side : side + 1, :] >> 4
        plain = (key_bin == bin_at).astype(jnp.float32)
        lower = (key_bin - 1 == bin_at).astype(jnp.float32)
        plain, lower = jnp.where(bin_at < 64, plain, 0.0), jnp.where(bin_at < 64, lower, 0.0)
        mine = slice(128 * side, 128 * (side + 1))
        other = slice(128 * (1 - side), 128 * (2 - side))
        change = lower - plain
        if side == 0:
            plain = jnp.where(bin_at - 71 == key_block, 1.0, plain)
        hot_ref[mine, 0:key_pad] = plain.astype(jnp.bfloat16)
        hot_ref[mine, (1 + side) * key_pad : (2 + side) * key_pad] = change.astype(jnp.bfloat16)
        hot_ref[other, (1 + side) * key_pad : (2 + side) * key_pad] = jnp.zeros((128, key_pad), jnp.bfloat16)
    half_bin = lax.broadcasted_iota(jnp.int32, (72, row_count), 0)
    for side in range(2):
        query_hot_ref[72 * side : 72 * (side + 1), :] = (
            (71 - (query_rows_ref[side : side + 1, :] >> 4) == half_bin).astype(jnp.float32).astype(jnp.bfloat16)
        )
    lane128 = lax.broadcasted_iota(jnp.int32, (row_count, 128), 1)
    place = query_places(seq_index, (row_count, 128), span, patch_span, text_slots)
    aim = place + lane128 - 32
    near = (lane128 < 64) & (aim >= 0) & (aim < text_slots + patch_span * count)
    apart = (aim >> 4) - (place >> 4)
    near = near & (apart >= -1) & (apart <= 1)
    band_ref[...] = jnp.where(near, aim, -1)
    pair_width = 128
    line_back_ref[...] = jnp.zeros_like(line_back_ref)
    plane_back_ref[...] = jnp.zeros_like(plane_back_ref)

    def attend(pair, carry):
        at = pl.ds(pl.multiple_of(pair * pair_width, pair_width), pair_width)
        both_query = pair_masked(query_ref[:, at])
        both_back = pair_masked(mixture_back_ref[:, at])
        back[...] = dot_nt(both_back, value_ref[:, at])
        for start in range(0, 2 * row_count, CHUNK):
            there = slice(start, start + CHUNK)
            here = slice(start % row_count, start % row_count + CHUNK)
            parts, total = [], None
            for block_at in range(0, key_pad, 128):
                lane = slice(block_at, block_at + 128)
                part = weights_ref[pair, there, lane].astype(jnp.float32)
                product = part * back[there, lane]
                total = product if total is None else total + product
                parts.append(part)
            mean = jnp.sum(total, axis=1, keepdims=True)
            for index, part in enumerate(parts):
                lane = slice(128 * index, 128 * (index + 1))
                step = (part * (back[there, lane] - mean)).astype(jnp.bfloat16)
                steps[there, lane] = step
                steps[there, key_pad + 128 * index : key_pad + 128 * (index + 1)] = step * mask_ref[here, lane]
                steps[there, 2 * key_pad + 128 * index : 2 * key_pad + 128 * (index + 1)] = (
                    step * mask_ref[here, key_pad + 128 * index : key_pad + 128 * (index + 1)]
                )
        query_back_ref[:, at] = (pair_merged(dot_nn(steps[:, 0:key_pad], key_ref[:, at])) * 0.125).astype(
            jnp.bfloat16
        )
        for kind, value in enumerate(
            (dot_tn(steps[:, 0:key_pad], both_query), dot_tn(weights_ref[pair], both_back))
        ):
            value = value.astype(jnp.bfloat16)
            for where in range(count):
                step_at = seq_index ^ where
                slot = (step_at & 1) * 2 + (step_at >> 1)
                block_back_ref[slot, kind, 0:span, at] = value[where * span : (where + 1) * span]
                block_back_ref[slot, kind, span:row_count, at] = value[
                    text_slots + where * patch_span : text_slots + (where + 1) * patch_span
                ]
        bins = dot_nt(steps[...], hot_ref[...])
        low_bins = bins.astype(jnp.bfloat16)
        lane_one = lax.broadcasted_iota(jnp.int32, (1, 128), 1)
        far = lane128 - 72 - (place >> 4)
        in_line = (lane128 >= 72) & (lane128 < 72 + key_pad // 16)
        for side in range(2):
            head = pl.ds(2 * pair + side, 1)
            own = slice(side * row_count, (side + 1) * row_count)
            both = dot_nn(query_hot_ref[...], low_bins[own])
            for plane in range(2):
                table = both[72 * plane : 72 * (plane + 1), 128 * plane : 128 * (plane + 1)]
                wide_lane = lax.broadcasted_iota(jnp.int32, table.shape, 1)
                table = jnp.where(wide_lane < 72, table, 0.0)
                table = jnp.concatenate([table, jnp.zeros_like(table)], axis=1)
                sheared = pltpu.roll(table, 0, 1, stride=1, stride_axis=0)
                plane_back_ref[plane, head, :] = jnp.sum(sheared, axis=0, keepdims=True)
            line_bins = bins[own, 0:128]
            low_tail = jnp.sum(jnp.where(in_line & (far <= -2), line_bins, 0.0), axis=(0, 1), keepdims=True)
            high_tail = jnp.sum(jnp.where(in_line & (far >= 2), line_bins, 0.0), axis=(0, 1), keepdims=True)
            band = jnp.zeros((1, 128), jnp.float32)
            base = side * row_count
            for first, rows_here, block in (
                (0, span, seq_index),
                (0, 32, jnp.maximum(seq_index - 1, 0)),
                (span - 32, 32, seq_index + 1),
                (span, patch_span, count - 1),
                (span, patch_span, count),
            ):
                aims = band_ref[first : first + rows_here, :]
                source = steps[
                    base + first : base + first + rows_here, pl.ds(pl.multiple_of(block * 128, 128), 128)
                ].astype(jnp.float32)
                taken = jnp.take_along_axis(source, aims & 127, axis=1)
                right = (aims >> 7) == block
                if first == 0 and rows_here == 32:
                    right = right & (seq_index > 0)
                band = band + jnp.sum(jnp.where(right, taken, 0.0), axis=0, keepdims=True)
            line_back_ref[head, :] = (
                band + jnp.where(lane_one == 0, low_tail, 0.0) + jnp.where(lane_one == 63, high_tail, 0.0)
            )
        return carry

    lax.fori_loop(0, width // pair_width, attend, 0)


def backward_page(scalars, columns, rows, query_rows, queries, keys, values, mixture_back, weights):
    row_count, width = queries.shape
    key_pad = keys.shape[0]
    heads = 2 * weights.shape[0]
    return pl.pallas_call(
        backward_page_kernel,
        out_shape=(
            jax.ShapeDtypeStruct((row_count, width), jnp.bfloat16),
            jax.ShapeDtypeStruct((4, 2, row_count, width), jnp.bfloat16),
            jax.ShapeDtypeStruct((2, heads, 256), jnp.float32),
            jax.ShapeDtypeStruct((heads, 128), jnp.float32),
        ),
        in_specs=[pl.BlockSpec(memory_space=pltpu.SMEM)] + in_vmem(8),
        out_specs=tuple(in_vmem(4)),
        scratch_shapes=[
            pltpu.VMEM((2 * row_count, key_pad), jnp.float32),
            pltpu.VMEM((2 * row_count, 3 * key_pad), jnp.bfloat16),
            pltpu.VMEM((row_count, 2 * key_pad), jnp.bfloat16),
            pltpu.VMEM((256, 3 * key_pad), jnp.bfloat16),
            pltpu.VMEM((144, row_count), jnp.bfloat16),
            pltpu.VMEM((row_count, 128), jnp.int32),
        ],
        compiler_params=pltpu.CompilerParams(vmem_limit_bytes=KERNEL_VMEM),
        cost_estimate=pl.CostEstimate(flops=3_000_000_000, bytes_accessed=6_000_000, transcendentals=1_000_000),
        name="backward_page",
    )(scalars, columns, rows, query_rows, queries, keys, values, mixture_back, weights)


def early_orders(far, side):
    return (far[1], far[0], side) + tuple(far[2:]), (far[0], far[1], side) + tuple(far[2:])


def late_orders(far, side):
    return (side,) + tuple(far), (far[0], side) + tuple(far[1:])


def slot_of_bits(bits):
    slot = 0
    for bit in bits:
        slot = slot * 2 + bit
    return slot


def apart(one, other):
    return (one + other) % 2


def early_slots(scalar_ref, page, column, levels):
    far = [apart((page >> level) & 1, (scalar_ref[2] >> level) & 1) for level in range(levels)]
    side = apart(column, scalar_ref[3])
    return [slot_of_bits(order) for order in early_orders(far, side)]


NORM_CHUNK = 48


def norm_rows(values):
    mean = jnp.mean(values, axis=-1, keepdims=True)
    centred = values - mean
    scale = lax.rsqrt(jnp.mean(centred * centred, axis=-1, keepdims=True) + epsilon)
    return centred * scale, scale


def norm_back(delta, unit, scale):
    return scale * (
        delta
        - jnp.mean(delta, axis=-1, keepdims=True)
        - unit * jnp.mean(delta * unit, axis=-1, keepdims=True)
    )


def column_sum(values):
    return jnp.sum(values, axis=0, keepdims=True)


OUT_BIAS, DOWN_BIAS, FIRST_GAIN, FIRST_SHIFT, SECOND_GAIN, SECOND_SHIFT = range(6)
UP_BIAS = 6


def middle_kernel(
    pages, direct,
    scalar_ref, hidden_ref, mixture_ref, cotangent_ref, patch_cotangent_ref, out_weight_ref, up_weight_ref,
    down_weight_ref, vector_ref,
    output_ref, patch_output_ref, first_back_ref, mixture_back_ref, sums_ref, *rest,
):
    if direct:
        bundle_ref, *rest = rest
    else:
        normed_out_ref, up_out_ref, activated_out_ref, down_out_ref, attention_out_ref, *rest = rest
    state, unit, scale_ref, normed, activated, slope, up_back, down_back, attention_back, flipped = rest
    count, span, width = output_ref.shape
    patch_span = patch_output_ref.shape[1]
    row_count = span + patch_span
    total_rows = count * row_count
    wide = up_weight_ref.shape[1]
    lanes = 256
    sums_ref[...] = jnp.zeros_like(sums_ref)

    def tile_at(tile):
        return pl.ds(pl.multiple_of(tile * lanes, lanes), lanes)

    def attention_tile(tile, carry):
        at = tile_at(tile)
        state[:, at] = hidden_ref[:, at] + (dot_nn(mixture_ref[...], out_weight_ref[:, at]) + vector_ref[2:3, at])
        return carry

    lax.fori_loop(0, width // lanes, attention_tile, 0)

    def first_norm(chunk, carry):
        here = pl.ds(pl.multiple_of(chunk * NORM_CHUNK, 16), NORM_CHUNK)
        rows, scale = norm_rows(state[here, :])
        unit[here, :] = rows
        scale_ref[here, :] = jnp.broadcast_to(scale, (NORM_CHUNK, 128))
        rows = rows * vector_ref[4:5, :] + vector_ref[5:6, :]
        state[here, :] = rows
        normed[here, :] = rows.astype(jnp.bfloat16)
        return carry

    lax.fori_loop(0, total_rows // NORM_CHUNK, first_norm, 0)

    def up_tile(tile, carry):
        at = tile_at(tile)
        branch = dot_nn(normed[...], up_weight_ref[:, at]) + vector_ref[pl.ds(8 + tile // 3, 1), tile_at(tile % 3)]
        chance = 0.5 * (1.0 + lax.erf(branch * 0.7071067811865476))
        activated[:, at] = (branch * chance).astype(jnp.bfloat16)
        slope[:, at] = chance + branch * (jnp.exp(branch * branch * -0.5) * 0.3989422804014327)
        return carry

    lax.fori_loop(0, wide // lanes, up_tile, 0)

    def down_tile(tile, carry):
        at = tile_at(tile)
        state[:, at] = state[:, at] + (dot_nn(activated[...], down_weight_ref[:, at]) + vector_ref[3:4, at])
        return carry

    lax.fori_loop(0, width // lanes, down_tile, 0)

    def second_norm(start, rows_here, page, out_ref, delta_ref):
        here = pl.ds(pl.multiple_of(page * row_count + start, 16), rows_here)
        there = pl.ds(0 if start == span else start, rows_here)
        rows, scale = norm_rows(state[here, :])
        out_ref[page, there, :] = rows * vector_ref[6:7, :] + vector_ref[7:8, :]
        delta = delta_ref[page, there, :].astype(jnp.float32)
        back = norm_back(delta * vector_ref[6:7, :], rows, scale)
        state[here, :] = back
        low = back.astype(jnp.bfloat16)
        down_back[here, :] = low
        for index, value in (
            (SECOND_GAIN, delta * rows), (SECOND_SHIFT, delta), (DOWN_BIAS, low.astype(jnp.float32))
        ):
            sums_ref[index : index + 1, :] += column_sum(value)

    def second_page(page, carry):
        for start in range(0, span, 32):
            second_norm(start, 32, page, output_ref, cotangent_ref)
        second_norm(span, patch_span, page, patch_output_ref, patch_cotangent_ref)
        return carry

    lax.fori_loop(0, count, second_page, 0)

    def up_back_tile(tile, carry):
        at = tile_at(tile)
        low = (dot_nt(down_back[...], down_weight_ref[at, :]) * slope[:, at]).astype(jnp.bfloat16)
        up_back[:, at] = low
        sums_ref[pl.ds(UP_BIAS + tile // 3, 1), tile_at(tile % 3)] = column_sum(low.astype(jnp.float32))
        return carry

    lax.fori_loop(0, wide // lanes, up_back_tile, 0)

    def normed_back_tile(tile, carry):
        at = tile_at(tile)
        state[:, at] = state[:, at] + dot_nt(up_back[...], up_weight_ref[at, :])
        return carry

    lax.fori_loop(0, width // lanes, normed_back_tile, 0)

    def first_back(chunk, carry):
        here = pl.ds(pl.multiple_of(chunk * NORM_CHUNK, 16), NORM_CHUNK)
        delta, rows = state[here, :], unit[here, :]
        back = norm_back(delta * vector_ref[4:5, :], rows, scale_ref[here, 0:1])
        first_back_ref[here, :] = back
        low = back.astype(jnp.bfloat16)
        attention_back[here, :] = low
        for index, value in (
            (FIRST_GAIN, delta * rows), (FIRST_SHIFT, delta), (OUT_BIAS, low.astype(jnp.float32))
        ):
            sums_ref[index : index + 1, :] += column_sum(value)
        return carry

    lax.fori_loop(0, total_rows // NORM_CHUNK, first_back, 0)

    def mixture_tile(tile, carry):
        at = tile_at(tile)
        mixture_back_ref[:, at] = dot_nt(attention_back[...], out_weight_ref[at, :]).astype(jnp.bfloat16)
        return carry

    lax.fori_loop(0, width // lanes, mixture_tile, 0)
    if not direct:
        normed_out_ref[...] = normed[...]
        up_out_ref[...] = up_back[...]
        activated_out_ref[...] = activated[...]
        down_out_ref[...] = down_back[...]
        attention_out_ref[...] = attention_back[...]
        return
    levels = pages.bit_length() - 1
    core = scalar_ref[1]
    rows = width // pages
    tall = wide // pages
    block = 384
    groups = wide // (2 * block)
    flipped[...] = normed[...].T

    def up_weight_tile(tile, carry):
        column, group = tile // groups, tile % groups
        at = pl.ds(pl.multiple_of(tile * block, block), block)
        result = dot_nn(flipped[...], up_back[:, at]).astype(jnp.bfloat16)
        for page in range(pages):
            slot = early_slots(scalar_ref, page, column, levels)[0]
            bundle_ref[core, slot, pl.ds(pl.multiple_of(group * rows, 16), rows), :] = result[
                page * rows : (page + 1) * rows
            ]
        return carry

    lax.fori_loop(0, 2 * groups, up_weight_tile, 0)

    def down_weight_tile(page, carry):
        at = pl.ds(pl.multiple_of(page * tall, 128), tall)
        result = dot_tn(activated[:, at], down_back[...]).astype(jnp.bfloat16)
        for column in range(2):
            slot = early_slots(scalar_ref, page, column, levels)[1]
            bundle_ref[1 - core, slot, 0:tall, :] = result[:, column * block : (column + 1) * block]
        return carry

    lax.fori_loop(0, pages, down_weight_tile, 0)
    flipped[...] = mixture_ref[...].T
    half = rows // 2

    def out_weight_tile(column, carry):
        at = pl.ds(pl.multiple_of(column * block, block), block)
        result = dot_nn(flipped[...], attention_back[:, at]).astype(jnp.bfloat16)
        for page in range(pages):
            slots = early_slots(scalar_ref, page, column, levels)
            for order in range(2):
                first = page * rows + order * half
                bundle_ref[core if order == 0 else 1 - core, slots[order], tall : tall + half, :] = result[
                    first : first + half
                ]
        return carry

    lax.fori_loop(0, 2, out_weight_tile, 0)


def in_tiles(width, pages):
    return (width // pages) % 32 == 0 and pages >= 4


def middle(places, hidden, mixture, cotangent, patch_cotangent, matrices, vectors, pages):
    count, span, width = cotangent.shape
    patch_span = patch_cotangent.shape[1]
    total_rows = hidden.shape[0]
    wide = matrices[1].shape[1]
    direct = in_tiles(width, pages)
    bf16, f32 = jnp.bfloat16, jnp.float32
    if direct:
        extra = (jax.ShapeDtypeStruct((2, 2 * pages, (wide + width // 2) // pages, 384), bf16),)
    else:
        extra = tuple(
            jax.ShapeDtypeStruct((total_rows, size), bf16) for size in (width, wide, wide, width, width)
        )
    result = pl.pallas_call(
        functools.partial(middle_kernel, pages, direct),
        out_shape=(
            jax.ShapeDtypeStruct(cotangent.shape, f32),
            jax.ShapeDtypeStruct(patch_cotangent.shape, f32),
            jax.ShapeDtypeStruct((total_rows, width), f32),
            jax.ShapeDtypeStruct((total_rows, width), bf16),
            jax.ShapeDtypeStruct((16, width), f32),
        )
        + extra,
        in_specs=[pl.BlockSpec(memory_space=pltpu.SMEM)] + in_vmem(8),
        out_specs=tuple(in_vmem(5 + len(extra))),
        scratch_shapes=[
            pltpu.VMEM((total_rows, width), f32),
            pltpu.VMEM((total_rows, width), f32),
            pltpu.VMEM((total_rows, 128), f32),
            pltpu.VMEM((total_rows, width), bf16),
            pltpu.VMEM((total_rows, wide), bf16),
            pltpu.VMEM((total_rows, wide), f32),
            pltpu.VMEM((total_rows, wide), bf16),
            pltpu.VMEM((total_rows, width), bf16),
            pltpu.VMEM((total_rows, width), bf16),
            pltpu.VMEM((width, total_rows), bf16),
        ],
        compiler_params=pltpu.CompilerParams(vmem_limit_bytes=56 * 1024 * 1024),
        cost_estimate=pl.CostEstimate(flops=14_000_000_000, bytes_accessed=30_000_000, transcendentals=2_600_000),
        name="middle",
    )(places, hidden, mixture, cotangent, patch_cotangent, *matrices, vectors)
    first, rest = result[:5], result[5:]
    if direct:
        return first + rest
    normed, up_back, activated, down_back, attention_back = rest
    return first + (
        indexed_bundle(
            (
                ((normed, up_back, None), (mixture, attention_back, 0)),
                ((activated, down_back, None), (mixture, attention_back, 1)),
            ),
            places,
            pages,
        ),
    )


def indexed_bundle(matrices, scalars, pages):
    levels = pages.bit_length() - 1
    place = jnp.arange(2 * pages, dtype=jnp.int32)
    bits = [(place >> (levels - k)) & 1 for k in range(levels + 1)]
    halves = []
    for order, group in enumerate(matrices):
        side, near = (bits[0], bits[1]) if order == 0 else (bits[1], bits[0])
        far = near
        for level in range(1, levels):
            far = far + (bits[level + 1] << level)
        index = (far ^ scalars[2]) * 2 + (side ^ scalars[3])
        blocks = []
        for operand, gradient, part in group:
            rows = in_blocks(outer_dot(operand, gradient).astype(jnp.bfloat16), pages)
            if part is not None:
                half = rows.shape[1] // 2
                rows = rows[:, part * half : (part + 1) * half]
            blocks.append(rows)
        halves.append(jnp.concatenate(blocks, axis=1)[index])
    first, second = halves
    mine = scalars[1] == 0
    return jnp.stack([jnp.where(mine, first, second), jnp.where(mine, second, first)])


def in_blocks(matrix, pages):
    rows, columns = matrix.shape[0] // pages, matrix.shape[1] // 2
    lanes = min(columns, 384)
    blocks = matrix.reshape(pages, rows, 2, columns // lanes, lanes)
    return blocks.transpose(0, 2, 3, 1, 4).reshape(pages * 2, rows * columns // lanes, lanes)


class Halving:
    def __init__(self, keep, source, landing, landings, partners, sibling, sems, chunks):
        self.keep, self.landing, self.landings = keep, landing, landings
        total = keep.shape[0]
        unit = total // chunks
        send_sem, recv_sem = sems
        self.arrivals, self.sends, self.needs = {}, {}, {}
        used = 0
        for chunk in range(chunks):
            lo = total - (chunk + 1) * unit
            copy = remote(
                source.at[lo : lo + unit], landing.at[lo : lo + unit], send_sem.at[used], recv_sem.at[used], *sibling
            )
            self.arrivals["core", chunk] = (copy, landing, lo, unit)
            used += 1
        for step, (into, partner) in enumerate(zip(landings, partners, strict=True)):
            size = total >> (step + 1)
            piece = min(unit, size)
            for chunk in range(size // piece):
                lo = size - (chunk + 1) * piece
                copy = remote(
                    keep.at[size + lo : size + lo + piece], into.at[lo : lo + piece], send_sem.at[used],
                    recv_sem.at[used], *partner,
                )
                self.arrivals[step, chunk] = (copy, into, lo, piece)
                self.sends[step, chunk] = copy
                self.needs[step, chunk] = {
                    (source_step, block)
                    for block in range(size + lo, size + lo + piece)
                    for source_step in ("core", *range(step))
                }
                used += 1
        self.done = set()

    def start(self):
        for key, (copy, *_) in self.arrivals.items():
            if key[0] == "core":
                copy.start()

    def take(self, *key):
        copy, into, lo, count = self.arrivals[key]
        copy.wait_recv()

        def add(block, carry):
            self.keep[block] = self.keep[block] + into[block]
            return carry

        lax.fori_loop(lo, lo + count, add, 0)
        for block in range(lo, lo + count):
            self.done.add((key[0], block))
        for name in list(self.sends):
            if self.needs[name] <= self.done:
                self.sends.pop(name).start()

    def finish(self):
        for copy, *_ in self.arrivals.values():
            copy.wait_send()


def backward_kernel(
    pages,
    length_ref, query_ref, mixture_back_ref, columns_ref, rows_ref, query_rows_ref, tokens_ref, patches_ref, taps_ref,
    middle_sums_ref, bundle_any, weights_any, key_any, value_any, hidden_any, first_back_any, query_weight_any,
    key_weight_any, value_weight_any,
    tokens_back_ref, patches_back_ref, early_ref, late_ref, sums_ref,
    keep, landing, landings, late, late_landing, late_landings, weights_buf, key_buf, value_buf, outgoing, from_sib,
    from_far, matrices, hidden, flipped, total_back, query_back, key_back, value_back, back, steps, mask_ref, hot_ref,
    query_hot_ref, band_ref, table_acc, band_acc, table_out, text_rim, patch_rim, sums, sums_in,
    load_sem, page_sem, early_send, early_recv, late_send, late_recv, sib_send, sib_recv, far_send, far_recv, rim_send,
    rim_recv, sum_send, sum_recv,
):
    page_at, bits, seq, across, core = places_of(pages)
    levels = len(bits)
    count, span, width = tokens_ref.shape
    patch_span = patches_ref.shape[1]
    row_count = span + patch_span
    total_rows = count * row_count
    key_pad = key_buf.shape[1]
    text_slots = 4 * span
    pairs = weights_buf.shape[1]
    heads = 2 * pairs
    f32, bf16 = jnp.float32, jnp.bfloat16

    sibling = (page_at, sibling_of(seq))
    opposite = (page_at, across_of(seq))
    diagonal = (page_at, sibling_of(across_of(seq)))
    flips = [(1 - 2 * bit) * 2**level for level, bit in enumerate(bits)]
    on_page = [(page_at + flip, seq) for flip in flips]
    either = lambda first, second: first + core * (second - first)
    early_partners = [
        (page_at + either(flips[1], flips[0]), seq),
        (page_at + either(flips[0], flips[1]), seq),
        opposite,
    ] + on_page[2:]
    late_partners = [
        (page_at + core * flips[0], seq + (1 - core) * (2 - 4 * across)),
        (page_at + (1 - core) * flips[0], seq + core * (2 - 4 * across)),
    ] + on_page[1:]
    barrier = pltpu.get_barrier_semaphore()
    everyone = [sibling, opposite, diagonal] + on_page
    for peer in everyone:
        pl.semaphore_signal(barrier, inc=1, device_id=peer, device_id_type=MESH)

    keep_load = pltpu.make_async_copy(bundle_any.at[0], keep, load_sem.at[0])
    later_loads = [
        pltpu.make_async_copy(source, target, load_sem.at[1 + index])
        for index, (source, target) in enumerate(
            (
                (query_weight_any, matrices.at[0]), (key_weight_any, matrices.at[1]),
                (value_weight_any, matrices.at[2]), (hidden_any, hidden), (first_back_any, total_back),
            )
        )
    ]

    def page_loads(page):
        slot = page % 2
        return [
            pltpu.make_async_copy(source.at[page], target.at[slot], page_sem.at[index, slot])
            for index, (source, target) in enumerate(
                ((weights_any, weights_buf), (key_any, key_buf), (value_any, value_buf))
            )
        ]

    for copy in page_loads(0):
        copy.start()
    keep_load.start()
    for copy in later_loads:
        copy.start()
    pl.semaphore_wait(barrier, len(everyone))
    early = Halving(
        keep, bundle_any.at[1], landing, landings, early_partners, sibling, (early_send, early_recv), 8
    )
    late_sum = Halving(
        late.at[0], late.at[1], late_landing, late_landings, late_partners, sibling, (late_send, late_recv), 4
    )
    early.start()

    lane128 = lax.broadcasted_iota(jnp.int32, (row_count, 128), 1)
    place = query_places(seq, (row_count, 128), span, patch_span, text_slots)
    aim = place + lane128 - 32
    blocks_on = (aim >> 4) - (place >> 4)
    near = (lane128 < 64) & (aim >= 0) & (aim < text_slots + patch_span * 4) & (blocks_on >= -1) & (blocks_on <= 1)
    band_ref[...] = jnp.where(near, aim, -1)
    table_acc[...] = jnp.zeros_like(table_acc)
    band_acc[...] = jnp.zeros_like(band_acc)
    lane_of_row = lax.broadcasted_iota(jnp.int32, (48, row_count), 1)
    place_of_row = jnp.where(
        lane_of_row < span, seq * span + lane_of_row, text_slots + seq * patch_span + lane_of_row - span
    )
    query_hot_ref[144:192, :] = (
        ((place_of_row >> 4) == lax.broadcasted_iota(jnp.int32, (48, row_count), 0)).astype(f32).astype(bf16)
    )
    pair_width = 128

    def start_page(page):
        slot = page % 2
        for copy in page_loads(page):
            copy.wait()

        @pl.when(page < count - 1)
        def _():
            for copy in page_loads(page + 1):
                copy.start()

        bin_at = lax.broadcasted_iota(jnp.int32, (128, key_pad), 0) - 1
        key_block = lax.broadcasted_iota(jnp.int32, (128, key_pad), 1) >> 4
        half_bin = lax.broadcasted_iota(jnp.int32, (72, row_count), 0)
        for side in range(2):
            key_row = rows_ref[page, side : side + 1, :]
            query_column = columns_ref[page, :, 128 * side : 128 * side + 1]
            mask_ref[:, side * key_pad : (side + 1) * key_pad] = (
                ((key_row & 15) < (query_column & 15)).astype(f32).astype(bf16)
            )
            key_bin = key_row >> 4
            plain = jnp.where(bin_at < 64, (key_bin == bin_at).astype(f32), 0.0)
            lower = jnp.where(bin_at < 64, (key_bin - 1 == bin_at).astype(f32), 0.0)
            mine = slice(128 * side, 128 * (side + 1))
            other = slice(128 * (1 - side), 128 * (2 - side))
            change = lower - plain
            if side == 0:
                plain = jnp.where(bin_at - 71 == key_block, 1.0, plain)
            hot_ref[mine, 0:key_pad] = plain.astype(bf16)
            hot_ref[mine, (1 + side) * key_pad : (2 + side) * key_pad] = change.astype(bf16)
            hot_ref[other, (1 + side) * key_pad : (2 + side) * key_pad] = jnp.zeros((128, key_pad), bf16)
            query_bin = query_rows_ref[page, side : side + 1, 0:row_count] >> 4
            query_hot_ref[72 * side : 72 * (side + 1), :] = (71 - query_bin == half_bin).astype(f32).astype(bf16)

    def attend(page, pair):
        slot = page % 2
        at = pl.ds(pl.multiple_of(pair * pair_width, pair_width), pair_width)
        own_rows = pl.ds(pl.multiple_of(page * row_count, 16), row_count)
        both_query = pair_masked(query_ref[own_rows, at])
        both_back = pair_masked(mixture_back_ref[own_rows, at])
        back[...] = dot_nt(both_back, value_buf[slot, :, at])
        for start in range(0, 2 * row_count, CHUNK):
            there = slice(start, start + CHUNK)
            here = slice(start % row_count, start % row_count + CHUNK)
            parts, total = [], None
            for block_at in range(0, key_pad, 128):
                lane = slice(block_at, block_at + 128)
                part = weights_buf[slot, pair, there, lane].astype(f32)
                product = part * back[there, lane]
                total = product if total is None else total + product
                parts.append(part)
            mean = jnp.sum(total, axis=1, keepdims=True)
            for index, part in enumerate(parts):
                lane = slice(128 * index, 128 * (index + 1))
                step = (part * (back[there, lane] - mean)).astype(bf16)
                steps[there, lane] = step
                steps[there, key_pad + 128 * index : key_pad + 128 * (index + 1)] = step * mask_ref[here, lane]
                steps[there, 2 * key_pad + 128 * index : 2 * key_pad + 128 * (index + 1)] = (
                    step * mask_ref[here, key_pad + 128 * index : key_pad + 128 * (index + 1)]
                )
        query_back[own_rows, at] = (
            pair_merged(dot_nn(steps[:, 0:key_pad], key_buf[slot, :, at])) * 0.125
        ).astype(bf16)
        for kind, value in enumerate(
            (dot_tn(steps[:, 0:key_pad], both_query), dot_tn(weights_buf[slot, pair], both_back))
        ):
            value = value.astype(bf16)
            for where in range(4):
                place_at = apart(where % 2, core) * 2 + apart(where // 2, across)
                outgoing[page, place_at, kind, 0:span, at] = value[where * span : (where + 1) * span]
                outgoing[page, place_at, kind, span:row_count, at] = value[
                    text_slots + where * patch_span : text_slots + (where + 1) * patch_span
                ]
        bins = dot_nt(steps[...], hot_ref[...]).astype(bf16)
        for side in range(2):
            head = 2 * pair + side
            base = side * row_count
            both = dot_nn(query_hot_ref[...], bins[base : base + row_count])
            table_acc[head, 0:72, :] += both[0:72, 0:128]
            table_acc[head, 72:144, :] += both[72:144, 128:256]
            table_acc[head, 144:192, :] += both[144:192, 0:128]
            for first, rows_here, block, into in bands():
                source = steps[
                    base + first : base + first + rows_here, pl.ds(pl.multiple_of(block * 128, 128), 128)
                ]
                band_acc[head, into : into + rows_here, :] += source.astype(f32)

    def bands():
        before = seq - (seq + 3) // 4
        return (
            (0, span, seq, 0),
            (0, 32, before, span),
            (span - 32, 32, seq + 1, span + 32),
            (span, patch_span, 3, span + 64),
            (span, patch_span, 4, span + 64 + patch_span),
        )

    def sib_copy(page):
        return remote(outgoing.at[page, 2:4], from_sib.at[page], sib_send.at[page], sib_recv.at[page], *sibling)

    def far_copy(page):
        return remote(outgoing.at[page, 1], from_far.at[page], far_send.at[page], far_recv.at[page], *opposite)

    def pass_on(page):
        sib_copy(page).wait_recv()
        for kind in range(2):
            outgoing[page, 1, kind] = outgoing[page, 1, kind] + from_sib[page, 1, kind]
        far_copy(page).start()

    events = {
        1: [("core", 0), ("core", 1)], 2: [("core", 2), ("core", 3)], 4: [("core", 4), ("core", 5)],
        6: [("core", 6), ("core", 7)], 8: [(0, 0)], 12: [(0, 1), (1, 0)], 17: [(0, 2), (1, 1)],
    }

    def step_body(turn, carry):
        page, pair = turn // pairs, turn % pairs

        @pl.when(pair == 0)
        def _():
            start_page(page)

        for at_turn, names in events.items():

            @pl.when(turn == at_turn)
            def _(names=names, at_turn=at_turn):
                if at_turn == min(events):
                    keep_load.wait()
                for name in names:
                    early.take(*name)

        @pl.when((pair == 2) & (page > 0))
        def _():
            pass_on(page - 1)

        attend(page, pair)

        @pl.when(pair == pairs - 1)
        def _():
            sib_copy(page).start()

        return carry

    lax.fori_loop(0, count * pairs, step_body, 0)

    for copy in later_loads:
        copy.wait()
    flipped[...] = hidden[...].T
    lanes = 384
    rows = width // pages
    half = rows // 2

    def weight_columns(index, gradient):
        def tile(column, carry):
            at = pl.ds(pl.multiple_of(column * lanes, lanes), lanes)
            result = dot_nn(flipped[...], gradient[:, at]).astype(bf16)
            for page in range(pages):
                far = [apart((page >> level) & 1, bit) for level, bit in enumerate(bits)]
                slots = [slot_of_bits(order) for order in late_orders(far, apart(column, across))]
                first = page * rows
                if index < 2:
                    late[core if index == 0 else 1 - core, slots[index], 0:rows, :] = result[first : first + rows]
                else:
                    late[core, slots[0], rows : rows + half, :] = result[first : first + half]
                    late[1 - core, slots[1], rows : rows + half, :] = result[first + half : first + rows]
            return carry

        lax.fori_loop(0, 2, tile, 0)

    def project_back(gradient, matrix):
        def tile(column, carry):
            at = pl.ds(pl.multiple_of(column * 256, 256), 256)
            total_back[:, at] = total_back[:, at] + dot_nt(gradient[...], matrices[matrix, at, :])
            return carry

        lax.fori_loop(0, width // 256, tile, 0)

    pass_on(count - 1)
    weight_columns(0, query_back)
    project_back(query_back, 0)
    sums[0, 0:16, :] = middle_sums_ref[...]
    sums[0, 10:11, :] = column_sum(query_back[...].astype(f32))

    def head_tables(head, carry):
        for plane in range(2):
            table = table_acc[head, 72 * plane : 72 * (plane + 1), :]
            lane = lax.broadcasted_iota(jnp.int32, table.shape, 1)
            table = jnp.where(lane < 72, table, 0.0)
            table = jnp.concatenate([table, jnp.zeros_like(table)], axis=1)
            sheared = pltpu.roll(table, 0, 1, stride=1, stride_axis=0)
            table_out[head, 0:1, 256 * plane : 256 * (plane + 1)] = column_sum(sheared)
        table = table_acc[head, 144:192, :]
        lane = lax.broadcasted_iota(jnp.int32, table.shape, 1)
        apart_by = lane - 72 - lax.broadcasted_iota(jnp.int32, table.shape, 0)
        in_line = (lane >= 72) & (lane < 72 + 36)
        low_tail = jnp.sum(column_sum(jnp.where(in_line & (apart_by <= -2), table, 0.0)), axis=1, keepdims=True)
        high_tail = jnp.sum(column_sum(jnp.where(in_line & (apart_by >= 2), table, 0.0)), axis=1, keepdims=True)
        band = jnp.zeros((1, 128), f32)
        for first, rows_here, block, into in bands():
            aims = band_ref[first : first + rows_here, :]
            taken = jnp.take_along_axis(band_acc[head, into : into + rows_here, :], aims & 127, axis=1)
            right = (aims >> 7) == block
            if into == span:
                right = right & (seq > 0)
            band = band + column_sum(jnp.where(right, taken, 0.0))
        lane_one = lax.broadcasted_iota(jnp.int32, (1, 128), 1)
        table_out[head, 0:1, 512:640] = (
            band + jnp.where(lane_one == 0, low_tail, 0.0) + jnp.where(lane_one == 63, high_tail, 0.0)
        )
        table_out[head, 0:1, 640:768] = jnp.zeros((1, 128), f32)
        return carry

    lax.fori_loop(0, heads, head_tables, 0)
    for head in range(heads):
        at_row = 8 + head
        sums[1, at_row : at_row + 1, :] = table_out[head, 0:1, :]
    early.take(0, 3)

    for page in range(count):
        far_copy(page).wait_recv()
        own_rows = slice(page * row_count, (page + 1) * row_count)
        for kind, target in enumerate((key_back, value_back)):
            target[own_rows, :] = (
                (outgoing[page, 0, kind].astype(f32) + from_sib[page, 0, kind].astype(f32))
                + from_far[page, kind].astype(f32)
            ).astype(bf16)
    weight_columns(1, key_back)
    weight_columns(2, value_back)
    late_sum.start()
    project_back(key_back, 1)
    project_back(value_back, 2)
    sums[0, 11:12, :] = column_sum(value_back[...].astype(f32))
    for page in range(count):
        first = page * row_count
        text_rim[page, 16 : 16 + span, :] = total_back[first : first + span, :].astype(bf16)
        patch_rim[page, 16 : 16 + patch_span, :] = total_back[first + span : first + row_count, :].astype(bf16)
    after, before = (page_at, (seq + 1) % 4), (page_at, (seq + 3) % 4)
    rim_copies = [
        remote(
            source.at[:, start : start + 16], source.at[:, stop : stop + 16], rim_send.at[index], rim_recv.at[index],
            *peer,
        )
        for index, (source, start, stop, peer) in enumerate(
            (
                (text_rim, span, 0, after), (text_rim, 16, 16 + span, before),
                (patch_rim, 16, 0, after), (patch_rim, 16, 32, before),
            )
        )
    ]
    for copy in rim_copies:
        copy.start()
    for chunk in range(4):
        late_sum.take("core", chunk)
    early.take(2, 0)
    for copy in rim_copies:
        copy.wait()
    sums[1, 0:8, :] = jnp.zeros((8, width), f32)
    sums[1, 20:24, :] = jnp.zeros((4, width), f32)
    sums[0, 16:24, :] = jnp.zeros((8, width), f32)

    def position_tile(tile, carry):
        at = pl.ds(pl.multiple_of(tile * 256, 256), 256)
        text_taps = [jnp.zeros((1, 256), f32) for _ in range(7)]
        patch_taps = [jnp.zeros((1, 256), f32) for _ in range(9)]
        for page in range(count):
            first = page * row_count
            window = text_rim[page, :, at].astype(f32)
            window_row = lax.broadcasted_iota(jnp.int32, (span + 32, 1), 0)
            inside = ((window_row >= 16) | (seq > 0)) & ((window_row < 16 + span) | (seq < 3))
            window = jnp.where(inside, window, 0.0)
            live = seq * span + lax.broadcasted_iota(jnp.int32, (span, 1), 0) < length_ref[page]
            masked = jnp.where(live, tokens_ref[page, :, at].astype(f32), 0.0)
            total = jnp.zeros((span, 256), f32)
            for distance in range(-3, 4):
                shifted = window[16 - distance : 16 - distance + span]
                if distance == 0:
                    weight = taps_ref[1:2, at] + taps_ref[4:5, at] + taps_ref[7:8, at]
                else:
                    tap = 3 * (abs(distance) - 1) + (2 if distance > 0 else 0)
                    weight = taps_ref[tap : tap + 1, at]
                total = total + shifted * weight
                text_taps[distance + 3] = text_taps[distance + 3] + column_sum(shifted * masked)
            tokens_back_ref[page, :, at] = total_back[first : first + span, at] + jnp.where(live, total, 0.0)
            window = patch_rim[page, :, at].astype(f32)
            window_row = lax.broadcasted_iota(jnp.int32, (48, 1), 0)
            inside = ((window_row >= 16) | (seq > 0)) & ((window_row < 32) | (seq < 3))
            window = jnp.where(inside, window, 0.0)
            cell = seq * patch_span + lax.broadcasted_iota(jnp.int32, (patch_span, 1), 0)
            live = ((cell >> 3) < GRID_SIDE - 1) & ((cell & 7) < GRID_SIDE - 1)
            masked = jnp.where(live, patches_ref[page, :, at].astype(f32), 0.0)
            total = jnp.zeros((patch_span, 256), f32)
            for tap in range(9):
                distance = GRID_SIDE * (tap // 3 - 1) + tap % 3 - 1
                shifted = window[16 - distance : 32 - distance]
                total = total + shifted * taps_ref[9 + tap : 10 + tap, at]
                patch_taps[tap] = patch_taps[tap] + column_sum(shifted * masked)
            patches_back_ref[page, :, at] = total_back[first + span : first + row_count, at] + jnp.where(
                live, total, 0.0
            )
        for index, value in enumerate(text_taps):
            sums[0, 16 + index : 17 + index, at] = value
        for index, value in enumerate(patch_taps):
            if index == 0:
                sums[0, 23:24, at] = value
            else:
                sums[1, index - 1 : index, at] = value
        return carry

    lax.fori_loop(0, width // 256, position_tile, 0)

    sum_partners = [opposite] + on_page
    sum_copies = [remote(sums.at[1 - core], sums_in.at[0], sum_send.at[0], sum_recv.at[0], *sibling)] + [
        remote(sums.at[core], sums_in.at[1 + index], sum_send.at[1 + index], sum_recv.at[1 + index], *partner)
        for index, partner in enumerate(sum_partners)
    ]
    last = remote(
        sums.at[core], sums_in.at[2 + levels], sum_send.at[2 + levels], sum_recv.at[2 + levels], *sibling
    )
    sum_copies[0].start()

    def sum_step(index):
        sum_copies[index].wait()
        sums[core] = sums[core] + sums_in[index]
        (sum_copies + [last])[index + 1].start()

    sum_step(0)
    late_sum.take(0, 0)
    sum_step(1)
    late_sum.take(0, 1)
    late_sum.take(1, 0)
    sum_step(2)
    for step in range(3, levels + 1):
        early.take(step, 0)
    for step in range(2, levels + 1):
        late_sum.take(step, 0)
        if step + 1 <= levels + 1:
            sum_step(step + 1)
    last.wait()
    sums_ref[core] = sums[core]
    sums_ref[1 - core] = sums_in[2 + levels]
    early_ref[...] = keep[0]
    late_ref[...] = late[0, 0]
    early.finish()
    late_sum.finish()
    for page in range(count):
        sib_copy(page).wait_send()
        far_copy(page).wait_send()


def backward(pages, lengths, local_values, far_values, tokens, patches):
    count, span, width = tokens.shape
    patch_span = patches.shape[1]
    row_count = span + patch_span
    total_rows = count * row_count
    bundle, weights, keys = far_values[0], far_values[1], far_values[2]
    pairs, key_pad = weights.shape[1], keys.shape[1]
    blocks, early_rows, lanes = bundle.shape[1:]
    late_rows = 3 * width // (2 * pages)
    levels = pages.bit_length() - 1
    bf16, f32, i32 = jnp.bfloat16, jnp.float32, jnp.int32
    dma = pltpu.SemaphoreType.DMA

    def landings(rows):
        return [VMEM((blocks >> (step + 1), rows, lanes), bf16) for step in range(levels + 1)]

    early_count = 8 + 4 + 2 + (levels - 1)
    late_count = 4 + 2 + levels
    return pl.pallas_call(
        functools.partial(backward_kernel, pages),
        out_shape=(
            jax.ShapeDtypeStruct(tokens.shape, f32),
            jax.ShapeDtypeStruct(patches.shape, f32),
            jax.ShapeDtypeStruct((early_rows, lanes), bf16),
            jax.ShapeDtypeStruct((late_rows, lanes), bf16),
            jax.ShapeDtypeStruct((2, 24, width), f32),
        ),
        in_specs=[pl.BlockSpec(memory_space=pltpu.SMEM)]
        + in_vmem(len(local_values))
        + [pl.BlockSpec(memory_space=pl.ANY)] * len(far_values),
        out_specs=tuple(in_vmem(5)),
        scratch_shapes=[
            VMEM((blocks, early_rows, lanes), bf16),
            VMEM((blocks, early_rows, lanes), bf16),
            landings(early_rows),
            VMEM((2, blocks, late_rows, lanes), bf16),
            VMEM((blocks, late_rows, lanes), bf16),
            landings(late_rows),
            VMEM((2, pairs, 2 * row_count, key_pad), bf16),
            VMEM((2, key_pad, width), bf16),
            VMEM((2, key_pad, width), bf16),
            VMEM((count, 4, 2, row_count, width), bf16),
            VMEM((count, 2, 2, row_count, width), bf16),
            VMEM((count, 2, row_count, width), bf16),
            VMEM((3, width, width), bf16),
            VMEM((total_rows, width), bf16),
            VMEM((width, total_rows), bf16),
            VMEM((total_rows, width), f32),
            VMEM((total_rows, width), bf16),
            VMEM((total_rows, width), bf16),
            VMEM((total_rows, width), bf16),
            VMEM((2 * row_count, key_pad), f32),
            VMEM((2 * row_count, 3 * key_pad), bf16),
            VMEM((row_count, 2 * key_pad), bf16),
            VMEM((256, 3 * key_pad), bf16),
            VMEM((192, row_count), bf16),
            VMEM((row_count, 128), i32),
            VMEM((2 * pairs, 192, 128), f32),
            VMEM((2 * pairs, span + 64 + 2 * patch_span, 128), f32),
            VMEM((2 * pairs, 8, width), f32),
            VMEM((count, span + 32, width), bf16),
            VMEM((count, patch_span + 32, width), bf16),
            VMEM((2, 24, width), f32),
            VMEM((3 + levels, 24, width), f32),
            dma((6,)), dma((3, 2)),
            dma((early_count,)), dma((early_count,)), dma((late_count,)), dma((late_count,)),
            dma((count,)), dma((count,)), dma((count,)), dma((count,)),
            dma((4,)), dma((4,)), dma((3 + levels,)), dma((3 + levels,)),
        ],
        compiler_params=pltpu.CompilerParams(
            collective_id=1, has_side_effects=True, vmem_limit_bytes=62 * 1024 * 1024
        ),
        cost_estimate=pl.CostEstimate(flops=12_000_000_000, bytes_accessed=40_000_000, transcendentals=0),
        name="backward",
    )(lengths, *local_values, *far_values)


def exchange(value, pages, step):
    moves = []
    for page in range(pages):
        for seq in range(4):
            on_page, on_seq = page, seq
            if (seq % 2 == step) if step < 2 else False:
                on_seq = seq ^ 2
            else:
                on_page = page ^ (1 if step < 2 else 1 << (step - 1))
            moves.append((page * 4 + seq, on_page * 4 + on_seq))
    return lax.ppermute(value, ("page", "seq"), moves)


def added(kept, got):
    return (kept.astype(jnp.float32) + got.astype(jnp.float32)).astype(jnp.bfloat16)


def bundle_sum(state, pages):
    for step in range(pages.bit_length()):
        half = state.shape[0] // 2
        state = added(state[:half], exchange(state[half:], pages, step))
    return state[0]


def bundle_parts(state, wide_rows, core):
    lanes = state.shape[1] // 2
    first = core == 0
    tail = state[wide_rows:]
    if wide_rows > 2 * tail.shape[0]:
        group = state[:wide_rows].reshape(4, wide_rows // 4, 2 * lanes)
        low = group[:2].transpose(1, 0, 2).reshape(-1, lanes)
        high = group[2:].transpose(1, 0, 2).reshape(-1, lanes)
    else:
        low, high = state[:wide_rows, :lanes], state[:wide_rows, lanes:]
    left, right = state[:wide_rows, :lanes], state[:wide_rows, lanes:]
    sent = jnp.concatenate(
        [jnp.where(first, high, left), jnp.where(first, tail[:, lanes:], tail[:, :lanes])], axis=0
    )
    got = swap(sent, "seq", 1)
    kept_tail = jnp.where(first, tail[:, :lanes], tail[:, lanes:])
    one = jnp.where(first, low, got[:wide_rows])
    two = jnp.where(first, got[:wide_rows], right)
    three = jnp.concatenate(
        [jnp.where(first, kept_tail, got[wide_rows:]), jnp.where(first, got[wide_rows:], kept_tail)], axis=0
    )
    return [value.astype(jnp.float32) for value in (one, two, three)]


def clipped(sums, centre, bins):
    first, last = centre + 1 - bins // 2, centre - 1 + bins // 2
    return jnp.concatenate(
        [
            jnp.sum(sums[..., :first], axis=-1, keepdims=True),
            sums[..., first:last],
            jnp.sum(sums[..., last:], axis=-1, keepdims=True),
        ],
        axis=-1,
    )


def grid_live(cells):
    return (cells // GRID_SIDE < GRID_SIDE - 1) & (cells % GRID_SIDE < GRID_SIDE - 1)


def grid_boxes(cells):
    return jnp.stack(
        [
            patch_pitch * (cells % GRID_SIDE) + patch_centre,
            patch_pitch * (cells // GRID_SIDE) + patch_centre,
        ]
    )


def shards(
    tokens,
    patches,
    page_length,
    box_position,
    query_weight,
    key_weight,
    value_weight,
    out_weight,
    up_weight,
    down_weight,
    conv_weight,
    patch_conv_weight,
    query_bias,
    value_bias,
    out_bias,
    up_bias,
    down_bias,
    attention_gain,
    attention_shift,
    feedforward_gain,
    feedforward_shift,
    reading_bias_table,
    horizontal_bias_table,
    vertical_bias_table,
    cotangent,
    patch_cotangent,
):
    conv_taps = conv_weight.astype(jnp.float32)
    patch_taps = patch_conv_weight.astype(jnp.float32)
    query_offset = query_bias.astype(jnp.float32)
    value_offset = value_bias.astype(jnp.float32)
    out_offset = out_bias.astype(jnp.float32)
    up_offset = up_bias.astype(jnp.float32)
    down_offset = down_bias.astype(jnp.float32)
    first_gain = attention_gain.astype(jnp.float32)
    first_shift = attention_shift.astype(jnp.float32)
    second_gain = feedforward_gain.astype(jnp.float32)
    second_shift = feedforward_shift.astype(jnp.float32)
    page_count, span_size, model_width = tokens.shape
    patch_span = patches.shape[1]
    seq_count = lax.axis_size("seq")
    slot_size = span_size * seq_count
    patch_slots = patch_span * seq_count
    row_count = span_size + patch_span
    key_count = row_count * seq_count
    head_count = reading_bias_table.shape[0]
    head_size = model_width // head_count
    line_bins = reading_bias_table.shape[1]
    plane_bins = horizontal_bias_table.shape[1]
    score_scale = head_size ** (-0.5)
    seq_index = lax.axis_index("seq")
    text_places = seq_index * span_size + jnp.arange(span_size, dtype=jnp.int32)
    local_cells = seq_index * patch_span + jnp.arange(patch_span, dtype=jnp.int32)
    text_live = text_places[None, :] < page_length[:, None]
    patch_live = grid_live(local_cells)
    text_factor = text_live[:, :, None]
    patch_factor = patch_live[None, :, None]
    masked = tokens * text_factor.astype(jnp.bfloat16)
    rimmed = with_halo(masked, (("seq", 1),), 3)
    reach = GRID_SIDE + 1
    patch_masked = patches * patch_factor.astype(jnp.bfloat16)
    patch_rimmed = with_halo(patch_masked, (("seq", 1),), reach)
    pages = lax.axis_size("page")
    table = jnp.concatenate(
        [
            horizontal_bias_table,
            vertical_bias_table,
            reading_bias_table,
            jnp.zeros((head_count, 256 - 2 * plane_bins - line_bins), jnp.bfloat16),
        ],
        axis=1,
    ).astype(jnp.float32)
    taps = jnp.pad(
        jnp.concatenate([conv_weight, patch_conv_weight], axis=1).astype(jnp.float32).T, ((0, 6), (0, 0))
    )
    vectors = jnp.concatenate(
        [
            jnp.stack(
                [
                    query_bias, value_bias, out_bias, down_bias,
                    attention_gain, attention_shift, feedforward_gain, feedforward_shift,
                ]
            ),
            up_bias.reshape(-1, model_width),
        ]
    ).astype(jnp.float32)
    (
        hidden, hidden_low, queries, keys, values, mixture_low, weights, columns, key_rows, query_rows,
    ) = forward(
        pages, page_length, tokens, patches, box_position, taps, (query_weight, key_weight, value_weight),
        vectors, table,
    )
    places = jnp.stack(
        [seq_index, seq_index % 2, lax.axis_index("page"), seq_index // 2]
    ).astype(jnp.int32)
    def flat(value):
        return value.reshape(-1, value.shape[-1])

    output, patch_output, delta_first, delta_mixture, middle_sums, feedforward_bundle = middle(
        places, hidden, mixture_low, cotangent, patch_cotangent,
        (out_weight, up_weight, down_weight), vectors, pages,
    )
    if in_tiles(model_width, pages):
        tokens_gradient, patches_gradient, early_state, late_state, sums = backward(
            pages,
            page_length,
            (
                queries, delta_mixture, columns, key_rows, query_rows, tokens, patches, taps, middle_sums,
            ),
            (
                feedforward_bundle, weights, keys, values, hidden_low, delta_first, query_weight, key_weight,
                value_weight,
            ),
            tokens,
            patches,
        )
        query_part, key_part, value_part = bundle_parts(late_state, model_width // pages, places[1])
        up_part, down_part, out_part = bundle_parts(early_state, up_weight.shape[1] // pages, places[1])
        front, late_sums = sums[0], sums[1]
        text_columns = front[16:23]
        centre = text_columns[3]
        head_sums = late_sums[8 : 8 + head_count]
        plane_sums = head_sums[:, :512].reshape(head_count, 2, 256).transpose(1, 0, 2)
        plane_sums = clipped(plane_sums, 72, plane_bins)
        return (
            output,
            patch_output,
            tokens_gradient,
            patches_gradient,
            query_part,
            key_part,
            value_part,
            out_part,
            up_part.reshape(model_width // pages, -1),
            down_part,
            jnp.stack(
                [
                    text_columns[2], centre, text_columns[4],
                    text_columns[1], centre, text_columns[5],
                    text_columns[0], centre, text_columns[6],
                ],
                axis=1,
            ),
            jnp.concatenate([front[23:24], late_sums[0:8]], axis=0).T,
            front[10],
            front[11],
            front[OUT_BIAS],
            front[UP_BIAS : UP_BIAS + 4].reshape(-1),
            front[DOWN_BIAS],
            front[FIRST_GAIN],
            front[FIRST_SHIFT],
            front[SECOND_GAIN],
            front[SECOND_SHIFT],
            clipped(head_sums[:, 512:640], 32, line_bins),
            plane_sums[0],
            plane_sums[1],
        )
    delta_first = delta_first.reshape(page_count, row_count, model_width)
    delta_mixture = delta_mixture.reshape(page_count, row_count, model_width)
    early_state = added(feedforward_bundle[0], swap(feedforward_bundle[1], "seq", 1))
    delta_mixture, early_state = lax.optimization_barrier((delta_mixture, early_state))
    delta_query_pages, delta_key_pages, delta_value_pages = [], [], []
    delta_plane, delta_line = 0.0, 0.0
    for page in range(page_count):
        delta_page_queries, delta_blocks, plane_part, line_part = backward_page(
            places,
            columns[page][:, ::128],
            key_rows[page],
            query_rows[page][:, :row_count],
            queries[page * row_count : (page + 1) * row_count],
            keys[page],
            values[page],
            delta_mixture[page],
            weights[page],
        )
        got = swap(delta_blocks[2:], "seq", 1)
        chip_sum = delta_blocks[:2].astype(jnp.float32) + got.astype(jnp.float32)
        got = swap(chip_sum[1].astype(jnp.bfloat16), "seq", 2)
        whole = (chip_sum[0] + got.astype(jnp.float32)).astype(jnp.bfloat16)
        delta_query_pages.append(delta_page_queries)
        delta_key_pages.append(whole[0])
        delta_value_pages.append(whole[1])
        delta_plane = delta_plane + plane_part
        delta_line = delta_line + line_part
    delta_queries = jnp.stack(delta_query_pages)
    delta_keys = jnp.stack(delta_key_pages)
    delta_values = jnp.stack(delta_value_pages)
    delta_plane = clipped(delta_plane, 72, plane_bins)
    delta_line = clipped(delta_line, 32, line_bins)
    delta_across, delta_upward = delta_plane[0], delta_plane[1]
    delta_query_offset = row_sum(delta_queries)
    delta_value_offset = row_sum(delta_values)
    delta_hidden = (
        delta_first
        + back_dot(delta_queries, query_weight)
        + back_dot(delta_keys, key_weight)
        + back_dot(delta_values, value_weight)
    )
    delta_position = delta_hidden[:, :span_size].astype(jnp.bfloat16)
    delta_rim = with_halo(delta_position, (("seq", 1),), 3)
    delta_masked = jnp.zeros((page_count, span_size, model_width), jnp.float32)
    tap_columns = []
    for dilation in (1, 2, 3):
        for offset in (-1, 0, 1):
            column = 3 * (dilation - 1) + offset + 1
            anchor = 3 + offset * dilation
            anchor_back = 3 - offset * dilation
            delta_masked = (
                delta_masked
                + delta_rim[:, anchor_back : anchor_back + span_size, :] * conv_taps[:, column]
            )
            tap_columns.append(
                jnp.einsum(
                    "ptd,ptd->d",
                    delta_position,
                    rimmed[:, anchor : anchor + span_size, :],
                    preferred_element_type=jnp.float32,
                )
            )
    delta_taps = jnp.stack(tap_columns, axis=1)
    tokens_gradient = delta_hidden[:, :span_size] + delta_masked * text_factor.astype(jnp.float32)
    delta_patch_position = delta_hidden[:, span_size:].astype(jnp.bfloat16)
    delta_patch_rim = with_halo(delta_patch_position, (("seq", 1),), reach)
    delta_patch_masked = jnp.zeros((page_count, patch_span, model_width), jnp.float32)
    patch_columns = []
    for vertical in (-1, 0, 1):
        for horizontal in (-1, 0, 1):
            column = 3 * (vertical + 1) + horizontal + 1
            anchor = reach + vertical * GRID_SIDE + horizontal
            anchor_back = reach - vertical * GRID_SIDE - horizontal
            delta_patch_masked = (
                delta_patch_masked
                + delta_patch_rim[:, anchor_back : anchor_back + patch_span, :]
                * patch_taps[:, column]
            )
            patch_columns.append(
                jnp.einsum(
                    "ptd,ptd->d",
                    delta_patch_position,
                    patch_rimmed[:, anchor : anchor + patch_span, :],
                    preferred_element_type=jnp.float32,
                )
            )
    delta_patch_taps = jnp.stack(patch_columns, axis=1)
    patches_gradient = delta_hidden[:, span_size:] + delta_patch_masked * patch_factor.astype(
        jnp.float32
    )
    operands = [flat(value) for value in (hidden_low, delta_queries, delta_keys, delta_values)]
    tail_bundle = indexed_bundle(
        (
            ((operands[0], operands[1], None), (operands[0], operands[3], 0)),
            ((operands[0], operands[2], None), (operands[0], operands[3], 1)),
        ),
        places,
        pages,
    )
    tail_state = added(tail_bundle[0], swap(tail_bundle[1], "seq", 1))
    query_part, key_part, value_part = bundle_parts(
        bundle_sum(tail_state, pages), model_width // pages, places[1]
    )
    up_part, down_part, out_part = bundle_parts(
        bundle_sum(early_state, pages), up_weight.shape[1] // pages, places[1]
    )
    up_part = up_part.reshape(model_width // pages, -1)
    matrix_parts = (query_part, key_part, value_part, out_part, up_part, down_part)
    vector_parts = total_sum(
        (
            delta_taps,
            delta_patch_taps,
            delta_query_offset,
            delta_value_offset,
            middle_sums[OUT_BIAS],
            middle_sums[UP_BIAS : UP_BIAS + 4].reshape(-1),
            middle_sums[DOWN_BIAS],
            middle_sums[FIRST_GAIN],
            middle_sums[FIRST_SHIFT],
            middle_sums[SECOND_GAIN],
            middle_sums[SECOND_SHIFT],
            delta_line,
            delta_across,
            delta_upward,
        )
    )
    return (
        output,
        patch_output,
        tokens_gradient,
        patches_gradient,
        matrix_parts[0],
        matrix_parts[1],
        matrix_parts[2],
        matrix_parts[3],
        matrix_parts[4],
        matrix_parts[5],
        vector_parts[0],
        vector_parts[1],
        vector_parts[2],
        vector_parts[3],
        vector_parts[4],
        vector_parts[5],
        vector_parts[6],
        vector_parts[7],
        vector_parts[8],
        vector_parts[9],
        vector_parts[10],
        vector_parts[11],
        vector_parts[12],
        vector_parts[13],
    )


def solution(mesh):
    in_specs = (
        P("page", "seq", None),
        P("page", "seq", None),
        P("page"),
        P(None, "page", None),
        P(),
        P(),
        P(),
        P(),
        P(),
        P(),
        P(),
        P(),
        P(),
        P(),
        P(),
        P(),
        P(),
        P(),
        P(),
        P(),
        P(),
        P(),
        P(),
        P(),
        P("page", "seq", None),
        P("page", "seq", None),
    )
    out_specs = (
        P("page", "seq", None),
        P("page", "seq", None),
        P("page", "seq", None),
        P("page", "seq", None),
        P("page", "seq"),
        P("page", "seq"),
        P("page", "seq"),
        P("page", "seq"),
        P("page", "seq"),
        P("page", "seq"),
        P(),
        P(),
        P(),
        P(),
        P(),
        P(),
        P(),
        P(),
        P(),
        P(),
        P(),
        P(),
        P(),
        P(),
    )
    return jax.shard_map(shards, mesh=mesh, in_specs=in_specs, out_specs=out_specs, check_vma=False)
```

```python
import functools

import jax
import jax.numpy as jnp
from jax import lax
from jax.experimental import pallas as pl
from jax.experimental.pallas import tpu as pltpu
from jax.sharding import PartitionSpec as P

GRID_SIDE = 8


epsilon = 1e-05
coordinate_step = 16
masked_score = -1000000000.0
patch_pitch = 146
patch_centre = 73


def with_halo(cells, sides, width):
    for axis, dim in sides:
        count = lax.axis_size(axis)
        ends = count - 1
        head = lax.slice_in_dim(cells, 0, width, axis=dim)
        tail = lax.slice_in_dim(cells, cells.shape[dim] - width, cells.shape[dim], axis=dim)
        cells = jnp.concatenate(
            [
                lax.ppermute(tail, axis, [(i, (i + 1) % count) for i in range(ends)]),
                cells,
                lax.ppermute(head, axis, [((i + 1) % count, i) for i in range(ends)]),
            ],
            axis=dim,
        )
    return cells


def layer_norm(values, gain_vector, shift_vector):
    row_mean = jnp.mean(values, axis=-1, keepdims=True)
    centred = values - row_mean
    variance = jnp.mean(centred * centred, axis=-1, keepdims=True)
    return centred * lax.rsqrt(variance + epsilon) * gain_vector + shift_vector


def gelu_exact(values):
    return jax.nn.gelu(values, approximate=False)


def flat_dot(operand, matrix):
    front = operand.shape[:-1]
    result = jnp.dot(
        operand.reshape(-1, operand.shape[-1]), matrix, preferred_element_type=jnp.float32
    )
    return result.reshape(front + (matrix.shape[-1],))


def back_dot(operand, matrix):
    front = operand.shape[:-1]
    result = lax.dot_general(
        operand.reshape(-1, operand.shape[-1]),
        matrix,
        (((1,), (1,)), ((), ())),
        preferred_element_type=jnp.float32,
    )
    return result.reshape(front + (matrix.shape[0],))


def outer_dot(operand, gradient):
    return lax.dot_general(
        operand.reshape(-1, operand.shape[-1]),
        gradient.reshape(-1, gradient.shape[-1]),
        (((0,), (0,)), ((), ())),
        preferred_element_type=jnp.float32,
    )


def row_sum(gradient):
    return jnp.sum(gradient.astype(jnp.float32).reshape(-1, gradient.shape[-1]), axis=0)


def swap(value, axis, bit):
    count = lax.axis_size(axis)
    return lax.ppermute(value, axis, [(i, i ^ bit) for i in range(count)])


def total_sum(vectors):
    flat = jnp.concatenate([vector.reshape(-1) for vector in vectors])
    flat = jnp.pad(flat, (0, -flat.size % 1024)).reshape(-1, 128)
    for bit in (1, 2):
        flat = flat + swap(flat, "seq", bit)
    bit = 1
    while bit < lax.axis_size("page"):
        flat = flat + swap(flat, "page", bit)
        bit *= 2
    flat = flat.reshape(-1)
    result, start = [], 0
    for vector in vectors:
        result.append(flat[start : start + vector.size].reshape(vector.shape))
        start += vector.size
    return result


def query_places(seq_index, shape, span, patch_span, text_slots):
    row = lax.broadcasted_iota(jnp.int32, shape, 0)
    return jnp.where(
        row < span, seq_index * span + row, text_slots + seq_index * patch_span + row - span
    )


FIXED = 2048.0


def lookup(table_row, lanes):
    return jnp.take_along_axis(jnp.broadcast_to(table_row, lanes.shape), lanes, axis=1)


def pair_masked(pair):
    lane = lax.broadcasted_iota(jnp.int32, pair.shape, 1)
    half = pair.shape[1] // 2
    zero = jnp.zeros_like(pair)
    return jnp.concatenate(
        [jnp.where(lane < half, pair, zero), jnp.where(lane < half, zero, pair)], axis=0
    )


def pair_merged(both):
    rows, width = both.shape[0] // 2, both.shape[1]
    lane = lax.broadcasted_iota(jnp.int32, (rows, width), 1)
    return jnp.where(lane < width // 2, both[:rows], both[rows:])


def dot_nt(left, right):
    return lax.dot_general(left, right, (((1,), (1,)), ((), ())), preferred_element_type=jnp.float32)


def dot_nn(left, right):
    return lax.dot_general(left, right, (((1,), (0,)), ((), ())), preferred_element_type=jnp.float32)


def dot_tn(left, right):
    return lax.dot_general(left, right, (((0,), (0,)), ((), ())), preferred_element_type=jnp.float32)


CHUNK = 16


MESH = pl.DeviceIdType.MESH


def places_of(pages):
    page = lax.axis_index("page")
    seq = lax.axis_index("seq")
    bits = []
    rest = page
    for _ in range(pages.bit_length() - 1):
        bits.append(rest % 2)
        rest = rest // 2
    return page, bits, seq, seq // 2, seq % 2


def sibling_of(seq):
    return seq + 1 - 2 * (seq % 2)


def across_of(seq):
    return seq + 2 - 4 * (seq // 2)


def remote(source, target, send, receive, page, seq):
    return pltpu.make_async_remote_copy(
        src_ref=source, dst_ref=target, send_sem=send, recv_sem=receive, device_id=(page, seq), device_id_type=MESH
    )


def column_of(row):
    square = jnp.broadcast_to(row.astype(jnp.float32), (128, 128)).T
    return square[:, 0:1].astype(jnp.int32)


def forward_kernel(
    pages,
    staging, length_ref, box_ref, taps_ref, vector_ref, table_ref, tokens_any, patches_any, query_weight_any, key_weight_any,
    value_weight_any,
    hidden_ref, hidden_low_ref, query_ref, mixture_ref, columns_ref, rows_ref, query_rows_ref, key_any, value_any,
    weights_any,
    own, matrices, key_ref, value_ref, weights_ref, arrived, text, grid, low, scores, across_ref, upward_ref,
    live_ref, line_ref, packed_ref,
    load_sem, store_sem, send_sem, recv_sem,
):
    page_at, _, seq, _, _ = places_of(pages)
    count, span, width = tokens_any.shape
    patch_span = patches_any.shape[1]
    row_count = span + patch_span
    key_pad = key_ref.shape[1]
    text_slots = 4 * span
    rim = 8
    loads = [
        pltpu.make_async_copy(source, target, load_sem.at[index])
        for index, (source, target) in enumerate(
            (
                (tokens_any, own.at[:, 0:span]), (patches_any, own.at[:, span:row_count]),
                (key_weight_any, matrices.at[1]), (value_weight_any, matrices.at[2]), (query_weight_any, matrices.at[0]),
            )
        )
    ]
    for copy in loads:
        copy.start()

    def stores(page):
        return [
            pltpu.make_async_copy(source.at[page], target.at[page], store_sem.at[index, page])
            for index, (source, target) in enumerate(
                ((key_ref, key_any), (value_ref, value_any), (weights_ref, weights_any))
            )
        ]

    pairs = weights_ref.shape[1]
    peers = (sibling_of(seq), across_of(seq))
    barrier = pltpu.get_barrier_semaphore()
    for peer in peers:
        pl.semaphore_signal(barrier, inc=1, device_id=(page_at, peer), device_id_type=MESH)
    pl.semaphore_wait(barrier, 2)

    def first_copies(page, side):
        return (
            remote(
                tokens_any.at[page], arrived.at[side, page, 0:span], send_sem.at[2 * side, page],
                recv_sem.at[2 * side, page], page_at, peers[side],
            ),
            remote(
                patches_any.at[page], arrived.at[side, page, span:row_count], send_sem.at[2 * side + 1, page],
                recv_sem.at[2 * side + 1, page], page_at, peers[side],
            ),
        )

    def onward_copy(page):
        return remote(
            arrived.at[1, page], arrived.at[2, page], send_sem.at[4, page], recv_sem.at[4, page], page_at, peers[0]
        )

    for page in range(count):
        for side in range(2):
            for copy in first_copies(page, side):
                copy.start()

    for copy in staging:
        copy.wait()
    steps = jnp.floor(table_ref[...].astype(jnp.float32) * FIXED + 0.5).astype(jnp.int32)
    for pair in range(pairs):
        words = (steps[2 * pair : 2 * pair + 1] + 8192) + steps[2 * pair + 1 : 2 * pair + 2] * 65536
        packed_ref[0, pair : pair + 1, :] = words[:, 0:128]
        packed_ref[1, pair : pair + 1, :] = words[:, 128:256]
    key = lax.broadcasted_iota(jnp.int32, (row_count, key_pad), 1)
    place = query_places(seq, (row_count, key_pad), span, patch_span, text_slots)
    across_ref[...] = jnp.clip(key - place, -16, 15) + 16

    def fill(pair, carry):
        row = packed_ref[1, pl.ds(pair, 1), :]
        for at in range(0, key_pad, 128):
            line_ref[pair, :, at : at + 128] = lookup(row, across_ref[:, at : at + 128])
        return carry

    lax.fori_loop(0, pairs, fill, 0)
    text[0:rim, :] = jnp.zeros((rim, width), jnp.float32)
    text[rim + text_slots :, :] = jnp.zeros((rim, width), jnp.float32)
    grid[0:patch_span, :] = jnp.zeros((patch_span, width), jnp.float32)
    grid[patch_span * 5 :, :] = jnp.zeros((patch_span, width), jnp.float32)
    low[row_count * 4 :, :] = jnp.zeros((key_pad - row_count * 4, width), jnp.bfloat16)
    lanes = 256
    pair_width = 128
    power = 1.4426950408889634 / FIXED
    for copy in first_copies(0, 1):
        copy.wait_recv()
    onward_copy(0).start()
    for copy in loads:
        copy.wait()

    def page_step(page, carry):
        length = length_ref[page]
        base = page * row_count
        cell = lax.broadcasted_iota(jnp.int32, (1, 128), 1)
        query_cell = seq * patch_span + cell
        row_cell = seq * patch_span + lax.broadcasted_iota(jnp.int32, (patch_span, 1), 0)
        for plane in range(2):
            boxes = box_ref[plane]
            of_page = lax.broadcasted_iota(jnp.int32, boxes.shape, 0) == page
            box = jnp.sum(jnp.where(of_page, boxes, 0), axis=0, keepdims=True)
            patch = 146 * ((cell % GRID_SIDE) if plane == 0 else (cell // GRID_SIDE)) + 73
            own_patch = 146 * ((query_cell % GRID_SIDE) if plane == 0 else (query_cell // GRID_SIDE)) + 73
            column_patch = 146 * ((row_cell % GRID_SIDE) if plane == 0 else (row_cell // GRID_SIDE)) + 73
            rows_ref[page, plane : plane + 1, 0:text_slots] = box
            rows_ref[page, plane : plane + 1, text_slots:key_pad] = patch
            own_box = rows_ref[page, plane : plane + 1, pl.ds(pl.multiple_of(seq * span, 128), span)]
            query_rows_ref[page, plane : plane + 1, 0:span] = own_box
            query_rows_ref[page, plane : plane + 1, span:256] = own_patch
            columns_ref[page, 0:span, plane * 128 : (plane + 1) * 128] = jnp.broadcast_to(
                column_of(own_box), (span, 128)
            )
            columns_ref[page, span:row_count, plane * 128 : (plane + 1) * 128] = jnp.broadcast_to(
                column_patch, (patch_span, 128)
            )
        for plane, lanes_ref in enumerate((across_ref, upward_ref)):
            difference = rows_ref[page, plane : plane + 1, :] - columns_ref[page, :, plane * 128 : plane * 128 + 1]
            lanes_ref[...] = jnp.clip(difference >> 4, -32, 31) + (32 + 64 * plane)
        key_at = lax.broadcasted_iota(jnp.int32, live_ref.shape, 1)
        key_cell = key_at - text_slots
        live = (key_at < length) | (
            (key_cell >= 0) & ((key_cell >> 3) < GRID_SIDE - 1) & ((key_cell & 7) < GRID_SIDE - 1)
        )
        live_ref[...] = jnp.where(live, 0.0, masked_score * FIXED)
        for copy in first_copies(page, 0):
            copy.wait_recv()
        onward_copy(page).wait_recv()

        def block_of(step, start, stop, at):
            if step:
                return arrived[step - 1, page, start:stop, at].astype(jnp.float32)
            if start:
                return own[page, span:row_count, at].astype(jnp.float32)
            return own[page, 0:span, at].astype(jnp.float32)

        def slot_of(step):
            return (seq, peers[0], peers[1], sibling_of(peers[1]))[step]

        everything = slice(0, width)
        for step in range(4):
            where = slot_of(step)
            at_place = where * span + lax.broadcasted_iota(jnp.int32, (span, 1), 0)
            text[pl.ds(pl.multiple_of(rim + where * span, 8), span), :] = jnp.where(
                at_place < length, block_of(step, 0, span, everything), 0.0
            )
            at_cell = where * patch_span + lax.broadcasted_iota(jnp.int32, (patch_span, 1), 0)
            cell_live = ((at_cell >> 3) < GRID_SIDE - 1) & ((at_cell & 7) < GRID_SIDE - 1)
            grid[pl.ds(pl.multiple_of(patch_span + where * patch_span, 8), patch_span), :] = jnp.where(
                cell_live, block_of(step, span, row_count, everything), 0.0
            )
        for step in range(4):
            where = slot_of(step)

            def convolve(tile, carry):
                at = pl.ds(pl.multiple_of(tile * lanes, lanes), lanes)
                window = text[pl.ds(pl.multiple_of(where * span, 8), span + 2 * rim), at]
                centre = taps_ref[1:2, at] + taps_ref[4:5, at] + taps_ref[7:8, at]
                total = block_of(step, 0, span, at) + window[rim : rim + span] * centre
                for dilation in (1, 2, 3):
                    for offset in (-1, 1):
                        tap = 3 * (dilation - 1) + offset + 1
                        anchor = rim + offset * dilation
                        total = total + window[anchor : anchor + span] * taps_ref[tap : tap + 1, at]
                low[pl.ds(pl.multiple_of(where * span, 16), span), at] = total.astype(jnp.bfloat16)
                window = grid[pl.ds(pl.multiple_of(where * patch_span, 8), 3 * patch_span), at]
                patch_total = block_of(step, span, row_count, at)
                for vertical in (-1, 0, 1):
                    for horizontal in (-1, 0, 1):
                        tap = 9 + 3 * (vertical + 1) + horizontal + 1
                        anchor = patch_span + vertical * GRID_SIDE + horizontal
                        patch_total = patch_total + window[anchor : anchor + patch_span] * taps_ref[tap : tap + 1, at]
                low[pl.ds(pl.multiple_of(text_slots + where * patch_span, 16), patch_span), at] = (
                    patch_total.astype(jnp.bfloat16)
                )
                if step == 0:
                    for first, rows_here, value in ((0, span, total), (span, patch_span, patch_total)):
                        here = pl.ds(pl.multiple_of(base + first, 16), rows_here)
                        hidden_ref[here, at] = value
                        hidden_low_ref[here, at] = value.astype(jnp.bfloat16)
                return carry

            lax.fori_loop(0, width // lanes, convolve, 0)
        own_rows = pl.ds(pl.multiple_of(base, 16), row_count)

        def project(tile, carry):
            at = pl.ds(pl.multiple_of(tile * lanes, lanes), lanes)
            key_ref[page, :, at] = dot_nn(low[...], matrices[1, :, at]).astype(jnp.bfloat16)
            value_ref[page, :, at] = (dot_nn(low[...], matrices[2, :, at]) + vector_ref[1:2, at]).astype(
                jnp.bfloat16
            )
            query_ref[own_rows, at] = (
                (dot_nn(hidden_low_ref[own_rows, :], matrices[0, :, at]) + vector_ref[0:1, at])
                .astype(jnp.bfloat16)
                * jnp.bfloat16(0.125)
            )
            return carry

        lax.fori_loop(0, width // lanes, project, 0)

        @pl.when(page < count - 1)
        def _():
            for copy in first_copies(page + 1, 1):
                copy.wait_recv()
            onward_copy(page + 1).start()

        def attend(pair, carry):
            at = pl.ds(pl.multiple_of(pair * pair_width, pair_width), pair_width)
            scores[...] = dot_nt(pair_masked(query_ref[own_rows, at] * jnp.bfloat16(FIXED)), key_ref[page, :, at])
            plane_row = packed_ref[0, pl.ds(pair, 1), :]
            for start in range(0, row_count, CHUNK):
                here = slice(start, start + CHUNK)
                packed = []
                for block_at in range(0, key_pad, 128):
                    lane = slice(block_at, block_at + 128)
                    packed.append(
                        line_ref[pair, here, lane]
                        + lookup(plane_row, across_ref[here, lane])
                        + lookup(plane_row, upward_ref[here, lane])
                    )
                for side in range(2):
                    there = slice(side * row_count + start, side * row_count + start + CHUNK)
                    parts, top = [], None
                    for index, word in enumerate(packed):
                        lane = slice(128 * index, 128 * (index + 1))
                        field = (word >> 16) if side else (word & 0xFFFF)
                        part = (scores[there, lane] + field.astype(jnp.float32)) + live_ref[0:1, lane]
                        top = part if top is None else jnp.maximum(top, part)
                        parts.append(part)
                    top = jnp.max(top, axis=1, keepdims=True)
                    parts = [jnp.exp2((part - top) * power) for part in parts]
                    total = parts[0]
                    for part in parts[1:]:
                        total = total + part
                    inverse = 1.0 / jnp.sum(total, axis=1, keepdims=True)
                    for index, part in enumerate(parts):
                        weights_ref[page, pair, there, 128 * index : 128 * (index + 1)] = (part * inverse).astype(
                            jnp.bfloat16
                        )
            mixture_ref[own_rows, at] = pair_merged(
                dot_nn(weights_ref[page, pair], value_ref[page, :, at])
            ).astype(jnp.bfloat16)
            return carry

        lax.fori_loop(0, pairs, attend, 0)
        for copy in stores(page):
            copy.start()
        return carry

    lax.fori_loop(0, count, page_step, 0)
    for page in range(count):
        for side in range(2):
            for copy in first_copies(page, side):
                copy.wait_send()
        onward_copy(page).wait_send()
        for copy in stores(page):
            copy.wait()


VMEM = pltpu.VMEM
KERNEL_VMEM = 62 * 1024 * 1024


def in_vmem(count):
    return [pl.BlockSpec(memory_space=VMEM)] * count


def staged(kernel, first, count):
    def run(*refs):
        *refs, semaphore = refs
        refs, buffers = list(refs[:-count]), refs[-count:]
        copies = [
            pltpu.make_async_copy(refs[first + index], buffers[index], semaphore.at[index]) for index in range(count)
        ]
        for copy in copies:
            copy.start()
        refs[first : first + count] = buffers
        kernel(copies, *refs)

    return run


def stage_for(values):
    return [VMEM(value.shape, value.dtype) for value in values] + [pltpu.SemaphoreType.DMA((len(values),))]


def position():
    seq = lax.axis_index("seq")
    return seq, seq % 2, lax.axis_index("page"), seq // 2


def anywhere(count):
    return [pl.BlockSpec(memory_space=pl.ANY)] * count


def forward(pages, lengths, tokens, patches, box, taps, matrices, vectors, table):
    count, span, width = tokens.shape
    patch_span = patches.shape[1]
    row_count = span + patch_span
    total_rows = count * row_count
    key_pad = -(-4 * row_count // 128) * 128
    pairs = table.shape[0] // 2
    bf16, f32, i32 = jnp.bfloat16, jnp.float32, jnp.int32
    own = jax.ShapeDtypeStruct((total_rows, width), bf16)
    every = jax.ShapeDtypeStruct((count, key_pad, width), bf16)
    return pl.pallas_call(
        staged(functools.partial(forward_kernel, pages), 1, 4),
        out_shape=(
            jax.ShapeDtypeStruct((total_rows, width), f32), own, own, own,
            jax.ShapeDtypeStruct((count, row_count, 256), i32),
            jax.ShapeDtypeStruct((count, 8, key_pad), i32),
            jax.ShapeDtypeStruct((count, 8, 256), i32),
            every, every,
            jax.ShapeDtypeStruct((count, pairs, 2 * row_count, key_pad), bf16),
        ),
        in_specs=[pl.BlockSpec(memory_space=pltpu.SMEM)] + anywhere(9),
        out_specs=tuple(in_vmem(7) + anywhere(3)),
        scratch_shapes=[
            VMEM((count, row_count, width), bf16),
            VMEM((3, width, width), bf16),
            VMEM((count, key_pad, width), bf16),
            VMEM((count, key_pad, width), bf16),
            VMEM((count, pairs, 2 * row_count, key_pad), bf16),
            VMEM((3, count, row_count, width), bf16),
            VMEM((4 * span + 16, width), f32),
            VMEM((6 * patch_span, width), f32),
            VMEM((key_pad, width), bf16),
            VMEM((2 * row_count, key_pad), f32),
            VMEM((row_count, key_pad), i32),
            VMEM((row_count, key_pad), i32),
            VMEM((8, key_pad), f32),
            VMEM((pairs, row_count, key_pad), i32),
            VMEM((2, 8, 128), i32),
            pltpu.SemaphoreType.DMA((5,)),
            pltpu.SemaphoreType.DMA((3, count)),
            pltpu.SemaphoreType.DMA((5, count)),
            pltpu.SemaphoreType.DMA((5, count)),
        ]
        + stage_for((box, taps, vectors, table)),
        compiler_params=pltpu.CompilerParams(
            collective_id=0, has_side_effects=True, vmem_limit_bytes=KERNEL_VMEM
        ),
        cost_estimate=pl.CostEstimate(flops=8_000_000_000, bytes_accessed=25_000_000, transcendentals=3_000_000),
        name="forward",
    )(lengths, box, taps, vectors, table, tokens, patches, *matrices)


def backward_page_kernel(
    scalar_ref, columns_ref, rows_ref, query_rows_ref, query_ref, key_ref, value_ref, mixture_back_ref, weights_ref,
    query_back_ref, block_back_ref, plane_back_ref, line_back_ref,
    back, steps, mask_ref, hot_ref, query_hot_ref, band_ref,
):
    seq_index = scalar_ref[0]
    row_count, width = query_ref.shape
    key_pad = key_ref.shape[0]
    count = 4
    patch_span = GRID_SIDE * GRID_SIDE // count
    span = row_count - patch_span
    text_slots = span * count
    columns, rows = columns_ref[...], rows_ref[...]
    mask_ref[:, 0:key_pad] = ((rows[0:1, :] & 15) < (columns[:, 0:1] & 15)).astype(jnp.float32).astype(jnp.bfloat16)
    mask_ref[:, key_pad:] = ((rows[1:2, :] & 15) < (columns[:, 1:2] & 15)).astype(jnp.float32).astype(jnp.bfloat16)
    bin_at = lax.broadcasted_iota(jnp.int32, (128, key_pad), 0) - 1
    key_block = lax.broadcasted_iota(jnp.int32, (128, key_pad), 1) >> 4
    for side in range(2):
        key_bin = rows[side : side + 1, :] >> 4
        plain = (key_bin == bin_at).astype(jnp.float32)
        lower = (key_bin - 1 == bin_at).astype(jnp.float32)
        plain, lower = jnp.where(bin_at < 64, plain, 0.0), jnp.where(bin_at < 64, lower, 0.0)
        mine = slice(128 * side, 128 * (side + 1))
        other = slice(128 * (1 - side), 128 * (2 - side))
        change = lower - plain
        if side == 0:
            plain = jnp.where(bin_at - 71 == key_block, 1.0, plain)
        hot_ref[mine, 0:key_pad] = plain.astype(jnp.bfloat16)
        hot_ref[mine, (1 + side) * key_pad : (2 + side) * key_pad] = change.astype(jnp.bfloat16)
        hot_ref[other, (1 + side) * key_pad : (2 + side) * key_pad] = jnp.zeros((128, key_pad), jnp.bfloat16)
    half_bin = lax.broadcasted_iota(jnp.int32, (72, row_count), 0)
    for side in range(2):
        query_hot_ref[72 * side : 72 * (side + 1), :] = (
            (71 - (query_rows_ref[side : side + 1, :] >> 4) == half_bin).astype(jnp.float32).astype(jnp.bfloat16)
        )
    lane128 = lax.broadcasted_iota(jnp.int32, (row_count, 128), 1)
    place = query_places(seq_index, (row_count, 128), span, patch_span, text_slots)
    aim = place + lane128 - 32
    near = (lane128 < 64) & (aim >= 0) & (aim < text_slots + patch_span * count)
    apart = (aim >> 4) - (place >> 4)
    near = near & (apart >= -1) & (apart <= 1)
    band_ref[...] = jnp.where(near, aim, -1)
    pair_width = 128
    line_back_ref[...] = jnp.zeros_like(line_back_ref)
    plane_back_ref[...] = jnp.zeros_like(plane_back_ref)

    def attend(pair, carry):
        at = pl.ds(pl.multiple_of(pair * pair_width, pair_width), pair_width)
        both_query = pair_masked(query_ref[:, at])
        both_back = pair_masked(mixture_back_ref[:, at])
        back[...] = dot_nt(both_back, value_ref[:, at])
        for start in range(0, 2 * row_count, CHUNK):
            there = slice(start, start + CHUNK)
            here = slice(start % row_count, start % row_count + CHUNK)
            parts, total = [], None
            for block_at in range(0, key_pad, 128):
                lane = slice(block_at, block_at + 128)
                part = weights_ref[pair, there, lane].astype(jnp.float32)
                product = part * back[there, lane]
                total = product if total is None else total + product
                parts.append(part)
            mean = jnp.sum(total, axis=1, keepdims=True)
            for index, part in enumerate(parts):
                lane = slice(128 * index, 128 * (index + 1))
                step = (part * (back[there, lane] - mean)).astype(jnp.bfloat16)
                steps[there, lane] = step
                steps[there, key_pad + 128 * index : key_pad + 128 * (index + 1)] = step * mask_ref[here, lane]
                steps[there, 2 * key_pad + 128 * index : 2 * key_pad + 128 * (index + 1)] = (
                    step * mask_ref[here, key_pad + 128 * index : key_pad + 128 * (index + 1)]
                )
        query_back_ref[:, at] = (pair_merged(dot_nn(steps[:, 0:key_pad], key_ref[:, at])) * 0.125).astype(
            jnp.bfloat16
        )
        for kind, value in enumerate(
            (dot_tn(steps[:, 0:key_pad], both_query), dot_tn(weights_ref[pair], both_back))
        ):
            value = value.astype(jnp.bfloat16)
            for where in range(count):
                step_at = seq_index ^ where
                slot = (step_at & 1) * 2 + (step_at >> 1)
                block_back_ref[slot, kind, 0:span, at] = value[where * span : (where + 1) * span]
                block_back_ref[slot, kind, span:row_count, at] = value[
                    text_slots + where * patch_span : text_slots + (where + 1) * patch_span
                ]
        bins = dot_nt(steps[...], hot_ref[...])
        low_bins = bins.astype(jnp.bfloat16)
        lane_one = lax.broadcasted_iota(jnp.int32, (1, 128), 1)
        far = lane128 - 72 - (place >> 4)
        in_line = (lane128 >= 72) & (lane128 < 72 + key_pad // 16)
        for side in range(2):
            head = pl.ds(2 * pair + side, 1)
            own = slice(side * row_count, (side + 1) * row_count)
            both = dot_nn(query_hot_ref[...], low_bins[own])
            for plane in range(2):
                table = both[72 * plane : 72 * (plane + 1), 128 * plane : 128 * (plane + 1)]
                wide_lane = lax.broadcasted_iota(jnp.int32, table.shape, 1)
                table = jnp.where(wide_lane < 72, table, 0.0)
                table = jnp.concatenate([table, jnp.zeros_like(table)], axis=1)
                sheared = pltpu.roll(table, 0, 1, stride=1, stride_axis=0)
                plane_back_ref[plane, head, :] = jnp.sum(sheared, axis=0, keepdims=True)
            line_bins = bins[own, 0:128]
            low_tail = jnp.sum(jnp.where(in_line & (far <= -2), line_bins, 0.0), axis=(0, 1), keepdims=True)
            high_tail = jnp.sum(jnp.where(in_line & (far >= 2), line_bins, 0.0), axis=(0, 1), keepdims=True)
            band = jnp.zeros((1, 128), jnp.float32)
            base = side * row_count
            for first, rows_here, block in (
                (0, span, seq_index),
                (0, 32, jnp.maximum(seq_index - 1, 0)),
                (span - 32, 32, seq_index + 1),
                (span, patch_span, count - 1),
                (span, patch_span, count),
            ):
                aims = band_ref[first : first + rows_here, :]
                source = steps[
                    base + first : base + first + rows_here, pl.ds(pl.multiple_of(block * 128, 128), 128)
                ].astype(jnp.float32)
                taken = jnp.take_along_axis(source, aims & 127, axis=1)
                right = (aims >> 7) == block
                if first == 0 and rows_here == 32:
                    right = right & (seq_index > 0)
                band = band + jnp.sum(jnp.where(right, taken, 0.0), axis=0, keepdims=True)
            line_back_ref[head, :] = (
                band + jnp.where(lane_one == 0, low_tail, 0.0) + jnp.where(lane_one == 63, high_tail, 0.0)
            )
        return carry

    lax.fori_loop(0, width // pair_width, attend, 0)


def backward_page(scalars, columns, rows, query_rows, queries, keys, values, mixture_back, weights):
    row_count, width = queries.shape
    key_pad = keys.shape[0]
    heads = 2 * weights.shape[0]
    return pl.pallas_call(
        backward_page_kernel,
        out_shape=(
            jax.ShapeDtypeStruct((row_count, width), jnp.bfloat16),
            jax.ShapeDtypeStruct((4, 2, row_count, width), jnp.bfloat16),
            jax.ShapeDtypeStruct((2, heads, 256), jnp.float32),
            jax.ShapeDtypeStruct((heads, 128), jnp.float32),
        ),
        in_specs=[pl.BlockSpec(memory_space=pltpu.SMEM)] + in_vmem(8),
        out_specs=tuple(in_vmem(4)),
        scratch_shapes=[
            pltpu.VMEM((2 * row_count, key_pad), jnp.float32),
            pltpu.VMEM((2 * row_count, 3 * key_pad), jnp.bfloat16),
            pltpu.VMEM((row_count, 2 * key_pad), jnp.bfloat16),
            pltpu.VMEM((256, 3 * key_pad), jnp.bfloat16),
            pltpu.VMEM((144, row_count), jnp.bfloat16),
            pltpu.VMEM((row_count, 128), jnp.int32),
        ],
        compiler_params=pltpu.CompilerParams(vmem_limit_bytes=KERNEL_VMEM),
        cost_estimate=pl.CostEstimate(flops=3_000_000_000, bytes_accessed=6_000_000, transcendentals=1_000_000),
        name="backward_page",
    )(scalars, columns, rows, query_rows, queries, keys, values, mixture_back, weights)


def early_orders(far, side):
    return (far[1], far[0], side) + tuple(far[2:]), (far[0], far[1], side) + tuple(far[2:])


def slot_of_bits(bits):
    slot = 0
    for bit in bits:
        slot = slot * 2 + bit
    return slot


def apart(one, other):
    return (one + other) % 2


def early_slots(scalar_ref, page, column, levels):
    far = [apart((page >> level) & 1, (scalar_ref[2] >> level) & 1) for level in range(levels)]
    side = apart(column, scalar_ref[3])
    return [slot_of_bits(order) for order in early_orders(far, side)]


NORM_CHUNK = 48


def norm_rows(values):
    mean = jnp.mean(values, axis=-1, keepdims=True)
    centred = values - mean
    scale = lax.rsqrt(jnp.mean(centred * centred, axis=-1, keepdims=True) + epsilon)
    return centred * scale, scale


def norm_back(delta, unit, scale):
    return scale * (
        delta
        - jnp.mean(delta, axis=-1, keepdims=True)
        - unit * jnp.mean(delta * unit, axis=-1, keepdims=True)
    )


def column_sum(values):
    return jnp.sum(values, axis=0, keepdims=True)


OUT_BIAS, DOWN_BIAS, FIRST_GAIN, FIRST_SHIFT, SECOND_GAIN, SECOND_SHIFT = range(6)
UP_BIAS = 6


def middle_kernel(
    pages, direct,
    vector_any, *rest,
):
    scalar_ref = position()
    arguments, rest = (*rest[:7], vector_any), rest[7:]
    output_ref, patch_output_ref, first_back_ref, mixture_back_ref, sums_ref, *rest = rest
    *rest, load_sem, store_sem = rest
    copied, rest = rest[-8:], rest[:-8]
    hidden_ref, mixture_ref, cotangent_ref, patch_cotangent_ref, out_weight_ref, up_weight_ref, down_weight_ref, vector_ref = (
        copied
    )
    loads = [
        pltpu.make_async_copy(source, target, load_sem.at[index])
        for index, (source, target) in enumerate(zip(arguments, copied, strict=True))
    ]
    for index in (7, 1, 4, 0, 5, 6, 2, 3):
        loads[index].start()
    if direct:
        bundle_any, *rest, bundle_ref = rest
    else:
        normed_out_ref, up_out_ref, activated_out_ref, down_out_ref, attention_out_ref, *rest = rest
    state, unit, scale_ref, normed, activated, slope, up_back, down_back, attention_back, flipped = rest
    count, span, width = output_ref.shape
    patch_span = patch_output_ref.shape[1]
    row_count = span + patch_span
    total_rows = count * row_count
    wide = up_weight_ref.shape[1]
    lanes = 256
    sums_ref[...] = jnp.zeros_like(sums_ref)

    def tile_at(tile):
        return pl.ds(pl.multiple_of(tile * lanes, lanes), lanes)

    def attention_tile(tile, carry):
        at = tile_at(tile)
        state[:, at] = hidden_ref[:, at] + (dot_nn(mixture_ref[...], out_weight_ref[:, at]) + vector_ref[2:3, at])
        return carry

    for index in (0, 1, 4, 7):
        loads[index].wait()
    lax.fori_loop(0, width // lanes, attention_tile, 0)

    def first_norm(chunk, carry):
        here = pl.ds(pl.multiple_of(chunk * NORM_CHUNK, 16), NORM_CHUNK)
        rows, scale = norm_rows(state[here, :])
        unit[here, :] = rows
        scale_ref[here, :] = jnp.broadcast_to(scale, (NORM_CHUNK, 128))
        rows = rows * vector_ref[4:5, :] + vector_ref[5:6, :]
        state[here, :] = rows
        normed[here, :] = rows.astype(jnp.bfloat16)
        return carry

    lax.fori_loop(0, total_rows // NORM_CHUNK, first_norm, 0)

    def up_tile(tile, carry):
        at = tile_at(tile)
        branch = dot_nn(normed[...], up_weight_ref[:, at]) + vector_ref[pl.ds(8 + tile // 3, 1), tile_at(tile % 3)]
        chance = 0.5 * (1.0 + lax.erf(branch * 0.7071067811865476))
        activated[:, at] = (branch * chance).astype(jnp.bfloat16)
        slope[:, at] = chance + branch * (jnp.exp(branch * branch * -0.5) * 0.3989422804014327)
        return carry

    loads[5].wait()
    lax.fori_loop(0, wide // lanes, up_tile, 0)

    def down_tile(tile, carry):
        at = tile_at(tile)
        state[:, at] = state[:, at] + (dot_nn(activated[...], down_weight_ref[:, at]) + vector_ref[3:4, at])
        return carry

    for index in (2, 3, 6):
        loads[index].wait()
    lax.fori_loop(0, width // lanes, down_tile, 0)

    def second_norm(start, rows_here, page, out_ref, delta_ref):
        here = pl.ds(pl.multiple_of(page * row_count + start, 16), rows_here)
        there = pl.ds(0 if start == span else start, rows_here)
        rows, scale = norm_rows(state[here, :])
        out_ref[page, there, :] = rows * vector_ref[6:7, :] + vector_ref[7:8, :]
        delta = delta_ref[page, there, :].astype(jnp.float32)
        back = norm_back(delta * vector_ref[6:7, :], rows, scale)
        state[here, :] = back
        low = back.astype(jnp.bfloat16)
        down_back[here, :] = low
        for index, value in (
            (SECOND_GAIN, delta * rows), (SECOND_SHIFT, delta), (DOWN_BIAS, low.astype(jnp.float32))
        ):
            sums_ref[index : index + 1, :] += column_sum(value)

    def second_page(page, carry):
        for start in range(0, span, 32):
            second_norm(start, 32, page, output_ref, cotangent_ref)
        second_norm(span, patch_span, page, patch_output_ref, patch_cotangent_ref)
        return carry

    lax.fori_loop(0, count, second_page, 0)

    def up_back_tile(tile, carry):
        at = tile_at(tile)
        low = (dot_nt(down_back[...], down_weight_ref[at, :]) * slope[:, at]).astype(jnp.bfloat16)
        up_back[:, at] = low
        sums_ref[pl.ds(UP_BIAS + tile // 3, 1), tile_at(tile % 3)] = column_sum(low.astype(jnp.float32))
        return carry

    lax.fori_loop(0, wide // lanes, up_back_tile, 0)

    def normed_back_tile(tile, carry):
        at = tile_at(tile)
        state[:, at] = state[:, at] + dot_nt(up_back[...], up_weight_ref[at, :])
        return carry

    lax.fori_loop(0, width // lanes, normed_back_tile, 0)

    def first_back(chunk, carry):
        here = pl.ds(pl.multiple_of(chunk * NORM_CHUNK, 16), NORM_CHUNK)
        delta, rows = state[here, :], unit[here, :]
        back = norm_back(delta * vector_ref[4:5, :], rows, scale_ref[here, 0:1])
        first_back_ref[here, :] = back
        low = back.astype(jnp.bfloat16)
        attention_back[here, :] = low
        for index, value in (
            (FIRST_GAIN, delta * rows), (FIRST_SHIFT, delta), (OUT_BIAS, low.astype(jnp.float32))
        ):
            sums_ref[index : index + 1, :] += column_sum(value)
        return carry

    lax.fori_loop(0, total_rows // NORM_CHUNK, first_back, 0)

    def mixture_tile(tile, carry):
        at = tile_at(tile)
        mixture_back_ref[:, at] = dot_nt(attention_back[...], out_weight_ref[at, :]).astype(jnp.bfloat16)
        return carry

    lax.fori_loop(0, width // lanes, mixture_tile, 0)
    if not direct:
        normed_out_ref[...] = normed[...]
        up_out_ref[...] = up_back[...]
        activated_out_ref[...] = activated[...]
        down_out_ref[...] = down_back[...]
        attention_out_ref[...] = attention_back[...]
        return
    levels = pages.bit_length() - 1
    core = scalar_ref[1]
    rows = width // pages
    tall = wide // pages
    block = 384
    groups = wide // (2 * block)
    flipped[...] = normed[...].T

    def up_weight_tile(tile, carry):
        column, group = tile // groups, tile % groups
        at = pl.ds(pl.multiple_of(tile * block, block), block)
        result = dot_nn(flipped[...], up_back[:, at]).astype(jnp.bfloat16)
        for page in range(pages):
            slot = early_slots(scalar_ref, page, column, levels)[0]
            bundle_ref[core, slot, pl.ds(pl.multiple_of(group * rows, 16), rows), :] = result[
                page * rows : (page + 1) * rows
            ]
        return carry

    lax.fori_loop(0, 2 * groups, up_weight_tile, 0)
    stores = [
        pltpu.make_async_copy(bundle_ref.at[part], bundle_any.at[part], store_sem.at[index])
        for index, part in enumerate(
            (
                (core, slice(None), slice(0, tall)), (1 - core, slice(None), slice(0, tall)),
                (slice(None), slice(None), slice(tall, tall + rows // 2)),
            )
        )
    ]
    stores[0].start()

    def down_weight_tile(page, carry):
        at = pl.ds(pl.multiple_of(page * tall, 128), tall)
        result = dot_tn(activated[:, at], down_back[...]).astype(jnp.bfloat16)
        for column in range(2):
            slot = early_slots(scalar_ref, page, column, levels)[1]
            bundle_ref[1 - core, slot, 0:tall, :] = result[:, column * block : (column + 1) * block]
        return carry

    lax.fori_loop(0, pages, down_weight_tile, 0)
    stores[1].start()
    flipped[...] = mixture_ref[...].T
    half = rows // 2

    def out_weight_tile(column, carry):
        at = pl.ds(pl.multiple_of(column * block, block), block)
        result = dot_nn(flipped[...], attention_back[:, at]).astype(jnp.bfloat16)
        for page in range(pages):
            slots = early_slots(scalar_ref, page, column, levels)
            for order in range(2):
                first = page * rows + order * half
                bundle_ref[core if order == 0 else 1 - core, slots[order], tall : tall + half, :] = result[
                    first : first + half
                ]
        return carry

    lax.fori_loop(0, 2, out_weight_tile, 0)
    stores[2].start()
    for copy in stores:
        copy.wait()


def in_tiles(width, pages):
    return (width // pages) % 32 == 0 and pages >= 4


def middle(places, hidden, mixture, cotangent, patch_cotangent, matrices, vectors, pages):
    count, span, width = cotangent.shape
    patch_span = patch_cotangent.shape[1]
    total_rows = hidden.shape[0]
    wide = matrices[1].shape[1]
    direct = in_tiles(width, pages)
    bf16, f32 = jnp.bfloat16, jnp.float32
    if direct:
        extra = (jax.ShapeDtypeStruct((2, 2 * pages, (wide + width // 2) // pages, 384), bf16),)
    else:
        extra = tuple(
            jax.ShapeDtypeStruct((total_rows, size), bf16) for size in (width, wide, wide, width, width)
        )
    result = pl.pallas_call(
        functools.partial(middle_kernel, pages, direct),
        out_shape=(
            jax.ShapeDtypeStruct(cotangent.shape, f32),
            jax.ShapeDtypeStruct(patch_cotangent.shape, f32),
            jax.ShapeDtypeStruct((total_rows, width), f32),
            jax.ShapeDtypeStruct((total_rows, width), bf16),
            jax.ShapeDtypeStruct((16, width), f32),
        )
        + extra,
        in_specs=anywhere(8),
        out_specs=tuple(in_vmem(5) + (anywhere(1) if direct else in_vmem(len(extra)))),
        scratch_shapes=[
            pltpu.VMEM((total_rows, width), f32),
            pltpu.VMEM((total_rows, width), f32),
            pltpu.VMEM((total_rows, 128), f32),
            pltpu.VMEM((total_rows, width), bf16),
            pltpu.VMEM((total_rows, wide), bf16),
            pltpu.VMEM((total_rows, wide), f32),
            pltpu.VMEM((total_rows, wide), bf16),
            pltpu.VMEM((total_rows, width), bf16),
            pltpu.VMEM((total_rows, width), bf16),
            pltpu.VMEM((width, total_rows), bf16),
        ]
        + [pltpu.VMEM(value.shape, value.dtype) for value in (extra if direct else ())]
        + [
            pltpu.VMEM(value.shape, value.dtype)
            for value in (hidden, mixture, cotangent, patch_cotangent, *matrices, vectors)
        ]
        + [pltpu.SemaphoreType.DMA((8,)), pltpu.SemaphoreType.DMA((3,))],
        compiler_params=pltpu.CompilerParams(vmem_limit_bytes=KERNEL_VMEM),
        cost_estimate=pl.CostEstimate(flops=14_000_000_000, bytes_accessed=30_000_000, transcendentals=2_600_000),
        name="middle",
    )(vectors, hidden, mixture, cotangent, patch_cotangent, *matrices)
    first, rest = result[:5], result[5:]
    if direct:
        return first + rest
    normed, up_back, activated, down_back, attention_back = rest
    return first + (
        indexed_bundle(
            (
                ((normed, up_back, None), (mixture, attention_back, 0)),
                ((activated, down_back, None), (mixture, attention_back, 1)),
            ),
            places,
            pages,
        ),
    )


def indexed_bundle(matrices, scalars, pages):
    levels = pages.bit_length() - 1
    place = jnp.arange(2 * pages, dtype=jnp.int32)
    bits = [(place >> (levels - k)) & 1 for k in range(levels + 1)]
    halves = []
    for order, group in enumerate(matrices):
        side, near = (bits[0], bits[1]) if order == 0 else (bits[1], bits[0])
        far = near
        for level in range(1, levels):
            far = far + (bits[level + 1] << level)
        index = (far ^ scalars[2]) * 2 + (side ^ scalars[3])
        blocks = []
        for operand, gradient, part in group:
            rows = in_blocks(outer_dot(operand, gradient).astype(jnp.bfloat16), pages)
            if part is not None:
                half = rows.shape[1] // 2
                rows = rows[:, part * half : (part + 1) * half]
            blocks.append(rows)
        halves.append(jnp.concatenate(blocks, axis=1)[index])
    first, second = halves
    mine = scalars[1] == 0
    return jnp.stack([jnp.where(mine, first, second), jnp.where(mine, second, first)])


def in_blocks(matrix, pages):
    rows, columns = matrix.shape[0] // pages, matrix.shape[1] // 2
    lanes = min(columns, 384)
    blocks = matrix.reshape(pages, rows, 2, columns // lanes, lanes)
    return blocks.transpose(0, 2, 3, 1, 4).reshape(pages * 2, rows * columns // lanes, lanes)


class Halving:
    def __init__(self, keep, source, landing, landings, partners, sibling, sems, chunks):
        self.keep, self.landing, self.landings = keep, landing, landings
        total = keep.shape[0]
        unit = total // chunks
        send_sem, recv_sem = sems
        self.arrivals, self.sends, self.needs = {}, {}, {}
        used = 0
        for chunk in range(chunks):
            lo = total - (chunk + 1) * unit
            copy = remote(
                source.at[lo : lo + unit], landing.at[lo : lo + unit], send_sem.at[used], recv_sem.at[used], *sibling
            )
            self.arrivals["core", chunk] = (copy, landing, lo, unit)
            used += 1
        for step, (into, partner) in enumerate(zip(landings, partners, strict=True)):
            size = total >> (step + 1)
            piece = min(unit, size)
            for chunk in range(size // piece):
                lo = size - (chunk + 1) * piece
                copy = remote(
                    keep.at[size + lo : size + lo + piece], into.at[lo : lo + piece], send_sem.at[used],
                    recv_sem.at[used], *partner,
                )
                self.arrivals[step, chunk] = (copy, into, lo, piece)
                self.sends[step, chunk] = copy
                self.needs[step, chunk] = {
                    (source_step, block)
                    for block in range(size + lo, size + lo + piece)
                    for source_step in ("core", *range(step))
                }
                used += 1
        self.done = set()

    def start(self):
        for key, (copy, *_) in self.arrivals.items():
            if key[0] == "core":
                copy.start()

    def take(self, *key):
        copy, into, lo, count = self.arrivals[key]
        copy.wait_recv()

        def add(block, carry):
            self.keep[block] = self.keep[block] + into[block]
            return carry

        lax.fori_loop(lo, lo + count, add, 0)
        for block in range(lo, lo + count):
            self.done.add((key[0], block))
        for name in list(self.sends):
            if self.needs[name] <= self.done:
                self.sends.pop(name).start()

    def finish(self):
        for copy, *_ in self.arrivals.values():
            copy.wait_send()


def backward_kernel(
    pages,
    staging, length_ref, query_ref, mixture_back_ref, columns_ref, rows_ref, query_rows_ref, tokens_ref, patches_ref, taps_ref,
    middle_sums_ref, bundle_any, weights_any, key_any, value_any, hidden_any, first_back_any, query_weight_any,
    key_weight_any, value_weight_any,
    tokens_back_ref, patches_back_ref, early_ref, late_ref, sums_ref, up_in_ref, down_in_ref, mixed_in_ref,
    keep, landing, landings, late, late_landing, late_landings, weights_buf, key_buf, value_buf, outgoing, from_sib,
    from_far, matrices, hidden, flipped, total_back, query_back, key_back, value_back, back, steps, mask_ref, hot_ref,
    query_hot_ref, band_ref, table_acc, band_acc, table_out, text_rim, patch_rim, sums, sums_in,
    up_in, down_out, down_in, mixed_out, mixed_in,
    load_sem, page_sem, early_send, early_recv, late_send, late_recv, sib_send, sib_recv, far_send, far_recv, rim_send,
    rim_recv, sum_send, sum_recv, swap_send, swap_recv,
):
    page_at, bits, seq, across, core = places_of(pages)
    levels = len(bits)
    count, span, width = tokens_ref.shape
    patch_span = patches_ref.shape[1]
    row_count = span + patch_span
    total_rows = count * row_count
    key_pad = key_buf.shape[1]
    text_slots = 4 * span
    pairs = weights_buf.shape[1]
    heads = 2 * pairs
    f32, bf16 = jnp.float32, jnp.bfloat16

    sibling = (page_at, sibling_of(seq))
    opposite = (page_at, across_of(seq))
    diagonal = (page_at, sibling_of(across_of(seq)))
    flips = [(1 - 2 * bit) * 2**level for level, bit in enumerate(bits)]
    on_page = [(page_at + flip, seq) for flip in flips]
    either = lambda first, second: first + core * (second - first)
    early_partners = [
        (page_at + either(flips[1], flips[0]), seq),
        (page_at + either(flips[0], flips[1]), seq),
        opposite,
    ] + on_page[2:]
    barrier = pltpu.get_barrier_semaphore()
    everyone = [sibling, opposite, diagonal] + on_page
    for peer in everyone:
        pl.semaphore_signal(barrier, inc=1, device_id=peer, device_id_type=MESH)

    keep_load = pltpu.make_async_copy(bundle_any.at[0], keep, load_sem.at[0])
    later_loads = [
        pltpu.make_async_copy(source, target, load_sem.at[1 + index])
        for index, (source, target) in enumerate(
            (
                (query_weight_any, matrices.at[0]), (key_weight_any, matrices.at[1]),
                (value_weight_any, matrices.at[2]), (hidden_any, hidden), (first_back_any, total_back),
            )
        )
    ]

    def page_loads(page):
        slot = page % 2
        return [
            pltpu.make_async_copy(source.at[page], target.at[slot], page_sem.at[index, slot])
            for index, (source, target) in enumerate(
                ((weights_any, weights_buf), (key_any, key_buf), (value_any, value_buf))
            )
        ]

    for copy in page_loads(0):
        copy.start()
    keep_load.start()
    for copy in later_loads:
        copy.start()
    pl.semaphore_wait(barrier, len(everyone))
    early = Halving(
        keep, bundle_any.at[1], landing, landings, early_partners, sibling, (early_send, early_recv), 8
    )
    late_sum = Halving(
        late.at[0], late.at[1], late_landing, late_landings, early_partners, sibling, (late_send, late_recv), 4
    )
    early.start()
    for copy in staging:
        copy.wait()

    lane128 = lax.broadcasted_iota(jnp.int32, (row_count, 128), 1)
    place = query_places(seq, (row_count, 128), span, patch_span, text_slots)
    aim = place + lane128 - 32
    blocks_on = (aim >> 4) - (place >> 4)
    near = (lane128 < 64) & (aim >= 0) & (aim < text_slots + patch_span * 4) & (blocks_on >= -1) & (blocks_on <= 1)
    band_ref[...] = jnp.where(near, aim, -1)
    table_acc[...] = jnp.zeros_like(table_acc)
    band_acc[...] = jnp.zeros_like(band_acc)
    lane_of_row = lax.broadcasted_iota(jnp.int32, (48, row_count), 1)
    place_of_row = jnp.where(
        lane_of_row < span, seq * span + lane_of_row, text_slots + seq * patch_span + lane_of_row - span
    )
    query_hot_ref[144:192, :] = (
        ((place_of_row >> 4) == lax.broadcasted_iota(jnp.int32, (48, row_count), 0)).astype(f32).astype(bf16)
    )
    pair_width = 128

    def start_page(page):
        slot = page % 2
        for copy in page_loads(page):
            copy.wait()

        @pl.when(page < count - 1)
        def _():
            for copy in page_loads(page + 1):
                copy.start()

        bin_at = lax.broadcasted_iota(jnp.int32, (128, key_pad), 0) - 1
        key_block = lax.broadcasted_iota(jnp.int32, (128, key_pad), 1) >> 4
        half_bin = lax.broadcasted_iota(jnp.int32, (72, row_count), 0)
        for side in range(2):
            key_row = rows_ref[page, side : side + 1, :]
            query_column = columns_ref[page, :, 128 * side : 128 * side + 1]
            mask_ref[:, side * key_pad : (side + 1) * key_pad] = (
                ((key_row & 15) < (query_column & 15)).astype(f32).astype(bf16)
            )
            key_bin = key_row >> 4
            plain = jnp.where(bin_at < 64, (key_bin == bin_at).astype(f32), 0.0)
            lower = jnp.where(bin_at < 64, (key_bin - 1 == bin_at).astype(f32), 0.0)
            mine = slice(128 * side, 128 * (side + 1))
            other = slice(128 * (1 - side), 128 * (2 - side))
            change = lower - plain
            if side == 0:
                plain = jnp.where(bin_at - 71 == key_block, 1.0, plain)
            hot_ref[mine, 0:key_pad] = plain.astype(bf16)
            hot_ref[mine, (1 + side) * key_pad : (2 + side) * key_pad] = change.astype(bf16)
            hot_ref[other, (1 + side) * key_pad : (2 + side) * key_pad] = jnp.zeros((128, key_pad), bf16)
            query_bin = query_rows_ref[page, side : side + 1, 0:row_count] >> 4
            query_hot_ref[72 * side : 72 * (side + 1), :] = (71 - query_bin == half_bin).astype(f32).astype(bf16)

    def attend(page, pair):
        slot = page % 2
        at = pl.ds(pl.multiple_of(pair * pair_width, pair_width), pair_width)
        own_rows = pl.ds(pl.multiple_of(page * row_count, 16), row_count)
        both_query = pair_masked(query_ref[own_rows, at])
        both_back = pair_masked(mixture_back_ref[own_rows, at])
        back[...] = dot_nt(both_back, value_buf[slot, :, at])
        for start in range(0, 2 * row_count, CHUNK):
            there = slice(start, start + CHUNK)
            here = slice(start % row_count, start % row_count + CHUNK)
            parts, total = [], None
            for block_at in range(0, key_pad, 128):
                lane = slice(block_at, block_at + 128)
                part = weights_buf[slot, pair, there, lane].astype(f32)
                product = part * back[there, lane]
                total = product if total is None else total + product
                parts.append(part)
            mean = jnp.sum(total, axis=1, keepdims=True)
            for index, part in enumerate(parts):
                lane = slice(128 * index, 128 * (index + 1))
                step = (part * (back[there, lane] - mean)).astype(bf16)
                steps[there, lane] = step
                steps[there, key_pad + 128 * index : key_pad + 128 * (index + 1)] = step * mask_ref[here, lane]
                steps[there, 2 * key_pad + 128 * index : 2 * key_pad + 128 * (index + 1)] = (
                    step * mask_ref[here, key_pad + 128 * index : key_pad + 128 * (index + 1)]
                )
        query_back[own_rows, at] = (
            pair_merged(dot_nn(steps[:, 0:key_pad], key_buf[slot, :, at])) * 0.125
        ).astype(bf16)
        for kind, value in enumerate(
            (dot_tn(steps[:, 0:key_pad], both_query), dot_tn(weights_buf[slot, pair], both_back))
        ):
            value = value.astype(bf16)
            for where in range(4):
                place_at = apart(where % 2, core) * 2 + apart(where // 2, across)
                outgoing[page, place_at, kind, 0:span, at] = value[where * span : (where + 1) * span]
                outgoing[page, place_at, kind, span:row_count, at] = value[
                    text_slots + where * patch_span : text_slots + (where + 1) * patch_span
                ]
        bins = dot_nt(steps[...], hot_ref[...]).astype(bf16)
        for side in range(2):
            head = 2 * pair + side
            base = side * row_count
            both = dot_nn(query_hot_ref[...], bins[base : base + row_count])
            table_acc[head, 0:72, :] += both[0:72, 0:128]
            table_acc[head, 72:144, :] += both[72:144, 128:256]
            table_acc[head, 144:192, :] += both[144:192, 0:128]
            for first, rows_here, block, into in bands():
                source = steps[
                    base + first : base + first + rows_here, pl.ds(pl.multiple_of(block * 128, 128), 128)
                ]
                band_acc[head, into : into + rows_here, :] += source.astype(f32)

    def bands():
        before = seq - (seq + 3) // 4
        return (
            (0, span, seq, 0),
            (0, 32, before, span),
            (span - 32, 32, seq + 1, span + 32),
            (span, patch_span, 3, span + 64),
            (span, patch_span, 4, span + 64 + patch_span),
        )

    def sib_copy(page):
        return remote(outgoing.at[page, 2:4], from_sib.at[page], sib_send.at[page], sib_recv.at[page], *sibling)

    def far_copy(page):
        return remote(outgoing.at[page, 1], from_far.at[page], far_send.at[page], far_recv.at[page], *opposite)

    def pass_on(page):
        sib_copy(page).wait_recv()
        for kind in range(2):
            outgoing[page, 1, kind] = outgoing[page, 1, kind] + from_sib[page, 1, kind]
        far_copy(page).start()

    events = {
        1: [("core", 0), ("core", 1)], 2: [("core", 2), ("core", 3)], 4: [("core", 4), ("core", 5)],
        6: [("core", 6), ("core", 7)], 8: [(0, 0)], 12: [(0, 1)],
    }

    def step_body(turn, carry):
        page, pair = turn // pairs, turn % pairs

        @pl.when(pair == 0)
        def _():
            start_page(page)

        for at_turn, names in events.items():

            @pl.when(turn == at_turn)
            def _(names=names, at_turn=at_turn):
                if at_turn == min(events):
                    keep_load.wait()
                for name in names:
                    early.take(*name)

        @pl.when((pair == 2) & (page > 0))
        def _():
            pass_on(page - 1)

        attend(page, pair)

        @pl.when(pair == pairs - 1)
        def _():
            sib_copy(page).start()

        return carry

    lax.fori_loop(0, count * pairs, step_body, 0)

    for copy in later_loads:
        copy.wait()
    flipped[...] = hidden[...].T
    lanes = 384
    rows = width // pages
    half = rows // 2

    def weight_columns(index, gradient):
        def tile(column, carry):
            at = pl.ds(pl.multiple_of(column * lanes, lanes), lanes)
            result = dot_nn(flipped[...], gradient[:, at]).astype(bf16)
            for page in range(pages):
                far = [apart((page >> level) & 1, bit) for level, bit in enumerate(bits)]
                slots = [slot_of_bits(order) for order in early_orders(far, apart(column, across))]
                first = page * rows
                if index < 2:
                    late[core if index == 0 else 1 - core, slots[index], 0:rows, :] = result[first : first + rows]
                else:
                    late[core, slots[0], rows : rows + half, :] = result[first : first + half]
                    late[1 - core, slots[1], rows : rows + half, :] = result[first + half : first + rows]
            return carry

        lax.fori_loop(0, 2, tile, 0)

    def project_back(gradient, matrix):
        def tile(column, carry):
            at = pl.ds(pl.multiple_of(column * 256, 256), 256)
            total_back[:, at] = total_back[:, at] + dot_nt(gradient[...], matrices[matrix, at, :])
            return carry

        lax.fori_loop(0, width // 256, tile, 0)

    pass_on(count - 1)
    weight_columns(0, query_back)
    project_back(query_back, 0)
    sums[0, 0:16, :] = middle_sums_ref[...]
    sums[0, 10:11, :] = column_sum(query_back[...].astype(f32))

    def head_tables(head, carry):
        for plane in range(2):
            table = table_acc[head, 72 * plane : 72 * (plane + 1), :]
            lane = lax.broadcasted_iota(jnp.int32, table.shape, 1)
            table = jnp.where(lane < 72, table, 0.0)
            table = jnp.concatenate([table, jnp.zeros_like(table)], axis=1)
            sheared = pltpu.roll(table, 0, 1, stride=1, stride_axis=0)
            table_out[head, 0:1, 256 * plane : 256 * (plane + 1)] = column_sum(sheared)
        table = table_acc[head, 144:192, :]
        lane = lax.broadcasted_iota(jnp.int32, table.shape, 1)
        apart_by = lane - 72 - lax.broadcasted_iota(jnp.int32, table.shape, 0)
        in_line = (lane >= 72) & (lane < 72 + 36)
        low_tail = jnp.sum(column_sum(jnp.where(in_line & (apart_by <= -2), table, 0.0)), axis=1, keepdims=True)
        high_tail = jnp.sum(column_sum(jnp.where(in_line & (apart_by >= 2), table, 0.0)), axis=1, keepdims=True)
        band = jnp.zeros((1, 128), f32)
        for first, rows_here, block, into in bands():
            aims = band_ref[first : first + rows_here, :]
            taken = jnp.take_along_axis(band_acc[head, into : into + rows_here, :], aims & 127, axis=1)
            right = (aims >> 7) == block
            if into == span:
                right = right & (seq > 0)
            band = band + column_sum(jnp.where(right, taken, 0.0))
        lane_one = lax.broadcasted_iota(jnp.int32, (1, 128), 1)
        table_out[head, 0:1, 512:640] = (
            band + jnp.where(lane_one == 0, low_tail, 0.0) + jnp.where(lane_one == 63, high_tail, 0.0)
        )
        table_out[head, 0:1, 640:768] = jnp.zeros((1, 128), f32)
        return carry

    lax.fori_loop(0, heads, head_tables, 0)
    for head in range(heads):
        at_row = 8 + head
        sums[1, at_row : at_row + 1, :] = table_out[head, 0:1, :]

    for page in range(count):
        far_copy(page).wait_recv()
        own_rows = slice(page * row_count, (page + 1) * row_count)
        for kind, target in enumerate((key_back, value_back)):
            target[own_rows, :] = (
                (outgoing[page, 0, kind].astype(f32) + from_sib[page, 0, kind].astype(f32))
                + from_far[page, kind].astype(f32)
            ).astype(bf16)
    weight_columns(1, key_back)
    weight_columns(2, value_back)
    late_sum.start()
    for name in ((0, 2), (1, 0)):
        early.take(*name)
    project_back(key_back, 1)
    project_back(value_back, 2)
    sums[0, 11:12, :] = column_sum(value_back[...].astype(f32))
    for page in range(count):
        first = page * row_count
        text_rim[page, 16 : 16 + span, :] = total_back[first : first + span, :].astype(bf16)
        patch_rim[page, 16 : 16 + patch_span, :] = total_back[first + span : first + row_count, :].astype(bf16)
    after, before = (page_at, (seq + 1) % 4), (page_at, (seq + 3) % 4)
    rim_copies = [
        remote(
            source.at[:, start : start + 16], source.at[:, stop : stop + 16], rim_send.at[index], rim_recv.at[index],
            *peer,
        )
        for index, (source, start, stop, peer) in enumerate(
            (
                (text_rim, span, 0, after), (text_rim, 16, 16 + span, before),
                (patch_rim, 16, 0, after), (patch_rim, 16, 32, before),
            )
        )
    ]
    for copy in rim_copies:
        copy.start()
    for chunk in range(4):
        late_sum.take("core", chunk)
    for name in ((0, 3), (1, 1)):
        early.take(*name)
    for copy in rim_copies:
        copy.wait()
    sums[1, 0:8, :] = jnp.zeros((8, width), f32)
    sums[1, 20:24, :] = jnp.zeros((4, width), f32)
    sums[0, 16:24, :] = jnp.zeros((8, width), f32)

    def position_tile(tile, carry):
        at = pl.ds(pl.multiple_of(tile * 256, 256), 256)
        text_taps = [jnp.zeros((1, 256), f32) for _ in range(7)]
        patch_taps = [jnp.zeros((1, 256), f32) for _ in range(9)]
        for page in range(count):
            first = page * row_count
            window = text_rim[page, :, at].astype(f32)
            window_row = lax.broadcasted_iota(jnp.int32, (span + 32, 1), 0)
            inside = ((window_row >= 16) | (seq > 0)) & ((window_row < 16 + span) | (seq < 3))
            window = jnp.where(inside, window, 0.0)
            live = seq * span + lax.broadcasted_iota(jnp.int32, (span, 1), 0) < length_ref[page]
            masked = jnp.where(live, tokens_ref[page, :, at].astype(f32), 0.0)
            total = jnp.zeros((span, 256), f32)
            for distance in range(-3, 4):
                shifted = window[16 - distance : 16 - distance + span]
                if distance == 0:
                    weight = taps_ref[1:2, at] + taps_ref[4:5, at] + taps_ref[7:8, at]
                else:
                    tap = 3 * (abs(distance) - 1) + (2 if distance > 0 else 0)
                    weight = taps_ref[tap : tap + 1, at]
                total = total + shifted * weight
                text_taps[distance + 3] = text_taps[distance + 3] + column_sum(shifted * masked)
            tokens_back_ref[page, :, at] = total_back[first : first + span, at] + jnp.where(live, total, 0.0)
            window = patch_rim[page, :, at].astype(f32)
            window_row = lax.broadcasted_iota(jnp.int32, (48, 1), 0)
            inside = ((window_row >= 16) | (seq > 0)) & ((window_row < 32) | (seq < 3))
            window = jnp.where(inside, window, 0.0)
            cell = seq * patch_span + lax.broadcasted_iota(jnp.int32, (patch_span, 1), 0)
            live = ((cell >> 3) < GRID_SIDE - 1) & ((cell & 7) < GRID_SIDE - 1)
            masked = jnp.where(live, patches_ref[page, :, at].astype(f32), 0.0)
            total = jnp.zeros((patch_span, 256), f32)
            for tap in range(9):
                distance = GRID_SIDE * (tap // 3 - 1) + tap % 3 - 1
                shifted = window[16 - distance : 32 - distance]
                total = total + shifted * taps_ref[9 + tap : 10 + tap, at]
                patch_taps[tap] = patch_taps[tap] + column_sum(shifted * masked)
            patches_back_ref[page, :, at] = total_back[first + span : first + row_count, at] + jnp.where(
                live, total, 0.0
            )
        for index, value in enumerate(text_taps):
            sums[0, 16 + index : 17 + index, at] = value
        for index, value in enumerate(patch_taps):
            if index == 0:
                sums[0, 23:24, at] = value
            else:
                sums[1, index - 1 : index, at] = value
        return carry

    lax.fori_loop(0, width // 256, position_tile, 0)

    sum_partners = [opposite] + on_page
    sum_copies = [remote(sums.at[1 - core], sums_in.at[0], sum_send.at[0], sum_recv.at[0], *sibling)] + [
        remote(sums.at[core], sums_in.at[1 + index], sum_send.at[1 + index], sum_recv.at[1 + index], *partner)
        for index, partner in enumerate(sum_partners)
    ]
    last = remote(
        sums.at[core], sums_in.at[2 + levels], sum_send.at[2 + levels], sum_recv.at[2 + levels], *sibling
    )
    sum_copies[0].start()

    def sum_step(index):
        sum_copies[index].wait()
        sums[core] = sums[core] + sums_in[index]
        (sum_copies + [last])[index + 1].start()

    late_sum.take(0, 0)
    sum_step(0)
    late_sum.take(0, 1)
    early.take(2, 0)
    sum_step(1)
    late_sum.take(1, 0)
    sum_step(2)
    for step in range(2, levels + 1):
        late_sum.take(step, 0)
        sum_step(step + 1)
    for step in range(3, levels + 1):
        early.take(step, 0)
    last.wait()
    sums_ref[core] = sums[core]
    sums_ref[1 - core] = sums_in[2 + levels]
    wide_rows = 4 * rows
    block = keep[0].astype(f32)
    low, high = block[:, 0 : lanes // 2], pltpu.roll(block, lanes // 2, 1)[:, 0 : lanes // 2]
    down_out[...] = low[0:wide_rows].astype(bf16)
    mixed_out[0:half, :] = jnp.where(core == 0, high[wide_rows:], low[wide_rows:]).astype(bf16)
    block = late[0, 0].astype(f32)
    low, high = block[:, 0 : lanes // 2], pltpu.roll(block, lanes // 2, 1)[:, 0 : lanes // 2]
    mixed_out[half:, :] = jnp.where(core == 0, high, low).astype(bf16)
    swaps = [
        remote(source, target, swap_send.at[index], swap_recv.at[index], *sibling)
        for index, (source, target) in enumerate(
            ((keep.at[0, 2 * rows : 4 * rows], up_in), (down_out, down_in), (mixed_out, mixed_in))
        )
    ]
    for copy in swaps:
        copy.start()
    early_ref[...] = keep[0]
    late_ref[...] = late[0, 0]
    for copy in swaps:
        copy.wait()
    up_in_ref[...] = up_in[...]
    down_in_ref[...] = down_in[...]
    mixed_in_ref[...] = mixed_in[...]
    early.finish()
    late_sum.finish()
    for page in range(count):
        sib_copy(page).wait_send()
        far_copy(page).wait_send()


def backward(pages, lengths, local_values, far_values, tokens, patches):
    count, span, width = tokens.shape
    patch_span = patches.shape[1]
    row_count = span + patch_span
    total_rows = count * row_count
    bundle, weights, keys = far_values[0], far_values[1], far_values[2]
    pairs, key_pad = weights.shape[1], keys.shape[1]
    blocks, early_rows, lanes = bundle.shape[1:]
    late_rows = 3 * width // (2 * pages)
    levels = pages.bit_length() - 1
    bf16, f32, i32 = jnp.bfloat16, jnp.float32, jnp.int32
    dma = pltpu.SemaphoreType.DMA

    def landings(rows):
        return [VMEM((blocks >> (step + 1), rows, lanes), bf16) for step in range(levels + 1)]

    early_count = 8 + 4 + 2 + (levels - 1)
    late_count = 4 + 2 + levels
    return pl.pallas_call(
        staged(functools.partial(backward_kernel, pages), 1, len(local_values)),
        out_shape=(
            jax.ShapeDtypeStruct(tokens.shape, f32),
            jax.ShapeDtypeStruct(patches.shape, f32),
            jax.ShapeDtypeStruct((early_rows, lanes), bf16),
            jax.ShapeDtypeStruct((late_rows, lanes), bf16),
            jax.ShapeDtypeStruct((2, 24, width), f32),
            jax.ShapeDtypeStruct((early_rows // 9 * 4, lanes), bf16),
            jax.ShapeDtypeStruct((early_rows // 9 * 8, lanes // 2), bf16),
            jax.ShapeDtypeStruct((early_rows // 9 + late_rows, lanes // 2), bf16),
        ),
        in_specs=[pl.BlockSpec(memory_space=pltpu.SMEM)]
        + anywhere(len(local_values) + len(far_values)),
        out_specs=tuple(in_vmem(8)),
        scratch_shapes=[
            VMEM((blocks, early_rows, lanes), bf16),
            VMEM((blocks, early_rows, lanes), bf16),
            landings(early_rows),
            VMEM((2, blocks, late_rows, lanes), bf16),
            VMEM((blocks, late_rows, lanes), bf16),
            landings(late_rows),
            VMEM((2, pairs, 2 * row_count, key_pad), bf16),
            VMEM((2, key_pad, width), bf16),
            VMEM((2, key_pad, width), bf16),
            VMEM((count, 4, 2, row_count, width), bf16),
            VMEM((count, 2, 2, row_count, width), bf16),
            VMEM((count, 2, row_count, width), bf16),
            VMEM((3, width, width), bf16),
            VMEM((total_rows, width), bf16),
            VMEM((width, total_rows), bf16),
            VMEM((total_rows, width), f32),
            VMEM((total_rows, width), bf16),
            VMEM((total_rows, width), bf16),
            VMEM((total_rows, width), bf16),
            VMEM((2 * row_count, key_pad), f32),
            VMEM((2 * row_count, 3 * key_pad), bf16),
            VMEM((row_count, 2 * key_pad), bf16),
            VMEM((256, 3 * key_pad), bf16),
            VMEM((192, row_count), bf16),
            VMEM((row_count, 128), i32),
            VMEM((2 * pairs, 192, 128), f32),
            VMEM((2 * pairs, span + 64 + 2 * patch_span, 128), f32),
            VMEM((2 * pairs, 8, width), f32),
            VMEM((count, span + 32, width), bf16),
            VMEM((count, patch_span + 32, width), bf16),
            VMEM((2, 24, width), f32),
            VMEM((3 + levels, 24, width), f32),
            VMEM((early_rows // 9 * 4, lanes), bf16),
            VMEM((early_rows // 9 * 8, lanes // 2), bf16),
            VMEM((early_rows // 9 * 8, lanes // 2), bf16),
            VMEM((early_rows // 9 + late_rows, lanes // 2), bf16),
            VMEM((early_rows // 9 + late_rows, lanes // 2), bf16),
            dma((6,)), dma((3, 2)),
            dma((early_count,)), dma((early_count,)), dma((late_count,)), dma((late_count,)),
            dma((count,)), dma((count,)), dma((count,)), dma((count,)),
            dma((4,)), dma((4,)), dma((3 + levels,)), dma((3 + levels,)), dma((3,)), dma((3,)),
        ]
        + stage_for(local_values),
        compiler_params=pltpu.CompilerParams(
            collective_id=1, has_side_effects=True, vmem_limit_bytes=KERNEL_VMEM
        ),
        cost_estimate=pl.CostEstimate(flops=12_000_000_000, bytes_accessed=40_000_000, transcendentals=0),
        name="backward",
    )(lengths, *local_values, *far_values)


def clip_lanes(sums, centre, bins):
    first, last = centre + 1 - bins // 2, centre - 1 + bins // 2
    lane = lax.broadcasted_iota(jnp.int32, sums.shape, 1)
    below = jnp.sum(jnp.where(lane < first, sums, 0.0), axis=1, keepdims=True)
    above = jnp.sum(jnp.where(lane >= last, sums, 0.0), axis=1, keepdims=True)
    moved = pltpu.roll(sums, sums.shape[1] - (first - 1), 1)
    moved = jnp.where(lane == 0, below, jnp.where(lane == bins - 1, above, moved))
    return moved[:, :bins]


def finish_kernel(
    staging, early_ref, late_ref, sums_ref, up_in_ref, down_in_ref, mixed_in_ref,
    query_ref, key_ref, value_ref, out_ref, up_ref, down_ref, taps_ref, patch_taps_ref, line_ref, across_ref,
    upward_ref, vector_ref,
):
    f32 = jnp.float32
    rows, columns = query_ref.shape
    half = rows // 2
    wide_rows = 4 * rows
    first = position()[1] == 0
    for copy in staging:
        copy.wait()
    heads = line_ref.shape[0]
    block = early_ref[...].astype(f32)
    low, high = block[:, 0:columns], pltpu.roll(block, columns, 1)[:, 0:columns]
    up = jnp.where(first, block[0 : 2 * rows], up_in_ref[...].astype(f32))
    up_ref[:, 0 : 2 * columns] = up[0:rows]
    up_ref[:, 2 * columns : 4 * columns] = up[rows : 2 * rows]
    down_ref[...] = jnp.where(first, down_in_ref[...].astype(f32), high[0:wide_rows])
    kept = jnp.where(first, low[wide_rows:], high[wide_rows:])
    got = mixed_in_ref[0:half, :].astype(f32)
    out_ref[0:half, :] = jnp.where(first, kept, got)
    out_ref[half:rows, :] = jnp.where(first, got, kept)
    block = late_ref[...].astype(f32)
    low, high = block[:, 0:columns], pltpu.roll(block, columns, 1)[:, 0:columns]
    kept = jnp.where(first, low, high)
    got = mixed_in_ref[half:, :].astype(f32)
    query_ref[...] = jnp.where(first, kept[0:rows], got[0:rows])
    key_ref[...] = jnp.where(first, got[0:rows], kept[0:rows])
    value_ref[0:half, :] = jnp.where(first, kept[rows:], got[rows:])
    value_ref[half:rows, :] = jnp.where(first, got[rows:], kept[rows:])
    front, back = sums_ref[0], sums_ref[1]
    width = front.shape[1]
    text = [front[16 + index : 17 + index] for index in range(7)]
    order = [text[2], text[3], text[4], text[1], text[3], text[5], text[0], text[3], text[6]]
    taps_ref[...] = jnp.concatenate(order, axis=0)
    patch_taps_ref[...] = jnp.concatenate([front[23:24], back[0:8]], axis=0)
    across_ref[...] = clip_lanes(back[8:24, 0:256], 72, across_ref.shape[1])[0:heads]
    upward_ref[...] = clip_lanes(back[8:24, 256:512], 72, upward_ref.shape[1])[0:heads]
    line_ref[...] = clip_lanes(back[8:24, 512:640], 32, line_ref.shape[1])[0:heads]
    vector_ref[...] = front[0:16]


def finish(values, width, heads, line_bins, plane_bins):
    rows, columns = values[1].shape[0] * 2 // 3, values[1].shape[1] // 2
    f32 = jnp.float32
    square = jax.ShapeDtypeStruct((rows, columns), f32)
    taps = jax.ShapeDtypeStruct((9, width), f32)
    plane = jax.ShapeDtypeStruct((heads, plane_bins), f32)
    return pl.pallas_call(
        staged(finish_kernel, 0, len(values)),
        out_shape=(
            square, square, square, square,
            jax.ShapeDtypeStruct((rows, 4 * columns), f32),
            jax.ShapeDtypeStruct((4 * rows, columns), f32),
            taps, taps,
            jax.ShapeDtypeStruct((heads, line_bins), f32), plane, plane,
            jax.ShapeDtypeStruct((16, width), f32),
        ),
        in_specs=anywhere(len(values)),
        out_specs=tuple(in_vmem(12)),
        scratch_shapes=stage_for(values),
        compiler_params=pltpu.CompilerParams(vmem_limit_bytes=KERNEL_VMEM),
        name="finish",
    )(*values)


def exchange(value, pages, step):
    moves = []
    for page in range(pages):
        for seq in range(4):
            on_page, on_seq = page, seq
            if (seq % 2 == step) if step < 2 else False:
                on_seq = seq ^ 2
            else:
                on_page = page ^ (1 if step < 2 else 1 << (step - 1))
            moves.append((page * 4 + seq, on_page * 4 + on_seq))
    return lax.ppermute(value, ("page", "seq"), moves)


def added(kept, got):
    return (kept.astype(jnp.float32) + got.astype(jnp.float32)).astype(jnp.bfloat16)


def bundle_sum(state, pages):
    for step in range(pages.bit_length()):
        half = state.shape[0] // 2
        state = added(state[:half], exchange(state[half:], pages, step))
    return state[0]


def bundle_parts(state, wide_rows, core):
    lanes = state.shape[1] // 2
    first = core == 0
    tail = state[wide_rows:]
    if wide_rows > 2 * tail.shape[0]:
        group = state[:wide_rows].reshape(4, wide_rows // 4, 2 * lanes)
        low = group[:2].transpose(1, 0, 2).reshape(-1, lanes)
        high = group[2:].transpose(1, 0, 2).reshape(-1, lanes)
    else:
        low, high = state[:wide_rows, :lanes], state[:wide_rows, lanes:]
    left, right = state[:wide_rows, :lanes], state[:wide_rows, lanes:]
    sent = jnp.concatenate(
        [jnp.where(first, high, left), jnp.where(first, tail[:, lanes:], tail[:, :lanes])], axis=0
    )
    got = swap(sent, "seq", 1)
    kept_tail = jnp.where(first, tail[:, :lanes], tail[:, lanes:])
    one = jnp.where(first, low, got[:wide_rows])
    two = jnp.where(first, got[:wide_rows], right)
    three = jnp.concatenate(
        [jnp.where(first, kept_tail, got[wide_rows:]), jnp.where(first, got[wide_rows:], kept_tail)], axis=0
    )
    return [value.astype(jnp.float32) for value in (one, two, three)]


def clipped(sums, centre, bins):
    first, last = centre + 1 - bins // 2, centre - 1 + bins // 2
    return jnp.concatenate(
        [
            jnp.sum(sums[..., :first], axis=-1, keepdims=True),
            sums[..., first:last],
            jnp.sum(sums[..., last:], axis=-1, keepdims=True),
        ],
        axis=-1,
    )


def grid_live(cells):
    return (cells // GRID_SIDE < GRID_SIDE - 1) & (cells % GRID_SIDE < GRID_SIDE - 1)


def grid_boxes(cells):
    return jnp.stack(
        [
            patch_pitch * (cells % GRID_SIDE) + patch_centre,
            patch_pitch * (cells // GRID_SIDE) + patch_centre,
        ]
    )


def shards(
    tokens,
    patches,
    page_length,
    box_position,
    query_weight,
    key_weight,
    value_weight,
    out_weight,
    up_weight,
    down_weight,
    conv_weight,
    patch_conv_weight,
    query_bias,
    value_bias,
    out_bias,
    up_bias,
    down_bias,
    attention_gain,
    attention_shift,
    feedforward_gain,
    feedforward_shift,
    reading_bias_table,
    horizontal_bias_table,
    vertical_bias_table,
    cotangent,
    patch_cotangent,
):
    conv_taps = conv_weight.astype(jnp.float32)
    patch_taps = patch_conv_weight.astype(jnp.float32)
    query_offset = query_bias.astype(jnp.float32)
    value_offset = value_bias.astype(jnp.float32)
    out_offset = out_bias.astype(jnp.float32)
    up_offset = up_bias.astype(jnp.float32)
    down_offset = down_bias.astype(jnp.float32)
    first_gain = attention_gain.astype(jnp.float32)
    first_shift = attention_shift.astype(jnp.float32)
    second_gain = feedforward_gain.astype(jnp.float32)
    second_shift = feedforward_shift.astype(jnp.float32)
    page_count, span_size, model_width = tokens.shape
    patch_span = patches.shape[1]
    seq_count = lax.axis_size("seq")
    slot_size = span_size * seq_count
    patch_slots = patch_span * seq_count
    row_count = span_size + patch_span
    key_count = row_count * seq_count
    head_count = reading_bias_table.shape[0]
    head_size = model_width // head_count
    line_bins = reading_bias_table.shape[1]
    plane_bins = horizontal_bias_table.shape[1]
    score_scale = head_size ** (-0.5)
    seq_index = lax.axis_index("seq")
    text_places = seq_index * span_size + jnp.arange(span_size, dtype=jnp.int32)
    local_cells = seq_index * patch_span + jnp.arange(patch_span, dtype=jnp.int32)
    text_live = text_places[None, :] < page_length[:, None]
    patch_live = grid_live(local_cells)
    text_factor = text_live[:, :, None]
    patch_factor = patch_live[None, :, None]
    masked = tokens * text_factor.astype(jnp.bfloat16)
    rimmed = with_halo(masked, (("seq", 1),), 3)
    reach = GRID_SIDE + 1
    patch_masked = patches * patch_factor.astype(jnp.bfloat16)
    patch_rimmed = with_halo(patch_masked, (("seq", 1),), reach)
    pages = lax.axis_size("page")
    table = jnp.concatenate(
        [
            horizontal_bias_table,
            vertical_bias_table,
            reading_bias_table,
            jnp.zeros((head_count, 256 - 2 * plane_bins - line_bins), jnp.bfloat16),
        ],
        axis=1,
    ).astype(jnp.float32)
    taps = jnp.pad(
        jnp.concatenate([conv_weight, patch_conv_weight], axis=1).astype(jnp.float32).T, ((0, 6), (0, 0))
    )
    vector_row = jnp.arange(8 + up_bias.shape[0] // model_width, dtype=jnp.int32)[:, None]
    vectors = jnp.pad(up_bias.reshape(-1, model_width), ((8, 0), (0, 0)))
    for index, vector in enumerate(
        (
            query_bias, value_bias, out_bias, down_bias, attention_gain, attention_shift, feedforward_gain,
            feedforward_shift,
        )
    ):
        vectors = jnp.where(vector_row == index, vector[None, :], vectors)
    vectors = vectors.astype(jnp.float32)
    (
        hidden, hidden_low, queries, mixture_low, columns, key_rows, query_rows, keys, values, weights,
    ) = forward(
        pages, page_length, tokens, patches, box_position, taps, (query_weight, key_weight, value_weight),
        vectors, table,
    )
    places = jnp.stack(
        [seq_index, seq_index % 2, lax.axis_index("page"), seq_index // 2]
    ).astype(jnp.int32)
    def flat(value):
        return value.reshape(-1, value.shape[-1])

    output, patch_output, delta_first, delta_mixture, middle_sums, feedforward_bundle = middle(
        places, hidden, mixture_low, cotangent, patch_cotangent,
        (out_weight, up_weight, down_weight), vectors, pages,
    )
    if in_tiles(model_width, pages):
        tokens_gradient, patches_gradient, early_state, late_state, sums, up_in, down_in, mixed_in = backward(
            pages,
            page_length,
            (
                queries, delta_mixture, columns, key_rows, query_rows, tokens, patches, taps, middle_sums,
            ),
            (
                feedforward_bundle, weights, keys, values, hidden_low, delta_first, query_weight, key_weight,
                value_weight,
            ),
            tokens,
            patches,
        )
        (
            query_part, key_part, value_part, out_part, up_part, down_part, text_part, patch_part, line_part,
            across_part, upward_part, vector_rows,
        ) = finish(
            (early_state, late_state, sums, up_in, down_in, mixed_in), model_width, head_count, line_bins,
            plane_bins,
        )
        return (
            output,
            patch_output,
            tokens_gradient,
            patches_gradient,
            query_part,
            key_part,
            value_part,
            out_part,
            up_part,
            down_part,
            text_part.T,
            patch_part.T,
            vector_rows[10],
            vector_rows[11],
            vector_rows[OUT_BIAS],
            vector_rows[UP_BIAS : UP_BIAS + 4].reshape(-1),
            vector_rows[DOWN_BIAS],
            vector_rows[FIRST_GAIN],
            vector_rows[FIRST_SHIFT],
            vector_rows[SECOND_GAIN],
            vector_rows[SECOND_SHIFT],
            line_part,
            across_part,
            upward_part,
        )
    delta_first = delta_first.reshape(page_count, row_count, model_width)
    delta_mixture = delta_mixture.reshape(page_count, row_count, model_width)
    early_state = added(feedforward_bundle[0], swap(feedforward_bundle[1], "seq", 1))
    delta_mixture, early_state = lax.optimization_barrier((delta_mixture, early_state))
    delta_query_pages, delta_key_pages, delta_value_pages = [], [], []
    delta_plane, delta_line = 0.0, 0.0
    for page in range(page_count):
        delta_page_queries, delta_blocks, plane_part, line_part = backward_page(
            places,
            columns[page][:, ::128],
            key_rows[page],
            query_rows[page][:, :row_count],
            queries[page * row_count : (page + 1) * row_count],
            keys[page],
            values[page],
            delta_mixture[page],
            weights[page],
        )
        got = swap(delta_blocks[2:], "seq", 1)
        chip_sum = delta_blocks[:2].astype(jnp.float32) + got.astype(jnp.float32)
        got = swap(chip_sum[1].astype(jnp.bfloat16), "seq", 2)
        whole = (chip_sum[0] + got.astype(jnp.float32)).astype(jnp.bfloat16)
        delta_query_pages.append(delta_page_queries)
        delta_key_pages.append(whole[0])
        delta_value_pages.append(whole[1])
        delta_plane = delta_plane + plane_part
        delta_line = delta_line + line_part
    delta_queries = jnp.stack(delta_query_pages)
    delta_keys = jnp.stack(delta_key_pages)
    delta_values = jnp.stack(delta_value_pages)
    delta_plane = clipped(delta_plane, 72, plane_bins)
    delta_line = clipped(delta_line, 32, line_bins)
    delta_across, delta_upward = delta_plane[0], delta_plane[1]
    delta_query_offset = row_sum(delta_queries)
    delta_value_offset = row_sum(delta_values)
    delta_hidden = (
        delta_first
        + back_dot(delta_queries, query_weight)
        + back_dot(delta_keys, key_weight)
        + back_dot(delta_values, value_weight)
    )
    delta_position = delta_hidden[:, :span_size].astype(jnp.bfloat16)
    delta_rim = with_halo(delta_position, (("seq", 1),), 3)
    delta_masked = jnp.zeros((page_count, span_size, model_width), jnp.float32)
    tap_columns = []
    for dilation in (1, 2, 3):
        for offset in (-1, 0, 1):
            column = 3 * (dilation - 1) + offset + 1
            anchor = 3 + offset * dilation
            anchor_back = 3 - offset * dilation
            delta_masked = (
                delta_masked
                + delta_rim[:, anchor_back : anchor_back + span_size, :] * conv_taps[:, column]
            )
            tap_columns.append(
                jnp.einsum(
                    "ptd,ptd->d",
                    delta_position,
                    rimmed[:, anchor : anchor + span_size, :],
                    preferred_element_type=jnp.float32,
                )
            )
    delta_taps = jnp.stack(tap_columns, axis=1)
    tokens_gradient = delta_hidden[:, :span_size] + delta_masked * text_factor.astype(jnp.float32)
    delta_patch_position = delta_hidden[:, span_size:].astype(jnp.bfloat16)
    delta_patch_rim = with_halo(delta_patch_position, (("seq", 1),), reach)
    delta_patch_masked = jnp.zeros((page_count, patch_span, model_width), jnp.float32)
    patch_columns = []
    for vertical in (-1, 0, 1):
        for horizontal in (-1, 0, 1):
            column = 3 * (vertical + 1) + horizontal + 1
            anchor = reach + vertical * GRID_SIDE + horizontal
            anchor_back = reach - vertical * GRID_SIDE - horizontal
            delta_patch_masked = (
                delta_patch_masked
                + delta_patch_rim[:, anchor_back : anchor_back + patch_span, :]
                * patch_taps[:, column]
            )
            patch_columns.append(
                jnp.einsum(
                    "ptd,ptd->d",
                    delta_patch_position,
                    patch_rimmed[:, anchor : anchor + patch_span, :],
                    preferred_element_type=jnp.float32,
                )
            )
    delta_patch_taps = jnp.stack(patch_columns, axis=1)
    patches_gradient = delta_hidden[:, span_size:] + delta_patch_masked * patch_factor.astype(
        jnp.float32
    )
    operands = [flat(value) for value in (hidden_low, delta_queries, delta_keys, delta_values)]
    tail_bundle = indexed_bundle(
        (
            ((operands[0], operands[1], None), (operands[0], operands[3], 0)),
            ((operands[0], operands[2], None), (operands[0], operands[3], 1)),
        ),
        places,
        pages,
    )
    tail_state = added(tail_bundle[0], swap(tail_bundle[1], "seq", 1))
    query_part, key_part, value_part = bundle_parts(
        bundle_sum(tail_state, pages), model_width // pages, places[1]
    )
    up_part, down_part, out_part = bundle_parts(
        bundle_sum(early_state, pages), up_weight.shape[1] // pages, places[1]
    )
    up_part = up_part.reshape(model_width // pages, -1)
    matrix_parts = (query_part, key_part, value_part, out_part, up_part, down_part)
    vector_parts = total_sum(
        (
            delta_taps,
            delta_patch_taps,
            delta_query_offset,
            delta_value_offset,
            middle_sums[OUT_BIAS],
            middle_sums[UP_BIAS : UP_BIAS + 4].reshape(-1),
            middle_sums[DOWN_BIAS],
            middle_sums[FIRST_GAIN],
            middle_sums[FIRST_SHIFT],
            middle_sums[SECOND_GAIN],
            middle_sums[SECOND_SHIFT],
            delta_line,
            delta_across,
            delta_upward,
        )
    )
    return (
        output,
        patch_output,
        tokens_gradient,
        patches_gradient,
        matrix_parts[0],
        matrix_parts[1],
        matrix_parts[2],
        matrix_parts[3],
        matrix_parts[4],
        matrix_parts[5],
        vector_parts[0],
        vector_parts[1],
        vector_parts[2],
        vector_parts[3],
        vector_parts[4],
        vector_parts[5],
        vector_parts[6],
        vector_parts[7],
        vector_parts[8],
        vector_parts[9],
        vector_parts[10],
        vector_parts[11],
        vector_parts[12],
        vector_parts[13],
    )


def solution(mesh):
    in_specs = (
        P("page", "seq", None),
        P("page", "seq", None),
        P("page"),
        P(None, "page", None),
        P(),
        P(),
        P(),
        P(),
        P(),
        P(),
        P(),
        P(),
        P(),
        P(),
        P(),
        P(),
        P(),
        P(),
        P(),
        P(),
        P(),
        P(),
        P(),
        P(),
        P("page", "seq", None),
        P("page", "seq", None),
    )
    out_specs = (
        P("page", "seq", None),
        P("page", "seq", None),
        P("page", "seq", None),
        P("page", "seq", None),
        P("page", "seq"),
        P("page", "seq"),
        P("page", "seq"),
        P("page", "seq"),
        P("page", "seq"),
        P("page", "seq"),
        P(),
        P(),
        P(),
        P(),
        P(),
        P(),
        P(),
        P(),
        P(),
        P(),
        P(),
        P(),
        P(),
        P(),
    )
    return jax.shard_map(shards, mesh=mesh, in_specs=in_specs, out_specs=out_specs, check_vma=False)
```

```python
import functools

import jax
import jax.numpy as jnp
from jax import lax
from jax.experimental import pallas as pl
from jax.experimental.pallas import tpu as pltpu
from jax.sharding import PartitionSpec as P

GRID_SIDE = 8


epsilon = 1e-05
coordinate_step = 16
masked_score = -1000000000.0
patch_pitch = 146
patch_centre = 73


def with_halo(cells, sides, width):
    for axis, dim in sides:
        count = lax.axis_size(axis)
        ends = count - 1
        head = lax.slice_in_dim(cells, 0, width, axis=dim)
        tail = lax.slice_in_dim(cells, cells.shape[dim] - width, cells.shape[dim], axis=dim)
        cells = jnp.concatenate(
            [
                lax.ppermute(tail, axis, [(i, (i + 1) % count) for i in range(ends)]),
                cells,
                lax.ppermute(head, axis, [((i + 1) % count, i) for i in range(ends)]),
            ],
            axis=dim,
        )
    return cells


def layer_norm(values, gain_vector, shift_vector):
    row_mean = jnp.mean(values, axis=-1, keepdims=True)
    centred = values - row_mean
    variance = jnp.mean(centred * centred, axis=-1, keepdims=True)
    return centred * lax.rsqrt(variance + epsilon) * gain_vector + shift_vector


def gelu_exact(values):
    return jax.nn.gelu(values, approximate=False)


def flat_dot(operand, matrix):
    front = operand.shape[:-1]
    result = jnp.dot(
        operand.reshape(-1, operand.shape[-1]), matrix, preferred_element_type=jnp.float32
    )
    return result.reshape(front + (matrix.shape[-1],))


def back_dot(operand, matrix):
    front = operand.shape[:-1]
    result = lax.dot_general(
        operand.reshape(-1, operand.shape[-1]),
        matrix,
        (((1,), (1,)), ((), ())),
        preferred_element_type=jnp.float32,
    )
    return result.reshape(front + (matrix.shape[0],))


def outer_dot(operand, gradient):
    return lax.dot_general(
        operand.reshape(-1, operand.shape[-1]),
        gradient.reshape(-1, gradient.shape[-1]),
        (((0,), (0,)), ((), ())),
        preferred_element_type=jnp.float32,
    )


def row_sum(gradient):
    return jnp.sum(gradient.astype(jnp.float32).reshape(-1, gradient.shape[-1]), axis=0)


def swap(value, axis, bit):
    count = lax.axis_size(axis)
    return lax.ppermute(value, axis, [(i, i ^ bit) for i in range(count)])


def total_sum(vectors):
    flat = jnp.concatenate([vector.reshape(-1) for vector in vectors])
    flat = jnp.pad(flat, (0, -flat.size % 1024)).reshape(-1, 128)
    for bit in (1, 2):
        flat = flat + swap(flat, "seq", bit)
    bit = 1
    while bit < lax.axis_size("page"):
        flat = flat + swap(flat, "page", bit)
        bit *= 2
    flat = flat.reshape(-1)
    result, start = [], 0
    for vector in vectors:
        result.append(flat[start : start + vector.size].reshape(vector.shape))
        start += vector.size
    return result


def query_places(seq_index, shape, span, patch_span, text_slots):
    row = lax.broadcasted_iota(jnp.int32, shape, 0)
    return jnp.where(
        row < span, seq_index * span + row, text_slots + seq_index * patch_span + row - span
    )


FIXED = 2048.0


def lookup(table_row, lanes):
    return jnp.take_along_axis(jnp.broadcast_to(table_row, lanes.shape), lanes, axis=1)


HEAD_LANES = 64


def split_heads(group):
    lane = lax.broadcasted_iota(jnp.int32, group.shape, 1) // HEAD_LANES
    zero = jnp.zeros_like(group)
    return jnp.concatenate(
        [jnp.where(lane == head, group, zero) for head in range(group.shape[1] // HEAD_LANES)], axis=0
    )


def merge_heads(rows):
    heads = rows.shape[1] // HEAD_LANES
    count = rows.shape[0] // heads
    lane = lax.broadcasted_iota(jnp.int32, (count, rows.shape[1]), 1) // HEAD_LANES
    merged = rows[:count]
    for head in range(1, heads):
        merged = jnp.where(lane == head, rows[head * count : (head + 1) * count], merged)
    return merged


def dot_nt(left, right):
    return lax.dot_general(left, right, (((1,), (1,)), ((), ())), preferred_element_type=jnp.float32)


def dot_nn(left, right):
    return lax.dot_general(left, right, (((1,), (0,)), ((), ())), preferred_element_type=jnp.float32)


def dot_tn(left, right):
    return lax.dot_general(left, right, (((0,), (0,)), ((), ())), preferred_element_type=jnp.float32)


CHUNK = 16


MESH = pl.DeviceIdType.MESH


def places_of(pages):
    page = lax.axis_index("page")
    seq = lax.axis_index("seq")
    bits = []
    rest = page
    for _ in range(pages.bit_length() - 1):
        bits.append(rest % 2)
        rest = rest // 2
    return page, bits, seq, seq // 2, seq % 2


def sibling_of(seq):
    return seq + 1 - 2 * (seq % 2)


def across_of(seq):
    return seq + 2 - 4 * (seq // 2)


def remote(source, target, send, receive, page, seq):
    return pltpu.make_async_remote_copy(
        src_ref=source, dst_ref=target, send_sem=send, recv_sem=receive, device_id=(page, seq), device_id_type=MESH
    )


def column_of(row):
    square = jnp.broadcast_to(row.astype(jnp.float32), (128, 128)).T
    return square[:, 0:1].astype(jnp.int32)


def forward_kernel(
    pages,
    staging, length_ref, box_ref, taps_ref, vector_ref, table_ref, tokens_any, patches_any, query_weight_any, key_weight_any,
    value_weight_any,
    hidden_ref, hidden_low_ref, query_ref, mixture_ref, columns_ref, rows_ref, query_rows_ref, key_any, value_any,
    weights_any,
    own, matrices, key_ref, value_ref, weights_ref, arrived, text, grid, low, scores, across_ref, upward_ref,
    live_ref, line_ref, packed_ref,
    load_sem, store_sem, send_sem, recv_sem,
):
    page_at, _, seq, _, _ = places_of(pages)
    count, span, width = tokens_any.shape
    patch_span = patches_any.shape[1]
    row_count = span + patch_span
    key_pad = key_ref.shape[1]
    text_slots = 4 * span
    rim = 8
    loads = [
        pltpu.make_async_copy(source, target, load_sem.at[index])
        for index, (source, target) in enumerate(
            (
                (tokens_any, own.at[:, 0:span]), (patches_any, own.at[:, span:row_count]),
                (key_weight_any, matrices.at[1]), (value_weight_any, matrices.at[2]), (query_weight_any, matrices.at[0]),
            )
        )
    ]
    for copy in loads:
        copy.start()

    def stores(page):
        return [
            pltpu.make_async_copy(source.at[page], target.at[page], store_sem.at[index, page])
            for index, (source, target) in enumerate(
                ((key_ref, key_any), (value_ref, value_any), (weights_ref, weights_any))
            )
        ]

    groups = weights_ref.shape[1]
    members = weights_ref.shape[2] // row_count
    pairs = groups * members // 2
    peers = (sibling_of(seq), across_of(seq))
    barrier = pltpu.get_barrier_semaphore()
    for peer in peers:
        pl.semaphore_signal(barrier, inc=1, device_id=(page_at, peer), device_id_type=MESH)
    pl.semaphore_wait(barrier, 2)

    def first_copies(page, side):
        return (
            remote(
                tokens_any.at[page], arrived.at[side, page, 0:span], send_sem.at[2 * side, page],
                recv_sem.at[2 * side, page], page_at, peers[side],
            ),
            remote(
                patches_any.at[page], arrived.at[side, page, span:row_count], send_sem.at[2 * side + 1, page],
                recv_sem.at[2 * side + 1, page], page_at, peers[side],
            ),
        )

    def onward_copy(page):
        return remote(
            arrived.at[1, page], arrived.at[2, page], send_sem.at[4, page], recv_sem.at[4, page], page_at, peers[0]
        )

    for page in range(count):
        for side in range(2):
            for copy in first_copies(page, side):
                copy.start()

    for copy in staging:
        copy.wait()
    steps = jnp.floor(table_ref[...].astype(jnp.float32) * FIXED + 0.5).astype(jnp.int32)
    for pair in range(pairs):
        words = (steps[2 * pair : 2 * pair + 1] + 8192) + steps[2 * pair + 1 : 2 * pair + 2] * 65536
        packed_ref[0, pair : pair + 1, :] = words[:, 0:128]
        packed_ref[1, pair : pair + 1, :] = words[:, 128:256]
    key = lax.broadcasted_iota(jnp.int32, (row_count, key_pad), 1)
    place = query_places(seq, (row_count, key_pad), span, patch_span, text_slots)
    across_ref[...] = jnp.clip(key - place, -16, 15) + 16

    def fill(pair, carry):
        row = packed_ref[1, pl.ds(pair, 1), :]
        for at in range(0, key_pad, 128):
            line_ref[pair, :, at : at + 128] = lookup(row, across_ref[:, at : at + 128])
        return carry

    lax.fori_loop(0, pairs, fill, 0)
    text[0:rim, :] = jnp.zeros((rim, width), jnp.float32)
    text[rim + text_slots :, :] = jnp.zeros((rim, width), jnp.float32)
    grid[0:patch_span, :] = jnp.zeros((patch_span, width), jnp.float32)
    grid[patch_span * 5 :, :] = jnp.zeros((patch_span, width), jnp.float32)
    low[row_count * 4 :, :] = jnp.zeros((key_pad - row_count * 4, width), jnp.bfloat16)
    lanes = 256
    group_width = members * HEAD_LANES
    power = 1.4426950408889634 / FIXED
    for copy in first_copies(0, 1):
        copy.wait_recv()
    onward_copy(0).start()
    for copy in loads:
        copy.wait()

    def page_step(page, carry):
        length = length_ref[page]
        base = page * row_count
        cell = lax.broadcasted_iota(jnp.int32, (1, 128), 1)
        query_cell = seq * patch_span + cell
        row_cell = seq * patch_span + lax.broadcasted_iota(jnp.int32, (patch_span, 1), 0)
        for plane in range(2):
            boxes = box_ref[plane]
            of_page = lax.broadcasted_iota(jnp.int32, boxes.shape, 0) == page
            box = jnp.sum(jnp.where(of_page, boxes, 0), axis=0, keepdims=True)
            patch = 146 * ((cell % GRID_SIDE) if plane == 0 else (cell // GRID_SIDE)) + 73
            own_patch = 146 * ((query_cell % GRID_SIDE) if plane == 0 else (query_cell // GRID_SIDE)) + 73
            column_patch = 146 * ((row_cell % GRID_SIDE) if plane == 0 else (row_cell // GRID_SIDE)) + 73
            rows_ref[page, plane : plane + 1, 0:text_slots] = box
            rows_ref[page, plane : plane + 1, text_slots:key_pad] = patch
            own_box = rows_ref[page, plane : plane + 1, pl.ds(pl.multiple_of(seq * span, 128), span)]
            query_rows_ref[page, plane : plane + 1, 0:span] = own_box
            query_rows_ref[page, plane : plane + 1, span:256] = own_patch
            columns_ref[page, 0:span, plane * 128 : (plane + 1) * 128] = jnp.broadcast_to(
                column_of(own_box), (span, 128)
            )
            columns_ref[page, span:row_count, plane * 128 : (plane + 1) * 128] = jnp.broadcast_to(
                column_patch, (patch_span, 128)
            )
        for plane, lanes_ref in enumerate((across_ref, upward_ref)):
            difference = rows_ref[page, plane : plane + 1, :] - columns_ref[page, :, plane * 128 : plane * 128 + 1]
            lanes_ref[...] = jnp.clip(difference >> 4, -32, 31) + (32 + 64 * plane)
        key_at = lax.broadcasted_iota(jnp.int32, live_ref.shape, 1)
        key_cell = key_at - text_slots
        live = (key_at < length) | (
            (key_cell >= 0) & ((key_cell >> 3) < GRID_SIDE - 1) & ((key_cell & 7) < GRID_SIDE - 1)
        )
        live_ref[...] = jnp.where(live, 0.0, masked_score * FIXED)
        for copy in first_copies(page, 0):
            copy.wait_recv()
        onward_copy(page).wait_recv()

        def block_of(step, start, stop, at):
            if step:
                return arrived[step - 1, page, start:stop, at].astype(jnp.float32)
            if start:
                return own[page, span:row_count, at].astype(jnp.float32)
            return own[page, 0:span, at].astype(jnp.float32)

        def slot_of(step):
            return (seq, peers[0], peers[1], sibling_of(peers[1]))[step]

        everything = slice(0, width)
        for step in range(4):
            where = slot_of(step)
            at_place = where * span + lax.broadcasted_iota(jnp.int32, (span, 1), 0)
            text[pl.ds(pl.multiple_of(rim + where * span, 8), span), :] = jnp.where(
                at_place < length, block_of(step, 0, span, everything), 0.0
            )
            at_cell = where * patch_span + lax.broadcasted_iota(jnp.int32, (patch_span, 1), 0)
            cell_live = ((at_cell >> 3) < GRID_SIDE - 1) & ((at_cell & 7) < GRID_SIDE - 1)
            grid[pl.ds(pl.multiple_of(patch_span + where * patch_span, 8), patch_span), :] = jnp.where(
                cell_live, block_of(step, span, row_count, everything), 0.0
            )
        for step in range(4):
            where = slot_of(step)

            def convolve(tile, carry):
                at = pl.ds(pl.multiple_of(tile * lanes, lanes), lanes)
                window = text[pl.ds(pl.multiple_of(where * span, 8), span + 2 * rim), at]
                centre = taps_ref[1:2, at] + taps_ref[4:5, at] + taps_ref[7:8, at]
                total = block_of(step, 0, span, at) + window[rim : rim + span] * centre
                for dilation in (1, 2, 3):
                    for offset in (-1, 1):
                        tap = 3 * (dilation - 1) + offset + 1
                        anchor = rim + offset * dilation
                        total = total + window[anchor : anchor + span] * taps_ref[tap : tap + 1, at]
                low[pl.ds(pl.multiple_of(where * span, 16), span), at] = total.astype(jnp.bfloat16)
                window = grid[pl.ds(pl.multiple_of(where * patch_span, 8), 3 * patch_span), at]
                patch_total = block_of(step, span, row_count, at)
                for vertical in (-1, 0, 1):
                    for horizontal in (-1, 0, 1):
                        tap = 9 + 3 * (vertical + 1) + horizontal + 1
                        anchor = patch_span + vertical * GRID_SIDE + horizontal
                        patch_total = patch_total + window[anchor : anchor + patch_span] * taps_ref[tap : tap + 1, at]
                low[pl.ds(pl.multiple_of(text_slots + where * patch_span, 16), patch_span), at] = (
                    patch_total.astype(jnp.bfloat16)
                )
                if step == 0:
                    for first, rows_here, value in ((0, span, total), (span, patch_span, patch_total)):
                        here = pl.ds(pl.multiple_of(base + first, 16), rows_here)
                        hidden_ref[here, at] = value
                        hidden_low_ref[here, at] = value.astype(jnp.bfloat16)
                return carry

            lax.fori_loop(0, width // lanes, convolve, 0)
        own_rows = pl.ds(pl.multiple_of(base, 16), row_count)

        key_ref[page] = dot_nn(low[...], matrices[1]).astype(jnp.bfloat16)
        value_ref[page] = (dot_nn(low[...], matrices[2]) + vector_ref[1:2, :]).astype(jnp.bfloat16)
        query_ref[own_rows, :] = (
            (dot_nn(hidden_low_ref[own_rows, :], matrices[0]) + vector_ref[0:1, :]).astype(jnp.bfloat16)
            * jnp.bfloat16(0.125)
        )

        @pl.when(page < count - 1)
        def _():
            for copy in first_copies(page + 1, 1):
                copy.wait_recv()
            onward_copy(page + 1).start()

        def attend(group, carry):
            at = pl.ds(pl.multiple_of(group * group_width, group_width), group_width)
            scores[...] = dot_nt(split_heads(query_ref[own_rows, at] * jnp.bfloat16(FIXED)), key_ref[page, :, at])
            for start, sub in ((start, sub) for start in range(0, row_count, CHUNK) for sub in range(members // 2)):
                pair = group * (members // 2) + sub
                plane_row = packed_ref[0, pl.ds(pair, 1), :]
                here = slice(start, start + CHUNK)
                packed = []
                for block_at in range(0, key_pad, 128):
                    lane = slice(block_at, block_at + 128)
                    packed.append(
                        line_ref[pair, here, lane]
                        + lookup(plane_row, across_ref[here, lane])
                        + lookup(plane_row, upward_ref[here, lane])
                    )
                for side in range(2):
                    first = (2 * sub + side) * row_count + start
                    there = slice(first, first + CHUNK)
                    parts, top = [], None
                    for index, word in enumerate(packed):
                        lane = slice(128 * index, 128 * (index + 1))
                        field = (word >> 16) if side else (word & 0xFFFF)
                        part = (scores[there, lane] + field.astype(jnp.float32)) + live_ref[0:1, lane]
                        top = part if top is None else jnp.maximum(top, part)
                        parts.append(part)
                    top = jnp.max(top, axis=1, keepdims=True)
                    parts = [jnp.exp2((part - top) * power) for part in parts]
                    total = parts[0]
                    for part in parts[1:]:
                        total = total + part
                    inverse = 1.0 / jnp.sum(total, axis=1, keepdims=True)
                    for index, part in enumerate(parts):
                        weights_ref[page, group, there, 128 * index : 128 * (index + 1)] = (part * inverse).astype(
                            jnp.bfloat16
                        )
            mixture_ref[own_rows, at] = merge_heads(
                dot_nn(weights_ref[page, group], value_ref[page, :, at])
            ).astype(jnp.bfloat16)
            return carry

        lax.fori_loop(0, groups, attend, 0)
        for copy in stores(page):
            copy.start()
        return carry

    lax.fori_loop(0, count, page_step, 0)
    for page in range(count):
        for side in range(2):
            for copy in first_copies(page, side):
                copy.wait_send()
        onward_copy(page).wait_send()
        for copy in stores(page):
            copy.wait()


VMEM = pltpu.VMEM
KERNEL_VMEM = 62 * 1024 * 1024


def in_vmem(count):
    return [pl.BlockSpec(memory_space=VMEM)] * count


def staged(kernel, first, count):
    def run(*refs):
        *refs, semaphore = refs
        refs, buffers = list(refs[:-count]), refs[-count:]
        copies = [
            pltpu.make_async_copy(refs[first + index], buffers[index], semaphore.at[index]) for index in range(count)
        ]
        for copy in copies:
            copy.start()
        refs[first : first + count] = buffers
        kernel(copies, *refs)

    return run


def stage_for(values):
    return [VMEM(value.shape, value.dtype) for value in values] + [pltpu.SemaphoreType.DMA((len(values),))]


def position():
    seq = lax.axis_index("seq")
    return seq, seq % 2, lax.axis_index("page"), seq // 2


def anywhere(count):
    return [pl.BlockSpec(memory_space=pl.ANY)] * count


def forward(pages, lengths, tokens, patches, box, taps, matrices, vectors, table):
    count, span, width = tokens.shape
    patch_span = patches.shape[1]
    row_count = span + patch_span
    total_rows = count * row_count
    key_pad = -(-4 * row_count // 128) * 128
    pairs = table.shape[0] // 2
    members = 4 if table.shape[0] % 4 == 0 else 2
    groups = table.shape[0] // members
    bf16, f32, i32 = jnp.bfloat16, jnp.float32, jnp.int32
    own = jax.ShapeDtypeStruct((total_rows, width), bf16)
    every = jax.ShapeDtypeStruct((count, key_pad, width), bf16)
    return pl.pallas_call(
        staged(functools.partial(forward_kernel, pages), 1, 4),
        out_shape=(
            jax.ShapeDtypeStruct((total_rows, width), f32), own, own, own,
            jax.ShapeDtypeStruct((count, row_count, 256), i32),
            jax.ShapeDtypeStruct((count, 8, key_pad), i32),
            jax.ShapeDtypeStruct((count, 8, 256), i32),
            every, every,
            jax.ShapeDtypeStruct((count, groups, members * row_count, key_pad), bf16),
        ),
        in_specs=[pl.BlockSpec(memory_space=pltpu.SMEM)] + anywhere(9),
        out_specs=tuple(in_vmem(7) + anywhere(3)),
        scratch_shapes=[
            VMEM((count, row_count, width), bf16),
            VMEM((3, width, width), bf16),
            VMEM((count, key_pad, width), bf16),
            VMEM((count, key_pad, width), bf16),
            VMEM((count, groups, members * row_count, key_pad), bf16),
            VMEM((3, count, row_count, width), bf16),
            VMEM((4 * span + 16, width), f32),
            VMEM((6 * patch_span, width), f32),
            VMEM((key_pad, width), bf16),
            VMEM((members * row_count, key_pad), f32),
            VMEM((row_count, key_pad), i32),
            VMEM((row_count, key_pad), i32),
            VMEM((8, key_pad), f32),
            VMEM((pairs, row_count, key_pad), i32),
            VMEM((2, 8, 128), i32),
            pltpu.SemaphoreType.DMA((5,)),
            pltpu.SemaphoreType.DMA((3, count)),
            pltpu.SemaphoreType.DMA((5, count)),
            pltpu.SemaphoreType.DMA((5, count)),
        ]
        + stage_for((box, taps, vectors, table)),
        compiler_params=pltpu.CompilerParams(
            collective_id=0, has_side_effects=True, vmem_limit_bytes=KERNEL_VMEM
        ),
        cost_estimate=pl.CostEstimate(flops=8_000_000_000, bytes_accessed=25_000_000, transcendentals=3_000_000),
        name="forward",
    )(lengths, box, taps, vectors, table, tokens, patches, *matrices)


def backward_page_kernel(
    scalar_ref, columns_ref, rows_ref, query_rows_ref, query_ref, key_ref, value_ref, mixture_back_ref, weights_ref,
    query_back_ref, block_back_ref, plane_back_ref, line_back_ref,
    back, steps, mask_ref, hot_ref, query_hot_ref, band_ref,
):
    seq_index = scalar_ref[0]
    row_count, width = query_ref.shape
    key_pad = key_ref.shape[0]
    count = 4
    patch_span = GRID_SIDE * GRID_SIDE // count
    span = row_count - patch_span
    text_slots = span * count
    columns, rows = columns_ref[...], rows_ref[...]
    mask_ref[:, 0:key_pad] = ((rows[0:1, :] & 15) < (columns[:, 0:1] & 15)).astype(jnp.float32).astype(jnp.bfloat16)
    mask_ref[:, key_pad:] = ((rows[1:2, :] & 15) < (columns[:, 1:2] & 15)).astype(jnp.float32).astype(jnp.bfloat16)
    bin_at = lax.broadcasted_iota(jnp.int32, (128, key_pad), 0) - 1
    key_block = lax.broadcasted_iota(jnp.int32, (128, key_pad), 1) >> 4
    for side in range(2):
        key_bin = rows[side : side + 1, :] >> 4
        plain = (key_bin == bin_at).astype(jnp.float32)
        lower = (key_bin - 1 == bin_at).astype(jnp.float32)
        plain, lower = jnp.where(bin_at < 64, plain, 0.0), jnp.where(bin_at < 64, lower, 0.0)
        mine = slice(128 * side, 128 * (side + 1))
        other = slice(128 * (1 - side), 128 * (2 - side))
        change = lower - plain
        if side == 0:
            plain = jnp.where(bin_at - 71 == key_block, 1.0, plain)
        hot_ref[mine, 0:key_pad] = plain.astype(jnp.bfloat16)
        hot_ref[mine, (1 + side) * key_pad : (2 + side) * key_pad] = change.astype(jnp.bfloat16)
        hot_ref[other, (1 + side) * key_pad : (2 + side) * key_pad] = jnp.zeros((128, key_pad), jnp.bfloat16)
    half_bin = lax.broadcasted_iota(jnp.int32, (72, row_count), 0)
    for side in range(2):
        query_hot_ref[72 * side : 72 * (side + 1), :] = (
            (71 - (query_rows_ref[side : side + 1, :] >> 4) == half_bin).astype(jnp.float32).astype(jnp.bfloat16)
        )
    lane128 = lax.broadcasted_iota(jnp.int32, (row_count, 128), 1)
    place = query_places(seq_index, (row_count, 128), span, patch_span, text_slots)
    aim = place + lane128 - 32
    near = (lane128 < 64) & (aim >= 0) & (aim < text_slots + patch_span * count)
    apart = (aim >> 4) - (place >> 4)
    near = near & (apart >= -1) & (apart <= 1)
    band_ref[...] = jnp.where(near, aim, -1)
    pair_width = 128
    line_back_ref[...] = jnp.zeros_like(line_back_ref)
    plane_back_ref[...] = jnp.zeros_like(plane_back_ref)

    def attend(pair, carry):
        at = pl.ds(pl.multiple_of(pair * pair_width, pair_width), pair_width)
        both_query = split_heads(query_ref[:, at])
        both_back = split_heads(mixture_back_ref[:, at])
        back[...] = dot_nt(both_back, value_ref[:, at])
        for start in range(0, 2 * row_count, CHUNK):
            there = slice(start, start + CHUNK)
            here = slice(start % row_count, start % row_count + CHUNK)
            parts, total = [], None
            for block_at in range(0, key_pad, 128):
                lane = slice(block_at, block_at + 128)
                part = weights_ref[pair, there, lane].astype(jnp.float32)
                product = part * back[there, lane]
                total = product if total is None else total + product
                parts.append(part)
            mean = jnp.sum(total, axis=1, keepdims=True)
            for index, part in enumerate(parts):
                lane = slice(128 * index, 128 * (index + 1))
                step = (part * (back[there, lane] - mean)).astype(jnp.bfloat16)
                steps[there, lane] = step
                steps[there, key_pad + 128 * index : key_pad + 128 * (index + 1)] = step * mask_ref[here, lane]
                steps[there, 2 * key_pad + 128 * index : 2 * key_pad + 128 * (index + 1)] = (
                    step * mask_ref[here, key_pad + 128 * index : key_pad + 128 * (index + 1)]
                )
        query_back_ref[:, at] = (merge_heads(dot_nn(steps[:, 0:key_pad], key_ref[:, at])) * 0.125).astype(
            jnp.bfloat16
        )
        for kind, value in enumerate(
            (dot_tn(steps[:, 0:key_pad], both_query), dot_tn(weights_ref[pair], both_back))
        ):
            value = value.astype(jnp.bfloat16)
            for where in range(count):
                step_at = seq_index ^ where
                slot = (step_at & 1) * 2 + (step_at >> 1)
                block_back_ref[slot, kind, 0:span, at] = value[where * span : (where + 1) * span]
                block_back_ref[slot, kind, span:row_count, at] = value[
                    text_slots + where * patch_span : text_slots + (where + 1) * patch_span
                ]
        bins = dot_nt(steps[...], hot_ref[...])
        low_bins = bins.astype(jnp.bfloat16)
        lane_one = lax.broadcasted_iota(jnp.int32, (1, 128), 1)
        far = lane128 - 72 - (place >> 4)
        in_line = (lane128 >= 72) & (lane128 < 72 + key_pad // 16)
        for side in range(2):
            head = pl.ds(2 * pair + side, 1)
            own = slice(side * row_count, (side + 1) * row_count)
            both = dot_nn(query_hot_ref[...], low_bins[own])
            for plane in range(2):
                table = both[72 * plane : 72 * (plane + 1), 128 * plane : 128 * (plane + 1)]
                wide_lane = lax.broadcasted_iota(jnp.int32, table.shape, 1)
                table = jnp.where(wide_lane < 72, table, 0.0)
                table = jnp.concatenate([table, jnp.zeros_like(table)], axis=1)
                sheared = pltpu.roll(table, 0, 1, stride=1, stride_axis=0)
                plane_back_ref[plane, head, :] = jnp.sum(sheared, axis=0, keepdims=True)
            line_bins = bins[own, 0:128]
            low_tail = jnp.sum(jnp.where(in_line & (far <= -2), line_bins, 0.0), axis=(0, 1), keepdims=True)
            high_tail = jnp.sum(jnp.where(in_line & (far >= 2), line_bins, 0.0), axis=(0, 1), keepdims=True)
            band = jnp.zeros((1, 128), jnp.float32)
            base = side * row_count
            for first, rows_here, block in (
                (0, span, seq_index),
                (0, 32, jnp.maximum(seq_index - 1, 0)),
                (span - 32, 32, seq_index + 1),
                (span, patch_span, count - 1),
                (span, patch_span, count),
            ):
                aims = band_ref[first : first + rows_here, :]
                source = steps[
                    base + first : base + first + rows_here, pl.ds(pl.multiple_of(block * 128, 128), 128)
                ].astype(jnp.float32)
                taken = jnp.take_along_axis(source, aims & 127, axis=1)
                right = (aims >> 7) == block
                if first == 0 and rows_here == 32:
                    right = right & (seq_index > 0)
                band = band + jnp.sum(jnp.where(right, taken, 0.0), axis=0, keepdims=True)
            line_back_ref[head, :] = (
                band + jnp.where(lane_one == 0, low_tail, 0.0) + jnp.where(lane_one == 63, high_tail, 0.0)
            )
        return carry

    lax.fori_loop(0, width // pair_width, attend, 0)


def backward_page(scalars, columns, rows, query_rows, queries, keys, values, mixture_back, weights):
    row_count, width = queries.shape
    key_pad = keys.shape[0]
    heads = 2 * weights.shape[0]
    return pl.pallas_call(
        backward_page_kernel,
        out_shape=(
            jax.ShapeDtypeStruct((row_count, width), jnp.bfloat16),
            jax.ShapeDtypeStruct((4, 2, row_count, width), jnp.bfloat16),
            jax.ShapeDtypeStruct((2, heads, 256), jnp.float32),
            jax.ShapeDtypeStruct((heads, 128), jnp.float32),
        ),
        in_specs=[pl.BlockSpec(memory_space=pltpu.SMEM)] + in_vmem(8),
        out_specs=tuple(in_vmem(4)),
        scratch_shapes=[
            pltpu.VMEM((2 * row_count, key_pad), jnp.float32),
            pltpu.VMEM((2 * row_count, 3 * key_pad), jnp.bfloat16),
            pltpu.VMEM((row_count, 2 * key_pad), jnp.bfloat16),
            pltpu.VMEM((256, 3 * key_pad), jnp.bfloat16),
            pltpu.VMEM((144, row_count), jnp.bfloat16),
            pltpu.VMEM((row_count, 128), jnp.int32),
        ],
        compiler_params=pltpu.CompilerParams(vmem_limit_bytes=KERNEL_VMEM),
        cost_estimate=pl.CostEstimate(flops=3_000_000_000, bytes_accessed=6_000_000, transcendentals=1_000_000),
        name="backward_page",
    )(scalars, columns, rows, query_rows, queries, keys, values, mixture_back, weights)


def early_orders(far, side):
    return (far[1], far[0], side) + tuple(far[2:]), (far[0], far[1], side) + tuple(far[2:])


def slot_of_bits(bits):
    slot = 0
    for bit in bits:
        slot = slot * 2 + bit
    return slot


def apart(one, other):
    return (one + other) % 2


def early_slots(scalar_ref, page, column, levels):
    far = [apart((page >> level) & 1, (scalar_ref[2] >> level) & 1) for level in range(levels)]
    side = apart(column, scalar_ref[3])
    return [slot_of_bits(order) for order in early_orders(far, side)]


NORM_CHUNK = 48


def norm_rows(values):
    mean = jnp.mean(values, axis=-1, keepdims=True)
    centred = values - mean
    scale = lax.rsqrt(jnp.mean(centred * centred, axis=-1, keepdims=True) + epsilon)
    return centred * scale, scale


def norm_back(delta, unit, scale):
    return scale * (
        delta
        - jnp.mean(delta, axis=-1, keepdims=True)
        - unit * jnp.mean(delta * unit, axis=-1, keepdims=True)
    )


def column_sum(values):
    return jnp.sum(values, axis=0, keepdims=True)


OUT_BIAS, DOWN_BIAS, FIRST_GAIN, FIRST_SHIFT, SECOND_GAIN, SECOND_SHIFT = range(6)
UP_BIAS = 6


def middle_kernel(
    pages, direct,
    vector_any, *rest,
):
    scalar_ref = position()
    arguments, rest = (*rest[:7], vector_any), rest[7:]
    output_ref, patch_output_ref, first_back_ref, mixture_back_ref, sums_ref, *rest = rest
    *rest, load_sem, store_sem = rest
    copied, rest = rest[-8:], rest[:-8]
    hidden_ref, mixture_ref, cotangent_ref, patch_cotangent_ref, out_weight_ref, up_weight_ref, down_weight_ref, vector_ref = (
        copied
    )
    loads = [
        pltpu.make_async_copy(source, target, load_sem.at[index])
        for index, (source, target) in enumerate(zip(arguments, copied, strict=True))
    ]
    for index in (7, 1, 4, 0, 5, 6, 2, 3):
        loads[index].start()
    if direct:
        bundle_any, *rest, bundle_ref = rest
    else:
        normed_out_ref, up_out_ref, activated_out_ref, down_out_ref, attention_out_ref, *rest = rest
    state, unit, scale_ref, normed, activated, slope, up_back, down_back, attention_back, flipped = rest
    count, span, width = output_ref.shape
    patch_span = patch_output_ref.shape[1]
    row_count = span + patch_span
    total_rows = count * row_count
    wide = up_weight_ref.shape[1]
    lanes = width
    sums_ref[...] = jnp.zeros_like(sums_ref)

    def tile_at(tile):
        return pl.ds(pl.multiple_of(tile * lanes, lanes), lanes)

    def attention_tile(tile, carry):
        at = tile_at(tile)
        state[:, at] = hidden_ref[:, at] + (dot_nn(mixture_ref[...], out_weight_ref[:, at]) + vector_ref[2:3, at])
        return carry

    for index in (0, 1, 4, 7):
        loads[index].wait()
    lax.fori_loop(0, width // lanes, attention_tile, 0)

    def first_norm(chunk, carry):
        here = pl.ds(pl.multiple_of(chunk * NORM_CHUNK, 16), NORM_CHUNK)
        rows, scale = norm_rows(state[here, :])
        unit[here, :] = rows
        scale_ref[here, :] = jnp.broadcast_to(scale, (NORM_CHUNK, 128))
        rows = rows * vector_ref[4:5, :] + vector_ref[5:6, :]
        state[here, :] = rows
        normed[here, :] = rows.astype(jnp.bfloat16)
        return carry

    lax.fori_loop(0, total_rows // NORM_CHUNK, first_norm, 0)

    def up_tile(tile, carry):
        at = tile_at(tile)
        branch = dot_nn(normed[...], up_weight_ref[:, at]) + vector_ref[pl.ds(8 + tile, 1), :]
        chance = 0.5 * (1.0 + lax.erf(branch * 0.7071067811865476))
        activated[:, at] = (branch * chance).astype(jnp.bfloat16)
        slope[:, at] = chance + branch * (jnp.exp(branch * branch * -0.5) * 0.3989422804014327)
        return carry

    loads[5].wait()
    lax.fori_loop(0, wide // lanes, up_tile, 0)

    def down_tile(tile, carry):
        at = tile_at(tile)
        state[:, at] = state[:, at] + (dot_nn(activated[...], down_weight_ref[:, at]) + vector_ref[3:4, at])
        return carry

    for index in (2, 3, 6):
        loads[index].wait()
    lax.fori_loop(0, width // lanes, down_tile, 0)

    def second_norm(start, rows_here, page, out_ref, delta_ref):
        here = pl.ds(pl.multiple_of(page * row_count + start, 16), rows_here)
        there = pl.ds(0 if start == span else start, rows_here)
        rows, scale = norm_rows(state[here, :])
        out_ref[page, there, :] = rows * vector_ref[6:7, :] + vector_ref[7:8, :]
        delta = delta_ref[page, there, :].astype(jnp.float32)
        back = norm_back(delta * vector_ref[6:7, :], rows, scale)
        state[here, :] = back
        low = back.astype(jnp.bfloat16)
        down_back[here, :] = low
        for index, value in (
            (SECOND_GAIN, delta * rows), (SECOND_SHIFT, delta), (DOWN_BIAS, low.astype(jnp.float32))
        ):
            sums_ref[index : index + 1, :] += column_sum(value)

    def second_page(page, carry):
        for start in range(0, span, 32):
            second_norm(start, 32, page, output_ref, cotangent_ref)
        second_norm(span, patch_span, page, patch_output_ref, patch_cotangent_ref)
        return carry

    lax.fori_loop(0, count, second_page, 0)

    def up_back_tile(tile, carry):
        at = tile_at(tile)
        low = (dot_nt(down_back[...], down_weight_ref[at, :]) * slope[:, at]).astype(jnp.bfloat16)
        up_back[:, at] = low
        sums_ref[pl.ds(UP_BIAS + tile, 1), :] = column_sum(low.astype(jnp.float32))
        return carry

    lax.fori_loop(0, wide // lanes, up_back_tile, 0)

    def normed_back_tile(tile, carry):
        at = tile_at(tile)
        state[:, at] = state[:, at] + dot_nt(up_back[...], up_weight_ref[at, :])
        return carry

    lax.fori_loop(0, width // lanes, normed_back_tile, 0)

    def first_back(chunk, carry):
        here = pl.ds(pl.multiple_of(chunk * NORM_CHUNK, 16), NORM_CHUNK)
        delta, rows = state[here, :], unit[here, :]
        back = norm_back(delta * vector_ref[4:5, :], rows, scale_ref[here, 0:1])
        first_back_ref[here, :] = back
        low = back.astype(jnp.bfloat16)
        attention_back[here, :] = low
        for index, value in (
            (FIRST_GAIN, delta * rows), (FIRST_SHIFT, delta), (OUT_BIAS, low.astype(jnp.float32))
        ):
            sums_ref[index : index + 1, :] += column_sum(value)
        return carry

    lax.fori_loop(0, total_rows // NORM_CHUNK, first_back, 0)

    def mixture_tile(tile, carry):
        at = tile_at(tile)
        mixture_back_ref[:, at] = dot_nt(attention_back[...], out_weight_ref[at, :]).astype(jnp.bfloat16)
        return carry

    lax.fori_loop(0, width // lanes, mixture_tile, 0)
    if not direct:
        normed_out_ref[...] = normed[...]
        up_out_ref[...] = up_back[...]
        activated_out_ref[...] = activated[...]
        down_out_ref[...] = down_back[...]
        attention_out_ref[...] = attention_back[...]
        return
    levels = pages.bit_length() - 1
    core = scalar_ref[1]
    rows = width // pages
    tall = wide // pages
    block = 384
    groups = wide // (2 * block)
    flipped[...] = normed[...].T

    def up_weight_tile(tile, carry):
        at = pl.ds(pl.multiple_of(tile * 2 * block, 2 * block), 2 * block)
        result = dot_nn(flipped[...], up_back[:, at]).astype(jnp.bfloat16)
        for part in range(2):
            column, group = (2 * tile + part) // groups, (2 * tile + part) % groups
            for page in range(pages):
                slot = early_slots(scalar_ref, page, column, levels)[0]
                bundle_ref[core, slot, pl.ds(pl.multiple_of(group * rows, 16), rows), :] = result[
                    page * rows : (page + 1) * rows, part * block : (part + 1) * block
                ]
        return carry

    lax.fori_loop(0, groups, up_weight_tile, 0)
    stores = [
        pltpu.make_async_copy(bundle_ref.at[part], bundle_any.at[part], store_sem.at[index])
        for index, part in enumerate(
            (
                (core, slice(None), slice(0, tall)), (1 - core, slice(None), slice(0, tall)),
                (slice(None), slice(None), slice(tall, tall + rows // 2)),
            )
        )
    ]
    stores[0].start()

    def down_weight_tile(page, carry):
        at = pl.ds(pl.multiple_of(page * tall, 128), tall)
        result = dot_tn(activated[:, at], down_back[...]).astype(jnp.bfloat16)
        for column in range(2):
            slot = early_slots(scalar_ref, page, column, levels)[1]
            bundle_ref[1 - core, slot, 0:tall, :] = result[:, column * block : (column + 1) * block]
        return carry

    lax.fori_loop(0, pages, down_weight_tile, 0)
    stores[1].start()
    flipped[...] = mixture_ref[...].T
    half = rows // 2

    result = dot_nn(flipped[...], attention_back[...]).astype(jnp.bfloat16)
    for column in range(2):
        for page in range(pages):
            slots = early_slots(scalar_ref, page, column, levels)
            for order in range(2):
                first = page * rows + order * half
                bundle_ref[core if order == 0 else 1 - core, slots[order], tall : tall + half, :] = result[
                    first : first + half, column * block : (column + 1) * block
                ]
    stores[2].start()
    for copy in stores:
        copy.wait()


def in_tiles(width, pages):
    return (width // pages) % 32 == 0 and pages >= 4


def middle(places, hidden, mixture, cotangent, patch_cotangent, matrices, vectors, pages):
    count, span, width = cotangent.shape
    patch_span = patch_cotangent.shape[1]
    total_rows = hidden.shape[0]
    wide = matrices[1].shape[1]
    direct = in_tiles(width, pages)
    bf16, f32 = jnp.bfloat16, jnp.float32
    if direct:
        extra = (jax.ShapeDtypeStruct((2, 2 * pages, (wide + width // 2) // pages, 384), bf16),)
    else:
        extra = tuple(
            jax.ShapeDtypeStruct((total_rows, size), bf16) for size in (width, wide, wide, width, width)
        )
    result = pl.pallas_call(
        functools.partial(middle_kernel, pages, direct),
        out_shape=(
            jax.ShapeDtypeStruct(cotangent.shape, f32),
            jax.ShapeDtypeStruct(patch_cotangent.shape, f32),
            jax.ShapeDtypeStruct((total_rows, width), f32),
            jax.ShapeDtypeStruct((total_rows, width), bf16),
            jax.ShapeDtypeStruct((16, width), f32),
        )
        + extra,
        in_specs=anywhere(8),
        out_specs=tuple(in_vmem(5) + (anywhere(1) if direct else in_vmem(len(extra)))),
        scratch_shapes=[
            pltpu.VMEM((total_rows, width), f32),
            pltpu.VMEM((total_rows, width), f32),
            pltpu.VMEM((total_rows, 128), f32),
            pltpu.VMEM((total_rows, width), bf16),
            pltpu.VMEM((total_rows, wide), bf16),
            pltpu.VMEM((total_rows, wide), f32),
            pltpu.VMEM((total_rows, wide), bf16),
            pltpu.VMEM((total_rows, width), bf16),
            pltpu.VMEM((total_rows, width), bf16),
            pltpu.VMEM((width, total_rows), bf16),
        ]
        + [pltpu.VMEM(value.shape, value.dtype) for value in (extra if direct else ())]
        + [
            pltpu.VMEM(value.shape, value.dtype)
            for value in (hidden, mixture, cotangent, patch_cotangent, *matrices, vectors)
        ]
        + [pltpu.SemaphoreType.DMA((8,)), pltpu.SemaphoreType.DMA((3,))],
        compiler_params=pltpu.CompilerParams(vmem_limit_bytes=KERNEL_VMEM),
        cost_estimate=pl.CostEstimate(flops=14_000_000_000, bytes_accessed=30_000_000, transcendentals=2_600_000),
        name="middle",
    )(vectors, hidden, mixture, cotangent, patch_cotangent, *matrices)
    first, rest = result[:5], result[5:]
    if direct:
        return first + rest
    normed, up_back, activated, down_back, attention_back = rest
    return first + (
        indexed_bundle(
            (
                ((normed, up_back, None), (mixture, attention_back, 0)),
                ((activated, down_back, None), (mixture, attention_back, 1)),
            ),
            places,
            pages,
        ),
    )


def indexed_bundle(matrices, scalars, pages):
    levels = pages.bit_length() - 1
    place = jnp.arange(2 * pages, dtype=jnp.int32)
    bits = [(place >> (levels - k)) & 1 for k in range(levels + 1)]
    halves = []
    for order, group in enumerate(matrices):
        side, near = (bits[0], bits[1]) if order == 0 else (bits[1], bits[0])
        far = near
        for level in range(1, levels):
            far = far + (bits[level + 1] << level)
        index = (far ^ scalars[2]) * 2 + (side ^ scalars[3])
        blocks = []
        for operand, gradient, part in group:
            rows = in_blocks(outer_dot(operand, gradient).astype(jnp.bfloat16), pages)
            if part is not None:
                half = rows.shape[1] // 2
                rows = rows[:, part * half : (part + 1) * half]
            blocks.append(rows)
        halves.append(jnp.concatenate(blocks, axis=1)[index])
    first, second = halves
    mine = scalars[1] == 0
    return jnp.stack([jnp.where(mine, first, second), jnp.where(mine, second, first)])


def in_blocks(matrix, pages):
    rows, columns = matrix.shape[0] // pages, matrix.shape[1] // 2
    lanes = min(columns, 384)
    blocks = matrix.reshape(pages, rows, 2, columns // lanes, lanes)
    return blocks.transpose(0, 2, 3, 1, 4).reshape(pages * 2, rows * columns // lanes, lanes)


class Halving:
    def __init__(self, keep, source, landing, landings, partners, sibling, sems, chunks):
        self.keep, self.landing, self.landings = keep, landing, landings
        total = keep.shape[0]
        unit = total // chunks
        send_sem, recv_sem = sems
        self.arrivals, self.sends, self.needs = {}, {}, {}
        used = 0
        for chunk in range(chunks):
            lo = total - (chunk + 1) * unit
            copy = remote(
                source.at[lo : lo + unit], landing.at[lo : lo + unit], send_sem.at[used], recv_sem.at[used], *sibling
            )
            self.arrivals["core", chunk] = (copy, landing, lo, unit)
            used += 1
        for step, (into, partner) in enumerate(zip(landings, partners, strict=True)):
            size = total >> (step + 1)
            piece = min(unit, size)
            for chunk in range(size // piece):
                lo = size - (chunk + 1) * piece
                copy = remote(
                    keep.at[size + lo : size + lo + piece], into.at[lo : lo + piece], send_sem.at[used],
                    recv_sem.at[used], *partner,
                )
                self.arrivals[step, chunk] = (copy, into, lo, piece)
                self.sends[step, chunk] = copy
                self.needs[step, chunk] = {
                    (source_step, block)
                    for block in range(size + lo, size + lo + piece)
                    for source_step in ("core", *range(step))
                }
                used += 1
        self.done = set()

    def start(self):
        for key, (copy, *_) in self.arrivals.items():
            if key[0] == "core":
                copy.start()

    def take(self, *key):
        copy, into, lo, count = self.arrivals[key]
        copy.wait_recv()

        def add(block, carry):
            self.keep[block] = self.keep[block] + into[block]
            return carry

        lax.fori_loop(lo, lo + count, add, 0)
        for block in range(lo, lo + count):
            self.done.add((key[0], block))
        for name in list(self.sends):
            if self.needs[name] <= self.done:
                self.sends.pop(name).start()

    def finish(self):
        for copy, *_ in self.arrivals.values():
            copy.wait_send()


def backward_kernel(
    pages,
    staging, length_ref, query_ref, mixture_back_ref, columns_ref, rows_ref, query_rows_ref, tokens_ref, patches_ref, taps_ref,
    middle_sums_ref, bundle_any, weights_any, key_any, value_any, hidden_any, first_back_any, query_weight_any,
    key_weight_any, value_weight_any,
    tokens_back_ref, patches_back_ref, early_ref, late_ref, sums_ref, up_in_ref, down_in_ref, mixed_in_ref,
    keep, landing, landings, late, late_landing, late_landings, weights_buf, key_buf, value_buf, outgoing, from_sib,
    from_far, matrices, flipped, total_back, query_back, key_back, value_back, back, steps, mask_ref, hot_ref,
    query_hot_ref, band_ref, table_acc, band_acc, table_out, text_rim, patch_rim, sums, sums_in,
    up_in, down_out, down_in, mixed_out, mixed_in,
    load_sem, page_sem, early_send, early_recv, late_send, late_recv, sib_send, sib_recv, far_send, far_recv, rim_send,
    rim_recv, sum_send, sum_recv, swap_send, swap_recv,
):
    page_at, bits, seq, across, core = places_of(pages)
    levels = len(bits)
    count, span, width = tokens_ref.shape
    patch_span = patches_ref.shape[1]
    row_count = span + patch_span
    total_rows = count * row_count
    key_pad = key_buf.shape[1]
    text_slots = 4 * span
    groups = weights_buf.shape[1]
    members = weights_buf.shape[2] // row_count
    heads = groups * members
    group_width = members * HEAD_LANES
    f32, bf16 = jnp.float32, jnp.bfloat16

    sibling = (page_at, sibling_of(seq))
    opposite = (page_at, across_of(seq))
    diagonal = (page_at, sibling_of(across_of(seq)))
    flips = [(1 - 2 * bit) * 2**level for level, bit in enumerate(bits)]
    on_page = [(page_at + flip, seq) for flip in flips]
    either = lambda first, second: first + core * (second - first)
    early_partners = [
        (page_at + either(flips[1], flips[0]), seq),
        (page_at + either(flips[0], flips[1]), seq),
        opposite,
    ] + on_page[2:]
    barrier = pltpu.get_barrier_semaphore()
    everyone = [sibling, opposite, diagonal] + on_page
    for peer in everyone:
        pl.semaphore_signal(barrier, inc=1, device_id=peer, device_id_type=MESH)

    keep_load = pltpu.make_async_copy(bundle_any.at[0], keep, load_sem.at[0])
    later_loads = [
        pltpu.make_async_copy(source, target, load_sem.at[1 + index])
        for index, (source, target) in enumerate(
            (
                (query_weight_any, matrices.at[0]), (key_weight_any, matrices.at[1]),
                (value_weight_any, matrices.at[2]), (hidden_any, key_back), (first_back_any, total_back),
            )
        )
    ]

    def page_loads(page):
        slot = page % 2
        return [
            pltpu.make_async_copy(source.at[page], target.at[slot], page_sem.at[index, slot])
            for index, (source, target) in enumerate(
                ((weights_any, weights_buf), (key_any, key_buf), (value_any, value_buf))
            )
        ]

    for copy in page_loads(0):
        copy.start()
    keep_load.start()
    pl.semaphore_wait(barrier, len(everyone))
    early = Halving(
        keep, bundle_any.at[1], landing, landings, early_partners, sibling, (early_send, early_recv), 8
    )
    late_sum = Halving(
        late.at[0], late.at[1], late_landing, late_landings, early_partners, sibling, (late_send, late_recv), 4
    )
    early.start()
    for copy in staging:
        copy.wait()

    lane128 = lax.broadcasted_iota(jnp.int32, (row_count, 128), 1)
    place = query_places(seq, (row_count, 128), span, patch_span, text_slots)
    aim = place + lane128 - 32
    blocks_on = (aim >> 4) - (place >> 4)
    near = (lane128 < 64) & (aim >= 0) & (aim < text_slots + patch_span * 4) & (blocks_on >= -1) & (blocks_on <= 1)
    band_ref[...] = jnp.where(near, aim, -1)
    table_acc[...] = jnp.zeros_like(table_acc)
    band_acc[...] = jnp.zeros_like(band_acc)
    lane_of_row = lax.broadcasted_iota(jnp.int32, (48, row_count), 1)
    place_of_row = jnp.where(
        lane_of_row < span, seq * span + lane_of_row, text_slots + seq * patch_span + lane_of_row - span
    )
    query_hot_ref[144:192, :] = (
        ((place_of_row >> 4) == lax.broadcasted_iota(jnp.int32, (48, row_count), 0)).astype(f32).astype(bf16)
    )
    def start_page(page):
        slot = page % 2
        for copy in page_loads(page):
            copy.wait()

        @pl.when(page < count - 1)
        def _():
            for copy in page_loads(page + 1):
                copy.start()

        bin_at = lax.broadcasted_iota(jnp.int32, (128, key_pad), 0) - 1
        key_block = lax.broadcasted_iota(jnp.int32, (128, key_pad), 1) >> 4
        half_bin = lax.broadcasted_iota(jnp.int32, (72, row_count), 0)
        for side in range(2):
            key_row = rows_ref[page, side : side + 1, :]
            query_column = columns_ref[page, :, 128 * side : 128 * side + 1]
            mask_ref[:, side * key_pad : (side + 1) * key_pad] = (
                ((key_row & 15) < (query_column & 15)).astype(f32).astype(bf16)
            )
            key_bin = key_row >> 4
            plain = jnp.where(bin_at < 64, (key_bin == bin_at).astype(f32), 0.0)
            lower = jnp.where(bin_at < 64, (key_bin - 1 == bin_at).astype(f32), 0.0)
            mine = slice(128 * side, 128 * (side + 1))
            other = slice(128 * (1 - side), 128 * (2 - side))
            change = lower - plain
            if side == 0:
                plain = jnp.where(bin_at - 71 == key_block, 1.0, plain)
            hot_ref[mine, 0:key_pad] = plain.astype(bf16)
            hot_ref[mine, (1 + side) * key_pad : (2 + side) * key_pad] = change.astype(bf16)
            hot_ref[other, (1 + side) * key_pad : (2 + side) * key_pad] = jnp.zeros((128, key_pad), bf16)
            query_bin = query_rows_ref[page, side : side + 1, 0:row_count] >> 4
            query_hot_ref[72 * side : 72 * (side + 1), :] = (71 - query_bin == half_bin).astype(f32).astype(bf16)

    def attend(page, group):
        slot = page % 2
        at = pl.ds(pl.multiple_of(group * group_width, group_width), group_width)
        own_rows = pl.ds(pl.multiple_of(page * row_count, 16), row_count)
        both_query = split_heads(query_ref[own_rows, at])
        both_back = split_heads(mixture_back_ref[own_rows, at])
        back[...] = dot_nt(both_back, value_buf[slot, :, at])
        for start in range(0, members * row_count, CHUNK):
            there = slice(start, start + CHUNK)
            here = slice(start % row_count, start % row_count + CHUNK)
            parts, total = [], None
            for block_at in range(0, key_pad, 128):
                lane = slice(block_at, block_at + 128)
                part = weights_buf[slot, group, there, lane].astype(f32)
                product = part * back[there, lane]
                total = product if total is None else total + product
                parts.append(part)
            mean = jnp.sum(total, axis=1, keepdims=True)
            for index, part in enumerate(parts):
                lane = slice(128 * index, 128 * (index + 1))
                step = (part * (back[there, lane] - mean)).astype(bf16)
                steps[there, lane] = step
                steps[there, key_pad + 128 * index : key_pad + 128 * (index + 1)] = step * mask_ref[here, lane]
                steps[there, 2 * key_pad + 128 * index : 2 * key_pad + 128 * (index + 1)] = (
                    step * mask_ref[here, key_pad + 128 * index : key_pad + 128 * (index + 1)]
                )
        query_back[own_rows, at] = (
            merge_heads(dot_nn(steps[:, 0:key_pad], key_buf[slot, :, at])) * 0.125
        ).astype(bf16)
        for kind, value in enumerate(
            (dot_tn(steps[:, 0:key_pad], both_query), dot_tn(weights_buf[slot, group], both_back))
        ):
            value = value.astype(bf16)
            for where in range(4):
                place_at = apart(where % 2, core) * 2 + apart(where // 2, across)
                outgoing[page, place_at, kind, 0:span, at] = value[where * span : (where + 1) * span]
                outgoing[page, place_at, kind, span:row_count, at] = value[
                    text_slots + where * patch_span : text_slots + (where + 1) * patch_span
                ]
        bins = dot_nt(steps[...], hot_ref[...]).astype(bf16)
        for side in range(members):
            head = members * group + side
            base = side * row_count
            both = dot_nn(query_hot_ref[...], bins[base : base + row_count])
            table_acc[head, 0:72, :] += both[0:72, 0:128]
            table_acc[head, 72:144, :] += both[72:144, 128:256]
            table_acc[head, 144:192, :] += both[144:192, 0:128]
            for first, rows_here, block, into in bands():
                source = steps[
                    base + first : base + first + rows_here, pl.ds(pl.multiple_of(block * 128, 128), 128)
                ]
                band_acc[head, into : into + rows_here, :] += source.astype(f32)

    def bands():
        before = seq - (seq + 3) // 4
        return (
            (0, span, seq, 0),
            (0, 32, before, span),
            (span - 32, 32, seq + 1, span + 32),
            (span, patch_span, 3, span + 64),
            (span, patch_span, 4, span + 64 + patch_span),
        )

    def sib_copy(page):
        return remote(outgoing.at[page, 2:4], from_sib.at[page], sib_send.at[page], sib_recv.at[page], *sibling)

    def far_copy(page):
        return remote(outgoing.at[page, 1], from_far.at[page], far_send.at[page], far_recv.at[page], *opposite)

    def pass_on(page):
        sib_copy(page).wait_recv()
        for kind in range(2):
            outgoing[page, 1, kind] = outgoing[page, 1, kind] + from_sib[page, 1, kind]
        far_copy(page).start()

    events = {
        1: [("core", 0), ("core", 1)], 2: [("core", 2), ("core", 3)], 4: [("core", 4), ("core", 5)],
        6: [("core", 6), ("core", 7)], 8: [(0, 0)], 12: [(0, 1)],
    }
    last_turn = count * groups - 1

    def step_body(turn, carry):
        page, group = turn // groups, turn % groups

        @pl.when(group == 0)
        def _():
            start_page(page)

        for at_turn, names in events.items():

            @pl.when(turn == min(at_turn, last_turn))
            def _(names=names, at_turn=at_turn):
                if at_turn == min(events):
                    keep_load.wait()
                for name in names:
                    early.take(*name)

        @pl.when(turn == min(3, last_turn))
        def _():
            for copy in later_loads:
                copy.start()

        @pl.when((group == 1) & (page > 0))
        def _():
            pass_on(page - 1)

        attend(page, group)

        @pl.when(group == groups - 1)
        def _():
            sib_copy(page).start()

        return carry

    lax.fori_loop(0, count * groups, step_body, 0)

    for copy in later_loads:
        copy.wait()
    flipped[...] = key_back[...].T
    lanes = 384
    rows = width // pages
    half = rows // 2

    def weight_columns(index, gradient):
        def tile(four, carry):
            tile_rows = pl.ds(pl.multiple_of(four * 4 * rows, 128), 4 * rows)
            result = dot_nn(flipped[tile_rows, :], gradient[...]).astype(bf16)
            for inner in range(4):
                page = four * 4 + inner
                first = inner * rows
                for column in range(2):
                    far = [apart((page // 2**level) % 2, bit) for level, bit in enumerate(bits)]
                    slots = [slot_of_bits(order) for order in early_orders(far, apart(column, across))]
                    at = slice(column * lanes, (column + 1) * lanes)
                    if index < 2:
                        late[core if index == 0 else 1 - core, slots[index], 0:rows, :] = result[
                            first : first + rows, at
                        ]
                    else:
                        late[core, slots[0], rows : rows + half, :] = result[first : first + half, at]
                        late[1 - core, slots[1], rows : rows + half, :] = result[first + half : first + rows, at]
            return carry

        lax.fori_loop(0, pages // 4, tile, 0)

    def project_back(gradient, matrix):
        total_back[...] = total_back[...] + dot_nt(gradient[...], matrices[matrix])

    pass_on(count - 1)
    weight_columns(0, query_back)
    project_back(query_back, 0)
    sums[0, 0:16, :] = middle_sums_ref[...]
    sums[0, 10:11, :] = column_sum(query_back[...].astype(f32))

    def head_tables(head, carry):
        for plane in range(2):
            table = table_acc[head, 72 * plane : 72 * (plane + 1), :]
            lane = lax.broadcasted_iota(jnp.int32, table.shape, 1)
            table = jnp.where(lane < 72, table, 0.0)
            table = jnp.concatenate([table, jnp.zeros_like(table)], axis=1)
            sheared = pltpu.roll(table, 0, 1, stride=1, stride_axis=0)
            table_out[head, 0:1, 256 * plane : 256 * (plane + 1)] = column_sum(sheared)
        table = table_acc[head, 144:192, :]
        lane = lax.broadcasted_iota(jnp.int32, table.shape, 1)
        apart_by = lane - 72 - lax.broadcasted_iota(jnp.int32, table.shape, 0)
        in_line = (lane >= 72) & (lane < 72 + 36)
        low_tail = jnp.sum(column_sum(jnp.where(in_line & (apart_by <= -2), table, 0.0)), axis=1, keepdims=True)
        high_tail = jnp.sum(column_sum(jnp.where(in_line & (apart_by >= 2), table, 0.0)), axis=1, keepdims=True)
        band = jnp.zeros((1, 128), f32)
        for first, rows_here, block, into in bands():
            aims = band_ref[first : first + rows_here, :]
            taken = jnp.take_along_axis(band_acc[head, into : into + rows_here, :], aims & 127, axis=1)
            right = (aims >> 7) == block
            if into == span:
                right = right & (seq > 0)
            band = band + column_sum(jnp.where(right, taken, 0.0))
        lane_one = lax.broadcasted_iota(jnp.int32, (1, 128), 1)
        table_out[head, 0:1, 512:640] = (
            band + jnp.where(lane_one == 0, low_tail, 0.0) + jnp.where(lane_one == 63, high_tail, 0.0)
        )
        table_out[head, 0:1, 640:768] = jnp.zeros((1, 128), f32)
        return carry

    lax.fori_loop(0, heads, head_tables, 0)
    for head in range(heads):
        at_row = 8 + head
        sums[1, at_row : at_row + 1, :] = table_out[head, 0:1, :]

    for name in ((0, 2), (1, 0)):
        early.take(*name)
    for page in range(count):
        far_copy(page).wait_recv()
        own_rows = slice(page * row_count, (page + 1) * row_count)
        for kind, target in enumerate((key_back, value_back)):
            target[own_rows, :] = (
                (outgoing[page, 0, kind].astype(f32) + from_sib[page, 0, kind].astype(f32))
                + from_far[page, kind].astype(f32)
            ).astype(bf16)
    weight_columns(1, key_back)
    weight_columns(2, value_back)
    late_sum.start()
    project_back(key_back, 1)
    project_back(value_back, 2)
    sums[0, 11:12, :] = column_sum(value_back[...].astype(f32))
    for page in range(count):
        first = page * row_count
        text_rim[page, 16 : 16 + span, :] = total_back[first : first + span, :].astype(bf16)
        patch_rim[page, 16 : 16 + patch_span, :] = total_back[first + span : first + row_count, :].astype(bf16)
    after, before = (page_at, (seq + 1) % 4), (page_at, (seq + 3) % 4)
    rim_copies = [
        remote(
            source.at[:, start : start + 16], source.at[:, stop : stop + 16], rim_send.at[index], rim_recv.at[index],
            *peer,
        )
        for index, (source, start, stop, peer) in enumerate(
            (
                (text_rim, span, 0, after), (text_rim, 16, 16 + span, before),
                (patch_rim, 16, 0, after), (patch_rim, 16, 32, before),
            )
        )
    ]
    for copy in rim_copies:
        copy.start()
    for chunk in range(4):
        late_sum.take("core", chunk)
    for name in ((0, 3), (1, 1)):
        early.take(*name)
    for copy in rim_copies:
        copy.wait()
    sums[1, 0:8, :] = jnp.zeros((8, width), f32)
    sums[1, 20:24, :] = jnp.zeros((4, width), f32)
    sums[0, 16:24, :] = jnp.zeros((8, width), f32)

    def position_tile(tile, carry):
        at = pl.ds(pl.multiple_of(tile * 256, 256), 256)
        text_taps = [jnp.zeros((1, 256), f32) for _ in range(7)]
        patch_taps = [jnp.zeros((1, 256), f32) for _ in range(9)]
        for page in range(count):
            first = page * row_count
            window = text_rim[page, :, at].astype(f32)
            window_row = lax.broadcasted_iota(jnp.int32, (span + 32, 1), 0)
            inside = ((window_row >= 16) | (seq > 0)) & ((window_row < 16 + span) | (seq < 3))
            window = jnp.where(inside, window, 0.0)
            live = seq * span + lax.broadcasted_iota(jnp.int32, (span, 1), 0) < length_ref[page]
            masked = jnp.where(live, tokens_ref[page, :, at].astype(f32), 0.0)
            total = jnp.zeros((span, 256), f32)
            for distance in range(-3, 4):
                shifted = window[16 - distance : 16 - distance + span]
                if distance == 0:
                    weight = taps_ref[1:2, at] + taps_ref[4:5, at] + taps_ref[7:8, at]
                else:
                    tap = 3 * (abs(distance) - 1) + (2 if distance > 0 else 0)
                    weight = taps_ref[tap : tap + 1, at]
                total = total + shifted * weight
                text_taps[distance + 3] = text_taps[distance + 3] + column_sum(shifted * masked)
            tokens_back_ref[page, :, at] = total_back[first : first + span, at] + jnp.where(live, total, 0.0)
            window = patch_rim[page, :, at].astype(f32)
            window_row = lax.broadcasted_iota(jnp.int32, (48, 1), 0)
            inside = ((window_row >= 16) | (seq > 0)) & ((window_row < 32) | (seq < 3))
            window = jnp.where(inside, window, 0.0)
            cell = seq * patch_span + lax.broadcasted_iota(jnp.int32, (patch_span, 1), 0)
            live = ((cell >> 3) < GRID_SIDE - 1) & ((cell & 7) < GRID_SIDE - 1)
            masked = jnp.where(live, patches_ref[page, :, at].astype(f32), 0.0)
            total = jnp.zeros((patch_span, 256), f32)
            for tap in range(9):
                distance = GRID_SIDE * (tap // 3 - 1) + tap % 3 - 1
                shifted = window[16 - distance : 32 - distance]
                total = total + shifted * taps_ref[9 + tap : 10 + tap, at]
                patch_taps[tap] = patch_taps[tap] + column_sum(shifted * masked)
            patches_back_ref[page, :, at] = total_back[first + span : first + row_count, at] + jnp.where(
                live, total, 0.0
            )
        for index, value in enumerate(text_taps):
            sums[0, 16 + index : 17 + index, at] = value
        for index, value in enumerate(patch_taps):
            if index == 0:
                sums[0, 23:24, at] = value
            else:
                sums[1, index - 1 : index, at] = value
        return carry

    early.take(2, 0)
    lax.fori_loop(0, width // 256, position_tile, 0)

    sum_partners = [opposite] + on_page
    sum_copies = [remote(sums.at[1 - core], sums_in.at[0], sum_send.at[0], sum_recv.at[0], *sibling)] + [
        remote(sums.at[core], sums_in.at[1 + index], sum_send.at[1 + index], sum_recv.at[1 + index], *partner)
        for index, partner in enumerate(sum_partners)
    ]
    last = remote(
        sums.at[core], sums_in.at[2 + levels], sum_send.at[2 + levels], sum_recv.at[2 + levels], *sibling
    )
    sum_copies[0].start()

    def sum_step(index):
        sum_copies[index].wait()
        sums[core] = sums[core] + sums_in[index]
        (sum_copies + [last])[index + 1].start()

    late_sum.take(0, 0)
    sum_step(0)
    late_sum.take(0, 1)
    sum_step(1)
    late_sum.take(1, 0)
    sum_step(2)
    for step in range(2, levels + 1):
        late_sum.take(step, 0)
        sum_step(step + 1)
    for step in range(3, levels + 1):
        early.take(step, 0)
    last.wait()
    sums_ref[core] = sums[core]
    sums_ref[1 - core] = sums_in[2 + levels]
    wide_rows = 4 * rows
    block = keep[0].astype(f32)
    low, high = block[:, 0 : lanes // 2], pltpu.roll(block, lanes // 2, 1)[:, 0 : lanes // 2]
    down_out[...] = low[0:wide_rows].astype(bf16)
    mixed_out[0:half, :] = jnp.where(core == 0, high[wide_rows:], low[wide_rows:]).astype(bf16)
    block = late[0, 0].astype(f32)
    low, high = block[:, 0 : lanes // 2], pltpu.roll(block, lanes // 2, 1)[:, 0 : lanes // 2]
    mixed_out[half:, :] = jnp.where(core == 0, high, low).astype(bf16)
    swaps = [
        remote(source, target, swap_send.at[index], swap_recv.at[index], *sibling)
        for index, (source, target) in enumerate(
            ((keep.at[0, 2 * rows : 4 * rows], up_in), (down_out, down_in), (mixed_out, mixed_in))
        )
    ]
    for copy in swaps:
        copy.start()
    early_ref[...] = keep[0]
    late_ref[...] = late[0, 0]
    for copy in swaps:
        copy.wait()
    up_in_ref[...] = up_in[...]
    down_in_ref[...] = down_in[...]
    mixed_in_ref[...] = mixed_in[...]
    early.finish()
    late_sum.finish()
    for page in range(count):
        sib_copy(page).wait_send()
        far_copy(page).wait_send()


def backward(pages, lengths, local_values, far_values, tokens, patches):
    count, span, width = tokens.shape
    patch_span = patches.shape[1]
    row_count = span + patch_span
    total_rows = count * row_count
    bundle, weights, keys = far_values[0], far_values[1], far_values[2]
    groups, grouped_rows, key_pad = weights.shape[1:]
    heads = groups * grouped_rows // row_count
    blocks, early_rows, lanes = bundle.shape[1:]
    late_rows = 3 * width // (2 * pages)
    levels = pages.bit_length() - 1
    bf16, f32, i32 = jnp.bfloat16, jnp.float32, jnp.int32
    dma = pltpu.SemaphoreType.DMA

    def landings(rows):
        return [VMEM((blocks >> (step + 1), rows, lanes), bf16) for step in range(levels + 1)]

    early_count = 8 + 4 + 2 + (levels - 1)
    late_count = 4 + 2 + levels
    return pl.pallas_call(
        staged(functools.partial(backward_kernel, pages), 1, len(local_values)),
        out_shape=(
            jax.ShapeDtypeStruct(tokens.shape, f32),
            jax.ShapeDtypeStruct(patches.shape, f32),
            jax.ShapeDtypeStruct((early_rows, lanes), bf16),
            jax.ShapeDtypeStruct((late_rows, lanes), bf16),
            jax.ShapeDtypeStruct((2, 24, width), f32),
            jax.ShapeDtypeStruct((early_rows // 9 * 4, lanes), bf16),
            jax.ShapeDtypeStruct((early_rows // 9 * 8, lanes // 2), bf16),
            jax.ShapeDtypeStruct((early_rows // 9 + late_rows, lanes // 2), bf16),
        ),
        in_specs=[pl.BlockSpec(memory_space=pltpu.SMEM)]
        + anywhere(len(local_values) + len(far_values)),
        out_specs=tuple(in_vmem(8)),
        scratch_shapes=[
            VMEM((blocks, early_rows, lanes), bf16),
            VMEM((blocks, early_rows, lanes), bf16),
            landings(early_rows),
            VMEM((2, blocks, late_rows, lanes), bf16),
            VMEM((blocks, late_rows, lanes), bf16),
            landings(late_rows),
            VMEM((2, groups, grouped_rows, key_pad), bf16),
            VMEM((2, key_pad, width), bf16),
            VMEM((2, key_pad, width), bf16),
            VMEM((count, 4, 2, row_count, width), bf16),
            VMEM((count, 2, 2, row_count, width), bf16),
            VMEM((count, 2, row_count, width), bf16),
            VMEM((3, width, width), bf16),
            VMEM((width, total_rows), bf16),
            VMEM((total_rows, width), f32),
            VMEM((total_rows, width), bf16),
            VMEM((total_rows, width), bf16),
            VMEM((total_rows, width), bf16),
            VMEM((grouped_rows, key_pad), f32),
            VMEM((grouped_rows, 3 * key_pad), bf16),
            VMEM((row_count, 2 * key_pad), bf16),
            VMEM((256, 3 * key_pad), bf16),
            VMEM((192, row_count), bf16),
            VMEM((row_count, 128), i32),
            VMEM((heads, 192, 128), f32),
            VMEM((heads, span + 64 + 2 * patch_span, 128), f32),
            VMEM((heads, 8, width), f32),
            VMEM((count, span + 32, width), bf16),
            VMEM((count, patch_span + 32, width), bf16),
            VMEM((2, 24, width), f32),
            VMEM((3 + levels, 24, width), f32),
            VMEM((early_rows // 9 * 4, lanes), bf16),
            VMEM((early_rows // 9 * 8, lanes // 2), bf16),
            VMEM((early_rows // 9 * 8, lanes // 2), bf16),
            VMEM((early_rows // 9 + late_rows, lanes // 2), bf16),
            VMEM((early_rows // 9 + late_rows, lanes // 2), bf16),
            dma((6,)), dma((3, 2)),
            dma((early_count,)), dma((early_count,)), dma((late_count,)), dma((late_count,)),
            dma((count,)), dma((count,)), dma((count,)), dma((count,)),
            dma((4,)), dma((4,)), dma((3 + levels,)), dma((3 + levels,)), dma((3,)), dma((3,)),
        ]
        + stage_for(local_values),
        compiler_params=pltpu.CompilerParams(
            collective_id=1, has_side_effects=True, vmem_limit_bytes=KERNEL_VMEM
        ),
        cost_estimate=pl.CostEstimate(flops=12_000_000_000, bytes_accessed=40_000_000, transcendentals=0),
        name="backward",
    )(lengths, *local_values, *far_values)


def clip_lanes(sums, centre, bins):
    first, last = centre + 1 - bins // 2, centre - 1 + bins // 2
    lane = lax.broadcasted_iota(jnp.int32, sums.shape, 1)
    below = jnp.sum(jnp.where(lane < first, sums, 0.0), axis=1, keepdims=True)
    above = jnp.sum(jnp.where(lane >= last, sums, 0.0), axis=1, keepdims=True)
    moved = pltpu.roll(sums, sums.shape[1] - (first - 1), 1)
    moved = jnp.where(lane == 0, below, jnp.where(lane == bins - 1, above, moved))
    return moved[:, :bins]


def finish_kernel(
    staging, early_ref, late_ref, sums_ref, up_in_ref, down_in_ref, mixed_in_ref,
    query_ref, key_ref, value_ref, out_ref, up_ref, down_ref, taps_ref, patch_taps_ref, line_ref, across_ref,
    upward_ref, vector_ref,
):
    f32 = jnp.float32
    rows, columns = query_ref.shape
    half = rows // 2
    wide_rows = 4 * rows
    first = position()[1] == 0
    for copy in staging:
        copy.wait()
    heads = line_ref.shape[0]
    block = early_ref[...].astype(f32)
    low, high = block[:, 0:columns], pltpu.roll(block, columns, 1)[:, 0:columns]
    up = jnp.where(first, block[0 : 2 * rows], up_in_ref[...].astype(f32))
    up_ref[:, 0 : 2 * columns] = up[0:rows]
    up_ref[:, 2 * columns : 4 * columns] = up[rows : 2 * rows]
    down_ref[...] = jnp.where(first, down_in_ref[...].astype(f32), high[0:wide_rows]).T
    kept = jnp.where(first, low[wide_rows:], high[wide_rows:])
    got = mixed_in_ref[0:half, :].astype(f32)
    out_ref[0:half, :] = jnp.where(first, kept, got)
    out_ref[half:rows, :] = jnp.where(first, got, kept)
    block = late_ref[...].astype(f32)
    low, high = block[:, 0:columns], pltpu.roll(block, columns, 1)[:, 0:columns]
    kept = jnp.where(first, low, high)
    got = mixed_in_ref[half:, :].astype(f32)
    query_ref[...] = jnp.where(first, kept[0:rows], got[0:rows])
    key_ref[...] = jnp.where(first, got[0:rows], kept[0:rows])
    value_ref[0:half, :] = jnp.where(first, kept[rows:], got[rows:])
    value_ref[half:rows, :] = jnp.where(first, got[rows:], kept[rows:])
    front, back = sums_ref[0], sums_ref[1]
    width = front.shape[1]
    text = [front[16 + index : 17 + index] for index in range(7)]
    order = [text[2], text[3], text[4], text[1], text[3], text[5], text[0], text[3], text[6]]
    taps_ref[...] = jnp.concatenate(order, axis=0)
    patch_taps_ref[...] = jnp.concatenate([front[23:24], back[0:8]], axis=0)
    across_ref[...] = clip_lanes(back[8:24, 0:256], 72, across_ref.shape[1])[0:heads]
    upward_ref[...] = clip_lanes(back[8:24, 256:512], 72, upward_ref.shape[1])[0:heads]
    line_ref[...] = clip_lanes(back[8:24, 512:640], 32, line_ref.shape[1])[0:heads]
    vector_ref[...] = front[0:16]


def finish(values, width, heads, line_bins, plane_bins):
    rows, columns = values[1].shape[0] * 2 // 3, values[1].shape[1] // 2
    f32 = jnp.float32
    square = jax.ShapeDtypeStruct((rows, columns), f32)
    taps = jax.ShapeDtypeStruct((9, width), f32)
    plane = jax.ShapeDtypeStruct((heads, plane_bins), f32)
    return pl.pallas_call(
        staged(finish_kernel, 0, len(values)),
        out_shape=(
            square, square, square, square,
            jax.ShapeDtypeStruct((rows, 4 * columns), f32),
            jax.ShapeDtypeStruct((columns, 4 * rows), f32),
            taps, taps,
            jax.ShapeDtypeStruct((heads, line_bins), f32), plane, plane,
            jax.ShapeDtypeStruct((16, width), f32),
        ),
        in_specs=anywhere(len(values)),
        out_specs=tuple(in_vmem(12)),
        scratch_shapes=stage_for(values),
        compiler_params=pltpu.CompilerParams(vmem_limit_bytes=KERNEL_VMEM),
        name="finish",
    )(*values)


def exchange(value, pages, step):
    moves = []
    for page in range(pages):
        for seq in range(4):
            on_page, on_seq = page, seq
            if (seq % 2 == step) if step < 2 else False:
                on_seq = seq ^ 2
            else:
                on_page = page ^ (1 if step < 2 else 1 << (step - 1))
            moves.append((page * 4 + seq, on_page * 4 + on_seq))
    return lax.ppermute(value, ("page", "seq"), moves)


def added(kept, got):
    return (kept.astype(jnp.float32) + got.astype(jnp.float32)).astype(jnp.bfloat16)


def bundle_sum(state, pages):
    for step in range(pages.bit_length()):
        half = state.shape[0] // 2
        state = added(state[:half], exchange(state[half:], pages, step))
    return state[0]


def bundle_parts(state, wide_rows, core):
    lanes = state.shape[1] // 2
    first = core == 0
    tail = state[wide_rows:]
    if wide_rows > 2 * tail.shape[0]:
        group = state[:wide_rows].reshape(4, wide_rows // 4, 2 * lanes)
        low = group[:2].transpose(1, 0, 2).reshape(-1, lanes)
        high = group[2:].transpose(1, 0, 2).reshape(-1, lanes)
    else:
        low, high = state[:wide_rows, :lanes], state[:wide_rows, lanes:]
    left, right = state[:wide_rows, :lanes], state[:wide_rows, lanes:]
    sent = jnp.concatenate(
        [jnp.where(first, high, left), jnp.where(first, tail[:, lanes:], tail[:, :lanes])], axis=0
    )
    got = swap(sent, "seq", 1)
    kept_tail = jnp.where(first, tail[:, :lanes], tail[:, lanes:])
    one = jnp.where(first, low, got[:wide_rows])
    two = jnp.where(first, got[:wide_rows], right)
    three = jnp.concatenate(
        [jnp.where(first, kept_tail, got[wide_rows:]), jnp.where(first, got[wide_rows:], kept_tail)], axis=0
    )
    return [value.astype(jnp.float32) for value in (one, two, three)]


def clipped(sums, centre, bins):
    first, last = centre + 1 - bins // 2, centre - 1 + bins // 2
    return jnp.concatenate(
        [
            jnp.sum(sums[..., :first], axis=-1, keepdims=True),
            sums[..., first:last],
            jnp.sum(sums[..., last:], axis=-1, keepdims=True),
        ],
        axis=-1,
    )


def grid_live(cells):
    return (cells // GRID_SIDE < GRID_SIDE - 1) & (cells % GRID_SIDE < GRID_SIDE - 1)


def grid_boxes(cells):
    return jnp.stack(
        [
            patch_pitch * (cells % GRID_SIDE) + patch_centre,
            patch_pitch * (cells // GRID_SIDE) + patch_centre,
        ]
    )


def shards(
    tokens,
    patches,
    page_length,
    box_position,
    query_weight,
    key_weight,
    value_weight,
    out_weight,
    up_weight,
    down_weight,
    conv_weight,
    patch_conv_weight,
    query_bias,
    value_bias,
    out_bias,
    up_bias,
    down_bias,
    attention_gain,
    attention_shift,
    feedforward_gain,
    feedforward_shift,
    reading_bias_table,
    horizontal_bias_table,
    vertical_bias_table,
    cotangent,
    patch_cotangent,
):
    conv_taps = conv_weight.astype(jnp.float32)
    patch_taps = patch_conv_weight.astype(jnp.float32)
    query_offset = query_bias.astype(jnp.float32)
    value_offset = value_bias.astype(jnp.float32)
    out_offset = out_bias.astype(jnp.float32)
    up_offset = up_bias.astype(jnp.float32)
    down_offset = down_bias.astype(jnp.float32)
    first_gain = attention_gain.astype(jnp.float32)
    first_shift = attention_shift.astype(jnp.float32)
    second_gain = feedforward_gain.astype(jnp.float32)
    second_shift = feedforward_shift.astype(jnp.float32)
    page_count, span_size, model_width = tokens.shape
    patch_span = patches.shape[1]
    seq_count = lax.axis_size("seq")
    slot_size = span_size * seq_count
    patch_slots = patch_span * seq_count
    row_count = span_size + patch_span
    key_count = row_count * seq_count
    head_count = reading_bias_table.shape[0]
    head_size = model_width // head_count
    line_bins = reading_bias_table.shape[1]
    plane_bins = horizontal_bias_table.shape[1]
    score_scale = head_size ** (-0.5)
    seq_index = lax.axis_index("seq")
    text_places = seq_index * span_size + jnp.arange(span_size, dtype=jnp.int32)
    local_cells = seq_index * patch_span + jnp.arange(patch_span, dtype=jnp.int32)
    text_live = text_places[None, :] < page_length[:, None]
    patch_live = grid_live(local_cells)
    text_factor = text_live[:, :, None]
    patch_factor = patch_live[None, :, None]
    masked = tokens * text_factor.astype(jnp.bfloat16)
    rimmed = with_halo(masked, (("seq", 1),), 3)
    reach = GRID_SIDE + 1
    patch_masked = patches * patch_factor.astype(jnp.bfloat16)
    patch_rimmed = with_halo(patch_masked, (("seq", 1),), reach)
    pages = lax.axis_size("page")
    table = jnp.concatenate(
        [
            horizontal_bias_table,
            vertical_bias_table,
            reading_bias_table,
            jnp.zeros((head_count, 256 - 2 * plane_bins - line_bins), jnp.bfloat16),
        ],
        axis=1,
    ).astype(jnp.float32)
    taps = jnp.pad(
        jnp.concatenate([conv_weight, patch_conv_weight], axis=1).astype(jnp.float32).T, ((0, 6), (0, 0))
    )
    vector_row = jnp.arange(8 + up_bias.shape[0] // model_width, dtype=jnp.int32)[:, None]
    vectors = jnp.pad(up_bias.reshape(-1, model_width), ((8, 0), (0, 0)))
    for index, vector in enumerate(
        (
            query_bias, value_bias, out_bias, down_bias, attention_gain, attention_shift, feedforward_gain,
            feedforward_shift,
        )
    ):
        vectors = jnp.where(vector_row == index, vector[None, :], vectors)
    vectors = vectors.astype(jnp.float32)
    (
        hidden, hidden_low, queries, mixture_low, columns, key_rows, query_rows, keys, values, weights,
    ) = forward(
        pages, page_length, tokens, patches, box_position, taps, (query_weight, key_weight, value_weight),
        vectors, table,
    )
    places = jnp.stack(
        [seq_index, seq_index % 2, lax.axis_index("page"), seq_index // 2]
    ).astype(jnp.int32)
    def flat(value):
        return value.reshape(-1, value.shape[-1])

    output, patch_output, delta_first, delta_mixture, middle_sums, feedforward_bundle = middle(
        places, hidden, mixture_low, cotangent, patch_cotangent,
        (out_weight, up_weight, down_weight), vectors, pages,
    )
    pair_rows = weights.reshape(page_count, head_count // 2, 2 * row_count, -1)
    if in_tiles(model_width, pages):
        tokens_gradient, patches_gradient, early_state, late_state, sums, up_in, down_in, mixed_in = backward(
            pages,
            page_length,
            (
                queries, delta_mixture, columns, key_rows, query_rows, tokens, patches, taps, middle_sums,
            ),
            (
                feedforward_bundle, pair_rows, keys, values, hidden_low, delta_first, query_weight, key_weight,
                value_weight,
            ),
            tokens,
            patches,
        )
        (
            query_part, key_part, value_part, out_part, up_part, down_part, text_part, patch_part, line_part,
            across_part, upward_part, vector_rows,
        ) = finish(
            (early_state, late_state, sums, up_in, down_in, mixed_in), model_width, head_count, line_bins,
            plane_bins,
        )
        return (
            output,
            patch_output,
            tokens_gradient,
            patches_gradient,
            query_part,
            key_part,
            value_part,
            out_part,
            up_part,
            down_part.T,
            text_part.T,
            patch_part.T,
            vector_rows[10],
            vector_rows[11],
            vector_rows[OUT_BIAS],
            vector_rows[UP_BIAS : UP_BIAS + 4].reshape(-1),
            vector_rows[DOWN_BIAS],
            vector_rows[FIRST_GAIN],
            vector_rows[FIRST_SHIFT],
            vector_rows[SECOND_GAIN],
            vector_rows[SECOND_SHIFT],
            line_part,
            across_part,
            upward_part,
        )
    delta_first = delta_first.reshape(page_count, row_count, model_width)
    delta_mixture = delta_mixture.reshape(page_count, row_count, model_width)
    early_state = added(feedforward_bundle[0], swap(feedforward_bundle[1], "seq", 1))
    delta_mixture, early_state = lax.optimization_barrier((delta_mixture, early_state))
    delta_query_pages, delta_key_pages, delta_value_pages = [], [], []
    delta_plane, delta_line = 0.0, 0.0
    for page in range(page_count):
        delta_page_queries, delta_blocks, plane_part, line_part = backward_page(
            places,
            columns[page][:, ::128],
            key_rows[page],
            query_rows[page][:, :row_count],
            queries[page * row_count : (page + 1) * row_count],
            keys[page],
            values[page],
            delta_mixture[page],
            pair_rows[page],
        )
        got = swap(delta_blocks[2:], "seq", 1)
        chip_sum = delta_blocks[:2].astype(jnp.float32) + got.astype(jnp.float32)
        got = swap(chip_sum[1].astype(jnp.bfloat16), "seq", 2)
        whole = (chip_sum[0] + got.astype(jnp.float32)).astype(jnp.bfloat16)
        delta_query_pages.append(delta_page_queries)
        delta_key_pages.append(whole[0])
        delta_value_pages.append(whole[1])
        delta_plane = delta_plane + plane_part
        delta_line = delta_line + line_part
    delta_queries = jnp.stack(delta_query_pages)
    delta_keys = jnp.stack(delta_key_pages)
    delta_values = jnp.stack(delta_value_pages)
    delta_plane = clipped(delta_plane, 72, plane_bins)
    delta_line = clipped(delta_line, 32, line_bins)
    delta_across, delta_upward = delta_plane[0], delta_plane[1]
    delta_query_offset = row_sum(delta_queries)
    delta_value_offset = row_sum(delta_values)
    delta_hidden = (
        delta_first
        + back_dot(delta_queries, query_weight)
        + back_dot(delta_keys, key_weight)
        + back_dot(delta_values, value_weight)
    )
    delta_position = delta_hidden[:, :span_size].astype(jnp.bfloat16)
    delta_rim = with_halo(delta_position, (("seq", 1),), 3)
    delta_masked = jnp.zeros((page_count, span_size, model_width), jnp.float32)
    tap_columns = []
    for dilation in (1, 2, 3):
        for offset in (-1, 0, 1):
            column = 3 * (dilation - 1) + offset + 1
            anchor = 3 + offset * dilation
            anchor_back = 3 - offset * dilation
            delta_masked = (
                delta_masked
                + delta_rim[:, anchor_back : anchor_back + span_size, :] * conv_taps[:, column]
            )
            tap_columns.append(
                jnp.einsum(
                    "ptd,ptd->d",
                    delta_position,
                    rimmed[:, anchor : anchor + span_size, :],
                    preferred_element_type=jnp.float32,
                )
            )
    delta_taps = jnp.stack(tap_columns, axis=1)
    tokens_gradient = delta_hidden[:, :span_size] + delta_masked * text_factor.astype(jnp.float32)
    delta_patch_position = delta_hidden[:, span_size:].astype(jnp.bfloat16)
    delta_patch_rim = with_halo(delta_patch_position, (("seq", 1),), reach)
    delta_patch_masked = jnp.zeros((page_count, patch_span, model_width), jnp.float32)
    patch_columns = []
    for vertical in (-1, 0, 1):
        for horizontal in (-1, 0, 1):
            column = 3 * (vertical + 1) + horizontal + 1
            anchor = reach + vertical * GRID_SIDE + horizontal
            anchor_back = reach - vertical * GRID_SIDE - horizontal
            delta_patch_masked = (
                delta_patch_masked
                + delta_patch_rim[:, anchor_back : anchor_back + patch_span, :]
                * patch_taps[:, column]
            )
            patch_columns.append(
                jnp.einsum(
                    "ptd,ptd->d",
                    delta_patch_position,
                    patch_rimmed[:, anchor : anchor + patch_span, :],
                    preferred_element_type=jnp.float32,
                )
            )
    delta_patch_taps = jnp.stack(patch_columns, axis=1)
    patches_gradient = delta_hidden[:, span_size:] + delta_patch_masked * patch_factor.astype(
        jnp.float32
    )
    operands = [flat(value) for value in (hidden_low, delta_queries, delta_keys, delta_values)]
    tail_bundle = indexed_bundle(
        (
            ((operands[0], operands[1], None), (operands[0], operands[3], 0)),
            ((operands[0], operands[2], None), (operands[0], operands[3], 1)),
        ),
        places,
        pages,
    )
    tail_state = added(tail_bundle[0], swap(tail_bundle[1], "seq", 1))
    query_part, key_part, value_part = bundle_parts(
        bundle_sum(tail_state, pages), model_width // pages, places[1]
    )
    up_part, down_part, out_part = bundle_parts(
        bundle_sum(early_state, pages), up_weight.shape[1] // pages, places[1]
    )
    up_part = up_part.reshape(model_width // pages, -1)
    matrix_parts = (query_part, key_part, value_part, out_part, up_part, down_part)
    vector_parts = total_sum(
        (
            delta_taps,
            delta_patch_taps,
            delta_query_offset,
            delta_value_offset,
            middle_sums[OUT_BIAS],
            middle_sums[UP_BIAS : UP_BIAS + 4].reshape(-1),
            middle_sums[DOWN_BIAS],
            middle_sums[FIRST_GAIN],
            middle_sums[FIRST_SHIFT],
            middle_sums[SECOND_GAIN],
            middle_sums[SECOND_SHIFT],
            delta_line,
            delta_across,
            delta_upward,
        )
    )
    return (
        output,
        patch_output,
        tokens_gradient,
        patches_gradient,
        matrix_parts[0],
        matrix_parts[1],
        matrix_parts[2],
        matrix_parts[3],
        matrix_parts[4],
        matrix_parts[5],
        vector_parts[0],
        vector_parts[1],
        vector_parts[2],
        vector_parts[3],
        vector_parts[4],
        vector_parts[5],
        vector_parts[6],
        vector_parts[7],
        vector_parts[8],
        vector_parts[9],
        vector_parts[10],
        vector_parts[11],
        vector_parts[12],
        vector_parts[13],
    )


def solution(mesh):
    in_specs = (
        P("page", "seq", None),
        P("page", "seq", None),
        P("page"),
        P(None, "page", None),
        P(),
        P(),
        P(),
        P(),
        P(),
        P(),
        P(),
        P(),
        P(),
        P(),
        P(),
        P(),
        P(),
        P(),
        P(),
        P(),
        P(),
        P(),
        P(),
        P(),
        P("page", "seq", None),
        P("page", "seq", None),
    )
    out_specs = (
        P("page", "seq", None),
        P("page", "seq", None),
        P("page", "seq", None),
        P("page", "seq", None),
        P("page", "seq"),
        P("page", "seq"),
        P("page", "seq"),
        P("page", "seq"),
        P("page", "seq"),
        P("page", "seq"),
        P(),
        P(),
        P(),
        P(),
        P(),
        P(),
        P(),
        P(),
        P(),
        P(),
        P(),
        P(),
        P(),
        P(),
    )
    return jax.shard_map(shards, mesh=mesh, in_specs=in_specs, out_specs=out_specs, check_vma=False)
```

```python
import functools

import jax
import jax.numpy as jnp
from jax import lax
from jax.experimental import pallas as pl
from jax.experimental.pallas import tpu as pltpu
from jax.sharding import PartitionSpec as P

GRID_SIDE = 8


epsilon = 1e-05
coordinate_step = 16
masked_score = -1000000000.0
patch_pitch = 146
patch_centre = 73


def with_halo(cells, sides, width):
    for axis, dim in sides:
        count = lax.axis_size(axis)
        ends = count - 1
        head = lax.slice_in_dim(cells, 0, width, axis=dim)
        tail = lax.slice_in_dim(cells, cells.shape[dim] - width, cells.shape[dim], axis=dim)
        cells = jnp.concatenate(
            [
                lax.ppermute(tail, axis, [(i, (i + 1) % count) for i in range(ends)]),
                cells,
                lax.ppermute(head, axis, [((i + 1) % count, i) for i in range(ends)]),
            ],
            axis=dim,
        )
    return cells


def layer_norm(values, gain_vector, shift_vector):
    row_mean = jnp.mean(values, axis=-1, keepdims=True)
    centred = values - row_mean
    variance = jnp.mean(centred * centred, axis=-1, keepdims=True)
    return centred * lax.rsqrt(variance + epsilon) * gain_vector + shift_vector


def gelu_exact(values):
    return jax.nn.gelu(values, approximate=False)


def flat_dot(operand, matrix):
    front = operand.shape[:-1]
    result = jnp.dot(
        operand.reshape(-1, operand.shape[-1]), matrix, preferred_element_type=jnp.float32
    )
    return result.reshape(front + (matrix.shape[-1],))


def back_dot(operand, matrix):
    front = operand.shape[:-1]
    result = lax.dot_general(
        operand.reshape(-1, operand.shape[-1]),
        matrix,
        (((1,), (1,)), ((), ())),
        preferred_element_type=jnp.float32,
    )
    return result.reshape(front + (matrix.shape[0],))


def outer_dot(operand, gradient):
    return lax.dot_general(
        operand.reshape(-1, operand.shape[-1]),
        gradient.reshape(-1, gradient.shape[-1]),
        (((0,), (0,)), ((), ())),
        preferred_element_type=jnp.float32,
    )


def row_sum(gradient):
    return jnp.sum(gradient.astype(jnp.float32).reshape(-1, gradient.shape[-1]), axis=0)


def swap(value, axis, bit):
    count = lax.axis_size(axis)
    return lax.ppermute(value, axis, [(i, i ^ bit) for i in range(count)])


def total_sum(vectors):
    flat = jnp.concatenate([vector.reshape(-1) for vector in vectors])
    flat = jnp.pad(flat, (0, -flat.size % 1024)).reshape(-1, 128)
    for bit in (1, 2):
        flat = flat + swap(flat, "seq", bit)
    bit = 1
    while bit < lax.axis_size("page"):
        flat = flat + swap(flat, "page", bit)
        bit *= 2
    flat = flat.reshape(-1)
    result, start = [], 0
    for vector in vectors:
        result.append(flat[start : start + vector.size].reshape(vector.shape))
        start += vector.size
    return result


def query_places(seq_index, shape, span, patch_span, text_slots):
    row = lax.broadcasted_iota(jnp.int32, shape, 0)
    return jnp.where(
        row < span, seq_index * span + row, text_slots + seq_index * patch_span + row - span
    )


FIXED = 2048.0


def lookup(table_row, lanes):
    return jnp.take_along_axis(jnp.broadcast_to(table_row, lanes.shape), lanes, axis=1)


HEAD_LANES = 64


def split_heads(group):
    lane = lax.broadcasted_iota(jnp.int32, group.shape, 1) // HEAD_LANES
    zero = jnp.zeros_like(group)
    return jnp.concatenate(
        [jnp.where(lane == head, group, zero) for head in range(group.shape[1] // HEAD_LANES)], axis=0
    )


def merge_heads(rows):
    heads = rows.shape[1] // HEAD_LANES
    count = rows.shape[0] // heads
    lane = lax.broadcasted_iota(jnp.int32, (count, rows.shape[1]), 1) // HEAD_LANES
    merged = rows[:count]
    for head in range(1, heads):
        merged = jnp.where(lane == head, rows[head * count : (head + 1) * count], merged)
    return merged


def dot_nt(left, right):
    return lax.dot_general(left, right, (((1,), (1,)), ((), ())), preferred_element_type=jnp.float32)


def dot_nn(left, right):
    return lax.dot_general(left, right, (((1,), (0,)), ((), ())), preferred_element_type=jnp.float32)


def dot_tn(left, right):
    return lax.dot_general(left, right, (((0,), (0,)), ((), ())), preferred_element_type=jnp.float32)


CHUNK = 16


MESH = pl.DeviceIdType.MESH


def places_of(pages):
    page = lax.axis_index("page")
    seq = lax.axis_index("seq")
    bits = []
    rest = page
    for _ in range(pages.bit_length() - 1):
        bits.append(rest % 2)
        rest = rest // 2
    return page, bits, seq, seq // 2, seq % 2


def sibling_of(seq):
    return seq + 1 - 2 * (seq % 2)


def across_of(seq):
    return seq + 2 - 4 * (seq // 2)


def remote(source, target, send, receive, page, seq):
    return pltpu.make_async_remote_copy(
        src_ref=source, dst_ref=target, send_sem=send, recv_sem=receive, device_id=(page, seq), device_id_type=MESH
    )


def column_of(row):
    square = jnp.broadcast_to(row.astype(jnp.float32), (128, 128)).T
    return square[:, 0:1].astype(jnp.int32)


def forward_kernel(
    pages,
    staging, length_ref, box_ref, text_taps_ref, patch_taps_ref, across_table_ref, upward_table_ref, line_table_ref,
    query_bias_ref, value_bias_ref, tokens_any, patches_any, query_weight_any, key_weight_any, value_weight_any,
    hidden_ref, hidden_low_ref, query_ref, mixture_ref, columns_ref, rows_ref, query_rows_ref, taps_ref, key_any,
    value_any, weights_any,
    own, matrices, key_ref, value_ref, weights_ref, arrived, text, grid, low, scores, across_ref, upward_ref,
    live_ref, line_ref, packed_ref, table_ref, vector_ref,
    load_sem, store_sem, send_sem, recv_sem,
):
    page_at, _, seq, _, _ = places_of(pages)
    count, span, width = tokens_any.shape
    patch_span = patches_any.shape[1]
    row_count = span + patch_span
    key_pad = key_ref.shape[1]
    text_slots = 4 * span
    rim = 8
    loads = [
        pltpu.make_async_copy(source, target, load_sem.at[index])
        for index, (source, target) in enumerate(
            (
                (tokens_any, own.at[:, 0:span]), (patches_any, own.at[:, span:row_count]),
                (key_weight_any, matrices.at[1]), (value_weight_any, matrices.at[2]), (query_weight_any, matrices.at[0]),
            )
        )
    ]
    for copy in loads:
        copy.start()

    def stores(page):
        return [
            pltpu.make_async_copy(source.at[page], target.at[page], store_sem.at[index, page])
            for index, (source, target) in enumerate(
                ((key_ref, key_any), (value_ref, value_any), (weights_ref, weights_any))
            )
        ]

    groups = weights_ref.shape[1]
    members = weights_ref.shape[2] // row_count
    pairs = groups * members // 2
    peers = (sibling_of(seq), across_of(seq))
    barrier = pltpu.get_barrier_semaphore()
    for peer in peers:
        pl.semaphore_signal(barrier, inc=1, device_id=(page_at, peer), device_id_type=MESH)
    pl.semaphore_wait(barrier, 2)

    def first_copies(page, side):
        return (
            remote(
                tokens_any.at[page], arrived.at[side, page, 0:span], send_sem.at[2 * side, page],
                recv_sem.at[2 * side, page], page_at, peers[side],
            ),
            remote(
                patches_any.at[page], arrived.at[side, page, span:row_count], send_sem.at[2 * side + 1, page],
                recv_sem.at[2 * side + 1, page], page_at, peers[side],
            ),
        )

    def onward_copy(page):
        return remote(
            arrived.at[1, page], arrived.at[2, page], send_sem.at[4, page], recv_sem.at[4, page], page_at, peers[0]
        )

    for page in range(count):
        for side in range(2):
            for copy in first_copies(page, side):
                copy.start()

    for copy in staging:
        copy.wait()
    table_ref[...] = jnp.zeros_like(table_ref)
    start = 0
    for source in (across_table_ref, upward_table_ref, line_table_ref):
        heads, bins = source.shape
        table_ref[0:heads, start : start + bins] = source[...].astype(jnp.float32)
        start += bins
    steps = jnp.floor(table_ref[...] * FIXED + 0.5).astype(jnp.int32)
    vector_ref[0:1, :] = query_bias_ref[...].astype(jnp.float32).reshape(1, width)
    vector_ref[1:2, :] = value_bias_ref[...].astype(jnp.float32).reshape(1, width)
    taps_ref[...] = jnp.zeros_like(taps_ref)
    taps_ref[0:9, :] = text_taps_ref[...].astype(jnp.float32)
    taps_ref[9:18, :] = patch_taps_ref[...].astype(jnp.float32)
    for pair in range(pairs):
        words = (steps[2 * pair : 2 * pair + 1] + 8192) + steps[2 * pair + 1 : 2 * pair + 2] * 65536
        packed_ref[0, pair : pair + 1, :] = words[:, 0:128]
        packed_ref[1, pair : pair + 1, :] = words[:, 128:256]
    key = lax.broadcasted_iota(jnp.int32, (row_count, key_pad), 1)
    place = query_places(seq, (row_count, key_pad), span, patch_span, text_slots)
    across_ref[...] = jnp.clip(key - place, -16, 15) + 16

    def fill(pair, carry):
        row = packed_ref[1, pl.ds(pair, 1), :]
        for at in range(0, key_pad, 128):
            line_ref[pair, :, at : at + 128] = lookup(row, across_ref[:, at : at + 128])
        return carry

    lax.fori_loop(0, pairs, fill, 0)
    text[0:rim, :] = jnp.zeros((rim, width), jnp.float32)
    text[rim + text_slots :, :] = jnp.zeros((rim, width), jnp.float32)
    grid[0:patch_span, :] = jnp.zeros((patch_span, width), jnp.float32)
    grid[patch_span * 5 :, :] = jnp.zeros((patch_span, width), jnp.float32)
    low[row_count * 4 :, :] = jnp.zeros((key_pad - row_count * 4, width), jnp.bfloat16)
    lanes = 256
    group_width = members * HEAD_LANES
    power = 1.4426950408889634 / FIXED
    for copy in first_copies(0, 1):
        copy.wait_recv()
    onward_copy(0).start()
    for copy in loads:
        copy.wait()

    def page_step(page, carry):
        length = length_ref[page]
        base = page * row_count
        cell = lax.broadcasted_iota(jnp.int32, (1, 128), 1)
        query_cell = seq * patch_span + cell
        row_cell = seq * patch_span + lax.broadcasted_iota(jnp.int32, (patch_span, 1), 0)
        for plane in range(2):
            box = box_ref[page, plane : plane + 1, :]
            patch = 146 * ((cell % GRID_SIDE) if plane == 0 else (cell // GRID_SIDE)) + 73
            own_patch = 146 * ((query_cell % GRID_SIDE) if plane == 0 else (query_cell // GRID_SIDE)) + 73
            column_patch = 146 * ((row_cell % GRID_SIDE) if plane == 0 else (row_cell // GRID_SIDE)) + 73
            rows_ref[page, plane : plane + 1, 0:text_slots] = box
            rows_ref[page, plane : plane + 1, text_slots:key_pad] = patch
            own_box = rows_ref[page, plane : plane + 1, pl.ds(pl.multiple_of(seq * span, 128), span)]
            query_rows_ref[page, plane : plane + 1, 0:span] = own_box
            query_rows_ref[page, plane : plane + 1, span:256] = own_patch
            columns_ref[page, 0:span, plane * 128 : (plane + 1) * 128] = jnp.broadcast_to(
                column_of(own_box), (span, 128)
            )
            columns_ref[page, span:row_count, plane * 128 : (plane + 1) * 128] = jnp.broadcast_to(
                column_patch, (patch_span, 128)
            )
        for plane, lanes_ref in enumerate((across_ref, upward_ref)):
            difference = rows_ref[page, plane : plane + 1, :] - columns_ref[page, :, plane * 128 : plane * 128 + 1]
            lanes_ref[...] = jnp.clip(difference >> 4, -32, 31) + (32 + 64 * plane)
        key_at = lax.broadcasted_iota(jnp.int32, live_ref.shape, 1)
        key_cell = key_at - text_slots
        live = (key_at < length) | (
            (key_cell >= 0) & ((key_cell >> 3) < GRID_SIDE - 1) & ((key_cell & 7) < GRID_SIDE - 1)
        )
        live_ref[...] = jnp.where(live, 0.0, masked_score * FIXED)
        for copy in first_copies(page, 0):
            copy.wait_recv()
        onward_copy(page).wait_recv()

        def block_of(step, start, stop, at):
            if step:
                return arrived[step - 1, page, start:stop, at].astype(jnp.float32)
            if start:
                return own[page, span:row_count, at].astype(jnp.float32)
            return own[page, 0:span, at].astype(jnp.float32)

        def slot_of(step):
            return (seq, peers[0], peers[1], sibling_of(peers[1]))[step]

        everything = slice(0, width)
        for step in range(4):
            where = slot_of(step)
            at_place = where * span + lax.broadcasted_iota(jnp.int32, (span, 1), 0)
            text[pl.ds(pl.multiple_of(rim + where * span, 8), span), :] = jnp.where(
                at_place < length, block_of(step, 0, span, everything), 0.0
            )
            at_cell = where * patch_span + lax.broadcasted_iota(jnp.int32, (patch_span, 1), 0)
            cell_live = ((at_cell >> 3) < GRID_SIDE - 1) & ((at_cell & 7) < GRID_SIDE - 1)
            grid[pl.ds(pl.multiple_of(patch_span + where * patch_span, 8), patch_span), :] = jnp.where(
                cell_live, block_of(step, span, row_count, everything), 0.0
            )
        for step in range(4):
            where = slot_of(step)

            def convolve(tile, carry):
                at = pl.ds(pl.multiple_of(tile * lanes, lanes), lanes)
                window = text[pl.ds(pl.multiple_of(where * span, 8), span + 2 * rim), at]
                centre = taps_ref[1:2, at] + taps_ref[4:5, at] + taps_ref[7:8, at]
                total = block_of(step, 0, span, at) + window[rim : rim + span] * centre
                for dilation in (1, 2, 3):
                    for offset in (-1, 1):
                        tap = 3 * (dilation - 1) + offset + 1
                        anchor = rim + offset * dilation
                        total = total + window[anchor : anchor + span] * taps_ref[tap : tap + 1, at]
                low[pl.ds(pl.multiple_of(where * span, 16), span), at] = total.astype(jnp.bfloat16)
                window = grid[pl.ds(pl.multiple_of(where * patch_span, 8), 3 * patch_span), at]
                patch_total = block_of(step, span, row_count, at)
                for vertical in (-1, 0, 1):
                    for horizontal in (-1, 0, 1):
                        tap = 9 + 3 * (vertical + 1) + horizontal + 1
                        anchor = patch_span + vertical * GRID_SIDE + horizontal
                        patch_total = patch_total + window[anchor : anchor + patch_span] * taps_ref[tap : tap + 1, at]
                low[pl.ds(pl.multiple_of(text_slots + where * patch_span, 16), patch_span), at] = (
                    patch_total.astype(jnp.bfloat16)
                )
                if step == 0:
                    for first, rows_here, value in ((0, span, total), (span, patch_span, patch_total)):
                        here = pl.ds(pl.multiple_of(base + first, 16), rows_here)
                        hidden_ref[here, at] = value
                        hidden_low_ref[here, at] = value.astype(jnp.bfloat16)
                return carry

            lax.fori_loop(0, width // lanes, convolve, 0)
        own_rows = pl.ds(pl.multiple_of(base, 16), row_count)

        key_ref[page] = dot_nn(low[...], matrices[1]).astype(jnp.bfloat16)
        value_ref[page] = (dot_nn(low[...], matrices[2]) + vector_ref[1:2, :]).astype(jnp.bfloat16)
        query_ref[own_rows, :] = (
            (dot_nn(hidden_low_ref[own_rows, :], matrices[0]) + vector_ref[0:1, :]).astype(jnp.bfloat16)
            * jnp.bfloat16(0.125)
        )

        @pl.when(page < count - 1)
        def _():
            for copy in first_copies(page + 1, 1):
                copy.wait_recv()
            onward_copy(page + 1).start()

        def attend(group, carry):
            at = pl.ds(pl.multiple_of(group * group_width, group_width), group_width)
            scores[...] = dot_nt(split_heads(query_ref[own_rows, at] * jnp.bfloat16(FIXED)), key_ref[page, :, at])
            for start, sub in ((start, sub) for start in range(0, row_count, CHUNK) for sub in range(members // 2)):
                pair = group * (members // 2) + sub
                plane_row = packed_ref[0, pl.ds(pair, 1), :]
                here = slice(start, start + CHUNK)
                packed = []
                for block_at in range(0, key_pad, 128):
                    lane = slice(block_at, block_at + 128)
                    packed.append(
                        line_ref[pair, here, lane]
                        + lookup(plane_row, across_ref[here, lane])
                        + lookup(plane_row, upward_ref[here, lane])
                    )
                for side in range(2):
                    first = (2 * sub + side) * row_count + start
                    there = slice(first, first + CHUNK)
                    parts, top = [], None
                    for index, word in enumerate(packed):
                        lane = slice(128 * index, 128 * (index + 1))
                        field = (word >> 16) if side else (word & 0xFFFF)
                        part = (scores[there, lane] + field.astype(jnp.float32)) + live_ref[0:1, lane]
                        top = part if top is None else jnp.maximum(top, part)
                        parts.append(part)
                    top = jnp.max(top, axis=1, keepdims=True)
                    parts = [jnp.exp2((part - top) * power) for part in parts]
                    total = parts[0]
                    for part in parts[1:]:
                        total = total + part
                    inverse = 1.0 / jnp.sum(total, axis=1, keepdims=True)
                    for index, part in enumerate(parts):
                        weights_ref[page, group, there, 128 * index : 128 * (index + 1)] = (part * inverse).astype(
                            jnp.bfloat16
                        )
            mixture_ref[own_rows, at] = merge_heads(
                dot_nn(weights_ref[page, group], value_ref[page, :, at])
            ).astype(jnp.bfloat16)
            return carry

        lax.fori_loop(0, groups, attend, 0)
        for copy in stores(page):
            copy.start()
        return carry

    lax.fori_loop(0, count, page_step, 0)
    for page in range(count):
        for side in range(2):
            for copy in first_copies(page, side):
                copy.wait_send()
        onward_copy(page).wait_send()
        for copy in stores(page):
            copy.wait()


VMEM = pltpu.VMEM
KERNEL_VMEM = 62 * 1024 * 1024


def in_vmem(count):
    return [pl.BlockSpec(memory_space=VMEM)] * count


def staged(kernel, first, count):
    def run(*refs):
        *refs, semaphore = refs
        refs, buffers = list(refs[:-count]), refs[-count:]
        copies = [
            pltpu.make_async_copy(refs[first + index], buffers[index], semaphore.at[index]) for index in range(count)
        ]
        for copy in copies:
            copy.start()
        refs[first : first + count] = buffers
        kernel(copies, *refs)

    return run


def stage_for(values):
    return [VMEM(value.shape, value.dtype) for value in values] + [pltpu.SemaphoreType.DMA((len(values),))]


def position():
    seq = lax.axis_index("seq")
    return seq, seq % 2, lax.axis_index("page"), seq // 2


def anywhere(count):
    return [pl.BlockSpec(memory_space=pl.ANY)] * count


def forward(pages, lengths, tokens, patches, box, taps, tables, biases, matrices):
    count, span, width = tokens.shape
    patch_span = patches.shape[1]
    row_count = span + patch_span
    total_rows = count * row_count
    key_pad = -(-4 * row_count // 128) * 128
    heads = tables[0].shape[0]
    pairs = heads // 2
    members = 4 if heads % 4 == 0 else 2
    groups = heads // members
    small = (box, *taps, *tables, *biases)
    bf16, f32, i32 = jnp.bfloat16, jnp.float32, jnp.int32
    own = jax.ShapeDtypeStruct((total_rows, width), bf16)
    every = jax.ShapeDtypeStruct((count, key_pad, width), bf16)
    return pl.pallas_call(
        staged(functools.partial(forward_kernel, pages), 1, len(small)),
        out_shape=(
            jax.ShapeDtypeStruct((total_rows, width), f32), own, own, own,
            jax.ShapeDtypeStruct((count, row_count, 256), i32),
            jax.ShapeDtypeStruct((count, 8, key_pad), i32),
            jax.ShapeDtypeStruct((count, 8, 256), i32),
            jax.ShapeDtypeStruct((24, width), f32),
            every, every,
            jax.ShapeDtypeStruct((count, groups, members * row_count, key_pad), bf16),
        ),
        in_specs=[pl.BlockSpec(memory_space=pltpu.SMEM)] + anywhere(len(small) + 5),
        out_specs=tuple(in_vmem(8) + anywhere(3)),
        scratch_shapes=[
            VMEM((count, row_count, width), bf16),
            VMEM((3, width, width), bf16),
            VMEM((count, key_pad, width), bf16),
            VMEM((count, key_pad, width), bf16),
            VMEM((count, groups, members * row_count, key_pad), bf16),
            VMEM((3, count, row_count, width), bf16),
            VMEM((4 * span + 16, width), f32),
            VMEM((6 * patch_span, width), f32),
            VMEM((key_pad, width), bf16),
            VMEM((members * row_count, key_pad), f32),
            VMEM((row_count, key_pad), i32),
            VMEM((row_count, key_pad), i32),
            VMEM((8, key_pad), f32),
            VMEM((pairs, row_count, key_pad), i32),
            VMEM((2, 8, 128), i32),
            VMEM((-(-heads // 8) * 8, 256), f32),
            VMEM((8, width), f32),
            pltpu.SemaphoreType.DMA((5,)),
            pltpu.SemaphoreType.DMA((3, count)),
            pltpu.SemaphoreType.DMA((5, count)),
            pltpu.SemaphoreType.DMA((5, count)),
        ]
        + stage_for(small),
        compiler_params=pltpu.CompilerParams(
            collective_id=0, has_side_effects=True, vmem_limit_bytes=KERNEL_VMEM
        ),
        cost_estimate=pl.CostEstimate(flops=8_000_000_000, bytes_accessed=25_000_000, transcendentals=3_000_000),
        name="forward",
    )(lengths, *small, tokens, patches, *matrices)


def backward_page_kernel(
    scalar_ref, columns_ref, rows_ref, query_rows_ref, query_ref, key_ref, value_ref, mixture_back_ref, weights_ref,
    query_back_ref, block_back_ref, plane_back_ref, line_back_ref,
    back, steps, mask_ref, hot_ref, query_hot_ref, band_ref,
):
    seq_index = scalar_ref[0]
    row_count, width = query_ref.shape
    key_pad = key_ref.shape[0]
    count = 4
    patch_span = GRID_SIDE * GRID_SIDE // count
    span = row_count - patch_span
    text_slots = span * count
    columns, rows = columns_ref[...], rows_ref[...]
    mask_ref[:, 0:key_pad] = ((rows[0:1, :] & 15) < (columns[:, 0:1] & 15)).astype(jnp.float32).astype(jnp.bfloat16)
    mask_ref[:, key_pad:] = ((rows[1:2, :] & 15) < (columns[:, 1:2] & 15)).astype(jnp.float32).astype(jnp.bfloat16)
    bin_at = lax.broadcasted_iota(jnp.int32, (128, key_pad), 0) - 1
    key_block = lax.broadcasted_iota(jnp.int32, (128, key_pad), 1) >> 4
    for side in range(2):
        key_bin = rows[side : side + 1, :] >> 4
        plain = (key_bin == bin_at).astype(jnp.float32)
        lower = (key_bin - 1 == bin_at).astype(jnp.float32)
        plain, lower = jnp.where(bin_at < 64, plain, 0.0), jnp.where(bin_at < 64, lower, 0.0)
        mine = slice(128 * side, 128 * (side + 1))
        other = slice(128 * (1 - side), 128 * (2 - side))
        change = lower - plain
        if side == 0:
            plain = jnp.where(bin_at - 71 == key_block, 1.0, plain)
        hot_ref[mine, 0:key_pad] = plain.astype(jnp.bfloat16)
        hot_ref[mine, (1 + side) * key_pad : (2 + side) * key_pad] = change.astype(jnp.bfloat16)
        hot_ref[other, (1 + side) * key_pad : (2 + side) * key_pad] = jnp.zeros((128, key_pad), jnp.bfloat16)
    half_bin = lax.broadcasted_iota(jnp.int32, (72, row_count), 0)
    for side in range(2):
        query_hot_ref[72 * side : 72 * (side + 1), :] = (
            (71 - (query_rows_ref[side : side + 1, :] >> 4) == half_bin).astype(jnp.float32).astype(jnp.bfloat16)
        )
    lane128 = lax.broadcasted_iota(jnp.int32, (row_count, 128), 1)
    place = query_places(seq_index, (row_count, 128), span, patch_span, text_slots)
    aim = place + lane128 - 32
    near = (lane128 < 64) & (aim >= 0) & (aim < text_slots + patch_span * count)
    apart = (aim >> 4) - (place >> 4)
    near = near & (apart >= -1) & (apart <= 1)
    band_ref[...] = jnp.where(near, aim, -1)
    pair_width = 128
    line_back_ref[...] = jnp.zeros_like(line_back_ref)
    plane_back_ref[...] = jnp.zeros_like(plane_back_ref)

    def attend(pair, carry):
        at = pl.ds(pl.multiple_of(pair * pair_width, pair_width), pair_width)
        both_query = split_heads(query_ref[:, at])
        both_back = split_heads(mixture_back_ref[:, at])
        back[...] = dot_nt(both_back, value_ref[:, at])
        for start in range(0, 2 * row_count, CHUNK):
            there = slice(start, start + CHUNK)
            here = slice(start % row_count, start % row_count + CHUNK)
            parts, total = [], None
            for block_at in range(0, key_pad, 128):
                lane = slice(block_at, block_at + 128)
                part = weights_ref[pair, there, lane].astype(jnp.float32)
                product = part * back[there, lane]
                total = product if total is None else total + product
                parts.append(part)
            mean = jnp.sum(total, axis=1, keepdims=True)
            for index, part in enumerate(parts):
                lane = slice(128 * index, 128 * (index + 1))
                step = (part * (back[there, lane] - mean)).astype(jnp.bfloat16)
                steps[there, lane] = step
                steps[there, key_pad + 128 * index : key_pad + 128 * (index + 1)] = step * mask_ref[here, lane]
                steps[there, 2 * key_pad + 128 * index : 2 * key_pad + 128 * (index + 1)] = (
                    step * mask_ref[here, key_pad + 128 * index : key_pad + 128 * (index + 1)]
                )
        query_back_ref[:, at] = (merge_heads(dot_nn(steps[:, 0:key_pad], key_ref[:, at])) * 0.125).astype(
            jnp.bfloat16
        )
        for kind, value in enumerate(
            (dot_tn(steps[:, 0:key_pad], both_query), dot_tn(weights_ref[pair], both_back))
        ):
            value = value.astype(jnp.bfloat16)
            for where in range(count):
                step_at = seq_index ^ where
                slot = (step_at & 1) * 2 + (step_at >> 1)
                block_back_ref[slot, kind, 0:span, at] = value[where * span : (where + 1) * span]
                block_back_ref[slot, kind, span:row_count, at] = value[
                    text_slots + where * patch_span : text_slots + (where + 1) * patch_span
                ]
        bins = dot_nt(steps[...], hot_ref[...])
        low_bins = bins.astype(jnp.bfloat16)
        lane_one = lax.broadcasted_iota(jnp.int32, (1, 128), 1)
        far = lane128 - 72 - (place >> 4)
        in_line = (lane128 >= 72) & (lane128 < 72 + key_pad // 16)
        for side in range(2):
            head = pl.ds(2 * pair + side, 1)
            own = slice(side * row_count, (side + 1) * row_count)
            both = dot_nn(query_hot_ref[...], low_bins[own])
            for plane in range(2):
                table = both[72 * plane : 72 * (plane + 1), 128 * plane : 128 * (plane + 1)]
                wide_lane = lax.broadcasted_iota(jnp.int32, table.shape, 1)
                table = jnp.where(wide_lane < 72, table, 0.0)
                table = jnp.concatenate([table, jnp.zeros_like(table)], axis=1)
                sheared = pltpu.roll(table, 0, 1, stride=1, stride_axis=0)
                plane_back_ref[plane, head, :] = jnp.sum(sheared, axis=0, keepdims=True)
            line_bins = bins[own, 0:128]
            low_tail = jnp.sum(jnp.where(in_line & (far <= -2), line_bins, 0.0), axis=(0, 1), keepdims=True)
            high_tail = jnp.sum(jnp.where(in_line & (far >= 2), line_bins, 0.0), axis=(0, 1), keepdims=True)
            band = jnp.zeros((1, 128), jnp.float32)
            base = side * row_count
            for first, rows_here, block in (
                (0, span, seq_index),
                (0, 32, jnp.maximum(seq_index - 1, 0)),
                (span - 32, 32, seq_index + 1),
                (span, patch_span, count - 1),
                (span, patch_span, count),
            ):
                aims = band_ref[first : first + rows_here, :]
                source = steps[
                    base + first : base + first + rows_here, pl.ds(pl.multiple_of(block * 128, 128), 128)
                ].astype(jnp.float32)
                taken = jnp.take_along_axis(source, aims & 127, axis=1)
                right = (aims >> 7) == block
                if first == 0 and rows_here == 32:
                    right = right & (seq_index > 0)
                band = band + jnp.sum(jnp.where(right, taken, 0.0), axis=0, keepdims=True)
            line_back_ref[head, :] = (
                band + jnp.where(lane_one == 0, low_tail, 0.0) + jnp.where(lane_one == 63, high_tail, 0.0)
            )
        return carry

    lax.fori_loop(0, width // pair_width, attend, 0)


def backward_page(scalars, columns, rows, query_rows, queries, keys, values, mixture_back, weights):
    row_count, width = queries.shape
    key_pad = keys.shape[0]
    heads = 2 * weights.shape[0]
    return pl.pallas_call(
        backward_page_kernel,
        out_shape=(
            jax.ShapeDtypeStruct((row_count, width), jnp.bfloat16),
            jax.ShapeDtypeStruct((4, 2, row_count, width), jnp.bfloat16),
            jax.ShapeDtypeStruct((2, heads, 256), jnp.float32),
            jax.ShapeDtypeStruct((heads, 128), jnp.float32),
        ),
        in_specs=[pl.BlockSpec(memory_space=pltpu.SMEM)] + in_vmem(8),
        out_specs=tuple(in_vmem(4)),
        scratch_shapes=[
            pltpu.VMEM((2 * row_count, key_pad), jnp.float32),
            pltpu.VMEM((2 * row_count, 3 * key_pad), jnp.bfloat16),
            pltpu.VMEM((row_count, 2 * key_pad), jnp.bfloat16),
            pltpu.VMEM((256, 3 * key_pad), jnp.bfloat16),
            pltpu.VMEM((144, row_count), jnp.bfloat16),
            pltpu.VMEM((row_count, 128), jnp.int32),
        ],
        compiler_params=pltpu.CompilerParams(vmem_limit_bytes=KERNEL_VMEM),
        cost_estimate=pl.CostEstimate(flops=3_000_000_000, bytes_accessed=6_000_000, transcendentals=1_000_000),
        name="backward_page",
    )(scalars, columns, rows, query_rows, queries, keys, values, mixture_back, weights)


def early_orders(far, side):
    return (far[1], far[0], side) + tuple(far[2:]), (far[0], far[1], side) + tuple(far[2:])


def slot_of_bits(bits):
    slot = 0
    for bit in bits:
        slot = slot * 2 + bit
    return slot


def apart(one, other):
    return (one + other) % 2


def early_slots(scalar_ref, page, column, levels):
    far = [apart((page >> level) & 1, (scalar_ref[2] >> level) & 1) for level in range(levels)]
    side = apart(column, scalar_ref[3])
    return [slot_of_bits(order) for order in early_orders(far, side)]


NORM_CHUNK = 48


def norm_rows(values):
    mean = jnp.mean(values, axis=-1, keepdims=True)
    centred = values - mean
    scale = lax.rsqrt(jnp.mean(centred * centred, axis=-1, keepdims=True) + epsilon)
    return centred * scale, scale


def norm_back(delta, unit, scale):
    return scale * (
        delta
        - jnp.mean(delta, axis=-1, keepdims=True)
        - unit * jnp.mean(delta * unit, axis=-1, keepdims=True)
    )


def column_sum(values):
    return jnp.sum(values, axis=0, keepdims=True)


OUT_BIAS, DOWN_BIAS, FIRST_GAIN, FIRST_SHIFT, SECOND_GAIN, SECOND_SHIFT = range(6)
UP_BIAS = 6


def middle_kernel(
    pages, direct,
    *rest,
):
    scalar_ref = position()
    arguments, rest = rest[:14], rest[14:]
    output_ref, patch_output_ref, first_back_ref, mixture_back_ref, sums_ref, *rest = rest
    *rest, vector_ref, load_sem, store_sem = rest
    copied, rest = rest[-14:], rest[:-14]
    hidden_ref, mixture_ref, cotangent_ref, patch_cotangent_ref, out_weight_ref, up_weight_ref, down_weight_ref = copied[:7]
    loads = [
        pltpu.make_async_copy(source, target, load_sem.at[index])
        for index, (source, target) in enumerate(zip(arguments, copied, strict=True))
    ]
    for index in (*range(7, 14), 1, 4, 0, 5, 6, 2, 3):
        loads[index].start()
    if direct:
        bundle_any, *rest, bundle_ref = rest
    else:
        normed_out_ref, up_out_ref, activated_out_ref, down_out_ref, attention_out_ref, *rest = rest
    state, unit, scale_ref, normed, activated, slope, up_back, down_back, attention_back, flipped = rest
    count, span, width = output_ref.shape
    patch_span = patch_output_ref.shape[1]
    row_count = span + patch_span
    total_rows = count * row_count
    wide = up_weight_ref.shape[1]
    lanes = width
    sums_ref[...] = jnp.zeros_like(sums_ref)

    def tile_at(tile):
        return pl.ds(pl.multiple_of(tile * lanes, lanes), lanes)

    def attention_tile(tile, carry):
        at = tile_at(tile)
        state[:, at] = hidden_ref[:, at] + (dot_nn(mixture_ref[...], out_weight_ref[:, at]) + vector_ref[2:3, at])
        return carry

    for index in (*range(7, 14), 0, 1, 4):
        loads[index].wait()
    for index, source in enumerate(copied[7:13]):
        vector_ref[2 + index : 3 + index, :] = source[...].astype(jnp.float32).reshape(1, width)
    for index in range(wide // width):
        part = copied[13][pl.ds(index * width, width)]
        vector_ref[8 + index : 9 + index, :] = part.astype(jnp.float32).reshape(1, width)
    lax.fori_loop(0, width // lanes, attention_tile, 0)

    def first_norm(chunk, carry):
        here = pl.ds(pl.multiple_of(chunk * NORM_CHUNK, 16), NORM_CHUNK)
        rows, scale = norm_rows(state[here, :])
        unit[here, :] = rows
        scale_ref[here, :] = jnp.broadcast_to(scale, (NORM_CHUNK, 128))
        rows = rows * vector_ref[4:5, :] + vector_ref[5:6, :]
        state[here, :] = rows
        normed[here, :] = rows.astype(jnp.bfloat16)
        return carry

    lax.fori_loop(0, total_rows // NORM_CHUNK, first_norm, 0)

    def up_tile(tile, carry):
        at = tile_at(tile)
        branch = dot_nn(normed[...], up_weight_ref[:, at]) + vector_ref[pl.ds(8 + tile, 1), :]
        chance = 0.5 * (1.0 + lax.erf(branch * 0.7071067811865476))
        activated[:, at] = (branch * chance).astype(jnp.bfloat16)
        slope[:, at] = chance + branch * (jnp.exp(branch * branch * -0.5) * 0.3989422804014327)
        return carry

    loads[5].wait()
    lax.fori_loop(0, wide // lanes, up_tile, 0)

    def down_tile(tile, carry):
        at = tile_at(tile)
        state[:, at] = state[:, at] + (dot_nn(activated[...], down_weight_ref[:, at]) + vector_ref[3:4, at])
        return carry

    for index in (2, 3, 6):
        loads[index].wait()
    lax.fori_loop(0, width // lanes, down_tile, 0)

    def second_norm(start, rows_here, page, out_ref, delta_ref):
        here = pl.ds(pl.multiple_of(page * row_count + start, 16), rows_here)
        there = pl.ds(0 if start == span else start, rows_here)
        rows, scale = norm_rows(state[here, :])
        out_ref[page, there, :] = rows * vector_ref[6:7, :] + vector_ref[7:8, :]
        delta = delta_ref[page, there, :].astype(jnp.float32)
        back = norm_back(delta * vector_ref[6:7, :], rows, scale)
        state[here, :] = back
        low = back.astype(jnp.bfloat16)
        down_back[here, :] = low
        for index, value in (
            (SECOND_GAIN, delta * rows), (SECOND_SHIFT, delta), (DOWN_BIAS, low.astype(jnp.float32))
        ):
            sums_ref[index : index + 1, :] += column_sum(value)

    def second_page(page, carry):
        for start in range(0, span, 32):
            second_norm(start, 32, page, output_ref, cotangent_ref)
        second_norm(span, patch_span, page, patch_output_ref, patch_cotangent_ref)
        return carry

    lax.fori_loop(0, count, second_page, 0)

    def up_back_tile(tile, carry):
        at = tile_at(tile)
        low = (dot_nt(down_back[...], down_weight_ref[at, :]) * slope[:, at]).astype(jnp.bfloat16)
        up_back[:, at] = low
        sums_ref[pl.ds(UP_BIAS + tile, 1), :] = column_sum(low.astype(jnp.float32))
        return carry

    lax.fori_loop(0, wide // lanes, up_back_tile, 0)

    def normed_back_tile(tile, carry):
        at = tile_at(tile)
        state[:, at] = state[:, at] + dot_nt(up_back[...], up_weight_ref[at, :])
        return carry

    lax.fori_loop(0, width // lanes, normed_back_tile, 0)

    def first_back(chunk, carry):
        here = pl.ds(pl.multiple_of(chunk * NORM_CHUNK, 16), NORM_CHUNK)
        delta, rows = state[here, :], unit[here, :]
        back = norm_back(delta * vector_ref[4:5, :], rows, scale_ref[here, 0:1])
        first_back_ref[here, :] = back
        low = back.astype(jnp.bfloat16)
        attention_back[here, :] = low
        for index, value in (
            (FIRST_GAIN, delta * rows), (FIRST_SHIFT, delta), (OUT_BIAS, low.astype(jnp.float32))
        ):
            sums_ref[index : index + 1, :] += column_sum(value)
        return carry

    lax.fori_loop(0, total_rows // NORM_CHUNK, first_back, 0)

    def mixture_tile(tile, carry):
        at = tile_at(tile)
        mixture_back_ref[:, at] = dot_nt(attention_back[...], out_weight_ref[at, :]).astype(jnp.bfloat16)
        return carry

    lax.fori_loop(0, width // lanes, mixture_tile, 0)
    if not direct:
        normed_out_ref[...] = normed[...]
        up_out_ref[...] = up_back[...]
        activated_out_ref[...] = activated[...]
        down_out_ref[...] = down_back[...]
        attention_out_ref[...] = attention_back[...]
        return
    levels = pages.bit_length() - 1
    core = scalar_ref[1]
    rows = width // pages
    tall = wide // pages
    block = 384
    groups = wide // (2 * block)
    flipped[...] = normed[...].T

    def up_weight_tile(tile, carry):
        at = pl.ds(pl.multiple_of(tile * 2 * block, 2 * block), 2 * block)
        result = dot_nn(flipped[...], up_back[:, at]).astype(jnp.bfloat16)
        for part in range(2):
            column, group = (2 * tile + part) // groups, (2 * tile + part) % groups
            for page in range(pages):
                slot = early_slots(scalar_ref, page, column, levels)[0]
                bundle_ref[core, slot, pl.ds(pl.multiple_of(group * rows, 16), rows), :] = result[
                    page * rows : (page + 1) * rows, part * block : (part + 1) * block
                ]
        return carry

    lax.fori_loop(0, groups, up_weight_tile, 0)
    stores = [
        pltpu.make_async_copy(bundle_ref.at[part], bundle_any.at[part], store_sem.at[index])
        for index, part in enumerate(
            (
                (core, slice(None), slice(0, tall)), (1 - core, slice(None), slice(0, tall)),
                (slice(None), slice(None), slice(tall, tall + rows // 2)),
            )
        )
    ]
    stores[0].start()

    def down_weight_tile(page, carry):
        at = pl.ds(pl.multiple_of(page * tall, 128), tall)
        result = dot_tn(activated[:, at], down_back[...]).astype(jnp.bfloat16)
        for column in range(2):
            slot = early_slots(scalar_ref, page, column, levels)[1]
            bundle_ref[1 - core, slot, 0:tall, :] = result[:, column * block : (column + 1) * block]
        return carry

    lax.fori_loop(0, pages, down_weight_tile, 0)
    stores[1].start()
    flipped[...] = mixture_ref[...].T
    half = rows // 2

    result = dot_nn(flipped[...], attention_back[...]).astype(jnp.bfloat16)
    for column in range(2):
        for page in range(pages):
            slots = early_slots(scalar_ref, page, column, levels)
            for order in range(2):
                first = page * rows + order * half
                bundle_ref[core if order == 0 else 1 - core, slots[order], tall : tall + half, :] = result[
                    first : first + half, column * block : (column + 1) * block
                ]
    stores[2].start()
    for copy in stores:
        copy.wait()


def in_tiles(width, pages):
    return (width // pages) % 32 == 0 and pages >= 4


def middle(places, hidden, mixture, cotangent, patch_cotangent, matrices, vectors, pages):
    count, span, width = cotangent.shape
    patch_span = patch_cotangent.shape[1]
    total_rows = hidden.shape[0]
    wide = matrices[1].shape[1]
    direct = in_tiles(width, pages)
    bf16, f32 = jnp.bfloat16, jnp.float32
    if direct:
        extra = (jax.ShapeDtypeStruct((2, 2 * pages, (wide + width // 2) // pages, 384), bf16),)
    else:
        extra = tuple(
            jax.ShapeDtypeStruct((total_rows, size), bf16) for size in (width, wide, wide, width, width)
        )
    result = pl.pallas_call(
        functools.partial(middle_kernel, pages, direct),
        out_shape=(
            jax.ShapeDtypeStruct(cotangent.shape, f32),
            jax.ShapeDtypeStruct(patch_cotangent.shape, f32),
            jax.ShapeDtypeStruct((total_rows, width), f32),
            jax.ShapeDtypeStruct((total_rows, width), bf16),
            jax.ShapeDtypeStruct((16, width), f32),
        )
        + extra,
        in_specs=anywhere(7 + len(vectors)),
        out_specs=tuple(in_vmem(5) + (anywhere(1) if direct else in_vmem(len(extra)))),
        scratch_shapes=[
            pltpu.VMEM((total_rows, width), f32),
            pltpu.VMEM((total_rows, width), f32),
            pltpu.VMEM((total_rows, 128), f32),
            pltpu.VMEM((total_rows, width), bf16),
            pltpu.VMEM((total_rows, wide), bf16),
            pltpu.VMEM((total_rows, wide), f32),
            pltpu.VMEM((total_rows, wide), bf16),
            pltpu.VMEM((total_rows, width), bf16),
            pltpu.VMEM((total_rows, width), bf16),
            pltpu.VMEM((width, total_rows), bf16),
        ]
        + [pltpu.VMEM(value.shape, value.dtype) for value in (extra if direct else ())]
        + [
            pltpu.VMEM(value.shape, value.dtype)
            for value in (hidden, mixture, cotangent, patch_cotangent, *matrices, *vectors)
        ]
        + [pltpu.VMEM((16, width), f32), pltpu.SemaphoreType.DMA((14,)), pltpu.SemaphoreType.DMA((3,))],
        compiler_params=pltpu.CompilerParams(vmem_limit_bytes=KERNEL_VMEM),
        cost_estimate=pl.CostEstimate(flops=14_000_000_000, bytes_accessed=30_000_000, transcendentals=2_600_000),
        name="middle",
    )(hidden, mixture, cotangent, patch_cotangent, *matrices, *vectors)
    first, rest = result[:5], result[5:]
    if direct:
        return first + rest
    normed, up_back, activated, down_back, attention_back = rest
    return first + (
        indexed_bundle(
            (
                ((normed, up_back, None), (mixture, attention_back, 0)),
                ((activated, down_back, None), (mixture, attention_back, 1)),
            ),
            places,
            pages,
        ),
    )


def indexed_bundle(matrices, scalars, pages):
    levels = pages.bit_length() - 1
    place = jnp.arange(2 * pages, dtype=jnp.int32)
    bits = [(place >> (levels - k)) & 1 for k in range(levels + 1)]
    halves = []
    for order, group in enumerate(matrices):
        side, near = (bits[0], bits[1]) if order == 0 else (bits[1], bits[0])
        far = near
        for level in range(1, levels):
            far = far + (bits[level + 1] << level)
        index = (far ^ scalars[2]) * 2 + (side ^ scalars[3])
        blocks = []
        for operand, gradient, part in group:
            rows = in_blocks(outer_dot(operand, gradient).astype(jnp.bfloat16), pages)
            if part is not None:
                half = rows.shape[1] // 2
                rows = rows[:, part * half : (part + 1) * half]
            blocks.append(rows)
        halves.append(jnp.concatenate(blocks, axis=1)[index])
    first, second = halves
    mine = scalars[1] == 0
    return jnp.stack([jnp.where(mine, first, second), jnp.where(mine, second, first)])


def in_blocks(matrix, pages):
    rows, columns = matrix.shape[0] // pages, matrix.shape[1] // 2
    lanes = min(columns, 384)
    blocks = matrix.reshape(pages, rows, 2, columns // lanes, lanes)
    return blocks.transpose(0, 2, 3, 1, 4).reshape(pages * 2, rows * columns // lanes, lanes)


class Halving:
    def __init__(self, keep, source, landing, landings, partners, sibling, sems, chunks):
        self.keep, self.landing, self.landings = keep, landing, landings
        total = keep.shape[0]
        unit = total // chunks
        send_sem, recv_sem = sems
        self.arrivals, self.sends, self.needs = {}, {}, {}
        used = 0
        for chunk in range(chunks):
            lo = total - (chunk + 1) * unit
            copy = remote(
                source.at[lo : lo + unit], landing.at[lo : lo + unit], send_sem.at[used], recv_sem.at[used], *sibling
            )
            self.arrivals["core", chunk] = (copy, landing, lo, unit)
            used += 1
        for step, (into, partner) in enumerate(zip(landings, partners, strict=True)):
            size = total >> (step + 1)
            piece = min(unit, size)
            for chunk in range(size // piece):
                lo = size - (chunk + 1) * piece
                copy = remote(
                    keep.at[size + lo : size + lo + piece], into.at[lo : lo + piece], send_sem.at[used],
                    recv_sem.at[used], *partner,
                )
                self.arrivals[step, chunk] = (copy, into, lo, piece)
                self.sends[step, chunk] = copy
                self.needs[step, chunk] = {
                    (source_step, block)
                    for block in range(size + lo, size + lo + piece)
                    for source_step in ("core", *range(step))
                }
                used += 1
        self.done = set()

    def start(self):
        for key, (copy, *_) in self.arrivals.items():
            if key[0] == "core":
                copy.start()

    def take(self, *key):
        copy, into, lo, count = self.arrivals[key]
        copy.wait_recv()

        def add(block, carry):
            self.keep[block] = self.keep[block] + into[block]
            return carry

        lax.fori_loop(lo, lo + count, add, 0)
        for block in range(lo, lo + count):
            self.done.add((key[0], block))
        for name in list(self.sends):
            if self.needs[name] <= self.done:
                self.sends.pop(name).start()

    def finish(self):
        for copy, *_ in self.arrivals.values():
            copy.wait_send()


def backward_kernel(
    pages,
    staging, length_ref, query_ref, mixture_back_ref, columns_ref, rows_ref, query_rows_ref, tokens_ref, patches_ref, taps_ref,
    middle_sums_ref, bundle_any, weights_any, key_any, value_any, hidden_any, first_back_any, query_weight_any,
    key_weight_any, value_weight_any,
    tokens_back_ref, patches_back_ref, early_ref, late_ref, sums_ref, up_in_ref, down_in_ref, mixed_in_ref,
    keep, landing, landings, late, late_landing, late_landings, weights_buf, key_buf, value_buf, outgoing, from_sib,
    from_far, matrices, flipped, total_back, query_back, key_back, value_back, back, steps, mask_ref, hot_ref,
    query_hot_ref, band_ref, table_acc, band_acc, table_out, text_rim, patch_rim, sums, sums_in,
    up_in, down_out, down_in, mixed_out, mixed_in,
    load_sem, page_sem, early_send, early_recv, late_send, late_recv, sib_send, sib_recv, far_send, far_recv, rim_send,
    rim_recv, sum_send, sum_recv, swap_send, swap_recv,
):
    page_at, bits, seq, across, core = places_of(pages)
    levels = len(bits)
    count, span, width = tokens_ref.shape
    patch_span = patches_ref.shape[1]
    row_count = span + patch_span
    total_rows = count * row_count
    key_pad = key_buf.shape[1]
    text_slots = 4 * span
    groups = weights_buf.shape[1]
    members = weights_buf.shape[2] // row_count
    heads = groups * members
    group_width = members * HEAD_LANES
    f32, bf16 = jnp.float32, jnp.bfloat16

    sibling = (page_at, sibling_of(seq))
    opposite = (page_at, across_of(seq))
    diagonal = (page_at, sibling_of(across_of(seq)))
    flips = [(1 - 2 * bit) * 2**level for level, bit in enumerate(bits)]
    on_page = [(page_at + flip, seq) for flip in flips]
    either = lambda first, second: first + core * (second - first)
    early_partners = [
        (page_at + either(flips[1], flips[0]), seq),
        (page_at + either(flips[0], flips[1]), seq),
        opposite,
    ] + on_page[2:]
    barrier = pltpu.get_barrier_semaphore()
    everyone = [sibling, opposite, diagonal] + on_page
    for peer in everyone:
        pl.semaphore_signal(barrier, inc=1, device_id=peer, device_id_type=MESH)

    keep_load = pltpu.make_async_copy(bundle_any.at[0], keep, load_sem.at[0])
    later_loads = [
        pltpu.make_async_copy(source, target, load_sem.at[1 + index])
        for index, (source, target) in enumerate(
            (
                (query_weight_any, matrices.at[0]), (key_weight_any, matrices.at[1]),
                (value_weight_any, matrices.at[2]), (hidden_any, key_back), (first_back_any, total_back),
            )
        )
    ]

    def page_loads(page):
        slot = page % 2
        return [
            pltpu.make_async_copy(source.at[page], target.at[slot], page_sem.at[index, slot])
            for index, (source, target) in enumerate(
                ((weights_any, weights_buf), (key_any, key_buf), (value_any, value_buf))
            )
        ]

    for copy in page_loads(0):
        copy.start()
    keep_load.start()
    pl.semaphore_wait(barrier, len(everyone))
    early = Halving(
        keep, bundle_any.at[1], landing, landings, early_partners, sibling, (early_send, early_recv), 8
    )
    late_sum = Halving(
        late.at[0], late.at[1], late_landing, late_landings, early_partners, sibling, (late_send, late_recv), 4
    )
    early.start()
    for copy in staging:
        copy.wait()

    lane128 = lax.broadcasted_iota(jnp.int32, (row_count, 128), 1)
    place = query_places(seq, (row_count, 128), span, patch_span, text_slots)
    aim = place + lane128 - 32
    blocks_on = (aim >> 4) - (place >> 4)
    near = (lane128 < 64) & (aim >= 0) & (aim < text_slots + patch_span * 4) & (blocks_on >= -1) & (blocks_on <= 1)
    band_ref[...] = jnp.where(near, aim, -1)
    table_acc[...] = jnp.zeros_like(table_acc)
    band_acc[...] = jnp.zeros_like(band_acc)
    lane_of_row = lax.broadcasted_iota(jnp.int32, (48, row_count), 1)
    place_of_row = jnp.where(
        lane_of_row < span, seq * span + lane_of_row, text_slots + seq * patch_span + lane_of_row - span
    )
    query_hot_ref[144:192, :] = (
        ((place_of_row >> 4) == lax.broadcasted_iota(jnp.int32, (48, row_count), 0)).astype(f32).astype(bf16)
    )
    def start_page(page):
        slot = page % 2
        for copy in page_loads(page):
            copy.wait()

        @pl.when(page < count - 1)
        def _():
            for copy in page_loads(page + 1):
                copy.start()

        bin_at = lax.broadcasted_iota(jnp.int32, (128, key_pad), 0) - 1
        key_block = lax.broadcasted_iota(jnp.int32, (128, key_pad), 1) >> 4
        half_bin = lax.broadcasted_iota(jnp.int32, (72, row_count), 0)
        for side in range(2):
            key_row = rows_ref[page, side : side + 1, :]
            query_column = columns_ref[page, :, 128 * side : 128 * side + 1]
            mask_ref[:, side * key_pad : (side + 1) * key_pad] = (
                ((key_row & 15) < (query_column & 15)).astype(f32).astype(bf16)
            )
            key_bin = key_row >> 4
            plain = jnp.where(bin_at < 64, (key_bin == bin_at).astype(f32), 0.0)
            lower = jnp.where(bin_at < 64, (key_bin - 1 == bin_at).astype(f32), 0.0)
            mine = slice(128 * side, 128 * (side + 1))
            other = slice(128 * (1 - side), 128 * (2 - side))
            change = lower - plain
            if side == 0:
                plain = jnp.where(bin_at - 71 == key_block, 1.0, plain)
            hot_ref[mine, 0:key_pad] = plain.astype(bf16)
            hot_ref[mine, (1 + side) * key_pad : (2 + side) * key_pad] = change.astype(bf16)
            hot_ref[other, (1 + side) * key_pad : (2 + side) * key_pad] = jnp.zeros((128, key_pad), bf16)
            query_bin = query_rows_ref[page, side : side + 1, 0:row_count] >> 4
            query_hot_ref[72 * side : 72 * (side + 1), :] = (71 - query_bin == half_bin).astype(f32).astype(bf16)

    def attend(page, group):
        slot = page % 2
        at = pl.ds(pl.multiple_of(group * group_width, group_width), group_width)
        own_rows = pl.ds(pl.multiple_of(page * row_count, 16), row_count)
        both_query = split_heads(query_ref[own_rows, at])
        both_back = split_heads(mixture_back_ref[own_rows, at])
        back[...] = dot_nt(both_back, value_buf[slot, :, at])
        for start in range(0, members * row_count, CHUNK):
            there = slice(start, start + CHUNK)
            here = slice(start % row_count, start % row_count + CHUNK)
            parts, total = [], None
            for block_at in range(0, key_pad, 128):
                lane = slice(block_at, block_at + 128)
                part = weights_buf[slot, group, there, lane].astype(f32)
                product = part * back[there, lane]
                total = product if total is None else total + product
                parts.append(part)
            mean = jnp.sum(total, axis=1, keepdims=True)
            for index, part in enumerate(parts):
                lane = slice(128 * index, 128 * (index + 1))
                step = (part * (back[there, lane] - mean)).astype(bf16)
                steps[there, lane] = step
                steps[there, key_pad + 128 * index : key_pad + 128 * (index + 1)] = step * mask_ref[here, lane]
                steps[there, 2 * key_pad + 128 * index : 2 * key_pad + 128 * (index + 1)] = (
                    step * mask_ref[here, key_pad + 128 * index : key_pad + 128 * (index + 1)]
                )
        query_back[own_rows, at] = (
            merge_heads(dot_nn(steps[:, 0:key_pad], key_buf[slot, :, at])) * 0.125
        ).astype(bf16)
        for kind, value in enumerate(
            (dot_tn(steps[:, 0:key_pad], both_query), dot_tn(weights_buf[slot, group], both_back))
        ):
            value = value.astype(bf16)
            for where in range(4):
                place_at = apart(where % 2, core) * 2 + apart(where // 2, across)
                outgoing[page, place_at, kind, 0:span, at] = value[where * span : (where + 1) * span]
                outgoing[page, place_at, kind, span:row_count, at] = value[
                    text_slots + where * patch_span : text_slots + (where + 1) * patch_span
                ]
        bins = dot_nt(steps[...], hot_ref[...]).astype(bf16)
        for side in range(members):
            head = members * group + side
            base = side * row_count
            both = dot_nn(query_hot_ref[...], bins[base : base + row_count])
            table_acc[head, 0:72, :] += both[0:72, 0:128]
            table_acc[head, 72:144, :] += both[72:144, 128:256]
            table_acc[head, 144:192, :] += both[144:192, 0:128]
            for first, rows_here, block, into in bands():
                source = steps[
                    base + first : base + first + rows_here, pl.ds(pl.multiple_of(block * 128, 128), 128)
                ]
                band_acc[head, into : into + rows_here, :] += source.astype(f32)

    def bands():
        before = seq - (seq + 3) // 4
        return (
            (0, span, seq, 0),
            (0, 32, before, span),
            (span - 32, 32, seq + 1, span + 32),
            (span, patch_span, 3, span + 64),
            (span, patch_span, 4, span + 64 + patch_span),
        )

    def sib_copy(page):
        return remote(outgoing.at[page, 2:4], from_sib.at[page], sib_send.at[page], sib_recv.at[page], *sibling)

    def far_copy(page):
        return remote(outgoing.at[page, 1], from_far.at[page], far_send.at[page], far_recv.at[page], *opposite)

    def pass_on(page):
        sib_copy(page).wait_recv()
        for kind in range(2):
            outgoing[page, 1, kind] = outgoing[page, 1, kind] + from_sib[page, 1, kind]
        far_copy(page).start()

    events = {
        1: [("core", 0), ("core", 1)], 2: [("core", 2), ("core", 3)], 4: [("core", 4), ("core", 5)],
        6: [("core", 6), ("core", 7)], 8: [(0, 0)], 12: [(0, 1)],
    }
    last_turn = count * groups - 1

    def step_body(turn, carry):
        page, group = turn // groups, turn % groups

        @pl.when(group == 0)
        def _():
            start_page(page)

        for at_turn, names in events.items():

            @pl.when(turn == min(at_turn, last_turn))
            def _(names=names, at_turn=at_turn):
                if at_turn == min(events):
                    keep_load.wait()
                for name in names:
                    early.take(*name)

        @pl.when(turn == min(3, last_turn))
        def _():
            for copy in later_loads:
                copy.start()

        @pl.when((group == 1) & (page > 0))
        def _():
            pass_on(page - 1)

        attend(page, group)

        @pl.when(group == groups - 1)
        def _():
            sib_copy(page).start()

        return carry

    lax.fori_loop(0, count * groups, step_body, 0)

    for copy in later_loads:
        copy.wait()
    flipped[...] = key_back[...].T
    lanes = 384
    rows = width // pages
    half = rows // 2

    def weight_columns(index, gradient):
        def tile(four, carry):
            tile_rows = pl.ds(pl.multiple_of(four * 4 * rows, 128), 4 * rows)
            result = dot_nn(flipped[tile_rows, :], gradient[...]).astype(bf16)
            for inner in range(4):
                page = four * 4 + inner
                first = inner * rows
                for column in range(2):
                    far = [apart((page // 2**level) % 2, bit) for level, bit in enumerate(bits)]
                    slots = [slot_of_bits(order) for order in early_orders(far, apart(column, across))]
                    at = slice(column * lanes, (column + 1) * lanes)
                    if index < 2:
                        late[core if index == 0 else 1 - core, slots[index], 0:rows, :] = result[
                            first : first + rows, at
                        ]
                    else:
                        late[core, slots[0], rows : rows + half, :] = result[first : first + half, at]
                        late[1 - core, slots[1], rows : rows + half, :] = result[first + half : first + rows, at]
            return carry

        lax.fori_loop(0, pages // 4, tile, 0)

    def project_back(gradient, matrix):
        total_back[...] = total_back[...] + dot_nt(gradient[...], matrices[matrix])

    pass_on(count - 1)
    weight_columns(0, query_back)
    project_back(query_back, 0)
    sums[0, 0:16, :] = middle_sums_ref[...]
    sums[0, 10:11, :] = column_sum(query_back[...].astype(f32))

    def head_tables(head, carry):
        for plane in range(2):
            table = table_acc[head, 72 * plane : 72 * (plane + 1), :]
            lane = lax.broadcasted_iota(jnp.int32, table.shape, 1)
            table = jnp.where(lane < 72, table, 0.0)
            table = jnp.concatenate([table, jnp.zeros_like(table)], axis=1)
            sheared = pltpu.roll(table, 0, 1, stride=1, stride_axis=0)
            table_out[head, 0:1, 256 * plane : 256 * (plane + 1)] = column_sum(sheared)
        table = table_acc[head, 144:192, :]
        lane = lax.broadcasted_iota(jnp.int32, table.shape, 1)
        apart_by = lane - 72 - lax.broadcasted_iota(jnp.int32, table.shape, 0)
        in_line = (lane >= 72) & (lane < 72 + 36)
        low_tail = jnp.sum(column_sum(jnp.where(in_line & (apart_by <= -2), table, 0.0)), axis=1, keepdims=True)
        high_tail = jnp.sum(column_sum(jnp.where(in_line & (apart_by >= 2), table, 0.0)), axis=1, keepdims=True)
        band = jnp.zeros((1, 128), f32)
        for first, rows_here, block, into in bands():
            aims = band_ref[first : first + rows_here, :]
            taken = jnp.take_along_axis(band_acc[head, into : into + rows_here, :], aims & 127, axis=1)
            right = (aims >> 7) == block
            if into == span:
                right = right & (seq > 0)
            band = band + column_sum(jnp.where(right, taken, 0.0))
        lane_one = lax.broadcasted_iota(jnp.int32, (1, 128), 1)
        table_out[head, 0:1, 512:640] = (
            band + jnp.where(lane_one == 0, low_tail, 0.0) + jnp.where(lane_one == 63, high_tail, 0.0)
        )
        table_out[head, 0:1, 640:768] = jnp.zeros((1, 128), f32)
        return carry

    lax.fori_loop(0, heads, head_tables, 0)
    for head in range(heads):
        at_row = 8 + head
        sums[1, at_row : at_row + 1, :] = table_out[head, 0:1, :]

    for name in ((0, 2), (1, 0)):
        early.take(*name)
    for page in range(count):
        far_copy(page).wait_recv()
        own_rows = slice(page * row_count, (page + 1) * row_count)
        for kind, target in enumerate((key_back, value_back)):
            target[own_rows, :] = (
                (outgoing[page, 0, kind].astype(f32) + from_sib[page, 0, kind].astype(f32))
                + from_far[page, kind].astype(f32)
            ).astype(bf16)
    weight_columns(1, key_back)
    weight_columns(2, value_back)
    late_sum.start()
    project_back(key_back, 1)
    project_back(value_back, 2)
    sums[0, 11:12, :] = column_sum(value_back[...].astype(f32))
    for page in range(count):
        first = page * row_count
        text_rim[page, 16 : 16 + span, :] = total_back[first : first + span, :].astype(bf16)
        patch_rim[page, 16 : 16 + patch_span, :] = total_back[first + span : first + row_count, :].astype(bf16)
    after, before = (page_at, (seq + 1) % 4), (page_at, (seq + 3) % 4)
    rim_copies = [
        remote(
            source.at[:, start : start + 16], source.at[:, stop : stop + 16], rim_send.at[index], rim_recv.at[index],
            *peer,
        )
        for index, (source, start, stop, peer) in enumerate(
            (
                (text_rim, span, 0, after), (text_rim, 16, 16 + span, before),
                (patch_rim, 16, 0, after), (patch_rim, 16, 32, before),
            )
        )
    ]
    for copy in rim_copies:
        copy.start()
    for chunk in range(4):
        late_sum.take("core", chunk)
    for name in ((0, 3), (1, 1)):
        early.take(*name)
    for copy in rim_copies:
        copy.wait()
    sums[1, 0:8, :] = jnp.zeros((8, width), f32)
    sums[1, 20:24, :] = jnp.zeros((4, width), f32)
    sums[0, 16:24, :] = jnp.zeros((8, width), f32)

    def position_tile(tile, carry):
        at = pl.ds(pl.multiple_of(tile * 256, 256), 256)
        text_taps = [jnp.zeros((1, 256), f32) for _ in range(7)]
        patch_taps = [jnp.zeros((1, 256), f32) for _ in range(9)]
        for page in range(count):
            first = page * row_count
            window = text_rim[page, :, at].astype(f32)
            window_row = lax.broadcasted_iota(jnp.int32, (span + 32, 1), 0)
            inside = ((window_row >= 16) | (seq > 0)) & ((window_row < 16 + span) | (seq < 3))
            window = jnp.where(inside, window, 0.0)
            live = seq * span + lax.broadcasted_iota(jnp.int32, (span, 1), 0) < length_ref[page]
            masked = jnp.where(live, tokens_ref[page, :, at].astype(f32), 0.0)
            total = jnp.zeros((span, 256), f32)
            for distance in range(-3, 4):
                shifted = window[16 - distance : 16 - distance + span]
                if distance == 0:
                    weight = taps_ref[1:2, at] + taps_ref[4:5, at] + taps_ref[7:8, at]
                else:
                    tap = 3 * (abs(distance) - 1) + (2 if distance > 0 else 0)
                    weight = taps_ref[tap : tap + 1, at]
                total = total + shifted * weight
                text_taps[distance + 3] = text_taps[distance + 3] + column_sum(shifted * masked)
            tokens_back_ref[page, :, at] = total_back[first : first + span, at] + jnp.where(live, total, 0.0)
            window = patch_rim[page, :, at].astype(f32)
            window_row = lax.broadcasted_iota(jnp.int32, (48, 1), 0)
            inside = ((window_row >= 16) | (seq > 0)) & ((window_row < 32) | (seq < 3))
            window = jnp.where(inside, window, 0.0)
            cell = seq * patch_span + lax.broadcasted_iota(jnp.int32, (patch_span, 1), 0)
            live = ((cell >> 3) < GRID_SIDE - 1) & ((cell & 7) < GRID_SIDE - 1)
            masked = jnp.where(live, patches_ref[page, :, at].astype(f32), 0.0)
            total = jnp.zeros((patch_span, 256), f32)
            for tap in range(9):
                distance = GRID_SIDE * (tap // 3 - 1) + tap % 3 - 1
                shifted = window[16 - distance : 32 - distance]
                total = total + shifted * taps_ref[9 + tap : 10 + tap, at]
                patch_taps[tap] = patch_taps[tap] + column_sum(shifted * masked)
            patches_back_ref[page, :, at] = total_back[first + span : first + row_count, at] + jnp.where(
                live, total, 0.0
            )
        for index, value in enumerate(text_taps):
            sums[0, 16 + index : 17 + index, at] = value
        for index, value in enumerate(patch_taps):
            if index == 0:
                sums[0, 23:24, at] = value
            else:
                sums[1, index - 1 : index, at] = value
        return carry

    early.take(2, 0)
    lax.fori_loop(0, width // 256, position_tile, 0)

    sum_partners = [opposite] + on_page
    sum_copies = [remote(sums.at[1 - core], sums_in.at[0], sum_send.at[0], sum_recv.at[0], *sibling)] + [
        remote(sums.at[core], sums_in.at[1 + index], sum_send.at[1 + index], sum_recv.at[1 + index], *partner)
        for index, partner in enumerate(sum_partners)
    ]
    last = remote(
        sums.at[core], sums_in.at[2 + levels], sum_send.at[2 + levels], sum_recv.at[2 + levels], *sibling
    )
    sum_copies[0].start()

    def sum_step(index):
        sum_copies[index].wait()
        sums[core] = sums[core] + sums_in[index]
        (sum_copies + [last])[index + 1].start()

    late_sum.take(0, 0)
    sum_step(0)
    late_sum.take(0, 1)
    sum_step(1)
    late_sum.take(1, 0)
    sum_step(2)
    for step in range(2, levels + 1):
        late_sum.take(step, 0)
        sum_step(step + 1)
    for step in range(3, levels + 1):
        early.take(step, 0)
    last.wait()
    sums_ref[core] = sums[core]
    sums_ref[1 - core] = sums_in[2 + levels]
    wide_rows = 4 * rows
    block = keep[0].astype(f32)
    low, high = block[:, 0 : lanes // 2], pltpu.roll(block, lanes // 2, 1)[:, 0 : lanes // 2]
    down_out[...] = low[0:wide_rows].astype(bf16)
    mixed_out[0:half, :] = jnp.where(core == 0, high[wide_rows:], low[wide_rows:]).astype(bf16)
    block = late[0, 0].astype(f32)
    low, high = block[:, 0 : lanes // 2], pltpu.roll(block, lanes // 2, 1)[:, 0 : lanes // 2]
    mixed_out[half:, :] = jnp.where(core == 0, high, low).astype(bf16)
    swaps = [
        remote(source, target, swap_send.at[index], swap_recv.at[index], *sibling)
        for index, (source, target) in enumerate(
            ((keep.at[0, 2 * rows : 4 * rows], up_in), (down_out, down_in), (mixed_out, mixed_in))
        )
    ]
    for copy in swaps:
        copy.start()
    early_ref[...] = keep[0]
    late_ref[...] = late[0, 0]
    for copy in swaps:
        copy.wait()
    up_in_ref[...] = up_in[...]
    down_in_ref[...] = down_in[...]
    mixed_in_ref[...] = mixed_in[...]
    early.finish()
    late_sum.finish()
    for page in range(count):
        sib_copy(page).wait_send()
        far_copy(page).wait_send()


def backward(pages, lengths, local_values, far_values, tokens, patches):
    count, span, width = tokens.shape
    patch_span = patches.shape[1]
    row_count = span + patch_span
    total_rows = count * row_count
    bundle, weights, keys = far_values[0], far_values[1], far_values[2]
    groups, grouped_rows, key_pad = weights.shape[1:]
    heads = groups * grouped_rows // row_count
    blocks, early_rows, lanes = bundle.shape[1:]
    late_rows = 3 * width // (2 * pages)
    levels = pages.bit_length() - 1
    bf16, f32, i32 = jnp.bfloat16, jnp.float32, jnp.int32
    dma = pltpu.SemaphoreType.DMA

    def landings(rows):
        return [VMEM((blocks >> (step + 1), rows, lanes), bf16) for step in range(levels + 1)]

    early_count = 8 + 4 + 2 + (levels - 1)
    late_count = 4 + 2 + levels
    return pl.pallas_call(
        staged(functools.partial(backward_kernel, pages), 1, len(local_values)),
        out_shape=(
            jax.ShapeDtypeStruct(tokens.shape, f32),
            jax.ShapeDtypeStruct(patches.shape, f32),
            jax.ShapeDtypeStruct((early_rows, lanes), bf16),
            jax.ShapeDtypeStruct((late_rows, lanes), bf16),
            jax.ShapeDtypeStruct((2, 24, width), f32),
            jax.ShapeDtypeStruct((early_rows // 9 * 4, lanes), bf16),
            jax.ShapeDtypeStruct((early_rows // 9 * 8, lanes // 2), bf16),
            jax.ShapeDtypeStruct((early_rows // 9 + late_rows, lanes // 2), bf16),
        ),
        in_specs=[pl.BlockSpec(memory_space=pltpu.SMEM)]
        + anywhere(len(local_values) + len(far_values)),
        out_specs=tuple(in_vmem(8)),
        scratch_shapes=[
            VMEM((blocks, early_rows, lanes), bf16),
            VMEM((blocks, early_rows, lanes), bf16),
            landings(early_rows),
            VMEM((2, blocks, late_rows, lanes), bf16),
            VMEM((blocks, late_rows, lanes), bf16),
            landings(late_rows),
            VMEM((2, groups, grouped_rows, key_pad), bf16),
            VMEM((2, key_pad, width), bf16),
            VMEM((2, key_pad, width), bf16),
            VMEM((count, 4, 2, row_count, width), bf16),
            VMEM((count, 2, 2, row_count, width), bf16),
            VMEM((count, 2, row_count, width), bf16),
            VMEM((3, width, width), bf16),
            VMEM((width, total_rows), bf16),
            VMEM((total_rows, width), f32),
            VMEM((total_rows, width), bf16),
            VMEM((total_rows, width), bf16),
            VMEM((total_rows, width), bf16),
            VMEM((grouped_rows, key_pad), f32),
            VMEM((grouped_rows, 3 * key_pad), bf16),
            VMEM((row_count, 2 * key_pad), bf16),
            VMEM((256, 3 * key_pad), bf16),
            VMEM((192, row_count), bf16),
            VMEM((row_count, 128), i32),
            VMEM((heads, 192, 128), f32),
            VMEM((heads, span + 64 + 2 * patch_span, 128), f32),
            VMEM((heads, 8, width), f32),
            VMEM((count, span + 32, width), bf16),
            VMEM((count, patch_span + 32, width), bf16),
            VMEM((2, 24, width), f32),
            VMEM((3 + levels, 24, width), f32),
            VMEM((early_rows // 9 * 4, lanes), bf16),
            VMEM((early_rows // 9 * 8, lanes // 2), bf16),
            VMEM((early_rows // 9 * 8, lanes // 2), bf16),
            VMEM((early_rows // 9 + late_rows, lanes // 2), bf16),
            VMEM((early_rows // 9 + late_rows, lanes // 2), bf16),
            dma((6,)), dma((3, 2)),
            dma((early_count,)), dma((early_count,)), dma((late_count,)), dma((late_count,)),
            dma((count,)), dma((count,)), dma((count,)), dma((count,)),
            dma((4,)), dma((4,)), dma((3 + levels,)), dma((3 + levels,)), dma((3,)), dma((3,)),
        ]
        + stage_for(local_values),
        compiler_params=pltpu.CompilerParams(
            collective_id=1, has_side_effects=True, vmem_limit_bytes=KERNEL_VMEM
        ),
        cost_estimate=pl.CostEstimate(flops=12_000_000_000, bytes_accessed=40_000_000, transcendentals=0),
        name="backward",
    )(lengths, *local_values, *far_values)


def clip_lanes(sums, centre, bins):
    first, last = centre + 1 - bins // 2, centre - 1 + bins // 2
    lane = lax.broadcasted_iota(jnp.int32, sums.shape, 1)
    below = jnp.sum(jnp.where(lane < first, sums, 0.0), axis=1, keepdims=True)
    above = jnp.sum(jnp.where(lane >= last, sums, 0.0), axis=1, keepdims=True)
    moved = pltpu.roll(sums, sums.shape[1] - (first - 1), 1)
    moved = jnp.where(lane == 0, below, jnp.where(lane == bins - 1, above, moved))
    return moved[:, :bins]


def finish_kernel(staging, early_ref, late_ref, sums_ref, up_in_ref, down_in_ref, mixed_in_ref, *rest):
    carried, rest = rest[:2], rest[2:]
    *rest, carry_sem = rest
    rest, targets = rest[:-2], rest[-2:]
    (
        query_ref, key_ref, value_ref, out_ref, up_ref, down_ref, taps_ref, patch_taps_ref, line_ref, across_ref,
        upward_ref, *vector_refs,
    ) = rest
    carries = [
        pltpu.make_async_copy(source, target, carry_sem.at[index])
        for index, (source, target) in enumerate(zip(carried, targets, strict=True))
    ]
    for copy in carries:
        copy.start()
    f32 = jnp.float32
    rows, columns = query_ref.shape
    half = rows // 2
    wide_rows = 4 * rows
    first = position()[1] == 0
    for copy in staging:
        copy.wait()
    heads = line_ref.shape[0]
    block = early_ref[...].astype(f32)
    low, high = block[:, 0:columns], pltpu.roll(block, columns, 1)[:, 0:columns]
    up = jnp.where(first, block[0 : 2 * rows], up_in_ref[...].astype(f32))
    up_ref[:, 0 : 2 * columns] = up[0:rows]
    up_ref[:, 2 * columns : 4 * columns] = up[rows : 2 * rows]
    down_ref[...] = jnp.where(first, down_in_ref[...].astype(f32), high[0:wide_rows]).T
    kept = jnp.where(first, low[wide_rows:], high[wide_rows:])
    got = mixed_in_ref[0:half, :].astype(f32)
    out_ref[0:half, :] = jnp.where(first, kept, got)
    out_ref[half:rows, :] = jnp.where(first, got, kept)
    block = late_ref[...].astype(f32)
    low, high = block[:, 0:columns], pltpu.roll(block, columns, 1)[:, 0:columns]
    kept = jnp.where(first, low, high)
    got = mixed_in_ref[half:, :].astype(f32)
    query_ref[...] = jnp.where(first, kept[0:rows], got[0:rows])
    key_ref[...] = jnp.where(first, got[0:rows], kept[0:rows])
    value_ref[0:half, :] = jnp.where(first, kept[rows:], got[rows:])
    value_ref[half:rows, :] = jnp.where(first, got[rows:], kept[rows:])
    front, back = sums_ref[0], sums_ref[1]
    width = front.shape[1]
    text = [front[16 + index : 17 + index] for index in range(7)]
    order = [text[2], text[3], text[4], text[1], text[3], text[5], text[0], text[3], text[6]]
    taps_ref[...] = jnp.concatenate(order, axis=0)
    patch_taps_ref[...] = jnp.concatenate([front[23:24], back[0:8]], axis=0)
    across_ref[...] = clip_lanes(back[8:24, 0:256], 72, across_ref.shape[1])[0:heads]
    upward_ref[...] = clip_lanes(back[8:24, 256:512], 72, upward_ref.shape[1])[0:heads]
    line_ref[...] = clip_lanes(back[8:24, 512:640], 32, line_ref.shape[1])[0:heads]
    for source, target in zip((10, 11, 0, UP_BIAS, 1, 2, 3, 4, 5), vector_refs, strict=True):
        for part in range(target.shape[0] // width):
            target[pl.ds(part * width, width)] = front[source + part, :]
    for copy in carries:
        copy.wait()


def finish(values, carried, width, wide, heads, line_bins, plane_bins):
    rows, columns = values[1].shape[0] * 2 // 3, values[1].shape[1] // 2
    f32 = jnp.float32
    square = jax.ShapeDtypeStruct((rows, columns), f32)
    taps = jax.ShapeDtypeStruct((9, width), f32)
    plane = jax.ShapeDtypeStruct((heads, plane_bins), f32)
    return pl.pallas_call(
        staged(finish_kernel, 0, len(values)),
        out_shape=(
            square, square, square, square,
            jax.ShapeDtypeStruct((rows, 4 * columns), f32),
            jax.ShapeDtypeStruct((columns, 4 * rows), f32),
            taps, taps,
            jax.ShapeDtypeStruct((heads, line_bins), f32), plane, plane,
            *(jax.ShapeDtypeStruct((size,), f32) for size in (width,) * 3 + (wide,) + (width,) * 5),
            *(jax.ShapeDtypeStruct(value.shape, f32) for value in carried),
        ),
        in_specs=anywhere(len(values) + len(carried)),
        out_specs=tuple(in_vmem(22)),
        scratch_shapes=[pltpu.SemaphoreType.DMA((2,))] + stage_for(values),
        compiler_params=pltpu.CompilerParams(vmem_limit_bytes=KERNEL_VMEM),
        name="finish",
    )(*values, *carried)


def exchange(value, pages, step):
    moves = []
    for page in range(pages):
        for seq in range(4):
            on_page, on_seq = page, seq
            if (seq % 2 == step) if step < 2 else False:
                on_seq = seq ^ 2
            else:
                on_page = page ^ (1 if step < 2 else 1 << (step - 1))
            moves.append((page * 4 + seq, on_page * 4 + on_seq))
    return lax.ppermute(value, ("page", "seq"), moves)


def added(kept, got):
    return (kept.astype(jnp.float32) + got.astype(jnp.float32)).astype(jnp.bfloat16)


def bundle_sum(state, pages):
    for step in range(pages.bit_length()):
        half = state.shape[0] // 2
        state = added(state[:half], exchange(state[half:], pages, step))
    return state[0]


def bundle_parts(state, wide_rows, core):
    lanes = state.shape[1] // 2
    first = core == 0
    tail = state[wide_rows:]
    if wide_rows > 2 * tail.shape[0]:
        group = state[:wide_rows].reshape(4, wide_rows // 4, 2 * lanes)
        low = group[:2].transpose(1, 0, 2).reshape(-1, lanes)
        high = group[2:].transpose(1, 0, 2).reshape(-1, lanes)
    else:
        low, high = state[:wide_rows, :lanes], state[:wide_rows, lanes:]
    left, right = state[:wide_rows, :lanes], state[:wide_rows, lanes:]
    sent = jnp.concatenate(
        [jnp.where(first, high, left), jnp.where(first, tail[:, lanes:], tail[:, :lanes])], axis=0
    )
    got = swap(sent, "seq", 1)
    kept_tail = jnp.where(first, tail[:, :lanes], tail[:, lanes:])
    one = jnp.where(first, low, got[:wide_rows])
    two = jnp.where(first, got[:wide_rows], right)
    three = jnp.concatenate(
        [jnp.where(first, kept_tail, got[wide_rows:]), jnp.where(first, got[wide_rows:], kept_tail)], axis=0
    )
    return [value.astype(jnp.float32) for value in (one, two, three)]


def clipped(sums, centre, bins):
    first, last = centre + 1 - bins // 2, centre - 1 + bins // 2
    return jnp.concatenate(
        [
            jnp.sum(sums[..., :first], axis=-1, keepdims=True),
            sums[..., first:last],
            jnp.sum(sums[..., last:], axis=-1, keepdims=True),
        ],
        axis=-1,
    )


def grid_live(cells):
    return (cells // GRID_SIDE < GRID_SIDE - 1) & (cells % GRID_SIDE < GRID_SIDE - 1)


def grid_boxes(cells):
    return jnp.stack(
        [
            patch_pitch * (cells % GRID_SIDE) + patch_centre,
            patch_pitch * (cells // GRID_SIDE) + patch_centre,
        ]
    )


def shards(
    tokens,
    patches,
    page_length,
    box_position,
    query_weight,
    key_weight,
    value_weight,
    out_weight,
    up_weight,
    down_weight,
    conv_weight,
    patch_conv_weight,
    query_bias,
    value_bias,
    out_bias,
    up_bias,
    down_bias,
    attention_gain,
    attention_shift,
    feedforward_gain,
    feedforward_shift,
    reading_bias_table,
    horizontal_bias_table,
    vertical_bias_table,
    cotangent,
    patch_cotangent,
):
    conv_taps = conv_weight.astype(jnp.float32)
    patch_taps = patch_conv_weight.astype(jnp.float32)
    query_offset = query_bias.astype(jnp.float32)
    value_offset = value_bias.astype(jnp.float32)
    out_offset = out_bias.astype(jnp.float32)
    up_offset = up_bias.astype(jnp.float32)
    down_offset = down_bias.astype(jnp.float32)
    first_gain = attention_gain.astype(jnp.float32)
    first_shift = attention_shift.astype(jnp.float32)
    second_gain = feedforward_gain.astype(jnp.float32)
    second_shift = feedforward_shift.astype(jnp.float32)
    page_count, span_size, model_width = tokens.shape
    patch_span = patches.shape[1]
    seq_count = lax.axis_size("seq")
    slot_size = span_size * seq_count
    patch_slots = patch_span * seq_count
    row_count = span_size + patch_span
    key_count = row_count * seq_count
    head_count = reading_bias_table.shape[0]
    head_size = model_width // head_count
    line_bins = reading_bias_table.shape[1]
    plane_bins = horizontal_bias_table.shape[1]
    score_scale = head_size ** (-0.5)
    seq_index = lax.axis_index("seq")
    text_places = seq_index * span_size + jnp.arange(span_size, dtype=jnp.int32)
    local_cells = seq_index * patch_span + jnp.arange(patch_span, dtype=jnp.int32)
    text_live = text_places[None, :] < page_length[:, None]
    patch_live = grid_live(local_cells)
    text_factor = text_live[:, :, None]
    patch_factor = patch_live[None, :, None]
    masked = tokens * text_factor.astype(jnp.bfloat16)
    rimmed = with_halo(masked, (("seq", 1),), 3)
    reach = GRID_SIDE + 1
    patch_masked = patches * patch_factor.astype(jnp.bfloat16)
    patch_rimmed = with_halo(patch_masked, (("seq", 1),), reach)
    pages = lax.axis_size("page")
    (
        hidden, hidden_low, queries, mixture_low, columns, key_rows, query_rows, taps, keys, values, weights,
    ) = forward(
        pages, page_length, tokens, patches, box_position.transpose(1, 0, 2), (conv_weight.T, patch_conv_weight.T),
        (horizontal_bias_table, vertical_bias_table, reading_bias_table), (query_bias, value_bias),
        (query_weight, key_weight, value_weight),
    )
    places = jnp.stack(
        [seq_index, seq_index % 2, lax.axis_index("page"), seq_index // 2]
    ).astype(jnp.int32)
    def flat(value):
        return value.reshape(-1, value.shape[-1])

    output, patch_output, delta_first, delta_mixture, middle_sums, feedforward_bundle = middle(
        places, hidden, mixture_low, cotangent, patch_cotangent,
        (out_weight, up_weight, down_weight),
        (
            out_bias, down_bias, attention_gain, attention_shift, feedforward_gain, feedforward_shift, up_bias,
        ),
        pages,
    )
    pair_rows = weights.reshape(page_count, head_count // 2, 2 * row_count, -1)
    if in_tiles(model_width, pages):
        tokens_back, patches_back, early_state, late_state, sums, up_in, down_in, mixed_in = backward(
            pages,
            page_length,
            (
                queries, delta_mixture, columns, key_rows, query_rows, tokens, patches, taps, middle_sums,
            ),
            (
                feedforward_bundle, pair_rows, keys, values, hidden_low, delta_first, query_weight, key_weight,
                value_weight,
            ),
            tokens,
            patches,
        )
        (
            query_part, key_part, value_part, out_part, up_part, down_part, text_part, patch_part, line_part,
            across_part, upward_part, *vector_parts, tokens_gradient, patches_gradient,
        ) = finish(
            (early_state, late_state, sums, up_in, down_in, mixed_in),
            (tokens_back, patches_back), model_width, up_weight.shape[1], head_count, line_bins,
            plane_bins,
        )
        return (
            output,
            patch_output,
            tokens_gradient,
            patches_gradient,
            query_part,
            key_part,
            value_part,
            out_part,
            up_part,
            down_part.T,
            text_part.T,
            patch_part.T,
            *vector_parts,
            line_part,
            across_part,
            upward_part,
        )
    delta_first = delta_first.reshape(page_count, row_count, model_width)
    delta_mixture = delta_mixture.reshape(page_count, row_count, model_width)
    early_state = added(feedforward_bundle[0], swap(feedforward_bundle[1], "seq", 1))
    delta_mixture, early_state = lax.optimization_barrier((delta_mixture, early_state))
    delta_query_pages, delta_key_pages, delta_value_pages = [], [], []
    delta_plane, delta_line = 0.0, 0.0
    for page in range(page_count):
        delta_page_queries, delta_blocks, plane_part, line_part = backward_page(
            places,
            columns[page][:, ::128],
            key_rows[page],
            query_rows[page][:, :row_count],
            queries[page * row_count : (page + 1) * row_count],
            keys[page],
            values[page],
            delta_mixture[page],
            pair_rows[page],
        )
        got = swap(delta_blocks[2:], "seq", 1)
        chip_sum = delta_blocks[:2].astype(jnp.float32) + got.astype(jnp.float32)
        got = swap(chip_sum[1].astype(jnp.bfloat16), "seq", 2)
        whole = (chip_sum[0] + got.astype(jnp.float32)).astype(jnp.bfloat16)
        delta_query_pages.append(delta_page_queries)
        delta_key_pages.append(whole[0])
        delta_value_pages.append(whole[1])
        delta_plane = delta_plane + plane_part
        delta_line = delta_line + line_part
    delta_queries = jnp.stack(delta_query_pages)
    delta_keys = jnp.stack(delta_key_pages)
    delta_values = jnp.stack(delta_value_pages)
    delta_plane = clipped(delta_plane, 72, plane_bins)
    delta_line = clipped(delta_line, 32, line_bins)
    delta_across, delta_upward = delta_plane[0], delta_plane[1]
    delta_query_offset = row_sum(delta_queries)
    delta_value_offset = row_sum(delta_values)
    delta_hidden = (
        delta_first
        + back_dot(delta_queries, query_weight)
        + back_dot(delta_keys, key_weight)
        + back_dot(delta_values, value_weight)
    )
    delta_position = delta_hidden[:, :span_size].astype(jnp.bfloat16)
    delta_rim = with_halo(delta_position, (("seq", 1),), 3)
    delta_masked = jnp.zeros((page_count, span_size, model_width), jnp.float32)
    tap_columns = []
    for dilation in (1, 2, 3):
        for offset in (-1, 0, 1):
            column = 3 * (dilation - 1) + offset + 1
            anchor = 3 + offset * dilation
            anchor_back = 3 - offset * dilation
            delta_masked = (
                delta_masked
                + delta_rim[:, anchor_back : anchor_back + span_size, :] * conv_taps[:, column]
            )
            tap_columns.append(
                jnp.einsum(
                    "ptd,ptd->d",
                    delta_position,
                    rimmed[:, anchor : anchor + span_size, :],
                    preferred_element_type=jnp.float32,
                )
            )
    delta_taps = jnp.stack(tap_columns, axis=1)
    tokens_gradient = delta_hidden[:, :span_size] + delta_masked * text_factor.astype(jnp.float32)
    delta_patch_position = delta_hidden[:, span_size:].astype(jnp.bfloat16)
    delta_patch_rim = with_halo(delta_patch_position, (("seq", 1),), reach)
    delta_patch_masked = jnp.zeros((page_count, patch_span, model_width), jnp.float32)
    patch_columns = []
    for vertical in (-1, 0, 1):
        for horizontal in (-1, 0, 1):
            column = 3 * (vertical + 1) + horizontal + 1
            anchor = reach + vertical * GRID_SIDE + horizontal
            anchor_back = reach - vertical * GRID_SIDE - horizontal
            delta_patch_masked = (
                delta_patch_masked
                + delta_patch_rim[:, anchor_back : anchor_back + patch_span, :]
                * patch_taps[:, column]
            )
            patch_columns.append(
                jnp.einsum(
                    "ptd,ptd->d",
                    delta_patch_position,
                    patch_rimmed[:, anchor : anchor + patch_span, :],
                    preferred_element_type=jnp.float32,
                )
            )
    delta_patch_taps = jnp.stack(patch_columns, axis=1)
    patches_gradient = delta_hidden[:, span_size:] + delta_patch_masked * patch_factor.astype(
        jnp.float32
    )
    operands = [flat(value) for value in (hidden_low, delta_queries, delta_keys, delta_values)]
    tail_bundle = indexed_bundle(
        (
            ((operands[0], operands[1], None), (operands[0], operands[3], 0)),
            ((operands[0], operands[2], None), (operands[0], operands[3], 1)),
        ),
        places,
        pages,
    )
    tail_state = added(tail_bundle[0], swap(tail_bundle[1], "seq", 1))
    query_part, key_part, value_part = bundle_parts(
        bundle_sum(tail_state, pages), model_width // pages, places[1]
    )
    up_part, down_part, out_part = bundle_parts(
        bundle_sum(early_state, pages), up_weight.shape[1] // pages, places[1]
    )
    up_part = up_part.reshape(model_width // pages, -1)
    matrix_parts = (query_part, key_part, value_part, out_part, up_part, down_part)
    vector_parts = total_sum(
        (
            delta_taps,
            delta_patch_taps,
            delta_query_offset,
            delta_value_offset,
            middle_sums[OUT_BIAS],
            middle_sums[UP_BIAS : UP_BIAS + 4].reshape(-1),
            middle_sums[DOWN_BIAS],
            middle_sums[FIRST_GAIN],
            middle_sums[FIRST_SHIFT],
            middle_sums[SECOND_GAIN],
            middle_sums[SECOND_SHIFT],
            delta_line,
            delta_across,
            delta_upward,
        )
    )
    return (
        output,
        patch_output,
        tokens_gradient,
        patches_gradient,
        matrix_parts[0],
        matrix_parts[1],
        matrix_parts[2],
        matrix_parts[3],
        matrix_parts[4],
        matrix_parts[5],
        vector_parts[0],
        vector_parts[1],
        vector_parts[2],
        vector_parts[3],
        vector_parts[4],
        vector_parts[5],
        vector_parts[6],
        vector_parts[7],
        vector_parts[8],
        vector_parts[9],
        vector_parts[10],
        vector_parts[11],
        vector_parts[12],
        vector_parts[13],
    )


def solution(mesh):
    in_specs = (
        P("page", "seq", None),
        P("page", "seq", None),
        P("page"),
        P(None, "page", None),
        P(),
        P(),
        P(),
        P(),
        P(),
        P(),
        P(),
        P(),
        P(),
        P(),
        P(),
        P(),
        P(),
        P(),
        P(),
        P(),
        P(),
        P(),
        P(),
        P(),
        P("page", "seq", None),
        P("page", "seq", None),
    )
    out_specs = (
        P("page", "seq", None),
        P("page", "seq", None),
        P("page", "seq", None),
        P("page", "seq", None),
        P("page", "seq"),
        P("page", "seq"),
        P("page", "seq"),
        P("page", "seq"),
        P("page", "seq"),
        P("page", "seq"),
        P(),
        P(),
        P(),
        P(),
        P(),
        P(),
        P(),
        P(),
        P(),
        P(),
        P(),
        P(),
        P(),
        P(),
    )
    return jax.shard_map(shards, mesh=mesh, in_specs=in_specs, out_specs=out_specs, check_vma=False)
```

```python
import functools

import jax
import jax.numpy as jnp
from jax import lax
from jax.experimental import pallas as pl
from jax.experimental.pallas import tpu as pltpu
from jax.sharding import PartitionSpec as P

GRID_SIDE = 8


epsilon = 1e-05
coordinate_step = 16
masked_score = -1000000000.0
patch_pitch = 146
patch_centre = 73


def with_halo(cells, sides, width):
    for axis, dim in sides:
        count = lax.axis_size(axis)
        ends = count - 1
        head = lax.slice_in_dim(cells, 0, width, axis=dim)
        tail = lax.slice_in_dim(cells, cells.shape[dim] - width, cells.shape[dim], axis=dim)
        cells = jnp.concatenate(
            [
                lax.ppermute(tail, axis, [(i, (i + 1) % count) for i in range(ends)]),
                cells,
                lax.ppermute(head, axis, [((i + 1) % count, i) for i in range(ends)]),
            ],
            axis=dim,
        )
    return cells


def layer_norm(values, gain_vector, shift_vector):
    row_mean = jnp.mean(values, axis=-1, keepdims=True)
    centred = values - row_mean
    variance = jnp.mean(centred * centred, axis=-1, keepdims=True)
    return centred * lax.rsqrt(variance + epsilon) * gain_vector + shift_vector


def gelu_exact(values):
    return jax.nn.gelu(values, approximate=False)


def flat_dot(operand, matrix):
    front = operand.shape[:-1]
    result = jnp.dot(
        operand.reshape(-1, operand.shape[-1]), matrix, preferred_element_type=jnp.float32
    )
    return result.reshape(front + (matrix.shape[-1],))


def back_dot(operand, matrix):
    front = operand.shape[:-1]
    result = lax.dot_general(
        operand.reshape(-1, operand.shape[-1]),
        matrix,
        (((1,), (1,)), ((), ())),
        preferred_element_type=jnp.float32,
    )
    return result.reshape(front + (matrix.shape[0],))


def outer_dot(operand, gradient):
    return lax.dot_general(
        operand.reshape(-1, operand.shape[-1]),
        gradient.reshape(-1, gradient.shape[-1]),
        (((0,), (0,)), ((), ())),
        preferred_element_type=jnp.float32,
    )


def row_sum(gradient):
    return jnp.sum(gradient.astype(jnp.float32).reshape(-1, gradient.shape[-1]), axis=0)


def swap(value, axis, bit):
    count = lax.axis_size(axis)
    return lax.ppermute(value, axis, [(i, i ^ bit) for i in range(count)])


def total_sum(vectors):
    flat = jnp.concatenate([vector.reshape(-1) for vector in vectors])
    flat = jnp.pad(flat, (0, -flat.size % 1024)).reshape(-1, 128)
    for bit in (1, 2):
        flat = flat + swap(flat, "seq", bit)
    bit = 1
    while bit < lax.axis_size("page"):
        flat = flat + swap(flat, "page", bit)
        bit *= 2
    flat = flat.reshape(-1)
    result, start = [], 0
    for vector in vectors:
        result.append(flat[start : start + vector.size].reshape(vector.shape))
        start += vector.size
    return result


def query_places(seq_index, shape, span, patch_span, text_slots):
    row = lax.broadcasted_iota(jnp.int32, shape, 0)
    return jnp.where(
        row < span, seq_index * span + row, text_slots + seq_index * patch_span + row - span
    )


FIXED = 2048.0


def lookup(table_row, lanes):
    return jnp.take_along_axis(jnp.broadcast_to(table_row, lanes.shape), lanes, axis=1)


HEAD_LANES = 64


def split_heads(group):
    lane = lax.broadcasted_iota(jnp.int32, group.shape, 1) // HEAD_LANES
    zero = jnp.zeros_like(group)
    return jnp.concatenate(
        [jnp.where(lane == head, group, zero) for head in range(group.shape[1] // HEAD_LANES)], axis=0
    )


def merge_heads(rows):
    heads = rows.shape[1] // HEAD_LANES
    count = rows.shape[0] // heads
    lane = lax.broadcasted_iota(jnp.int32, (count, rows.shape[1]), 1) // HEAD_LANES
    merged = rows[:count]
    for head in range(1, heads):
        merged = jnp.where(lane == head, rows[head * count : (head + 1) * count], merged)
    return merged


def dot_nt(left, right):
    return lax.dot_general(left, right, (((1,), (1,)), ((), ())), preferred_element_type=jnp.float32)


def dot_nn(left, right):
    return lax.dot_general(left, right, (((1,), (0,)), ((), ())), preferred_element_type=jnp.float32)


def dot_tn(left, right):
    return lax.dot_general(left, right, (((0,), (0,)), ((), ())), preferred_element_type=jnp.float32)


CHUNK = 16
FORWARD_CHUNK = 48


MESH = pl.DeviceIdType.MESH


def places_of(pages):
    page = lax.axis_index("page")
    seq = lax.axis_index("seq")
    bits = []
    rest = page
    for _ in range(pages.bit_length() - 1):
        bits.append(rest % 2)
        rest = rest // 2
    return page, bits, seq, seq // 2, seq % 2


def sibling_of(seq):
    return seq + 1 - 2 * (seq % 2)


def across_of(seq):
    return seq + 2 - 4 * (seq // 2)


def remote(source, target, send, receive, page, seq):
    return pltpu.make_async_remote_copy(
        src_ref=source, dst_ref=target, send_sem=send, recv_sem=receive, device_id=(page, seq), device_id_type=MESH
    )


def column_of(row):
    square = jnp.broadcast_to(row.astype(jnp.float32), (128, 128)).T
    return square[:, 0:1].astype(jnp.int32)


def forward_kernel(
    pages,
    staging, length_ref, box_ref, text_taps_ref, patch_taps_ref, across_table_ref, upward_table_ref, line_table_ref,
    query_bias_ref, value_bias_ref, tokens_any, patches_any, query_weight_any, key_weight_any, value_weight_any,
    hidden_ref, hidden_low_ref, query_ref, mixture_ref, columns_ref, rows_ref, query_rows_ref, taps_ref, key_any,
    value_any, weights_any,
    own, matrices, key_ref, value_ref, weights_ref, arrived, text, grid, low, scores, across_ref, upward_ref,
    live_ref, line_ref, packed_ref, table_ref, vector_ref,
    load_sem, store_sem, send_sem, recv_sem,
):
    page_at, _, seq, _, _ = places_of(pages)
    count, span, width = tokens_any.shape
    patch_span = patches_any.shape[1]
    row_count = span + patch_span
    key_pad = key_ref.shape[1]
    text_slots = 4 * span
    rim = 8
    loads = [
        pltpu.make_async_copy(source, target, load_sem.at[index])
        for index, (source, target) in enumerate(
            (
                (tokens_any, own.at[:, 0:span]), (patches_any, own.at[:, span:row_count]),
                (key_weight_any, matrices.at[1]), (value_weight_any, matrices.at[2]), (query_weight_any, matrices.at[0]),
            )
        )
    ]
    for copy in loads:
        copy.start()

    def stores(page):
        return [
            pltpu.make_async_copy(source.at[page], target.at[page], store_sem.at[index, page])
            for index, (source, target) in enumerate(
                ((key_ref, key_any), (value_ref, value_any), (weights_ref, weights_any))
            )
        ]

    groups = weights_ref.shape[1]
    members = weights_ref.shape[2] // row_count
    pairs = groups * members // 2
    peers = (sibling_of(seq), across_of(seq))
    barrier = pltpu.get_barrier_semaphore()
    for peer in peers:
        pl.semaphore_signal(barrier, inc=1, device_id=(page_at, peer), device_id_type=MESH)
    pl.semaphore_wait(barrier, 2)

    def first_copies(page, side):
        return (
            remote(
                tokens_any.at[page], arrived.at[side, page, 0:span], send_sem.at[2 * side, page],
                recv_sem.at[2 * side, page], page_at, peers[side],
            ),
            remote(
                patches_any.at[page], arrived.at[side, page, span:row_count], send_sem.at[2 * side + 1, page],
                recv_sem.at[2 * side + 1, page], page_at, peers[side],
            ),
        )

    def onward_copy(page):
        return remote(
            arrived.at[1, page], arrived.at[2, page], send_sem.at[4, page], recv_sem.at[4, page], page_at, peers[0]
        )

    for page in range(count):
        for side in range(2):
            for copy in first_copies(page, side):
                copy.start()

    for copy in staging:
        copy.wait()
    table_ref[...] = jnp.zeros_like(table_ref)
    start = 0
    for source in (across_table_ref, upward_table_ref, line_table_ref):
        heads, bins = source.shape
        table_ref[0:heads, start : start + bins] = source[...].astype(jnp.float32)
        start += bins
    steps = jnp.floor(table_ref[...] * FIXED + 0.5).astype(jnp.int32)
    vector_ref[0:1, :] = query_bias_ref[...].astype(jnp.float32).reshape(1, width)
    vector_ref[1:2, :] = value_bias_ref[...].astype(jnp.float32).reshape(1, width)
    taps_ref[...] = jnp.zeros_like(taps_ref)
    taps_ref[0:9, :] = text_taps_ref[...].astype(jnp.float32)
    taps_ref[9:18, :] = patch_taps_ref[...].astype(jnp.float32)
    for pair in range(pairs):
        words = (steps[2 * pair : 2 * pair + 1] + 8192) + steps[2 * pair + 1 : 2 * pair + 2] * 65536
        packed_ref[0, pair : pair + 1, :] = words[:, 0:128]
        packed_ref[1, pair : pair + 1, :] = words[:, 128:256]
    key = lax.broadcasted_iota(jnp.int32, (row_count, key_pad), 1)
    place = query_places(seq, (row_count, key_pad), span, patch_span, text_slots)
    across_ref[...] = jnp.clip(key - place, -16, 15) + 16

    def fill(pair, carry):
        row = packed_ref[1, pl.ds(pair, 1), :]
        for at in range(0, key_pad, 128):
            line_ref[pair, :, at : at + 128] = lookup(row, across_ref[:, at : at + 128])
        return carry

    lax.fori_loop(0, pairs, fill, 0)
    text[0:rim, :] = jnp.zeros((rim, width), jnp.float32)
    text[rim + text_slots :, :] = jnp.zeros((rim, width), jnp.float32)
    grid[0:patch_span, :] = jnp.zeros((patch_span, width), jnp.float32)
    grid[patch_span * 5 :, :] = jnp.zeros((patch_span, width), jnp.float32)
    low[row_count * 4 :, :] = jnp.zeros((key_pad - row_count * 4, width), jnp.bfloat16)
    lanes = 256
    group_width = members * HEAD_LANES
    power = 1.4426950408889634 / FIXED
    for copy in first_copies(0, 1):
        copy.wait_recv()
    onward_copy(0).start()
    for copy in loads:
        copy.wait()

    def page_step(page, carry):
        length = length_ref[page]
        base = page * row_count
        cell = lax.broadcasted_iota(jnp.int32, (1, 128), 1)
        query_cell = seq * patch_span + cell
        row_cell = seq * patch_span + lax.broadcasted_iota(jnp.int32, (patch_span, 1), 0)
        for plane in range(2):
            box = box_ref[page, plane : plane + 1, :]
            patch = 146 * ((cell % GRID_SIDE) if plane == 0 else (cell // GRID_SIDE)) + 73
            own_patch = 146 * ((query_cell % GRID_SIDE) if plane == 0 else (query_cell // GRID_SIDE)) + 73
            column_patch = 146 * ((row_cell % GRID_SIDE) if plane == 0 else (row_cell // GRID_SIDE)) + 73
            rows_ref[page, plane : plane + 1, 0:text_slots] = box
            rows_ref[page, plane : plane + 1, text_slots:key_pad] = patch
            own_box = rows_ref[page, plane : plane + 1, pl.ds(pl.multiple_of(seq * span, 128), span)]
            query_rows_ref[page, plane : plane + 1, 0:span] = own_box
            query_rows_ref[page, plane : plane + 1, span:256] = own_patch
            columns_ref[page, 0:span, plane * 128 : (plane + 1) * 128] = jnp.broadcast_to(
                column_of(own_box), (span, 128)
            )
            columns_ref[page, span:row_count, plane * 128 : (plane + 1) * 128] = jnp.broadcast_to(
                column_patch, (patch_span, 128)
            )
        for plane, lanes_ref in enumerate((across_ref, upward_ref)):
            difference = rows_ref[page, plane : plane + 1, :] - columns_ref[page, :, plane * 128 : plane * 128 + 1]
            lanes_ref[...] = jnp.clip(difference >> 4, -32, 31) + (32 + 64 * plane)
        key_at = lax.broadcasted_iota(jnp.int32, live_ref.shape, 1)
        key_cell = key_at - text_slots
        live = (key_at < length) | (
            (key_cell >= 0) & ((key_cell >> 3) < GRID_SIDE - 1) & ((key_cell & 7) < GRID_SIDE - 1)
        )
        live_ref[...] = jnp.where(live, 0.0, masked_score * FIXED)
        for copy in first_copies(page, 0):
            copy.wait_recv()
        onward_copy(page).wait_recv()

        def block_of(step, start, stop, at):
            if step:
                return arrived[step - 1, page, start:stop, at].astype(jnp.float32)
            if start:
                return own[page, span:row_count, at].astype(jnp.float32)
            return own[page, 0:span, at].astype(jnp.float32)

        def slot_of(step):
            return (seq, peers[0], peers[1], sibling_of(peers[1]))[step]

        everything = slice(0, width)
        for step in range(4):
            where = slot_of(step)
            at_place = where * span + lax.broadcasted_iota(jnp.int32, (span, 1), 0)
            text[pl.ds(pl.multiple_of(rim + where * span, 8), span), :] = jnp.where(
                at_place < length, block_of(step, 0, span, everything), 0.0
            )
            at_cell = where * patch_span + lax.broadcasted_iota(jnp.int32, (patch_span, 1), 0)
            cell_live = ((at_cell >> 3) < GRID_SIDE - 1) & ((at_cell & 7) < GRID_SIDE - 1)
            grid[pl.ds(pl.multiple_of(patch_span + where * patch_span, 8), patch_span), :] = jnp.where(
                cell_live, block_of(step, span, row_count, everything), 0.0
            )
        for step in range(4):
            where = slot_of(step)

            def convolve(tile, carry):
                at = pl.ds(pl.multiple_of(tile * lanes, lanes), lanes)
                window = text[pl.ds(pl.multiple_of(where * span, 8), span + 2 * rim), at]
                centre = taps_ref[1:2, at] + taps_ref[4:5, at] + taps_ref[7:8, at]
                total = block_of(step, 0, span, at) + window[rim : rim + span] * centre
                for dilation in (1, 2, 3):
                    for offset in (-1, 1):
                        tap = 3 * (dilation - 1) + offset + 1
                        anchor = rim + offset * dilation
                        total = total + window[anchor : anchor + span] * taps_ref[tap : tap + 1, at]
                low[pl.ds(pl.multiple_of(where * span, 16), span), at] = total.astype(jnp.bfloat16)
                window = grid[pl.ds(pl.multiple_of(where * patch_span, 8), 3 * patch_span), at]
                patch_total = block_of(step, span, row_count, at)
                for vertical in (-1, 0, 1):
                    for horizontal in (-1, 0, 1):
                        tap = 9 + 3 * (vertical + 1) + horizontal + 1
                        anchor = patch_span + vertical * GRID_SIDE + horizontal
                        patch_total = patch_total + window[anchor : anchor + patch_span] * taps_ref[tap : tap + 1, at]
                low[pl.ds(pl.multiple_of(text_slots + where * patch_span, 16), patch_span), at] = (
                    patch_total.astype(jnp.bfloat16)
                )
                if step == 0:
                    for first, rows_here, value in ((0, span, total), (span, patch_span, patch_total)):
                        here = pl.ds(pl.multiple_of(base + first, 16), rows_here)
                        hidden_ref[here, at] = value
                        hidden_low_ref[here, at] = value.astype(jnp.bfloat16)
                return carry

            lax.fori_loop(0, width // lanes, convolve, 0)
        own_rows = pl.ds(pl.multiple_of(base, 16), row_count)

        key_ref[page] = dot_nn(low[...], matrices[1]).astype(jnp.bfloat16)
        value_ref[page] = (dot_nn(low[...], matrices[2]) + vector_ref[1:2, :]).astype(jnp.bfloat16)
        query_ref[own_rows, :] = (
            (dot_nn(hidden_low_ref[own_rows, :], matrices[0]) + vector_ref[0:1, :]).astype(jnp.bfloat16)
            * jnp.bfloat16(0.125)
        )

        @pl.when(page < count - 1)
        def _():
            for copy in first_copies(page + 1, 1):
                copy.wait_recv()
            onward_copy(page + 1).start()

        def attend(group, carry):
            at = pl.ds(pl.multiple_of(group * group_width, group_width), group_width)
            scores[...] = dot_nt(split_heads(query_ref[own_rows, at] * jnp.bfloat16(FIXED)), key_ref[page, :, at])
            for start, sub in ((start, sub) for start in range(0, row_count, FORWARD_CHUNK) for sub in range(members // 2)):
                pair = group * (members // 2) + sub
                plane_row = packed_ref[0, pl.ds(pair, 1), :]
                here = slice(start, start + FORWARD_CHUNK)
                packed = []
                for block_at in range(0, key_pad, 128):
                    lane = slice(block_at, block_at + 128)
                    packed.append(
                        line_ref[pair, here, lane]
                        + lookup(plane_row, across_ref[here, lane])
                        + lookup(plane_row, upward_ref[here, lane])
                    )
                for side in range(2):
                    first = (2 * sub + side) * row_count + start
                    there = slice(first, first + FORWARD_CHUNK)
                    parts, top = [], None
                    for index, word in enumerate(packed):
                        lane = slice(128 * index, 128 * (index + 1))
                        field = (word >> 16) if side else (word & 0xFFFF)
                        part = (scores[there, lane] + field.astype(jnp.float32)) + live_ref[0:1, lane]
                        top = part if top is None else jnp.maximum(top, part)
                        parts.append(part)
                    top = jnp.max(top, axis=1, keepdims=True)
                    parts = [jnp.exp2((part - top) * power) for part in parts]
                    total = parts[0]
                    for part in parts[1:]:
                        total = total + part
                    inverse = 1.0 / jnp.sum(total, axis=1, keepdims=True)
                    for index, part in enumerate(parts):
                        weights_ref[page, group, there, 128 * index : 128 * (index + 1)] = (part * inverse).astype(
                            jnp.bfloat16
                        )
            mixture_ref[own_rows, at] = merge_heads(
                dot_nn(weights_ref[page, group], value_ref[page, :, at])
            ).astype(jnp.bfloat16)
            return carry

        lax.fori_loop(0, groups, attend, 0)
        for copy in stores(page):
            copy.start()
        return carry

    lax.fori_loop(0, count, page_step, 0)
    for page in range(count):
        for side in range(2):
            for copy in first_copies(page, side):
                copy.wait_send()
        onward_copy(page).wait_send()
        for copy in stores(page):
            copy.wait()


VMEM = pltpu.VMEM
KERNEL_VMEM = 62 * 1024 * 1024


def in_vmem(count):
    return [pl.BlockSpec(memory_space=VMEM)] * count


def staged(kernel, first, count):
    def run(*refs):
        *refs, semaphore = refs
        refs, buffers = list(refs[:-count]), refs[-count:]
        copies = [
            pltpu.make_async_copy(refs[first + index], buffers[index], semaphore.at[index]) for index in range(count)
        ]
        for copy in copies:
            copy.start()
        refs[first : first + count] = buffers
        kernel(copies, *refs)

    return run


def stage_for(values):
    return [VMEM(value.shape, value.dtype) for value in values] + [pltpu.SemaphoreType.DMA((len(values),))]


def position():
    seq = lax.axis_index("seq")
    return seq, seq % 2, lax.axis_index("page"), seq // 2


def anywhere(count):
    return [pl.BlockSpec(memory_space=pl.ANY)] * count


def forward(pages, lengths, tokens, patches, box, taps, tables, biases, matrices):
    count, span, width = tokens.shape
    patch_span = patches.shape[1]
    row_count = span + patch_span
    total_rows = count * row_count
    key_pad = -(-4 * row_count // 128) * 128
    heads = tables[0].shape[0]
    pairs = heads // 2
    members = 4 if heads % 4 == 0 else 2
    groups = heads // members
    small = (box, *taps, *tables, *biases)
    bf16, f32, i32 = jnp.bfloat16, jnp.float32, jnp.int32
    own = jax.ShapeDtypeStruct((total_rows, width), bf16)
    every = jax.ShapeDtypeStruct((count, key_pad, width), bf16)
    return pl.pallas_call(
        staged(functools.partial(forward_kernel, pages), 1, len(small)),
        out_shape=(
            jax.ShapeDtypeStruct((total_rows, width), f32), own, own, own,
            jax.ShapeDtypeStruct((count, row_count, 256), i32),
            jax.ShapeDtypeStruct((count, 8, key_pad), i32),
            jax.ShapeDtypeStruct((count, 8, 256), i32),
            jax.ShapeDtypeStruct((24, width), f32),
            every, every,
            jax.ShapeDtypeStruct((count, groups, members * row_count, key_pad), bf16),
        ),
        in_specs=[pl.BlockSpec(memory_space=pltpu.SMEM)] + anywhere(len(small) + 5),
        out_specs=tuple(in_vmem(8) + anywhere(3)),
        scratch_shapes=[
            VMEM((count, row_count, width), bf16),
            VMEM((3, width, width), bf16),
            VMEM((count, key_pad, width), bf16),
            VMEM((count, key_pad, width), bf16),
            VMEM((count, groups, members * row_count, key_pad), bf16),
            VMEM((3, count, row_count, width), bf16),
            VMEM((4 * span + 16, width), f32),
            VMEM((6 * patch_span, width), f32),
            VMEM((key_pad, width), bf16),
            VMEM((members * row_count, key_pad), f32),
            VMEM((row_count, key_pad), i32),
            VMEM((row_count, key_pad), i32),
            VMEM((8, key_pad), f32),
            VMEM((pairs, row_count, key_pad), i32),
            VMEM((2, 8, 128), i32),
            VMEM((-(-heads // 8) * 8, 256), f32),
            VMEM((8, width), f32),
            pltpu.SemaphoreType.DMA((5,)),
            pltpu.SemaphoreType.DMA((3, count)),
            pltpu.SemaphoreType.DMA((5, count)),
            pltpu.SemaphoreType.DMA((5, count)),
        ]
        + stage_for(small),
        compiler_params=pltpu.CompilerParams(
            collective_id=0, has_side_effects=True, vmem_limit_bytes=KERNEL_VMEM
        ),
        cost_estimate=pl.CostEstimate(flops=8_000_000_000, bytes_accessed=25_000_000, transcendentals=3_000_000),
        name="forward",
    )(lengths, *small, tokens, patches, *matrices)


def backward_page_kernel(
    scalar_ref, columns_ref, rows_ref, query_rows_ref, query_ref, key_ref, value_ref, mixture_back_ref, weights_ref,
    query_back_ref, block_back_ref, plane_back_ref, line_back_ref,
    back, steps, mask_ref, hot_ref, query_hot_ref, band_ref,
):
    seq_index = scalar_ref[0]
    row_count, width = query_ref.shape
    key_pad = key_ref.shape[0]
    count = 4
    patch_span = GRID_SIDE * GRID_SIDE // count
    span = row_count - patch_span
    text_slots = span * count
    columns, rows = columns_ref[...], rows_ref[...]
    mask_ref[:, 0:key_pad] = ((rows[0:1, :] & 15) < (columns[:, 0:1] & 15)).astype(jnp.float32).astype(jnp.bfloat16)
    mask_ref[:, key_pad:] = ((rows[1:2, :] & 15) < (columns[:, 1:2] & 15)).astype(jnp.float32).astype(jnp.bfloat16)
    bin_at = lax.broadcasted_iota(jnp.int32, (128, key_pad), 0) - 1
    key_block = lax.broadcasted_iota(jnp.int32, (128, key_pad), 1) >> 4
    for side in range(2):
        key_bin = rows[side : side + 1, :] >> 4
        plain = (key_bin == bin_at).astype(jnp.float32)
        lower = (key_bin - 1 == bin_at).astype(jnp.float32)
        plain, lower = jnp.where(bin_at < 64, plain, 0.0), jnp.where(bin_at < 64, lower, 0.0)
        mine = slice(128 * side, 128 * (side + 1))
        other = slice(128 * (1 - side), 128 * (2 - side))
        change = lower - plain
        if side == 0:
            plain = jnp.where(bin_at - 71 == key_block, 1.0, plain)
        hot_ref[mine, 0:key_pad] = plain.astype(jnp.bfloat16)
        hot_ref[mine, (1 + side) * key_pad : (2 + side) * key_pad] = change.astype(jnp.bfloat16)
        hot_ref[other, (1 + side) * key_pad : (2 + side) * key_pad] = jnp.zeros((128, key_pad), jnp.bfloat16)
    half_bin = lax.broadcasted_iota(jnp.int32, (72, row_count), 0)
    for side in range(2):
        query_hot_ref[72 * side : 72 * (side + 1), :] = (
            (71 - (query_rows_ref[side : side + 1, :] >> 4) == half_bin).astype(jnp.float32).astype(jnp.bfloat16)
        )
    lane128 = lax.broadcasted_iota(jnp.int32, (row_count, 128), 1)
    place = query_places(seq_index, (row_count, 128), span, patch_span, text_slots)
    aim = place + lane128 - 32
    near = (lane128 < 64) & (aim >= 0) & (aim < text_slots + patch_span * count)
    apart = (aim >> 4) - (place >> 4)
    near = near & (apart >= -1) & (apart <= 1)
    band_ref[...] = jnp.where(near, aim, -1)
    pair_width = 128
    line_back_ref[...] = jnp.zeros_like(line_back_ref)
    plane_back_ref[...] = jnp.zeros_like(plane_back_ref)

    def attend(pair, carry):
        at = pl.ds(pl.multiple_of(pair * pair_width, pair_width), pair_width)
        both_query = split_heads(query_ref[:, at])
        both_back = split_heads(mixture_back_ref[:, at])
        back[...] = dot_nt(both_back, value_ref[:, at])
        for start in range(0, 2 * row_count, CHUNK):
            there = slice(start, start + CHUNK)
            here = slice(start % row_count, start % row_count + CHUNK)
            parts, total = [], None
            for block_at in range(0, key_pad, 128):
                lane = slice(block_at, block_at + 128)
                part = weights_ref[pair, there, lane].astype(jnp.float32)
                product = part * back[there, lane]
                total = product if total is None else total + product
                parts.append(part)
            mean = jnp.sum(total, axis=1, keepdims=True)
            for index, part in enumerate(parts):
                lane = slice(128 * index, 128 * (index + 1))
                step = (part * (back[there, lane] - mean)).astype(jnp.bfloat16)
                steps[there, lane] = step
                steps[there, key_pad + 128 * index : key_pad + 128 * (index + 1)] = step * mask_ref[here, lane]
                steps[there, 2 * key_pad + 128 * index : 2 * key_pad + 128 * (index + 1)] = (
                    step * mask_ref[here, key_pad + 128 * index : key_pad + 128 * (index + 1)]
                )
        query_back_ref[:, at] = (merge_heads(dot_nn(steps[:, 0:key_pad], key_ref[:, at])) * 0.125).astype(
            jnp.bfloat16
        )
        for kind, value in enumerate(
            (dot_tn(steps[:, 0:key_pad], both_query), dot_tn(weights_ref[pair], both_back))
        ):
            value = value.astype(jnp.bfloat16)
            for where in range(count):
                step_at = seq_index ^ where
                slot = (step_at & 1) * 2 + (step_at >> 1)
                block_back_ref[slot, kind, 0:span, at] = value[where * span : (where + 1) * span]
                block_back_ref[slot, kind, span:row_count, at] = value[
                    text_slots + where * patch_span : text_slots + (where + 1) * patch_span
                ]
        bins = dot_nt(steps[...], hot_ref[...])
        low_bins = bins.astype(jnp.bfloat16)
        lane_one = lax.broadcasted_iota(jnp.int32, (1, 128), 1)
        far = lane128 - 72 - (place >> 4)
        in_line = (lane128 >= 72) & (lane128 < 72 + key_pad // 16)
        for side in range(2):
            head = pl.ds(2 * pair + side, 1)
            own = slice(side * row_count, (side + 1) * row_count)
            both = dot_nn(query_hot_ref[...], low_bins[own])
            for plane in range(2):
                table = both[72 * plane : 72 * (plane + 1), 128 * plane : 128 * (plane + 1)]
                wide_lane = lax.broadcasted_iota(jnp.int32, table.shape, 1)
                table = jnp.where(wide_lane < 72, table, 0.0)
                table = jnp.concatenate([table, jnp.zeros_like(table)], axis=1)
                sheared = pltpu.roll(table, 0, 1, stride=1, stride_axis=0)
                plane_back_ref[plane, head, :] = jnp.sum(sheared, axis=0, keepdims=True)
            line_bins = bins[own, 0:128]
            low_tail = jnp.sum(jnp.where(in_line & (far <= -2), line_bins, 0.0), axis=(0, 1), keepdims=True)
            high_tail = jnp.sum(jnp.where(in_line & (far >= 2), line_bins, 0.0), axis=(0, 1), keepdims=True)
            band = jnp.zeros((1, 128), jnp.float32)
            base = side * row_count
            for first, rows_here, block in (
                (0, span, seq_index),
                (0, 32, jnp.maximum(seq_index - 1, 0)),
                (span - 32, 32, seq_index + 1),
                (span, patch_span, count - 1),
                (span, patch_span, count),
            ):
                aims = band_ref[first : first + rows_here, :]
                source = steps[
                    base + first : base + first + rows_here, pl.ds(pl.multiple_of(block * 128, 128), 128)
                ].astype(jnp.float32)
                taken = jnp.take_along_axis(source, aims & 127, axis=1)
                right = (aims >> 7) == block
                if first == 0 and rows_here == 32:
                    right = right & (seq_index > 0)
                band = band + jnp.sum(jnp.where(right, taken, 0.0), axis=0, keepdims=True)
            line_back_ref[head, :] = (
                band + jnp.where(lane_one == 0, low_tail, 0.0) + jnp.where(lane_one == 63, high_tail, 0.0)
            )
        return carry

    lax.fori_loop(0, width // pair_width, attend, 0)


def backward_page(scalars, columns, rows, query_rows, queries, keys, values, mixture_back, weights):
    row_count, width = queries.shape
    key_pad = keys.shape[0]
    heads = 2 * weights.shape[0]
    return pl.pallas_call(
        backward_page_kernel,
        out_shape=(
            jax.ShapeDtypeStruct((row_count, width), jnp.bfloat16),
            jax.ShapeDtypeStruct((4, 2, row_count, width), jnp.bfloat16),
            jax.ShapeDtypeStruct((2, heads, 256), jnp.float32),
            jax.ShapeDtypeStruct((heads, 128), jnp.float32),
        ),
        in_specs=[pl.BlockSpec(memory_space=pltpu.SMEM)] + in_vmem(8),
        out_specs=tuple(in_vmem(4)),
        scratch_shapes=[
            pltpu.VMEM((2 * row_count, key_pad), jnp.float32),
            pltpu.VMEM((2 * row_count, 3 * key_pad), jnp.bfloat16),
            pltpu.VMEM((row_count, 2 * key_pad), jnp.bfloat16),
            pltpu.VMEM((256, 3 * key_pad), jnp.bfloat16),
            pltpu.VMEM((144, row_count), jnp.bfloat16),
            pltpu.VMEM((row_count, 128), jnp.int32),
        ],
        compiler_params=pltpu.CompilerParams(vmem_limit_bytes=KERNEL_VMEM),
        cost_estimate=pl.CostEstimate(flops=3_000_000_000, bytes_accessed=6_000_000, transcendentals=1_000_000),
        name="backward_page",
    )(scalars, columns, rows, query_rows, queries, keys, values, mixture_back, weights)


def early_orders(far, side):
    return (far[1], far[0], side) + tuple(far[2:]), (far[0], far[1], side) + tuple(far[2:])


def slot_of_bits(bits):
    slot = 0
    for bit in bits:
        slot = slot * 2 + bit
    return slot


def apart(one, other):
    return (one + other) % 2


def early_slots(scalar_ref, page, column, levels):
    far = [apart((page >> level) & 1, (scalar_ref[2] >> level) & 1) for level in range(levels)]
    side = apart(column, scalar_ref[3])
    return [slot_of_bits(order) for order in early_orders(far, side)]


NORM_CHUNK = 48


def norm_rows(values):
    mean = jnp.mean(values, axis=-1, keepdims=True)
    centred = values - mean
    scale = lax.rsqrt(jnp.mean(centred * centred, axis=-1, keepdims=True) + epsilon)
    return centred * scale, scale


def norm_back(delta, unit, scale):
    return scale * (
        delta
        - jnp.mean(delta, axis=-1, keepdims=True)
        - unit * jnp.mean(delta * unit, axis=-1, keepdims=True)
    )


def column_sum(values):
    return jnp.sum(values, axis=0, keepdims=True)


OUT_BIAS, DOWN_BIAS, FIRST_GAIN, FIRST_SHIFT, SECOND_GAIN, SECOND_SHIFT = range(6)
UP_BIAS = 6


def middle_kernel(
    pages, direct,
    *rest,
):
    scalar_ref = position()
    arguments, rest = rest[:14], rest[14:]
    output_ref, patch_output_ref, first_back_ref, mixture_back_ref, sums_ref, *rest = rest
    *rest, vector_ref, load_sem, store_sem = rest
    copied, rest = rest[-14:], rest[:-14]
    hidden_ref, mixture_ref, cotangent_ref, patch_cotangent_ref, out_weight_ref, up_weight_ref, down_weight_ref = copied[:7]
    loads = [
        pltpu.make_async_copy(source, target, load_sem.at[index])
        for index, (source, target) in enumerate(zip(arguments, copied, strict=True))
    ]
    for index in (*range(7, 14), 1, 4, 0, 5, 6, 2, 3):
        loads[index].start()
    if direct:
        bundle_any, *rest, bundle_ref = rest
    else:
        normed_out_ref, up_out_ref, activated_out_ref, down_out_ref, attention_out_ref, *rest = rest
    state, unit, scale_ref, normed, activated, slope, up_back, down_back, attention_back, flipped = rest
    count, span, width = output_ref.shape
    patch_span = patch_output_ref.shape[1]
    row_count = span + patch_span
    total_rows = count * row_count
    wide = up_weight_ref.shape[1]
    lanes = width
    sums_ref[...] = jnp.zeros_like(sums_ref)

    def tile_at(tile):
        return pl.ds(pl.multiple_of(tile * lanes, lanes), lanes)

    def attention_tile(tile, carry):
        at = tile_at(tile)
        state[:, at] = hidden_ref[:, at] + (dot_nn(mixture_ref[...], out_weight_ref[:, at]) + vector_ref[2:3, at])
        return carry

    for index in (*range(7, 14), 0, 1, 4):
        loads[index].wait()
    for index, source in enumerate(copied[7:13]):
        vector_ref[2 + index : 3 + index, :] = source[...].astype(jnp.float32).reshape(1, width)
    for index in range(wide // width):
        part = copied[13][pl.ds(index * width, width)]
        vector_ref[8 + index : 9 + index, :] = part.astype(jnp.float32).reshape(1, width)
    lax.fori_loop(0, width // lanes, attention_tile, 0)

    def first_norm(chunk, carry):
        here = pl.ds(pl.multiple_of(chunk * NORM_CHUNK, 16), NORM_CHUNK)
        rows, scale = norm_rows(state[here, :])
        unit[here, :] = rows
        scale_ref[here, :] = jnp.broadcast_to(scale, (NORM_CHUNK, 128))
        rows = rows * vector_ref[4:5, :] + vector_ref[5:6, :]
        state[here, :] = rows
        normed[here, :] = rows.astype(jnp.bfloat16)
        return carry

    lax.fori_loop(0, total_rows // NORM_CHUNK, first_norm, 0)

    def up_tile(tile, carry):
        at = tile_at(tile)
        branch = dot_nn(normed[...], up_weight_ref[:, at]) + vector_ref[pl.ds(8 + tile, 1), :]
        chance = 0.5 * (1.0 + lax.erf(branch * 0.7071067811865476))
        activated[:, at] = (branch * chance).astype(jnp.bfloat16)
        slope[:, at] = chance + branch * (jnp.exp(branch * branch * -0.5) * 0.3989422804014327)
        return carry

    loads[5].wait()
    lax.fori_loop(0, wide // lanes, up_tile, 0)

    def down_tile(tile, carry):
        at = tile_at(tile)
        state[:, at] = state[:, at] + (dot_nn(activated[...], down_weight_ref[:, at]) + vector_ref[3:4, at])
        return carry

    for index in (2, 3, 6):
        loads[index].wait()
    lax.fori_loop(0, width // lanes, down_tile, 0)

    def second_norm(start, rows_here, page, out_ref, delta_ref):
        here = pl.ds(pl.multiple_of(page * row_count + start, 16), rows_here)
        there = pl.ds(0 if start == span else start, rows_here)
        rows, scale = norm_rows(state[here, :])
        out_ref[page, there, :] = rows * vector_ref[6:7, :] + vector_ref[7:8, :]
        delta = delta_ref[page, there, :].astype(jnp.float32)
        back = norm_back(delta * vector_ref[6:7, :], rows, scale)
        state[here, :] = back
        low = back.astype(jnp.bfloat16)
        down_back[here, :] = low
        for index, value in (
            (SECOND_GAIN, delta * rows), (SECOND_SHIFT, delta), (DOWN_BIAS, low.astype(jnp.float32))
        ):
            sums_ref[index : index + 1, :] += column_sum(value)

    def second_page(page, carry):
        for start in range(0, span, 32):
            second_norm(start, 32, page, output_ref, cotangent_ref)
        second_norm(span, patch_span, page, patch_output_ref, patch_cotangent_ref)
        return carry

    lax.fori_loop(0, count, second_page, 0)

    def up_back_tile(tile, carry):
        at = tile_at(tile)
        low = (dot_nt(down_back[...], down_weight_ref[at, :]) * slope[:, at]).astype(jnp.bfloat16)
        up_back[:, at] = low
        sums_ref[pl.ds(UP_BIAS + tile, 1), :] = column_sum(low.astype(jnp.float32))
        return carry

    lax.fori_loop(0, wide // lanes, up_back_tile, 0)

    def normed_back_tile(tile, carry):
        at = tile_at(tile)
        state[:, at] = state[:, at] + dot_nt(up_back[...], up_weight_ref[at, :])
        return carry

    lax.fori_loop(0, width // lanes, normed_back_tile, 0)

    def first_back(chunk, carry):
        here = pl.ds(pl.multiple_of(chunk * NORM_CHUNK, 16), NORM_CHUNK)
        delta, rows = state[here, :], unit[here, :]
        back = norm_back(delta * vector_ref[4:5, :], rows, scale_ref[here, 0:1])
        first_back_ref[here, :] = back
        low = back.astype(jnp.bfloat16)
        attention_back[here, :] = low
        for index, value in (
            (FIRST_GAIN, delta * rows), (FIRST_SHIFT, delta), (OUT_BIAS, low.astype(jnp.float32))
        ):
            sums_ref[index : index + 1, :] += column_sum(value)
        return carry

    lax.fori_loop(0, total_rows // NORM_CHUNK, first_back, 0)

    def mixture_tile(tile, carry):
        at = tile_at(tile)
        mixture_back_ref[:, at] = dot_nt(attention_back[...], out_weight_ref[at, :]).astype(jnp.bfloat16)
        return carry

    lax.fori_loop(0, width // lanes, mixture_tile, 0)
    if not direct:
        normed_out_ref[...] = normed[...]
        up_out_ref[...] = up_back[...]
        activated_out_ref[...] = activated[...]
        down_out_ref[...] = down_back[...]
        attention_out_ref[...] = attention_back[...]
        return
    levels = pages.bit_length() - 1
    core = scalar_ref[1]
    rows = width // pages
    tall = wide // pages
    block = 384
    groups = wide // (2 * block)
    flipped[...] = normed[...].T

    def up_weight_tile(tile, carry):
        at = pl.ds(pl.multiple_of(tile * 2 * block, 2 * block), 2 * block)
        result = dot_nn(flipped[...], up_back[:, at]).astype(jnp.bfloat16)
        for part in range(2):
            column, group = (2 * tile + part) // groups, (2 * tile + part) % groups
            for page in range(pages):
                slot = early_slots(scalar_ref, page, column, levels)[0]
                bundle_ref[core, slot, pl.ds(pl.multiple_of(group * rows, 16), rows), :] = result[
                    page * rows : (page + 1) * rows, part * block : (part + 1) * block
                ]
        return carry

    lax.fori_loop(0, groups, up_weight_tile, 0)
    stores = [
        pltpu.make_async_copy(bundle_ref.at[part], bundle_any.at[part], store_sem.at[index])
        for index, part in enumerate(
            (
                (core, slice(None), slice(0, tall)), (1 - core, slice(None), slice(0, tall)),
                (slice(None), slice(None), slice(tall, tall + rows // 2)),
            )
        )
    ]
    stores[0].start()

    def down_weight_tile(page, carry):
        at = pl.ds(pl.multiple_of(page * tall, 128), tall)
        result = dot_tn(activated[:, at], down_back[...]).astype(jnp.bfloat16)
        for column in range(2):
            slot = early_slots(scalar_ref, page, column, levels)[1]
            bundle_ref[1 - core, slot, 0:tall, :] = result[:, column * block : (column + 1) * block]
        return carry

    lax.fori_loop(0, pages, down_weight_tile, 0)
    stores[1].start()
    flipped[...] = mixture_ref[...].T
    half = rows // 2

    result = dot_nn(flipped[...], attention_back[...]).astype(jnp.bfloat16)
    for column in range(2):
        for page in range(pages):
            slots = early_slots(scalar_ref, page, column, levels)
            for order in range(2):
                first = page * rows + order * half
                bundle_ref[core if order == 0 else 1 - core, slots[order], tall : tall + half, :] = result[
                    first : first + half, column * block : (column + 1) * block
                ]
    stores[2].start()
    for copy in stores:
        copy.wait()


def in_tiles(width, pages):
    return (width // pages) % 32 == 0 and pages >= 4


def middle(places, hidden, mixture, cotangent, patch_cotangent, matrices, vectors, pages):
    count, span, width = cotangent.shape
    patch_span = patch_cotangent.shape[1]
    total_rows = hidden.shape[0]
    wide = matrices[1].shape[1]
    direct = in_tiles(width, pages)
    bf16, f32 = jnp.bfloat16, jnp.float32
    if direct:
        extra = (jax.ShapeDtypeStruct((2, 2 * pages, (wide + width // 2) // pages, 384), bf16),)
    else:
        extra = tuple(
            jax.ShapeDtypeStruct((total_rows, size), bf16) for size in (width, wide, wide, width, width)
        )
    result = pl.pallas_call(
        functools.partial(middle_kernel, pages, direct),
        out_shape=(
            jax.ShapeDtypeStruct(cotangent.shape, f32),
            jax.ShapeDtypeStruct(patch_cotangent.shape, f32),
            jax.ShapeDtypeStruct((total_rows, width), f32),
            jax.ShapeDtypeStruct((total_rows, width), bf16),
            jax.ShapeDtypeStruct((16, width), f32),
        )
        + extra,
        in_specs=anywhere(7 + len(vectors)),
        out_specs=tuple(in_vmem(5) + (anywhere(1) if direct else in_vmem(len(extra)))),
        scratch_shapes=[
            pltpu.VMEM((total_rows, width), f32),
            pltpu.VMEM((total_rows, width), f32),
            pltpu.VMEM((total_rows, 128), f32),
            pltpu.VMEM((total_rows, width), bf16),
            pltpu.VMEM((total_rows, wide), bf16),
            pltpu.VMEM((total_rows, wide), f32),
            pltpu.VMEM((total_rows, wide), bf16),
            pltpu.VMEM((total_rows, width), bf16),
            pltpu.VMEM((total_rows, width), bf16),
            pltpu.VMEM((width, total_rows), bf16),
        ]
        + [pltpu.VMEM(value.shape, value.dtype) for value in (extra if direct else ())]
        + [
            pltpu.VMEM(value.shape, value.dtype)
            for value in (hidden, mixture, cotangent, patch_cotangent, *matrices, *vectors)
        ]
        + [pltpu.VMEM((16, width), f32), pltpu.SemaphoreType.DMA((14,)), pltpu.SemaphoreType.DMA((3,))],
        compiler_params=pltpu.CompilerParams(vmem_limit_bytes=KERNEL_VMEM),
        cost_estimate=pl.CostEstimate(flops=14_000_000_000, bytes_accessed=30_000_000, transcendentals=2_600_000),
        name="middle",
    )(hidden, mixture, cotangent, patch_cotangent, *matrices, *vectors)
    first, rest = result[:5], result[5:]
    if direct:
        return first + rest
    normed, up_back, activated, down_back, attention_back = rest
    return first + (
        indexed_bundle(
            (
                ((normed, up_back, None), (mixture, attention_back, 0)),
                ((activated, down_back, None), (mixture, attention_back, 1)),
            ),
            places,
            pages,
        ),
    )


def indexed_bundle(matrices, scalars, pages):
    levels = pages.bit_length() - 1
    place = jnp.arange(2 * pages, dtype=jnp.int32)
    bits = [(place >> (levels - k)) & 1 for k in range(levels + 1)]
    halves = []
    for order, group in enumerate(matrices):
        side, near = (bits[0], bits[1]) if order == 0 else (bits[1], bits[0])
        far = near
        for level in range(1, levels):
            far = far + (bits[level + 1] << level)
        index = (far ^ scalars[2]) * 2 + (side ^ scalars[3])
        blocks = []
        for operand, gradient, part in group:
            rows = in_blocks(outer_dot(operand, gradient).astype(jnp.bfloat16), pages)
            if part is not None:
                half = rows.shape[1] // 2
                rows = rows[:, part * half : (part + 1) * half]
            blocks.append(rows)
        halves.append(jnp.concatenate(blocks, axis=1)[index])
    first, second = halves
    mine = scalars[1] == 0
    return jnp.stack([jnp.where(mine, first, second), jnp.where(mine, second, first)])


def in_blocks(matrix, pages):
    rows, columns = matrix.shape[0] // pages, matrix.shape[1] // 2
    lanes = min(columns, 384)
    blocks = matrix.reshape(pages, rows, 2, columns // lanes, lanes)
    return blocks.transpose(0, 2, 3, 1, 4).reshape(pages * 2, rows * columns // lanes, lanes)


class Halving:
    def __init__(self, keep, source, landing, landings, partners, sibling, sems, chunks):
        self.keep, self.landing, self.landings = keep, landing, landings
        total = keep.shape[0]
        unit = total // chunks
        send_sem, recv_sem = sems
        self.arrivals, self.sends, self.needs = {}, {}, {}
        used = 0
        for chunk in range(chunks):
            lo = total - (chunk + 1) * unit
            copy = remote(
                source.at[lo : lo + unit], landing.at[lo : lo + unit], send_sem.at[used], recv_sem.at[used], *sibling
            )
            self.arrivals["core", chunk] = (copy, landing, lo, unit)
            used += 1
        for step, (into, partner) in enumerate(zip(landings, partners, strict=True)):
            size = total >> (step + 1)
            piece = min(unit, size)
            for chunk in range(size // piece):
                lo = size - (chunk + 1) * piece
                copy = remote(
                    keep.at[size + lo : size + lo + piece], into.at[lo : lo + piece], send_sem.at[used],
                    recv_sem.at[used], *partner,
                )
                self.arrivals[step, chunk] = (copy, into, lo, piece)
                self.sends[step, chunk] = copy
                self.needs[step, chunk] = {
                    (source_step, block)
                    for block in range(size + lo, size + lo + piece)
                    for source_step in ("core", *range(step))
                }
                used += 1
        self.done = set()

    def start(self):
        for key, (copy, *_) in self.arrivals.items():
            if key[0] == "core":
                copy.start()

    def take(self, *key):
        copy, into, lo, count = self.arrivals[key]
        copy.wait_recv()

        def add(block, carry):
            self.keep[block] = self.keep[block] + into[block]
            return carry

        lax.fori_loop(lo, lo + count, add, 0)
        for block in range(lo, lo + count):
            self.done.add((key[0], block))
        for name in list(self.sends):
            if self.needs[name] <= self.done:
                self.sends.pop(name).start()

    def finish(self):
        for copy, *_ in self.arrivals.values():
            copy.wait_send()


def backward_kernel(
    pages,
    staging, length_ref, query_ref, mixture_back_ref, columns_ref, rows_ref, query_rows_ref, tokens_ref, patches_ref, taps_ref,
    middle_sums_ref, bundle_any, weights_any, key_any, value_any, hidden_any, first_back_any, query_weight_any,
    key_weight_any, value_weight_any,
    tokens_back_ref, patches_back_ref, early_ref, late_ref, sums_ref, up_in_ref, down_in_ref, mixed_in_ref,
    keep, landing, landings, late, late_landing, late_landings, weights_buf, key_buf, value_buf, outgoing, from_sib,
    from_far, matrices, flipped, total_back, query_back, key_back, value_back, back, steps, mask_ref, hot_ref,
    query_hot_ref, band_ref, table_acc, band_acc, table_out, text_rim, patch_rim, sums, sums_in,
    up_in, down_out, down_in, mixed_out, mixed_in,
    load_sem, page_sem, early_send, early_recv, late_send, late_recv, sib_send, sib_recv, far_send, far_recv, rim_send,
    rim_recv, sum_send, sum_recv, swap_send, swap_recv,
):
    page_at, bits, seq, across, core = places_of(pages)
    levels = len(bits)
    count, span, width = tokens_ref.shape
    patch_span = patches_ref.shape[1]
    row_count = span + patch_span
    total_rows = count * row_count
    key_pad = key_buf.shape[1]
    text_slots = 4 * span
    groups = weights_buf.shape[1]
    members = weights_buf.shape[2] // row_count
    heads = groups * members
    group_width = members * HEAD_LANES
    f32, bf16 = jnp.float32, jnp.bfloat16

    sibling = (page_at, sibling_of(seq))
    opposite = (page_at, across_of(seq))
    diagonal = (page_at, sibling_of(across_of(seq)))
    flips = [(1 - 2 * bit) * 2**level for level, bit in enumerate(bits)]
    on_page = [(page_at + flip, seq) for flip in flips]
    either = lambda first, second: first + core * (second - first)
    early_partners = [
        (page_at + either(flips[1], flips[0]), seq),
        (page_at + either(flips[0], flips[1]), seq),
        opposite,
    ] + on_page[2:]
    barrier = pltpu.get_barrier_semaphore()
    everyone = [sibling, opposite, diagonal] + on_page
    for peer in everyone:
        pl.semaphore_signal(barrier, inc=1, device_id=peer, device_id_type=MESH)

    keep_load = pltpu.make_async_copy(bundle_any.at[0], keep, load_sem.at[0])
    later_loads = [
        pltpu.make_async_copy(source, target, load_sem.at[1 + index])
        for index, (source, target) in enumerate(
            (
                (query_weight_any, matrices.at[0]), (key_weight_any, matrices.at[1]),
                (value_weight_any, matrices.at[2]), (hidden_any, key_back), (first_back_any, total_back),
            )
        )
    ]

    def page_loads(page):
        slot = page % 2
        return [
            pltpu.make_async_copy(source.at[page], target.at[slot], page_sem.at[index, slot])
            for index, (source, target) in enumerate(
                ((weights_any, weights_buf), (key_any, key_buf), (value_any, value_buf))
            )
        ]

    for copy in page_loads(0):
        copy.start()
    keep_load.start()
    pl.semaphore_wait(barrier, len(everyone))
    early = Halving(
        keep, bundle_any.at[1], landing, landings, early_partners, sibling, (early_send, early_recv), 8
    )
    late_sum = Halving(
        late.at[0], late.at[1], late_landing, late_landings, early_partners, sibling, (late_send, late_recv), 4
    )
    early.start()
    for copy in staging:
        copy.wait()

    lane128 = lax.broadcasted_iota(jnp.int32, (row_count, 128), 1)
    place = query_places(seq, (row_count, 128), span, patch_span, text_slots)
    aim = place + lane128 - 32
    blocks_on = (aim >> 4) - (place >> 4)
    near = (lane128 < 64) & (aim >= 0) & (aim < text_slots + patch_span * 4) & (blocks_on >= -1) & (blocks_on <= 1)
    band_ref[...] = jnp.where(near, aim, -1)
    table_acc[...] = jnp.zeros_like(table_acc)
    band_acc[...] = jnp.zeros_like(band_acc)
    lane_of_row = lax.broadcasted_iota(jnp.int32, (48, row_count), 1)
    place_of_row = jnp.where(
        lane_of_row < span, seq * span + lane_of_row, text_slots + seq * patch_span + lane_of_row - span
    )
    query_hot_ref[144:192, :] = (
        ((place_of_row >> 4) == lax.broadcasted_iota(jnp.int32, (48, row_count), 0)).astype(f32).astype(bf16)
    )
    def start_page(page):
        slot = page % 2
        for copy in page_loads(page):
            copy.wait()

        @pl.when(page < count - 1)
        def _():
            for copy in page_loads(page + 1):
                copy.start()

        bin_at = lax.broadcasted_iota(jnp.int32, (128, key_pad), 0) - 1
        key_block = lax.broadcasted_iota(jnp.int32, (128, key_pad), 1) >> 4
        half_bin = lax.broadcasted_iota(jnp.int32, (72, row_count), 0)
        for side in range(2):
            key_row = rows_ref[page, side : side + 1, :]
            query_column = columns_ref[page, :, 128 * side : 128 * side + 1]
            mask_ref[:, side * key_pad : (side + 1) * key_pad] = (
                ((key_row & 15) < (query_column & 15)).astype(f32).astype(bf16)
            )
            key_bin = key_row >> 4
            plain = jnp.where(bin_at < 64, (key_bin == bin_at).astype(f32), 0.0)
            lower = jnp.where(bin_at < 64, (key_bin - 1 == bin_at).astype(f32), 0.0)
            mine = slice(128 * side, 128 * (side + 1))
            other = slice(128 * (1 - side), 128 * (2 - side))
            change = lower - plain
            if side == 0:
                plain = jnp.where(bin_at - 71 == key_block, 1.0, plain)
            hot_ref[mine, 0:key_pad] = plain.astype(bf16)
            hot_ref[mine, (1 + side) * key_pad : (2 + side) * key_pad] = change.astype(bf16)
            hot_ref[other, (1 + side) * key_pad : (2 + side) * key_pad] = jnp.zeros((128, key_pad), bf16)
            query_bin = query_rows_ref[page, side : side + 1, 0:row_count] >> 4
            query_hot_ref[72 * side : 72 * (side + 1), :] = (71 - query_bin == half_bin).astype(f32).astype(bf16)

    def attend(page, group):
        slot = page % 2
        at = pl.ds(pl.multiple_of(group * group_width, group_width), group_width)
        own_rows = pl.ds(pl.multiple_of(page * row_count, 16), row_count)
        both_query = split_heads(query_ref[own_rows, at])
        both_back = split_heads(mixture_back_ref[own_rows, at])
        back[...] = dot_nt(both_back, value_buf[slot, :, at])
        for start in range(0, members * row_count, CHUNK):
            there = slice(start, start + CHUNK)
            here = slice(start % row_count, start % row_count + CHUNK)
            parts, total = [], None
            for block_at in range(0, key_pad, 128):
                lane = slice(block_at, block_at + 128)
                part = weights_buf[slot, group, there, lane].astype(f32)
                product = part * back[there, lane]
                total = product if total is None else total + product
                parts.append(part)
            mean = jnp.sum(total, axis=1, keepdims=True)
            for index, part in enumerate(parts):
                lane = slice(128 * index, 128 * (index + 1))
                step = (part * (back[there, lane] - mean)).astype(bf16)
                steps[there, lane] = step
                steps[there, key_pad + 128 * index : key_pad + 128 * (index + 1)] = step * mask_ref[here, lane]
                steps[there, 2 * key_pad + 128 * index : 2 * key_pad + 128 * (index + 1)] = (
                    step * mask_ref[here, key_pad + 128 * index : key_pad + 128 * (index + 1)]
                )
        query_back[own_rows, at] = (
            merge_heads(dot_nn(steps[:, 0:key_pad], key_buf[slot, :, at])) * 0.125
        ).astype(bf16)
        for kind, value in enumerate(
            (dot_tn(steps[:, 0:key_pad], both_query), dot_tn(weights_buf[slot, group], both_back))
        ):
            value = value.astype(bf16)
            for where in range(4):
                place_at = apart(where % 2, core) * 2 + apart(where // 2, across)
                outgoing[page, place_at, kind, 0:span, at] = value[where * span : (where + 1) * span]
                outgoing[page, place_at, kind, span:row_count, at] = value[
                    text_slots + where * patch_span : text_slots + (where + 1) * patch_span
                ]
        bins = dot_nt(steps[...], hot_ref[...]).astype(bf16)
        for side in range(members):
            head = members * group + side
            base = side * row_count
            both = dot_nn(query_hot_ref[...], bins[base : base + row_count])
            table_acc[head, 0:72, :] += both[0:72, 0:128]
            table_acc[head, 72:144, :] += both[72:144, 128:256]
            table_acc[head, 144:192, :] += both[144:192, 0:128]
            for first, rows_here, block, into in bands():
                source = steps[
                    base + first : base + first + rows_here, pl.ds(pl.multiple_of(block * 128, 128), 128)
                ]
                band_acc[head, into : into + rows_here, :] += source.astype(f32)

    def bands():
        before = seq - (seq + 3) // 4
        return (
            (0, span, seq, 0),
            (0, 32, before, span),
            (span - 32, 32, seq + 1, span + 32),
            (span, patch_span, 3, span + 64),
            (span, patch_span, 4, span + 64 + patch_span),
        )

    def sib_copy(page, part):
        at = slice(part * width // 2, (part + 1) * width // 2)
        return remote(
            outgoing.at[page, 2:4, :, :, at], from_sib.at[page, :, :, :, at], sib_send.at[page, part],
            sib_recv.at[page, part], *sibling,
        )

    def far_copy(page, part):
        at = slice(part * width // 2, (part + 1) * width // 2)
        return remote(
            outgoing.at[page, 1, :, :, at], from_far.at[page, :, :, at], far_send.at[page, part],
            far_recv.at[page, part], *opposite,
        )

    def pass_on(page, part):
        sib_copy(page, part).wait_recv()
        at = slice(part * width // 2, (part + 1) * width // 2)
        for kind in range(2):
            outgoing[page, 1, kind, :, at] = outgoing[page, 1, kind, :, at] + from_sib[page, 1, kind, :, at]
        far_copy(page, part).start()

    events = {
        1: [("core", 0), ("core", 1)], 2: [("core", 2), ("core", 3)], 4: [("core", 4), ("core", 5)],
        6: [("core", 6), ("core", 7)], 8: [(0, 0)], 12: [(0, 1)],
    }
    last_turn = count * groups - 1

    def step_body(turn, carry):
        page, group = turn // groups, turn % groups

        @pl.when(group == 0)
        def _():
            start_page(page)

        for at_turn, names in events.items():

            @pl.when(turn == min(at_turn, last_turn))
            def _(names=names, at_turn=at_turn):
                if at_turn == min(events):
                    keep_load.wait()
                for name in names:
                    early.take(*name)

        @pl.when(turn == min(3, last_turn))
        def _():
            for copy in later_loads:
                copy.start()

        @pl.when((group == 2) & (page > 0))
        def _():
            pass_on(page - 1, 1)

        @pl.when(group == groups - 1)
        def _():
            pass_on(page, 0)

        attend(page, group)

        for part in range(2):

            @pl.when(group == (part + 1) * groups // 2 - 1)
            def _(part=part):
                sib_copy(page, part).start()

        return carry

    lax.fori_loop(0, count * groups, step_body, 0)

    for copy in later_loads:
        copy.wait()
    flipped[...] = key_back[...].T
    lanes = 384
    rows = width // pages
    half = rows // 2

    def weight_columns(index, gradient):
        def tile(four, carry):
            tile_rows = pl.ds(pl.multiple_of(four * 4 * rows, 128), 4 * rows)
            result = dot_nn(flipped[tile_rows, :], gradient[...]).astype(bf16)
            for inner in range(4):
                page = four * 4 + inner
                first = inner * rows
                for column in range(2):
                    far = [apart((page // 2**level) % 2, bit) for level, bit in enumerate(bits)]
                    slots = [slot_of_bits(order) for order in early_orders(far, apart(column, across))]
                    at = slice(column * lanes, (column + 1) * lanes)
                    if index < 2:
                        late[core if index == 0 else 1 - core, slots[index], 0:rows, :] = result[
                            first : first + rows, at
                        ]
                    else:
                        late[core, slots[0], rows : rows + half, :] = result[first : first + half, at]
                        late[1 - core, slots[1], rows : rows + half, :] = result[first + half : first + rows, at]
            return carry

        lax.fori_loop(0, pages // 4, tile, 0)

    def project_back(gradient, matrix):
        total_back[...] = total_back[...] + dot_nt(gradient[...], matrices[matrix])

    pass_on(count - 1, 1)
    weight_columns(0, query_back)
    project_back(query_back, 0)
    sums[0, 0:16, :] = middle_sums_ref[...]
    sums[0, 10:11, :] = column_sum(query_back[...].astype(f32))

    def head_tables(head, carry):
        for plane in range(2):
            table = table_acc[head, 72 * plane : 72 * (plane + 1), :]
            lane = lax.broadcasted_iota(jnp.int32, table.shape, 1)
            table = jnp.where(lane < 72, table, 0.0)
            table = jnp.concatenate([table, jnp.zeros_like(table)], axis=1)
            sheared = pltpu.roll(table, 0, 1, stride=1, stride_axis=0)
            table_out[head, 0:1, 256 * plane : 256 * (plane + 1)] = column_sum(sheared)
        table = table_acc[head, 144:192, :]
        lane = lax.broadcasted_iota(jnp.int32, table.shape, 1)
        apart_by = lane - 72 - lax.broadcasted_iota(jnp.int32, table.shape, 0)
        in_line = (lane >= 72) & (lane < 72 + 36)
        low_tail = jnp.sum(column_sum(jnp.where(in_line & (apart_by <= -2), table, 0.0)), axis=1, keepdims=True)
        high_tail = jnp.sum(column_sum(jnp.where(in_line & (apart_by >= 2), table, 0.0)), axis=1, keepdims=True)
        band = jnp.zeros((1, 128), f32)
        for first, rows_here, block, into in bands():
            aims = band_ref[first : first + rows_here, :]
            taken = jnp.take_along_axis(band_acc[head, into : into + rows_here, :], aims & 127, axis=1)
            right = (aims >> 7) == block
            if into == span:
                right = right & (seq > 0)
            band = band + column_sum(jnp.where(right, taken, 0.0))
        lane_one = lax.broadcasted_iota(jnp.int32, (1, 128), 1)
        table_out[head, 0:1, 512:640] = (
            band + jnp.where(lane_one == 0, low_tail, 0.0) + jnp.where(lane_one == 63, high_tail, 0.0)
        )
        table_out[head, 0:1, 640:768] = jnp.zeros((1, 128), f32)
        return carry

    lax.fori_loop(0, heads, head_tables, 0)
    for head in range(heads):
        at_row = 8 + head
        sums[1, at_row : at_row + 1, :] = table_out[head, 0:1, :]

    for name in ((0, 2), (1, 0)):
        early.take(*name)
    for page in range(count):
        for part in range(2):
            far_copy(page, part).wait_recv()
        own_rows = slice(page * row_count, (page + 1) * row_count)
        for kind, target in enumerate((key_back, value_back)):
            target[own_rows, :] = (
                (outgoing[page, 0, kind].astype(f32) + from_sib[page, 0, kind].astype(f32))
                + from_far[page, kind].astype(f32)
            ).astype(bf16)
    weight_columns(1, key_back)
    weight_columns(2, value_back)
    late_sum.start()
    project_back(key_back, 1)
    project_back(value_back, 2)
    sums[0, 11:12, :] = column_sum(value_back[...].astype(f32))
    for page in range(count):
        first = page * row_count
        text_rim[page, 16 : 16 + span, :] = total_back[first : first + span, :].astype(bf16)
        patch_rim[page, 16 : 16 + patch_span, :] = total_back[first + span : first + row_count, :].astype(bf16)
    after, before = (page_at, (seq + 1) % 4), (page_at, (seq + 3) % 4)
    rim_copies = [
        remote(
            source.at[:, start : start + 16], source.at[:, stop : stop + 16], rim_send.at[index], rim_recv.at[index],
            *peer,
        )
        for index, (source, start, stop, peer) in enumerate(
            (
                (text_rim, span, 0, after), (text_rim, 16, 16 + span, before),
                (patch_rim, 16, 0, after), (patch_rim, 16, 32, before),
            )
        )
    ]
    for copy in rim_copies:
        copy.start()
    for chunk in range(4):
        late_sum.take("core", chunk)
    for name in ((0, 3), (1, 1)):
        early.take(*name)
    for copy in rim_copies:
        copy.wait()
    sums[1, 0:8, :] = jnp.zeros((8, width), f32)
    sums[1, 20:24, :] = jnp.zeros((4, width), f32)
    sums[0, 16:24, :] = jnp.zeros((8, width), f32)

    def position_tile(tile, carry):
        at = pl.ds(pl.multiple_of(tile * 256, 256), 256)
        text_taps = [jnp.zeros((1, 256), f32) for _ in range(7)]
        patch_taps = [jnp.zeros((1, 256), f32) for _ in range(9)]
        for page in range(count):
            first = page * row_count
            window = text_rim[page, :, at].astype(f32)
            window_row = lax.broadcasted_iota(jnp.int32, (span + 32, 1), 0)
            inside = ((window_row >= 16) | (seq > 0)) & ((window_row < 16 + span) | (seq < 3))
            window = jnp.where(inside, window, 0.0)
            live = seq * span + lax.broadcasted_iota(jnp.int32, (span, 1), 0) < length_ref[page]
            masked = jnp.where(live, tokens_ref[page, :, at].astype(f32), 0.0)
            total = jnp.zeros((span, 256), f32)
            for distance in range(-3, 4):
                shifted = window[16 - distance : 16 - distance + span]
                if distance == 0:
                    weight = taps_ref[1:2, at] + taps_ref[4:5, at] + taps_ref[7:8, at]
                else:
                    tap = 3 * (abs(distance) - 1) + (2 if distance > 0 else 0)
                    weight = taps_ref[tap : tap + 1, at]
                total = total + shifted * weight
                text_taps[distance + 3] = text_taps[distance + 3] + column_sum(shifted * masked)
            tokens_back_ref[page, :, at] = total_back[first : first + span, at] + jnp.where(live, total, 0.0)
            window = patch_rim[page, :, at].astype(f32)
            window_row = lax.broadcasted_iota(jnp.int32, (48, 1), 0)
            inside = ((window_row >= 16) | (seq > 0)) & ((window_row < 32) | (seq < 3))
            window = jnp.where(inside, window, 0.0)
            cell = seq * patch_span + lax.broadcasted_iota(jnp.int32, (patch_span, 1), 0)
            live = ((cell >> 3) < GRID_SIDE - 1) & ((cell & 7) < GRID_SIDE - 1)
            masked = jnp.where(live, patches_ref[page, :, at].astype(f32), 0.0)
            total = jnp.zeros((patch_span, 256), f32)
            for tap in range(9):
                distance = GRID_SIDE * (tap // 3 - 1) + tap % 3 - 1
                shifted = window[16 - distance : 32 - distance]
                total = total + shifted * taps_ref[9 + tap : 10 + tap, at]
                patch_taps[tap] = patch_taps[tap] + column_sum(shifted * masked)
            patches_back_ref[page, :, at] = total_back[first + span : first + row_count, at] + jnp.where(
                live, total, 0.0
            )
        for index, value in enumerate(text_taps):
            sums[0, 16 + index : 17 + index, at] = value
        for index, value in enumerate(patch_taps):
            if index == 0:
                sums[0, 23:24, at] = value
            else:
                sums[1, index - 1 : index, at] = value
        return carry

    early.take(2, 0)
    lax.fori_loop(0, width // 256, position_tile, 0)

    sum_partners = [opposite] + on_page
    sum_copies = [remote(sums.at[1 - core], sums_in.at[0], sum_send.at[0], sum_recv.at[0], *sibling)] + [
        remote(sums.at[core], sums_in.at[1 + index], sum_send.at[1 + index], sum_recv.at[1 + index], *partner)
        for index, partner in enumerate(sum_partners)
    ]
    last = remote(
        sums.at[core], sums_in.at[2 + levels], sum_send.at[2 + levels], sum_recv.at[2 + levels], *sibling
    )
    sum_copies[0].start()

    def sum_step(index):
        sum_copies[index].wait()
        sums[core] = sums[core] + sums_in[index]
        (sum_copies + [last])[index + 1].start()

    late_sum.take(0, 0)
    sum_step(0)
    late_sum.take(0, 1)
    sum_step(1)
    late_sum.take(1, 0)
    sum_step(2)
    for step in range(2, levels + 1):
        late_sum.take(step, 0)
        sum_step(step + 1)
    for step in range(3, levels + 1):
        early.take(step, 0)
    last.wait()
    sums_ref[core] = sums[core]
    sums_ref[1 - core] = sums_in[2 + levels]
    wide_rows = 4 * rows
    block = keep[0].astype(f32)
    low, high = block[:, 0 : lanes // 2], pltpu.roll(block, lanes // 2, 1)[:, 0 : lanes // 2]
    down_out[...] = low[0:wide_rows].astype(bf16)
    mixed_out[0:half, :] = jnp.where(core == 0, high[wide_rows:], low[wide_rows:]).astype(bf16)
    block = late[0, 0].astype(f32)
    low, high = block[:, 0 : lanes // 2], pltpu.roll(block, lanes // 2, 1)[:, 0 : lanes // 2]
    mixed_out[half:, :] = jnp.where(core == 0, high, low).astype(bf16)
    swaps = [
        remote(source, target, swap_send.at[index], swap_recv.at[index], *sibling)
        for index, (source, target) in enumerate(
            ((keep.at[0, 2 * rows : 4 * rows], up_in), (down_out, down_in), (mixed_out, mixed_in))
        )
    ]
    for copy in swaps:
        copy.start()
    early_ref[...] = keep[0]
    late_ref[...] = late[0, 0]
    for copy in swaps:
        copy.wait()
    up_in_ref[...] = up_in[...]
    down_in_ref[...] = down_in[...]
    mixed_in_ref[...] = mixed_in[...]
    early.finish()
    late_sum.finish()
    for page in range(count):
        for part in range(2):
            sib_copy(page, part).wait_send()
            far_copy(page, part).wait_send()


def backward(pages, lengths, local_values, far_values, tokens, patches):
    count, span, width = tokens.shape
    patch_span = patches.shape[1]
    row_count = span + patch_span
    total_rows = count * row_count
    bundle, weights, keys = far_values[0], far_values[1], far_values[2]
    groups, grouped_rows, key_pad = weights.shape[1:]
    heads = groups * grouped_rows // row_count
    blocks, early_rows, lanes = bundle.shape[1:]
    late_rows = 3 * width // (2 * pages)
    levels = pages.bit_length() - 1
    bf16, f32, i32 = jnp.bfloat16, jnp.float32, jnp.int32
    dma = pltpu.SemaphoreType.DMA

    def landings(rows):
        return [VMEM((blocks >> (step + 1), rows, lanes), bf16) for step in range(levels + 1)]

    early_count = 8 + 4 + 2 + (levels - 1)
    late_count = 4 + 2 + levels
    return pl.pallas_call(
        staged(functools.partial(backward_kernel, pages), 1, len(local_values)),
        out_shape=(
            jax.ShapeDtypeStruct(tokens.shape, f32),
            jax.ShapeDtypeStruct(patches.shape, f32),
            jax.ShapeDtypeStruct((early_rows, lanes), bf16),
            jax.ShapeDtypeStruct((late_rows, lanes), bf16),
            jax.ShapeDtypeStruct((2, 24, width), f32),
            jax.ShapeDtypeStruct((early_rows // 9 * 4, lanes), bf16),
            jax.ShapeDtypeStruct((early_rows // 9 * 8, lanes // 2), bf16),
            jax.ShapeDtypeStruct((early_rows // 9 + late_rows, lanes // 2), bf16),
        ),
        in_specs=[pl.BlockSpec(memory_space=pltpu.SMEM)]
        + anywhere(len(local_values) + len(far_values)),
        out_specs=tuple(in_vmem(8)),
        scratch_shapes=[
            VMEM((blocks, early_rows, lanes), bf16),
            VMEM((blocks, early_rows, lanes), bf16),
            landings(early_rows),
            VMEM((2, blocks, late_rows, lanes), bf16),
            VMEM((blocks, late_rows, lanes), bf16),
            landings(late_rows),
            VMEM((2, groups, grouped_rows, key_pad), bf16),
            VMEM((2, key_pad, width), bf16),
            VMEM((2, key_pad, width), bf16),
            VMEM((count, 4, 2, row_count, width), bf16),
            VMEM((count, 2, 2, row_count, width), bf16),
            VMEM((count, 2, row_count, width), bf16),
            VMEM((3, width, width), bf16),
            VMEM((width, total_rows), bf16),
            VMEM((total_rows, width), f32),
            VMEM((total_rows, width), bf16),
            VMEM((total_rows, width), bf16),
            VMEM((total_rows, width), bf16),
            VMEM((grouped_rows, key_pad), f32),
            VMEM((grouped_rows, 3 * key_pad), bf16),
            VMEM((row_count, 2 * key_pad), bf16),
            VMEM((256, 3 * key_pad), bf16),
            VMEM((192, row_count), bf16),
            VMEM((row_count, 128), i32),
            VMEM((heads, 192, 128), f32),
            VMEM((heads, span + 64 + 2 * patch_span, 128), f32),
            VMEM((heads, 8, width), f32),
            VMEM((count, span + 32, width), bf16),
            VMEM((count, patch_span + 32, width), bf16),
            VMEM((2, 24, width), f32),
            VMEM((3 + levels, 24, width), f32),
            VMEM((early_rows // 9 * 4, lanes), bf16),
            VMEM((early_rows // 9 * 8, lanes // 2), bf16),
            VMEM((early_rows // 9 * 8, lanes // 2), bf16),
            VMEM((early_rows // 9 + late_rows, lanes // 2), bf16),
            VMEM((early_rows // 9 + late_rows, lanes // 2), bf16),
            dma((6,)), dma((3, 2)),
            dma((early_count,)), dma((early_count,)), dma((late_count,)), dma((late_count,)),
            dma((count, 2)), dma((count, 2)), dma((count, 2)), dma((count, 2)),
            dma((4,)), dma((4,)), dma((3 + levels,)), dma((3 + levels,)), dma((3,)), dma((3,)),
        ]
        + stage_for(local_values),
        compiler_params=pltpu.CompilerParams(
            collective_id=1, has_side_effects=True, vmem_limit_bytes=KERNEL_VMEM
        ),
        cost_estimate=pl.CostEstimate(flops=12_000_000_000, bytes_accessed=40_000_000, transcendentals=0),
        name="backward",
    )(lengths, *local_values, *far_values)


def clip_lanes(sums, centre, bins):
    first, last = centre + 1 - bins // 2, centre - 1 + bins // 2
    lane = lax.broadcasted_iota(jnp.int32, sums.shape, 1)
    below = jnp.sum(jnp.where(lane < first, sums, 0.0), axis=1, keepdims=True)
    above = jnp.sum(jnp.where(lane >= last, sums, 0.0), axis=1, keepdims=True)
    moved = pltpu.roll(sums, sums.shape[1] - (first - 1), 1)
    moved = jnp.where(lane == 0, below, jnp.where(lane == bins - 1, above, moved))
    return moved[:, :bins]


def finish_kernel(staging, early_ref, late_ref, sums_ref, up_in_ref, down_in_ref, mixed_in_ref, *rest):
    carried, rest = rest[:2], rest[2:]
    *rest, carry_sem = rest
    rest, targets = rest[:-2], rest[-2:]
    (
        query_ref, key_ref, value_ref, out_ref, up_ref, down_ref, taps_ref, patch_taps_ref, line_ref, across_ref,
        upward_ref, *vector_refs,
    ) = rest
    carries = [
        pltpu.make_async_copy(source, target, carry_sem.at[index])
        for index, (source, target) in enumerate(zip(carried, targets, strict=True))
    ]
    for copy in carries:
        copy.start()
    f32 = jnp.float32
    rows, columns = query_ref.shape
    half = rows // 2
    wide_rows = 4 * rows
    first = position()[1] == 0
    for copy in staging:
        copy.wait()
    heads = line_ref.shape[0]
    block = early_ref[...].astype(f32)
    low, high = block[:, 0:columns], pltpu.roll(block, columns, 1)[:, 0:columns]
    up = jnp.where(first, block[0 : 2 * rows], up_in_ref[...].astype(f32))
    up_ref[:, 0 : 2 * columns] = up[0:rows]
    up_ref[:, 2 * columns : 4 * columns] = up[rows : 2 * rows]
    down_ref[...] = jnp.where(first, down_in_ref[...].astype(f32), high[0:wide_rows]).T
    kept = jnp.where(first, low[wide_rows:], high[wide_rows:])
    got = mixed_in_ref[0:half, :].astype(f32)
    out_ref[0:half, :] = jnp.where(first, kept, got)
    out_ref[half:rows, :] = jnp.where(first, got, kept)
    block = late_ref[...].astype(f32)
    low, high = block[:, 0:columns], pltpu.roll(block, columns, 1)[:, 0:columns]
    kept = jnp.where(first, low, high)
    got = mixed_in_ref[half:, :].astype(f32)
    query_ref[...] = jnp.where(first, kept[0:rows], got[0:rows])
    key_ref[...] = jnp.where(first, got[0:rows], kept[0:rows])
    value_ref[0:half, :] = jnp.where(first, kept[rows:], got[rows:])
    value_ref[half:rows, :] = jnp.where(first, got[rows:], kept[rows:])
    front, back = sums_ref[0], sums_ref[1]
    width = front.shape[1]
    text = [front[16 + index : 17 + index] for index in range(7)]
    order = [text[2], text[3], text[4], text[1], text[3], text[5], text[0], text[3], text[6]]
    taps_ref[...] = jnp.concatenate(order, axis=0)
    patch_taps_ref[...] = jnp.concatenate([front[23:24], back[0:8]], axis=0)
    across_ref[...] = clip_lanes(back[8:24, 0:256], 72, across_ref.shape[1])[0:heads]
    upward_ref[...] = clip_lanes(back[8:24, 256:512], 72, upward_ref.shape[1])[0:heads]
    line_ref[...] = clip_lanes(back[8:24, 512:640], 32, line_ref.shape[1])[0:heads]
    for source, target in zip((10, 11, 0, UP_BIAS, 1, 2, 3, 4, 5), vector_refs, strict=True):
        for part in range(target.shape[0] // width):
            target[pl.ds(part * width, width)] = front[source + part, :]
    for copy in carries:
        copy.wait()


def finish(values, carried, width, wide, heads, line_bins, plane_bins):
    rows, columns = values[1].shape[0] * 2 // 3, values[1].shape[1] // 2
    f32 = jnp.float32
    square = jax.ShapeDtypeStruct((rows, columns), f32)
    taps = jax.ShapeDtypeStruct((9, width), f32)
    plane = jax.ShapeDtypeStruct((heads, plane_bins), f32)
    return pl.pallas_call(
        staged(finish_kernel, 0, len(values)),
        out_shape=(
            square, square, square, square,
            jax.ShapeDtypeStruct((rows, 4 * columns), f32),
            jax.ShapeDtypeStruct((columns, 4 * rows), f32),
            taps, taps,
            jax.ShapeDtypeStruct((heads, line_bins), f32), plane, plane,
            *(jax.ShapeDtypeStruct((size,), f32) for size in (width,) * 3 + (wide,) + (width,) * 5),
            *(jax.ShapeDtypeStruct(value.shape, f32) for value in carried),
        ),
        in_specs=anywhere(len(values) + len(carried)),
        out_specs=tuple(in_vmem(22)),
        scratch_shapes=[pltpu.SemaphoreType.DMA((2,))] + stage_for(values),
        compiler_params=pltpu.CompilerParams(vmem_limit_bytes=KERNEL_VMEM),
        name="finish",
    )(*values, *carried)


def exchange(value, pages, step):
    moves = []
    for page in range(pages):
        for seq in range(4):
            on_page, on_seq = page, seq
            if (seq % 2 == step) if step < 2 else False:
                on_seq = seq ^ 2
            else:
                on_page = page ^ (1 if step < 2 else 1 << (step - 1))
            moves.append((page * 4 + seq, on_page * 4 + on_seq))
    return lax.ppermute(value, ("page", "seq"), moves)


def added(kept, got):
    return (kept.astype(jnp.float32) + got.astype(jnp.float32)).astype(jnp.bfloat16)


def bundle_sum(state, pages):
    for step in range(pages.bit_length()):
        half = state.shape[0] // 2
        state = added(state[:half], exchange(state[half:], pages, step))
    return state[0]


def bundle_parts(state, wide_rows, core):
    lanes = state.shape[1] // 2
    first = core == 0
    tail = state[wide_rows:]
    if wide_rows > 2 * tail.shape[0]:
        group = state[:wide_rows].reshape(4, wide_rows // 4, 2 * lanes)
        low = group[:2].transpose(1, 0, 2).reshape(-1, lanes)
        high = group[2:].transpose(1, 0, 2).reshape(-1, lanes)
    else:
        low, high = state[:wide_rows, :lanes], state[:wide_rows, lanes:]
    left, right = state[:wide_rows, :lanes], state[:wide_rows, lanes:]
    sent = jnp.concatenate(
        [jnp.where(first, high, left), jnp.where(first, tail[:, lanes:], tail[:, :lanes])], axis=0
    )
    got = swap(sent, "seq", 1)
    kept_tail = jnp.where(first, tail[:, :lanes], tail[:, lanes:])
    one = jnp.where(first, low, got[:wide_rows])
    two = jnp.where(first, got[:wide_rows], right)
    three = jnp.concatenate(
        [jnp.where(first, kept_tail, got[wide_rows:]), jnp.where(first, got[wide_rows:], kept_tail)], axis=0
    )
    return [value.astype(jnp.float32) for value in (one, two, three)]


def clipped(sums, centre, bins):
    first, last = centre + 1 - bins // 2, centre - 1 + bins // 2
    return jnp.concatenate(
        [
            jnp.sum(sums[..., :first], axis=-1, keepdims=True),
            sums[..., first:last],
            jnp.sum(sums[..., last:], axis=-1, keepdims=True),
        ],
        axis=-1,
    )


def grid_live(cells):
    return (cells // GRID_SIDE < GRID_SIDE - 1) & (cells % GRID_SIDE < GRID_SIDE - 1)


def grid_boxes(cells):
    return jnp.stack(
        [
            patch_pitch * (cells % GRID_SIDE) + patch_centre,
            patch_pitch * (cells // GRID_SIDE) + patch_centre,
        ]
    )


def shards(
    tokens,
    patches,
    page_length,
    box_position,
    query_weight,
    key_weight,
    value_weight,
    out_weight,
    up_weight,
    down_weight,
    conv_weight,
    patch_conv_weight,
    query_bias,
    value_bias,
    out_bias,
    up_bias,
    down_bias,
    attention_gain,
    attention_shift,
    feedforward_gain,
    feedforward_shift,
    reading_bias_table,
    horizontal_bias_table,
    vertical_bias_table,
    cotangent,
    patch_cotangent,
):
    conv_taps = conv_weight.astype(jnp.float32)
    patch_taps = patch_conv_weight.astype(jnp.float32)
    query_offset = query_bias.astype(jnp.float32)
    value_offset = value_bias.astype(jnp.float32)
    out_offset = out_bias.astype(jnp.float32)
    up_offset = up_bias.astype(jnp.float32)
    down_offset = down_bias.astype(jnp.float32)
    first_gain = attention_gain.astype(jnp.float32)
    first_shift = attention_shift.astype(jnp.float32)
    second_gain = feedforward_gain.astype(jnp.float32)
    second_shift = feedforward_shift.astype(jnp.float32)
    page_count, span_size, model_width = tokens.shape
    patch_span = patches.shape[1]
    seq_count = lax.axis_size("seq")
    slot_size = span_size * seq_count
    patch_slots = patch_span * seq_count
    row_count = span_size + patch_span
    key_count = row_count * seq_count
    head_count = reading_bias_table.shape[0]
    head_size = model_width // head_count
    line_bins = reading_bias_table.shape[1]
    plane_bins = horizontal_bias_table.shape[1]
    score_scale = head_size ** (-0.5)
    seq_index = lax.axis_index("seq")
    text_places = seq_index * span_size + jnp.arange(span_size, dtype=jnp.int32)
    local_cells = seq_index * patch_span + jnp.arange(patch_span, dtype=jnp.int32)
    text_live = text_places[None, :] < page_length[:, None]
    patch_live = grid_live(local_cells)
    text_factor = text_live[:, :, None]
    patch_factor = patch_live[None, :, None]
    masked = tokens * text_factor.astype(jnp.bfloat16)
    rimmed = with_halo(masked, (("seq", 1),), 3)
    reach = GRID_SIDE + 1
    patch_masked = patches * patch_factor.astype(jnp.bfloat16)
    patch_rimmed = with_halo(patch_masked, (("seq", 1),), reach)
    pages = lax.axis_size("page")
    (
        hidden, hidden_low, queries, mixture_low, columns, key_rows, query_rows, taps, keys, values, weights,
    ) = forward(
        pages, page_length, tokens, patches, box_position.transpose(1, 0, 2), (conv_weight.T, patch_conv_weight.T),
        (horizontal_bias_table, vertical_bias_table, reading_bias_table), (query_bias, value_bias),
        (query_weight, key_weight, value_weight),
    )
    places = jnp.stack(
        [seq_index, seq_index % 2, lax.axis_index("page"), seq_index // 2]
    ).astype(jnp.int32)
    def flat(value):
        return value.reshape(-1, value.shape[-1])

    output, patch_output, delta_first, delta_mixture, middle_sums, feedforward_bundle = middle(
        places, hidden, mixture_low, cotangent, patch_cotangent,
        (out_weight, up_weight, down_weight),
        (
            out_bias, down_bias, attention_gain, attention_shift, feedforward_gain, feedforward_shift, up_bias,
        ),
        pages,
    )
    pair_rows = weights.reshape(page_count, head_count // 2, 2 * row_count, -1)
    if in_tiles(model_width, pages):
        tokens_back, patches_back, early_state, late_state, sums, up_in, down_in, mixed_in = backward(
            pages,
            page_length,
            (
                queries, delta_mixture, columns, key_rows, query_rows, tokens, patches, taps, middle_sums,
            ),
            (
                feedforward_bundle, pair_rows, keys, values, hidden_low, delta_first, query_weight, key_weight,
                value_weight,
            ),
            tokens,
            patches,
        )
        (
            query_part, key_part, value_part, out_part, up_part, down_part, text_part, patch_part, line_part,
            across_part, upward_part, *vector_parts, tokens_gradient, patches_gradient,
        ) = finish(
            (early_state, late_state, sums, up_in, down_in, mixed_in),
            (tokens_back, patches_back), model_width, up_weight.shape[1], head_count, line_bins,
            plane_bins,
        )
        return (
            output,
            patch_output,
            tokens_gradient,
            patches_gradient,
            query_part,
            key_part,
            value_part,
            out_part,
            up_part,
            down_part.T,
            text_part.T,
            patch_part.T,
            *vector_parts,
            line_part,
            across_part,
            upward_part,
        )
    delta_first = delta_first.reshape(page_count, row_count, model_width)
    delta_mixture = delta_mixture.reshape(page_count, row_count, model_width)
    early_state = added(feedforward_bundle[0], swap(feedforward_bundle[1], "seq", 1))
    delta_mixture, early_state = lax.optimization_barrier((delta_mixture, early_state))
    delta_query_pages, delta_key_pages, delta_value_pages = [], [], []
    delta_plane, delta_line = 0.0, 0.0
    for page in range(page_count):
        delta_page_queries, delta_blocks, plane_part, line_part = backward_page(
            places,
            columns[page][:, ::128],
            key_rows[page],
            query_rows[page][:, :row_count],
            queries[page * row_count : (page + 1) * row_count],
            keys[page],
            values[page],
            delta_mixture[page],
            pair_rows[page],
        )
        got = swap(delta_blocks[2:], "seq", 1)
        chip_sum = delta_blocks[:2].astype(jnp.float32) + got.astype(jnp.float32)
        got = swap(chip_sum[1].astype(jnp.bfloat16), "seq", 2)
        whole = (chip_sum[0] + got.astype(jnp.float32)).astype(jnp.bfloat16)
        delta_query_pages.append(delta_page_queries)
        delta_key_pages.append(whole[0])
        delta_value_pages.append(whole[1])
        delta_plane = delta_plane + plane_part
        delta_line = delta_line + line_part
    delta_queries = jnp.stack(delta_query_pages)
    delta_keys = jnp.stack(delta_key_pages)
    delta_values = jnp.stack(delta_value_pages)
    delta_plane = clipped(delta_plane, 72, plane_bins)
    delta_line = clipped(delta_line, 32, line_bins)
    delta_across, delta_upward = delta_plane[0], delta_plane[1]
    delta_query_offset = row_sum(delta_queries)
    delta_value_offset = row_sum(delta_values)
    delta_hidden = (
        delta_first
        + back_dot(delta_queries, query_weight)
        + back_dot(delta_keys, key_weight)
        + back_dot(delta_values, value_weight)
    )
    delta_position = delta_hidden[:, :span_size].astype(jnp.bfloat16)
    delta_rim = with_halo(delta_position, (("seq", 1),), 3)
    delta_masked = jnp.zeros((page_count, span_size, model_width), jnp.float32)
    tap_columns = []
    for dilation in (1, 2, 3):
        for offset in (-1, 0, 1):
            column = 3 * (dilation - 1) + offset + 1
            anchor = 3 + offset * dilation
            anchor_back = 3 - offset * dilation
            delta_masked = (
                delta_masked
                + delta_rim[:, anchor_back : anchor_back + span_size, :] * conv_taps[:, column]
            )
            tap_columns.append(
                jnp.einsum(
                    "ptd,ptd->d",
                    delta_position,
                    rimmed[:, anchor : anchor + span_size, :],
                    preferred_element_type=jnp.float32,
                )
            )
    delta_taps = jnp.stack(tap_columns, axis=1)
    tokens_gradient = delta_hidden[:, :span_size] + delta_masked * text_factor.astype(jnp.float32)
    delta_patch_position = delta_hidden[:, span_size:].astype(jnp.bfloat16)
    delta_patch_rim = with_halo(delta_patch_position, (("seq", 1),), reach)
    delta_patch_masked = jnp.zeros((page_count, patch_span, model_width), jnp.float32)
    patch_columns = []
    for vertical in (-1, 0, 1):
        for horizontal in (-1, 0, 1):
            column = 3 * (vertical + 1) + horizontal + 1
            anchor = reach + vertical * GRID_SIDE + horizontal
            anchor_back = reach - vertical * GRID_SIDE - horizontal
            delta_patch_masked = (
                delta_patch_masked
                + delta_patch_rim[:, anchor_back : anchor_back + patch_span, :]
                * patch_taps[:, column]
            )
            patch_columns.append(
                jnp.einsum(
                    "ptd,ptd->d",
                    delta_patch_position,
                    patch_rimmed[:, anchor : anchor + patch_span, :],
                    preferred_element_type=jnp.float32,
                )
            )
    delta_patch_taps = jnp.stack(patch_columns, axis=1)
    patches_gradient = delta_hidden[:, span_size:] + delta_patch_masked * patch_factor.astype(
        jnp.float32
    )
    operands = [flat(value) for value in (hidden_low, delta_queries, delta_keys, delta_values)]
    tail_bundle = indexed_bundle(
        (
            ((operands[0], operands[1], None), (operands[0], operands[3], 0)),
            ((operands[0], operands[2], None), (operands[0], operands[3], 1)),
        ),
        places,
        pages,
    )
    tail_state = added(tail_bundle[0], swap(tail_bundle[1], "seq", 1))
    query_part, key_part, value_part = bundle_parts(
        bundle_sum(tail_state, pages), model_width // pages, places[1]
    )
    up_part, down_part, out_part = bundle_parts(
        bundle_sum(early_state, pages), up_weight.shape[1] // pages, places[1]
    )
    up_part = up_part.reshape(model_width // pages, -1)
    matrix_parts = (query_part, key_part, value_part, out_part, up_part, down_part)
    vector_parts = total_sum(
        (
            delta_taps,
            delta_patch_taps,
            delta_query_offset,
            delta_value_offset,
            middle_sums[OUT_BIAS],
            middle_sums[UP_BIAS : UP_BIAS + 4].reshape(-1),
            middle_sums[DOWN_BIAS],
            middle_sums[FIRST_GAIN],
            middle_sums[FIRST_SHIFT],
            middle_sums[SECOND_GAIN],
            middle_sums[SECOND_SHIFT],
            delta_line,
            delta_across,
            delta_upward,
        )
    )
    return (
        output,
        patch_output,
        tokens_gradient,
        patches_gradient,
        matrix_parts[0],
        matrix_parts[1],
        matrix_parts[2],
        matrix_parts[3],
        matrix_parts[4],
        matrix_parts[5],
        vector_parts[0],
        vector_parts[1],
        vector_parts[2],
        vector_parts[3],
        vector_parts[4],
        vector_parts[5],
        vector_parts[6],
        vector_parts[7],
        vector_parts[8],
        vector_parts[9],
        vector_parts[10],
        vector_parts[11],
        vector_parts[12],
        vector_parts[13],
    )


def solution(mesh):
    in_specs = (
        P("page", "seq", None),
        P("page", "seq", None),
        P("page"),
        P(None, "page", None),
        P(),
        P(),
        P(),
        P(),
        P(),
        P(),
        P(),
        P(),
        P(),
        P(),
        P(),
        P(),
        P(),
        P(),
        P(),
        P(),
        P(),
        P(),
        P(),
        P(),
        P("page", "seq", None),
        P("page", "seq", None),
    )
    out_specs = (
        P("page", "seq", None),
        P("page", "seq", None),
        P("page", "seq", None),
        P("page", "seq", None),
        P("page", "seq"),
        P("page", "seq"),
        P("page", "seq"),
        P("page", "seq"),
        P("page", "seq"),
        P("page", "seq"),
        P(),
        P(),
        P(),
        P(),
        P(),
        P(),
        P(),
        P(),
        P(),
        P(),
        P(),
        P(),
        P(),
        P(),
    )
    return jax.shard_map(shards, mesh=mesh, in_specs=in_specs, out_specs=out_specs, check_vma=False)
```

```python
import functools

import jax
import jax.numpy as jnp
from jax import lax
from jax.experimental import pallas as pl
from jax.experimental.pallas import tpu as pltpu
from jax.sharding import PartitionSpec as P

GRID_SIDE = 8


epsilon = 1e-05
coordinate_step = 16
masked_score = -1000000000.0
patch_pitch = 146
patch_centre = 73


def with_halo(cells, sides, width):
    for axis, dim in sides:
        count = lax.axis_size(axis)
        ends = count - 1
        head = lax.slice_in_dim(cells, 0, width, axis=dim)
        tail = lax.slice_in_dim(cells, cells.shape[dim] - width, cells.shape[dim], axis=dim)
        cells = jnp.concatenate(
            [
                lax.ppermute(tail, axis, [(i, (i + 1) % count) for i in range(ends)]),
                cells,
                lax.ppermute(head, axis, [((i + 1) % count, i) for i in range(ends)]),
            ],
            axis=dim,
        )
    return cells


def layer_norm(values, gain_vector, shift_vector):
    row_mean = jnp.mean(values, axis=-1, keepdims=True)
    centred = values - row_mean
    variance = jnp.mean(centred * centred, axis=-1, keepdims=True)
    return centred * lax.rsqrt(variance + epsilon) * gain_vector + shift_vector


def gelu_exact(values):
    return jax.nn.gelu(values, approximate=False)


def flat_dot(operand, matrix):
    front = operand.shape[:-1]
    result = jnp.dot(
        operand.reshape(-1, operand.shape[-1]), matrix, preferred_element_type=jnp.float32
    )
    return result.reshape(front + (matrix.shape[-1],))


def back_dot(operand, matrix):
    front = operand.shape[:-1]
    result = lax.dot_general(
        operand.reshape(-1, operand.shape[-1]),
        matrix,
        (((1,), (1,)), ((), ())),
        preferred_element_type=jnp.float32,
    )
    return result.reshape(front + (matrix.shape[0],))


def outer_dot(operand, gradient):
    return lax.dot_general(
        operand.reshape(-1, operand.shape[-1]),
        gradient.reshape(-1, gradient.shape[-1]),
        (((0,), (0,)), ((), ())),
        preferred_element_type=jnp.float32,
    )


def row_sum(gradient):
    return jnp.sum(gradient.astype(jnp.float32).reshape(-1, gradient.shape[-1]), axis=0)


def swap(value, axis, bit):
    count = lax.axis_size(axis)
    return lax.ppermute(value, axis, [(i, i ^ bit) for i in range(count)])


def total_sum(vectors):
    flat = jnp.concatenate([vector.reshape(-1) for vector in vectors])
    flat = jnp.pad(flat, (0, -flat.size % 1024)).reshape(-1, 128)
    for bit in (1, 2):
        flat = flat + swap(flat, "seq", bit)
    bit = 1
    while bit < lax.axis_size("page"):
        flat = flat + swap(flat, "page", bit)
        bit *= 2
    flat = flat.reshape(-1)
    result, start = [], 0
    for vector in vectors:
        result.append(flat[start : start + vector.size].reshape(vector.shape))
        start += vector.size
    return result


def query_places(seq_index, shape, span, patch_span, text_slots):
    row = lax.broadcasted_iota(jnp.int32, shape, 0)
    return jnp.where(
        row < span, seq_index * span + row, text_slots + seq_index * patch_span + row - span
    )


FIXED = 2048.0


def lookup(table_row, lanes):
    return jnp.take_along_axis(jnp.broadcast_to(table_row, lanes.shape), lanes, axis=1)


HEAD_LANES = 64


def split_heads(group):
    lane = lax.broadcasted_iota(jnp.int32, group.shape, 1) // HEAD_LANES
    zero = jnp.zeros_like(group)
    return jnp.concatenate(
        [jnp.where(lane == head, group, zero) for head in range(group.shape[1] // HEAD_LANES)], axis=0
    )


def merge_heads(rows):
    heads = rows.shape[1] // HEAD_LANES
    count = rows.shape[0] // heads
    lane = lax.broadcasted_iota(jnp.int32, (count, rows.shape[1]), 1) // HEAD_LANES
    merged = rows[:count]
    for head in range(1, heads):
        merged = jnp.where(lane == head, rows[head * count : (head + 1) * count], merged)
    return merged


def dot_nt(left, right):
    return lax.dot_general(left, right, (((1,), (1,)), ((), ())), preferred_element_type=jnp.float32)


def dot_nn(left, right):
    return lax.dot_general(left, right, (((1,), (0,)), ((), ())), preferred_element_type=jnp.float32)


def dot_tn(left, right):
    return lax.dot_general(left, right, (((0,), (0,)), ((), ())), preferred_element_type=jnp.float32)


CHUNK = 48
FORWARD_CHUNK = 48


MESH = pl.DeviceIdType.MESH


def places_of(pages):
    page = lax.axis_index("page")
    seq = lax.axis_index("seq")
    bits = []
    rest = page
    for _ in range(pages.bit_length() - 1):
        bits.append(rest % 2)
        rest = rest // 2
    return page, bits, seq, seq // 2, seq % 2


def sibling_of(seq):
    return seq + 1 - 2 * (seq % 2)


def across_of(seq):
    return seq + 2 - 4 * (seq // 2)


def remote(source, target, send, receive, page, seq):
    return pltpu.make_async_remote_copy(
        src_ref=source, dst_ref=target, send_sem=send, recv_sem=receive, device_id=(page, seq), device_id_type=MESH
    )


def column_of(row):
    square = jnp.broadcast_to(row.astype(jnp.float32), (128, 128)).T
    return square[:, 0:1].astype(jnp.int32)


def forward_kernel(
    pages,
    staging, length_ref, box_ref, text_taps_ref, patch_taps_ref, across_table_ref, upward_table_ref, line_table_ref,
    query_bias_ref, value_bias_ref, tokens_any, patches_any, query_weight_any, key_weight_any, value_weight_any,
    hidden_ref, hidden_low_ref, query_ref, mixture_ref, columns_ref, rows_ref, query_rows_ref, taps_ref, key_any,
    value_any, weights_any,
    own, matrices, key_ref, value_ref, weights_ref, arrived, text, grid, low, scores, across_ref, upward_ref,
    live_ref, line_ref, packed_ref, table_ref, vector_ref,
    load_sem, store_sem, send_sem, recv_sem,
):
    page_at, _, seq, _, _ = places_of(pages)
    count, span, width = tokens_any.shape
    patch_span = patches_any.shape[1]
    row_count = span + patch_span
    key_pad = key_ref.shape[1]
    text_slots = 4 * span
    rim = 8
    loads = [
        pltpu.make_async_copy(source, target, load_sem.at[index])
        for index, (source, target) in enumerate(
            (
                (tokens_any, own.at[:, 0:span]), (patches_any, own.at[:, span:row_count]),
                (key_weight_any, matrices.at[1]), (value_weight_any, matrices.at[2]), (query_weight_any, matrices.at[0]),
            )
        )
    ]
    for copy in loads:
        copy.start()

    def stores(page):
        return [
            pltpu.make_async_copy(source.at[page], target.at[page], store_sem.at[index, page])
            for index, (source, target) in enumerate(
                ((key_ref, key_any), (value_ref, value_any), (weights_ref, weights_any))
            )
        ]

    groups = weights_ref.shape[1]
    members = weights_ref.shape[2] // row_count
    pairs = groups * members // 2
    peers = (sibling_of(seq), across_of(seq))
    barrier = pltpu.get_barrier_semaphore()
    for peer in peers:
        pl.semaphore_signal(barrier, inc=1, device_id=(page_at, peer), device_id_type=MESH)
    pl.semaphore_wait(barrier, 2)

    def first_copies(page, side):
        return (
            remote(
                tokens_any.at[page], arrived.at[side, page, 0:span], send_sem.at[2 * side, page],
                recv_sem.at[2 * side, page], page_at, peers[side],
            ),
            remote(
                patches_any.at[page], arrived.at[side, page, span:row_count], send_sem.at[2 * side + 1, page],
                recv_sem.at[2 * side + 1, page], page_at, peers[side],
            ),
        )

    def onward_copy(page):
        return remote(
            arrived.at[1, page], arrived.at[2, page], send_sem.at[4, page], recv_sem.at[4, page], page_at, peers[0]
        )

    for page in range(count):
        for side in range(2):
            for copy in first_copies(page, side):
                copy.start()

    for copy in staging:
        copy.wait()
    table_ref[...] = jnp.zeros_like(table_ref)
    start = 0
    for source in (across_table_ref, upward_table_ref, line_table_ref):
        heads, bins = source.shape
        table_ref[0:heads, start : start + bins] = source[...].astype(jnp.float32)
        start += bins
    steps = jnp.floor(table_ref[...] * FIXED + 0.5).astype(jnp.int32)
    vector_ref[0:1, :] = query_bias_ref[...].astype(jnp.float32).reshape(1, width)
    vector_ref[1:2, :] = value_bias_ref[...].astype(jnp.float32).reshape(1, width)
    taps_ref[...] = jnp.zeros_like(taps_ref)
    taps_ref[0:9, :] = text_taps_ref[...].astype(jnp.float32)
    taps_ref[9:18, :] = patch_taps_ref[...].astype(jnp.float32)
    for pair in range(pairs):
        words = (steps[2 * pair : 2 * pair + 1] + 8192) + steps[2 * pair + 1 : 2 * pair + 2] * 65536
        packed_ref[0, pair : pair + 1, :] = words[:, 0:128]
        packed_ref[1, pair : pair + 1, :] = words[:, 128:256]
    key = lax.broadcasted_iota(jnp.int32, (row_count, key_pad), 1)
    place = query_places(seq, (row_count, key_pad), span, patch_span, text_slots)
    across_ref[...] = jnp.clip(key - place, -16, 15) + 16

    def fill(pair, carry):
        row = packed_ref[1, pl.ds(pair, 1), :]
        for at in range(0, key_pad, 128):
            line_ref[pair, :, at : at + 128] = lookup(row, across_ref[:, at : at + 128])
        return carry

    lax.fori_loop(0, pairs, fill, 0)
    text[0:rim, :] = jnp.zeros((rim, width), jnp.float32)
    text[rim + text_slots :, :] = jnp.zeros((rim, width), jnp.float32)
    grid[0:patch_span, :] = jnp.zeros((patch_span, width), jnp.float32)
    grid[patch_span * 5 :, :] = jnp.zeros((patch_span, width), jnp.float32)
    low[row_count * 4 :, :] = jnp.zeros((key_pad - row_count * 4, width), jnp.bfloat16)
    lanes = 256
    group_width = members * HEAD_LANES
    power = 1.4426950408889634 / FIXED
    for copy in first_copies(0, 1):
        copy.wait_recv()
    onward_copy(0).start()
    for copy in loads:
        copy.wait()

    def page_step(page, carry):
        length = length_ref[page]
        base = page * row_count
        cell = lax.broadcasted_iota(jnp.int32, (1, 128), 1)
        query_cell = seq * patch_span + cell
        row_cell = seq * patch_span + lax.broadcasted_iota(jnp.int32, (patch_span, 1), 0)
        for plane in range(2):
            box = box_ref[page, plane : plane + 1, :]
            patch = 146 * ((cell % GRID_SIDE) if plane == 0 else (cell // GRID_SIDE)) + 73
            own_patch = 146 * ((query_cell % GRID_SIDE) if plane == 0 else (query_cell // GRID_SIDE)) + 73
            column_patch = 146 * ((row_cell % GRID_SIDE) if plane == 0 else (row_cell // GRID_SIDE)) + 73
            rows_ref[page, plane : plane + 1, 0:text_slots] = box
            rows_ref[page, plane : plane + 1, text_slots:key_pad] = patch
            own_box = rows_ref[page, plane : plane + 1, pl.ds(pl.multiple_of(seq * span, 128), span)]
            query_rows_ref[page, plane : plane + 1, 0:span] = own_box
            query_rows_ref[page, plane : plane + 1, span:256] = own_patch
            columns_ref[page, 0:span, plane * 128 : (plane + 1) * 128] = jnp.broadcast_to(
                column_of(own_box), (span, 128)
            )
            columns_ref[page, span:row_count, plane * 128 : (plane + 1) * 128] = jnp.broadcast_to(
                column_patch, (patch_span, 128)
            )
        for plane, lanes_ref in enumerate((across_ref, upward_ref)):
            difference = rows_ref[page, plane : plane + 1, :] - columns_ref[page, :, plane * 128 : plane * 128 + 1]
            lanes_ref[...] = jnp.clip(difference >> 4, -32, 31) + (32 + 64 * plane)
        key_at = lax.broadcasted_iota(jnp.int32, live_ref.shape, 1)
        key_cell = key_at - text_slots
        live = (key_at < length) | (
            (key_cell >= 0) & ((key_cell >> 3) < GRID_SIDE - 1) & ((key_cell & 7) < GRID_SIDE - 1)
        )
        live_ref[...] = jnp.where(live, 0.0, masked_score * FIXED)
        for copy in first_copies(page, 0):
            copy.wait_recv()
        onward_copy(page).wait_recv()

        def block_of(step, start, stop, at):
            if step:
                return arrived[step - 1, page, start:stop, at].astype(jnp.float32)
            if start:
                return own[page, span:row_count, at].astype(jnp.float32)
            return own[page, 0:span, at].astype(jnp.float32)

        def slot_of(step):
            return (seq, peers[0], peers[1], sibling_of(peers[1]))[step]

        everything = slice(0, width)
        for step in range(4):
            where = slot_of(step)
            at_place = where * span + lax.broadcasted_iota(jnp.int32, (span, 1), 0)
            text[pl.ds(pl.multiple_of(rim + where * span, 8), span), :] = jnp.where(
                at_place < length, block_of(step, 0, span, everything), 0.0
            )
            at_cell = where * patch_span + lax.broadcasted_iota(jnp.int32, (patch_span, 1), 0)
            cell_live = ((at_cell >> 3) < GRID_SIDE - 1) & ((at_cell & 7) < GRID_SIDE - 1)
            grid[pl.ds(pl.multiple_of(patch_span + where * patch_span, 8), patch_span), :] = jnp.where(
                cell_live, block_of(step, span, row_count, everything), 0.0
            )
        for step in range(4):
            where = slot_of(step)

            def convolve(tile, carry):
                at = pl.ds(pl.multiple_of(tile * lanes, lanes), lanes)
                window = text[pl.ds(pl.multiple_of(where * span, 8), span + 2 * rim), at]
                centre = taps_ref[1:2, at] + taps_ref[4:5, at] + taps_ref[7:8, at]
                total = block_of(step, 0, span, at) + window[rim : rim + span] * centre
                for dilation in (1, 2, 3):
                    for offset in (-1, 1):
                        tap = 3 * (dilation - 1) + offset + 1
                        anchor = rim + offset * dilation
                        total = total + window[anchor : anchor + span] * taps_ref[tap : tap + 1, at]
                low[pl.ds(pl.multiple_of(where * span, 16), span), at] = total.astype(jnp.bfloat16)
                window = grid[pl.ds(pl.multiple_of(where * patch_span, 8), 3 * patch_span), at]
                patch_total = block_of(step, span, row_count, at)
                for vertical in (-1, 0, 1):
                    for horizontal in (-1, 0, 1):
                        tap = 9 + 3 * (vertical + 1) + horizontal + 1
                        anchor = patch_span + vertical * GRID_SIDE + horizontal
                        patch_total = patch_total + window[anchor : anchor + patch_span] * taps_ref[tap : tap + 1, at]
                low[pl.ds(pl.multiple_of(text_slots + where * patch_span, 16), patch_span), at] = (
                    patch_total.astype(jnp.bfloat16)
                )
                if step == 0:
                    for first, rows_here, value in ((0, span, total), (span, patch_span, patch_total)):
                        here = pl.ds(pl.multiple_of(base + first, 16), rows_here)
                        hidden_ref[here, at] = value
                        hidden_low_ref[here, at] = value.astype(jnp.bfloat16)
                return carry

            lax.fori_loop(0, width // lanes, convolve, 0)
        own_rows = pl.ds(pl.multiple_of(base, 16), row_count)

        key_ref[page] = dot_nn(low[...], matrices[1]).astype(jnp.bfloat16)
        value_ref[page] = (dot_nn(low[...], matrices[2]) + vector_ref[1:2, :]).astype(jnp.bfloat16)
        query_ref[own_rows, :] = (
            (dot_nn(hidden_low_ref[own_rows, :], matrices[0]) + vector_ref[0:1, :]).astype(jnp.bfloat16)
            * jnp.bfloat16(0.125)
        )

        @pl.when(page < count - 1)
        def _():
            for copy in first_copies(page + 1, 1):
                copy.wait_recv()
            onward_copy(page + 1).start()

        def attend(group, carry):
            at = pl.ds(pl.multiple_of(group * group_width, group_width), group_width)
            scores[...] = dot_nt(split_heads(query_ref[own_rows, at] * jnp.bfloat16(FIXED)), key_ref[page, :, at])
            for start, sub in ((start, sub) for start in range(0, row_count, FORWARD_CHUNK) for sub in range(members // 2)):
                pair = group * (members // 2) + sub
                plane_row = packed_ref[0, pl.ds(pair, 1), :]
                here = slice(start, start + FORWARD_CHUNK)
                packed = []
                for block_at in range(0, key_pad, 128):
                    lane = slice(block_at, block_at + 128)
                    packed.append(
                        line_ref[pair, here, lane]
                        + lookup(plane_row, across_ref[here, lane])
                        + lookup(plane_row, upward_ref[here, lane])
                    )
                for side in range(2):
                    first = (2 * sub + side) * row_count + start
                    there = slice(first, first + FORWARD_CHUNK)
                    parts, top = [], None
                    for index, word in enumerate(packed):
                        lane = slice(128 * index, 128 * (index + 1))
                        field = (word >> 16) if side else (word & 0xFFFF)
                        part = (scores[there, lane] + field.astype(jnp.float32)) + live_ref[0:1, lane]
                        top = part if top is None else jnp.maximum(top, part)
                        parts.append(part)
                    top = jnp.max(top, axis=1, keepdims=True)
                    parts = [jnp.exp2((part - top) * power) for part in parts]
                    total = parts[0]
                    for part in parts[1:]:
                        total = total + part
                    inverse = 1.0 / jnp.sum(total, axis=1, keepdims=True)
                    for index, part in enumerate(parts):
                        weights_ref[page, group, there, 128 * index : 128 * (index + 1)] = (part * inverse).astype(
                            jnp.bfloat16
                        )
            mixture_ref[own_rows, at] = merge_heads(
                dot_nn(weights_ref[page, group], value_ref[page, :, at])
            ).astype(jnp.bfloat16)
            return carry

        lax.fori_loop(0, groups, attend, 0)
        for copy in stores(page):
            copy.start()
        return carry

    lax.fori_loop(0, count, page_step, 0)
    for page in range(count):
        for side in range(2):
            for copy in first_copies(page, side):
                copy.wait_send()
        onward_copy(page).wait_send()
        for copy in stores(page):
            copy.wait()


VMEM = pltpu.VMEM
KERNEL_VMEM = 62 * 1024 * 1024


def in_vmem(count):
    return [pl.BlockSpec(memory_space=VMEM)] * count


def staged(kernel, first, count):
    def run(*refs):
        *refs, semaphore = refs
        refs, buffers = list(refs[:-count]), refs[-count:]
        copies = [
            pltpu.make_async_copy(refs[first + index], buffers[index], semaphore.at[index]) for index in range(count)
        ]
        for copy in copies:
            copy.start()
        refs[first : first + count] = buffers
        kernel(copies, *refs)

    return run


def stage_for(values):
    return [VMEM(value.shape, value.dtype) for value in values] + [pltpu.SemaphoreType.DMA((len(values),))]


def position():
    seq = lax.axis_index("seq")
    return seq, seq % 2, lax.axis_index("page"), seq // 2


def anywhere(count):
    return [pl.BlockSpec(memory_space=pl.ANY)] * count


def forward(pages, lengths, tokens, patches, box, taps, tables, biases, matrices):
    count, span, width = tokens.shape
    patch_span = patches.shape[1]
    row_count = span + patch_span
    total_rows = count * row_count
    key_pad = -(-4 * row_count // 128) * 128
    heads = tables[0].shape[0]
    pairs = heads // 2
    members = 4 if heads % 4 == 0 else 2
    groups = heads // members
    small = (box, *taps, *tables, *biases)
    bf16, f32, i32 = jnp.bfloat16, jnp.float32, jnp.int32
    own = jax.ShapeDtypeStruct((total_rows, width), bf16)
    every = jax.ShapeDtypeStruct((count, key_pad, width), bf16)
    return pl.pallas_call(
        staged(functools.partial(forward_kernel, pages), 1, len(small)),
        out_shape=(
            jax.ShapeDtypeStruct((total_rows, width), f32), own, own, own,
            jax.ShapeDtypeStruct((count, row_count, 256), i32),
            jax.ShapeDtypeStruct((count, 8, key_pad), i32),
            jax.ShapeDtypeStruct((count, 8, 256), i32),
            jax.ShapeDtypeStruct((24, width), f32),
            every, every,
            jax.ShapeDtypeStruct((count, groups, members * row_count, key_pad), bf16),
        ),
        in_specs=[pl.BlockSpec(memory_space=pltpu.SMEM)] + anywhere(len(small) + 5),
        out_specs=tuple(in_vmem(8) + anywhere(3)),
        scratch_shapes=[
            VMEM((count, row_count, width), bf16),
            VMEM((3, width, width), bf16),
            VMEM((count, key_pad, width), bf16),
            VMEM((count, key_pad, width), bf16),
            VMEM((count, groups, members * row_count, key_pad), bf16),
            VMEM((3, count, row_count, width), bf16),
            VMEM((4 * span + 16, width), f32),
            VMEM((6 * patch_span, width), f32),
            VMEM((key_pad, width), bf16),
            VMEM((members * row_count, key_pad), f32),
            VMEM((row_count, key_pad), i32),
            VMEM((row_count, key_pad), i32),
            VMEM((8, key_pad), f32),
            VMEM((pairs, row_count, key_pad), i32),
            VMEM((2, 8, 128), i32),
            VMEM((-(-heads // 8) * 8, 256), f32),
            VMEM((8, width), f32),
            pltpu.SemaphoreType.DMA((5,)),
            pltpu.SemaphoreType.DMA((3, count)),
            pltpu.SemaphoreType.DMA((5, count)),
            pltpu.SemaphoreType.DMA((5, count)),
        ]
        + stage_for(small),
        compiler_params=pltpu.CompilerParams(
            collective_id=0, has_side_effects=True, vmem_limit_bytes=KERNEL_VMEM
        ),
        cost_estimate=pl.CostEstimate(flops=8_000_000_000, bytes_accessed=25_000_000, transcendentals=3_000_000),
        name="forward",
    )(lengths, *small, tokens, patches, *matrices)


def backward_page_kernel(
    scalar_ref, columns_ref, rows_ref, query_rows_ref, query_ref, key_ref, value_ref, mixture_back_ref, weights_ref,
    query_back_ref, block_back_ref, plane_back_ref, line_back_ref,
    back, steps, mask_ref, hot_ref, query_hot_ref, band_ref,
):
    seq_index = scalar_ref[0]
    row_count, width = query_ref.shape
    key_pad = key_ref.shape[0]
    count = 4
    patch_span = GRID_SIDE * GRID_SIDE // count
    span = row_count - patch_span
    text_slots = span * count
    columns, rows = columns_ref[...], rows_ref[...]
    mask_ref[:, 0:key_pad] = ((rows[0:1, :] & 15) < (columns[:, 0:1] & 15)).astype(jnp.float32).astype(jnp.bfloat16)
    mask_ref[:, key_pad:] = ((rows[1:2, :] & 15) < (columns[:, 1:2] & 15)).astype(jnp.float32).astype(jnp.bfloat16)
    bin_at = lax.broadcasted_iota(jnp.int32, (128, key_pad), 0) - 1
    key_block = lax.broadcasted_iota(jnp.int32, (128, key_pad), 1) >> 4
    for side in range(2):
        key_bin = rows[side : side + 1, :] >> 4
        plain = (key_bin == bin_at).astype(jnp.float32)
        lower = (key_bin - 1 == bin_at).astype(jnp.float32)
        plain, lower = jnp.where(bin_at < 64, plain, 0.0), jnp.where(bin_at < 64, lower, 0.0)
        mine = slice(128 * side, 128 * (side + 1))
        other = slice(128 * (1 - side), 128 * (2 - side))
        change = lower - plain
        if side == 0:
            plain = jnp.where(bin_at - 71 == key_block, 1.0, plain)
        hot_ref[mine, 0:key_pad] = plain.astype(jnp.bfloat16)
        hot_ref[mine, (1 + side) * key_pad : (2 + side) * key_pad] = change.astype(jnp.bfloat16)
        hot_ref[other, (1 + side) * key_pad : (2 + side) * key_pad] = jnp.zeros((128, key_pad), jnp.bfloat16)
    half_bin = lax.broadcasted_iota(jnp.int32, (72, row_count), 0)
    for side in range(2):
        query_hot_ref[72 * side : 72 * (side + 1), :] = (
            (71 - (query_rows_ref[side : side + 1, :] >> 4) == half_bin).astype(jnp.float32).astype(jnp.bfloat16)
        )
    lane128 = lax.broadcasted_iota(jnp.int32, (row_count, 128), 1)
    place = query_places(seq_index, (row_count, 128), span, patch_span, text_slots)
    aim = place + lane128 - 32
    near = (lane128 < 64) & (aim >= 0) & (aim < text_slots + patch_span * count)
    apart = (aim >> 4) - (place >> 4)
    near = near & (apart >= -1) & (apart <= 1)
    band_ref[...] = jnp.where(near, aim, -1)
    pair_width = 128
    line_back_ref[...] = jnp.zeros_like(line_back_ref)
    plane_back_ref[...] = jnp.zeros_like(plane_back_ref)

    def attend(pair, carry):
        at = pl.ds(pl.multiple_of(pair * pair_width, pair_width), pair_width)
        both_query = split_heads(query_ref[:, at])
        both_back = split_heads(mixture_back_ref[:, at])
        back[...] = dot_nt(both_back, value_ref[:, at])
        for start in range(0, 2 * row_count, CHUNK):
            there = slice(start, start + CHUNK)
            here = slice(start % row_count, start % row_count + CHUNK)
            parts, total = [], None
            for block_at in range(0, key_pad, 128):
                lane = slice(block_at, block_at + 128)
                part = weights_ref[pair, there, lane].astype(jnp.float32)
                product = part * back[there, lane]
                total = product if total is None else total + product
                parts.append(part)
            mean = jnp.sum(total, axis=1, keepdims=True)
            for index, part in enumerate(parts):
                lane = slice(128 * index, 128 * (index + 1))
                step = (part * (back[there, lane] - mean)).astype(jnp.bfloat16)
                steps[there, lane] = step
                steps[there, key_pad + 128 * index : key_pad + 128 * (index + 1)] = step * mask_ref[here, lane]
                steps[there, 2 * key_pad + 128 * index : 2 * key_pad + 128 * (index + 1)] = (
                    step * mask_ref[here, key_pad + 128 * index : key_pad + 128 * (index + 1)]
                )
        query_back_ref[:, at] = (merge_heads(dot_nn(steps[:, 0:key_pad], key_ref[:, at])) * 0.125).astype(
            jnp.bfloat16
        )
        for kind, value in enumerate(
            (dot_tn(steps[:, 0:key_pad], both_query), dot_tn(weights_ref[pair], both_back))
        ):
            value = value.astype(jnp.bfloat16)
            for where in range(count):
                step_at = seq_index ^ where
                slot = (step_at & 1) * 2 + (step_at >> 1)
                block_back_ref[slot, kind, 0:span, at] = value[where * span : (where + 1) * span]
                block_back_ref[slot, kind, span:row_count, at] = value[
                    text_slots + where * patch_span : text_slots + (where + 1) * patch_span
                ]
        bins = dot_nt(steps[...], hot_ref[...])
        low_bins = bins.astype(jnp.bfloat16)
        lane_one = lax.broadcasted_iota(jnp.int32, (1, 128), 1)
        far = lane128 - 72 - (place >> 4)
        in_line = (lane128 >= 72) & (lane128 < 72 + key_pad // 16)
        for side in range(2):
            head = pl.ds(2 * pair + side, 1)
            own = slice(side * row_count, (side + 1) * row_count)
            both = dot_nn(query_hot_ref[...], low_bins[own])
            for plane in range(2):
                table = both[72 * plane : 72 * (plane + 1), 128 * plane : 128 * (plane + 1)]
                wide_lane = lax.broadcasted_iota(jnp.int32, table.shape, 1)
                table = jnp.where(wide_lane < 72, table, 0.0)
                table = jnp.concatenate([table, jnp.zeros_like(table)], axis=1)
                sheared = pltpu.roll(table, 0, 1, stride=1, stride_axis=0)
                plane_back_ref[plane, head, :] = jnp.sum(sheared, axis=0, keepdims=True)
            line_bins = bins[own, 0:128]
            low_tail = jnp.sum(jnp.where(in_line & (far <= -2), line_bins, 0.0), axis=(0, 1), keepdims=True)
            high_tail = jnp.sum(jnp.where(in_line & (far >= 2), line_bins, 0.0), axis=(0, 1), keepdims=True)
            band = jnp.zeros((1, 128), jnp.float32)
            base = side * row_count
            for first, rows_here, block in (
                (0, span, seq_index),
                (0, 32, jnp.maximum(seq_index - 1, 0)),
                (span - 32, 32, seq_index + 1),
                (span, patch_span, count - 1),
                (span, patch_span, count),
            ):
                aims = band_ref[first : first + rows_here, :]
                source = steps[
                    base + first : base + first + rows_here, pl.ds(pl.multiple_of(block * 128, 128), 128)
                ].astype(jnp.float32)
                taken = jnp.take_along_axis(source, aims & 127, axis=1)
                right = (aims >> 7) == block
                if first == 0 and rows_here == 32:
                    right = right & (seq_index > 0)
                band = band + jnp.sum(jnp.where(right, taken, 0.0), axis=0, keepdims=True)
            line_back_ref[head, :] = (
                band + jnp.where(lane_one == 0, low_tail, 0.0) + jnp.where(lane_one == 63, high_tail, 0.0)
            )
        return carry

    lax.fori_loop(0, width // pair_width, attend, 0)


def backward_page(scalars, columns, rows, query_rows, queries, keys, values, mixture_back, weights):
    row_count, width = queries.shape
    key_pad = keys.shape[0]
    heads = 2 * weights.shape[0]
    return pl.pallas_call(
        backward_page_kernel,
        out_shape=(
            jax.ShapeDtypeStruct((row_count, width), jnp.bfloat16),
            jax.ShapeDtypeStruct((4, 2, row_count, width), jnp.bfloat16),
            jax.ShapeDtypeStruct((2, heads, 256), jnp.float32),
            jax.ShapeDtypeStruct((heads, 128), jnp.float32),
        ),
        in_specs=[pl.BlockSpec(memory_space=pltpu.SMEM)] + in_vmem(8),
        out_specs=tuple(in_vmem(4)),
        scratch_shapes=[
            pltpu.VMEM((2 * row_count, key_pad), jnp.float32),
            pltpu.VMEM((2 * row_count, 3 * key_pad), jnp.bfloat16),
            pltpu.VMEM((row_count, 2 * key_pad), jnp.bfloat16),
            pltpu.VMEM((256, 3 * key_pad), jnp.bfloat16),
            pltpu.VMEM((144, row_count), jnp.bfloat16),
            pltpu.VMEM((row_count, 128), jnp.int32),
        ],
        compiler_params=pltpu.CompilerParams(vmem_limit_bytes=KERNEL_VMEM),
        cost_estimate=pl.CostEstimate(flops=3_000_000_000, bytes_accessed=6_000_000, transcendentals=1_000_000),
        name="backward_page",
    )(scalars, columns, rows, query_rows, queries, keys, values, mixture_back, weights)


def early_orders(far, side):
    return (far[1], far[0], side) + tuple(far[2:]), (far[0], far[1], side) + tuple(far[2:])


def slot_of_bits(bits):
    slot = 0
    for bit in bits:
        slot = slot * 2 + bit
    return slot


def apart(one, other):
    return (one + other) % 2


def early_slots(scalar_ref, page, column, levels):
    far = [apart((page >> level) & 1, (scalar_ref[2] >> level) & 1) for level in range(levels)]
    side = apart(column, scalar_ref[3])
    return [slot_of_bits(order) for order in early_orders(far, side)]


NORM_CHUNK = 48


def norm_rows(values):
    mean = jnp.mean(values, axis=-1, keepdims=True)
    centred = values - mean
    scale = lax.rsqrt(jnp.mean(centred * centred, axis=-1, keepdims=True) + epsilon)
    return centred * scale, scale


def norm_back(delta, unit, scale):
    return scale * (
        delta
        - jnp.mean(delta, axis=-1, keepdims=True)
        - unit * jnp.mean(delta * unit, axis=-1, keepdims=True)
    )


def column_sum(values):
    return jnp.sum(values, axis=0, keepdims=True)


OUT_BIAS, DOWN_BIAS, FIRST_GAIN, FIRST_SHIFT, SECOND_GAIN, SECOND_SHIFT = range(6)
UP_BIAS = 6


def middle_kernel(
    pages, direct,
    *rest,
):
    scalar_ref = position()
    arguments, rest = rest[:14], rest[14:]
    output_ref, patch_output_ref, first_back_ref, mixture_back_ref, sums_ref, *rest = rest
    *rest, vector_ref, load_sem, store_sem = rest
    copied, rest = rest[-14:], rest[:-14]
    hidden_ref, mixture_ref, cotangent_ref, patch_cotangent_ref, out_weight_ref, up_weight_ref, down_weight_ref = copied[:7]
    loads = [
        pltpu.make_async_copy(source, target, load_sem.at[index])
        for index, (source, target) in enumerate(zip(arguments, copied, strict=True))
    ]
    for index in (*range(7, 14), 1, 4, 0, 5, 6, 2, 3):
        loads[index].start()
    if direct:
        bundle_any, *rest, bundle_ref = rest
    else:
        normed_out_ref, up_out_ref, activated_out_ref, down_out_ref, attention_out_ref, *rest = rest
    state, unit, scale_ref, normed, activated, slope, up_back, down_back, attention_back, flipped = rest
    count, span, width = output_ref.shape
    patch_span = patch_output_ref.shape[1]
    row_count = span + patch_span
    total_rows = count * row_count
    wide = up_weight_ref.shape[1]
    lanes = width
    sums_ref[...] = jnp.zeros_like(sums_ref)

    def tile_at(tile):
        return pl.ds(pl.multiple_of(tile * lanes, lanes), lanes)

    def attention_tile(tile, carry):
        at = tile_at(tile)
        state[:, at] = hidden_ref[:, at] + (dot_nn(mixture_ref[...], out_weight_ref[:, at]) + vector_ref[2:3, at])
        return carry

    for index in (*range(7, 14), 0, 1, 4):
        loads[index].wait()
    for index, source in enumerate(copied[7:13]):
        vector_ref[2 + index : 3 + index, :] = source[...].astype(jnp.float32).reshape(1, width)
    for index in range(wide // width):
        part = copied[13][pl.ds(index * width, width)]
        vector_ref[8 + index : 9 + index, :] = part.astype(jnp.float32).reshape(1, width)
    lax.fori_loop(0, width // lanes, attention_tile, 0)

    def first_norm(chunk, carry):
        here = pl.ds(pl.multiple_of(chunk * NORM_CHUNK, 16), NORM_CHUNK)
        rows, scale = norm_rows(state[here, :])
        unit[here, :] = rows
        scale_ref[here, :] = jnp.broadcast_to(scale, (NORM_CHUNK, 128))
        rows = rows * vector_ref[4:5, :] + vector_ref[5:6, :]
        state[here, :] = rows
        normed[here, :] = rows.astype(jnp.bfloat16)
        return carry

    lax.fori_loop(0, total_rows // NORM_CHUNK, first_norm, 0)

    def up_tile(tile, carry):
        at = tile_at(tile)
        branch = dot_nn(normed[...], up_weight_ref[:, at]) + vector_ref[pl.ds(8 + tile, 1), :]
        chance = 0.5 * (1.0 + lax.erf(branch * 0.7071067811865476))
        activated[:, at] = (branch * chance).astype(jnp.bfloat16)
        slope[:, at] = chance + branch * (jnp.exp(branch * branch * -0.5) * 0.3989422804014327)
        return carry

    loads[5].wait()
    lax.fori_loop(0, wide // lanes, up_tile, 0)

    def down_tile(tile, carry):
        at = tile_at(tile)
        state[:, at] = state[:, at] + (dot_nn(activated[...], down_weight_ref[:, at]) + vector_ref[3:4, at])
        return carry

    for index in (2, 3, 6):
        loads[index].wait()
    lax.fori_loop(0, width // lanes, down_tile, 0)

    def second_norm(start, rows_here, page, out_ref, delta_ref):
        here = pl.ds(pl.multiple_of(page * row_count + start, 16), rows_here)
        there = pl.ds(0 if start == span else start, rows_here)
        rows, scale = norm_rows(state[here, :])
        out_ref[page, there, :] = rows * vector_ref[6:7, :] + vector_ref[7:8, :]
        delta = delta_ref[page, there, :].astype(jnp.float32)
        back = norm_back(delta * vector_ref[6:7, :], rows, scale)
        state[here, :] = back
        low = back.astype(jnp.bfloat16)
        down_back[here, :] = low
        for index, value in (
            (SECOND_GAIN, delta * rows), (SECOND_SHIFT, delta), (DOWN_BIAS, low.astype(jnp.float32))
        ):
            sums_ref[index : index + 1, :] += column_sum(value)

    def second_page(page, carry):
        for start in range(0, span, 32):
            second_norm(start, 32, page, output_ref, cotangent_ref)
        second_norm(span, patch_span, page, patch_output_ref, patch_cotangent_ref)
        return carry

    lax.fori_loop(0, count, second_page, 0)

    def up_back_tile(tile, carry):
        at = tile_at(tile)
        low = (dot_nt(down_back[...], down_weight_ref[at, :]) * slope[:, at]).astype(jnp.bfloat16)
        up_back[:, at] = low
        sums_ref[pl.ds(UP_BIAS + tile, 1), :] = column_sum(low.astype(jnp.float32))
        return carry

    lax.fori_loop(0, wide // lanes, up_back_tile, 0)

    def normed_back_tile(tile, carry):
        at = tile_at(tile)
        state[:, at] = state[:, at] + dot_nt(up_back[...], up_weight_ref[at, :])
        return carry

    lax.fori_loop(0, width // lanes, normed_back_tile, 0)

    def first_back(chunk, carry):
        here = pl.ds(pl.multiple_of(chunk * NORM_CHUNK, 16), NORM_CHUNK)
        delta, rows = state[here, :], unit[here, :]
        back = norm_back(delta * vector_ref[4:5, :], rows, scale_ref[here, 0:1])
        first_back_ref[here, :] = back
        low = back.astype(jnp.bfloat16)
        attention_back[here, :] = low
        for index, value in (
            (FIRST_GAIN, delta * rows), (FIRST_SHIFT, delta), (OUT_BIAS, low.astype(jnp.float32))
        ):
            sums_ref[index : index + 1, :] += column_sum(value)
        return carry

    lax.fori_loop(0, total_rows // NORM_CHUNK, first_back, 0)

    def mixture_tile(tile, carry):
        at = tile_at(tile)
        mixture_back_ref[:, at] = dot_nt(attention_back[...], out_weight_ref[at, :]).astype(jnp.bfloat16)
        return carry

    lax.fori_loop(0, width // lanes, mixture_tile, 0)
    if not direct:
        normed_out_ref[...] = normed[...]
        up_out_ref[...] = up_back[...]
        activated_out_ref[...] = activated[...]
        down_out_ref[...] = down_back[...]
        attention_out_ref[...] = attention_back[...]
        return
    levels = pages.bit_length() - 1
    core = scalar_ref[1]
    rows = width // pages
    tall = wide // pages
    block = 384
    groups = wide // (2 * block)
    flipped[...] = normed[...].T

    def up_weight_tile(tile, carry):
        at = pl.ds(pl.multiple_of(tile * 2 * block, 2 * block), 2 * block)
        result = dot_nn(flipped[...], up_back[:, at]).astype(jnp.bfloat16)
        for part in range(2):
            column, group = (2 * tile + part) // groups, (2 * tile + part) % groups
            for page in range(pages):
                slot = early_slots(scalar_ref, page, column, levels)[0]
                bundle_ref[core, slot, pl.ds(pl.multiple_of(group * rows, 16), rows), :] = result[
                    page * rows : (page + 1) * rows, part * block : (part + 1) * block
                ]
        return carry

    lax.fori_loop(0, groups, up_weight_tile, 0)
    stores = [
        pltpu.make_async_copy(bundle_ref.at[part], bundle_any.at[part], store_sem.at[index])
        for index, part in enumerate(
            (
                (core, slice(None), slice(0, tall)), (1 - core, slice(None), slice(0, tall)),
                (slice(None), slice(None), slice(tall, tall + rows // 2)),
            )
        )
    ]
    stores[0].start()

    def down_weight_tile(four, carry):
        at = pl.ds(pl.multiple_of(four * 4 * tall, 128), 4 * tall)
        result = dot_tn(activated[:, at], down_back[...]).astype(jnp.bfloat16)
        for inner in range(4):
            for column in range(2):
                slot = early_slots(scalar_ref, 4 * four + inner, column, levels)[1]
                bundle_ref[1 - core, slot, 0:tall, :] = result[
                    inner * tall : (inner + 1) * tall, column * block : (column + 1) * block
                ]
        return carry

    lax.fori_loop(0, pages // 4, down_weight_tile, 0)
    stores[1].start()
    flipped[...] = mixture_ref[...].T
    half = rows // 2

    result = dot_nn(flipped[...], attention_back[...]).astype(jnp.bfloat16)
    for column in range(2):
        for page in range(pages):
            slots = early_slots(scalar_ref, page, column, levels)
            for order in range(2):
                first = page * rows + order * half
                bundle_ref[core if order == 0 else 1 - core, slots[order], tall : tall + half, :] = result[
                    first : first + half, column * block : (column + 1) * block
                ]
    stores[2].start()
    for copy in stores:
        copy.wait()


def in_tiles(width, pages):
    return (width // pages) % 32 == 0 and pages >= 4


def middle(places, hidden, mixture, cotangent, patch_cotangent, matrices, vectors, pages):
    count, span, width = cotangent.shape
    patch_span = patch_cotangent.shape[1]
    total_rows = hidden.shape[0]
    wide = matrices[1].shape[1]
    direct = in_tiles(width, pages)
    bf16, f32 = jnp.bfloat16, jnp.float32
    if direct:
        extra = (jax.ShapeDtypeStruct((2, 2 * pages, (wide + width // 2) // pages, 384), bf16),)
    else:
        extra = tuple(
            jax.ShapeDtypeStruct((total_rows, size), bf16) for size in (width, wide, wide, width, width)
        )
    result = pl.pallas_call(
        functools.partial(middle_kernel, pages, direct),
        out_shape=(
            jax.ShapeDtypeStruct(cotangent.shape, f32),
            jax.ShapeDtypeStruct(patch_cotangent.shape, f32),
            jax.ShapeDtypeStruct((total_rows, width), f32),
            jax.ShapeDtypeStruct((total_rows, width), bf16),
            jax.ShapeDtypeStruct((16, width), f32),
        )
        + extra,
        in_specs=anywhere(7 + len(vectors)),
        out_specs=tuple(in_vmem(5) + (anywhere(1) if direct else in_vmem(len(extra)))),
        scratch_shapes=[
            pltpu.VMEM((total_rows, width), f32),
            pltpu.VMEM((total_rows, width), f32),
            pltpu.VMEM((total_rows, 128), f32),
            pltpu.VMEM((total_rows, width), bf16),
            pltpu.VMEM((total_rows, wide), bf16),
            pltpu.VMEM((total_rows, wide), f32),
            pltpu.VMEM((total_rows, wide), bf16),
            pltpu.VMEM((total_rows, width), bf16),
            pltpu.VMEM((total_rows, width), bf16),
            pltpu.VMEM((width, total_rows), bf16),
        ]
        + [pltpu.VMEM(value.shape, value.dtype) for value in (extra if direct else ())]
        + [
            pltpu.VMEM(value.shape, value.dtype)
            for value in (hidden, mixture, cotangent, patch_cotangent, *matrices, *vectors)
        ]
        + [pltpu.VMEM((16, width), f32), pltpu.SemaphoreType.DMA((14,)), pltpu.SemaphoreType.DMA((3,))],
        compiler_params=pltpu.CompilerParams(vmem_limit_bytes=KERNEL_VMEM),
        cost_estimate=pl.CostEstimate(flops=14_000_000_000, bytes_accessed=30_000_000, transcendentals=2_600_000),
        name="middle",
    )(hidden, mixture, cotangent, patch_cotangent, *matrices, *vectors)
    first, rest = result[:5], result[5:]
    if direct:
        return first + rest
    normed, up_back, activated, down_back, attention_back = rest
    return first + (
        indexed_bundle(
            (
                ((normed, up_back, None), (mixture, attention_back, 0)),
                ((activated, down_back, None), (mixture, attention_back, 1)),
            ),
            places,
            pages,
        ),
    )


def indexed_bundle(matrices, scalars, pages):
    levels = pages.bit_length() - 1
    place = jnp.arange(2 * pages, dtype=jnp.int32)
    bits = [(place >> (levels - k)) & 1 for k in range(levels + 1)]
    halves = []
    for order, group in enumerate(matrices):
        side, near = (bits[0], bits[1]) if order == 0 else (bits[1], bits[0])
        far = near
        for level in range(1, levels):
            far = far + (bits[level + 1] << level)
        index = (far ^ scalars[2]) * 2 + (side ^ scalars[3])
        blocks = []
        for operand, gradient, part in group:
            rows = in_blocks(outer_dot(operand, gradient).astype(jnp.bfloat16), pages)
            if part is not None:
                half = rows.shape[1] // 2
                rows = rows[:, part * half : (part + 1) * half]
            blocks.append(rows)
        halves.append(jnp.concatenate(blocks, axis=1)[index])
    first, second = halves
    mine = scalars[1] == 0
    return jnp.stack([jnp.where(mine, first, second), jnp.where(mine, second, first)])


def in_blocks(matrix, pages):
    rows, columns = matrix.shape[0] // pages, matrix.shape[1] // 2
    lanes = min(columns, 384)
    blocks = matrix.reshape(pages, rows, 2, columns // lanes, lanes)
    return blocks.transpose(0, 2, 3, 1, 4).reshape(pages * 2, rows * columns // lanes, lanes)


class Halving:
    def __init__(self, keep, source, landing, landings, partners, sibling, sems, chunks):
        self.keep, self.landing, self.landings = keep, landing, landings
        total = keep.shape[0]
        unit = total // chunks
        send_sem, recv_sem = sems
        self.arrivals, self.sends, self.needs = {}, {}, {}
        used = 0
        for chunk in range(chunks):
            lo = total - (chunk + 1) * unit
            copy = remote(
                source.at[lo : lo + unit], landing.at[lo : lo + unit], send_sem.at[used], recv_sem.at[used], *sibling
            )
            self.arrivals["core", chunk] = (copy, landing, lo, unit)
            used += 1
        for step, (into, partner) in enumerate(zip(landings, partners, strict=True)):
            size = total >> (step + 1)
            piece = min(unit, size)
            for chunk in range(size // piece):
                lo = size - (chunk + 1) * piece
                copy = remote(
                    keep.at[size + lo : size + lo + piece], into.at[lo : lo + piece], send_sem.at[used],
                    recv_sem.at[used], *partner,
                )
                self.arrivals[step, chunk] = (copy, into, lo, piece)
                self.sends[step, chunk] = copy
                self.needs[step, chunk] = {
                    (source_step, block)
                    for block in range(size + lo, size + lo + piece)
                    for source_step in ("core", *range(step))
                }
                used += 1
        self.done = set()

    def start(self):
        for key, (copy, *_) in self.arrivals.items():
            if key[0] == "core":
                copy.start()

    def take(self, *key):
        copy, into, lo, count = self.arrivals[key]
        copy.wait_recv()

        def add(block, carry):
            self.keep[block] = self.keep[block] + into[block]
            return carry

        lax.fori_loop(lo, lo + count, add, 0)
        for block in range(lo, lo + count):
            self.done.add((key[0], block))
        for name in list(self.sends):
            if self.needs[name] <= self.done:
                self.sends.pop(name).start()

    def finish(self):
        for copy, *_ in self.arrivals.values():
            copy.wait_send()


def backward_kernel(
    pages,
    staging, length_ref, query_ref, mixture_back_ref, columns_ref, rows_ref, query_rows_ref, tokens_ref, patches_ref, taps_ref,
    middle_sums_ref, bundle_any, weights_any, key_any, value_any, hidden_any, first_back_any, query_weight_any,
    key_weight_any, value_weight_any,
    tokens_back_ref, patches_back_ref, early_ref, late_ref, sums_ref, up_in_ref, down_in_ref, mixed_in_ref,
    keep, landing, landings, late, late_landing, late_landings, weights_buf, key_buf, value_buf, outgoing, from_sib,
    from_far, matrices, flipped, total_back, query_back, key_back, value_back, back, steps, mask_ref, hot_ref,
    query_hot_ref, band_ref, table_acc, band_acc, table_out, text_rim, patch_rim, sums, sums_in,
    up_in, down_out, down_in, mixed_out, mixed_in,
    load_sem, page_sem, early_send, early_recv, late_send, late_recv, sib_send, sib_recv, far_send, far_recv, rim_send,
    rim_recv, sum_send, sum_recv, swap_send, swap_recv,
):
    page_at, bits, seq, across, core = places_of(pages)
    levels = len(bits)
    count, span, width = tokens_ref.shape
    patch_span = patches_ref.shape[1]
    row_count = span + patch_span
    total_rows = count * row_count
    key_pad = key_buf.shape[1]
    text_slots = 4 * span
    groups = weights_buf.shape[1]
    members = weights_buf.shape[2] // row_count
    heads = groups * members
    group_width = members * HEAD_LANES
    f32, bf16 = jnp.float32, jnp.bfloat16

    sibling = (page_at, sibling_of(seq))
    opposite = (page_at, across_of(seq))
    diagonal = (page_at, sibling_of(across_of(seq)))
    flips = [(1 - 2 * bit) * 2**level for level, bit in enumerate(bits)]
    on_page = [(page_at + flip, seq) for flip in flips]
    either = lambda first, second: first + core * (second - first)
    early_partners = [
        (page_at + either(flips[1], flips[0]), seq),
        (page_at + either(flips[0], flips[1]), seq),
        opposite,
    ] + on_page[2:]
    barrier = pltpu.get_barrier_semaphore()
    everyone = [sibling, opposite, diagonal] + on_page
    for peer in everyone:
        pl.semaphore_signal(barrier, inc=1, device_id=peer, device_id_type=MESH)

    keep_load = pltpu.make_async_copy(bundle_any.at[0], keep, load_sem.at[0])
    later_loads = [
        pltpu.make_async_copy(source, target, load_sem.at[1 + index])
        for index, (source, target) in enumerate(
            (
                (query_weight_any, matrices.at[0]), (key_weight_any, matrices.at[1]),
                (value_weight_any, matrices.at[2]), (hidden_any, key_back), (first_back_any, total_back),
            )
        )
    ]

    def page_loads(page):
        slot = page % 2
        return [
            pltpu.make_async_copy(source.at[page], target.at[slot], page_sem.at[index, slot])
            for index, (source, target) in enumerate(
                ((weights_any, weights_buf), (key_any, key_buf), (value_any, value_buf))
            )
        ]

    for copy in page_loads(0):
        copy.start()
    keep_load.start()
    pl.semaphore_wait(barrier, len(everyone))
    early = Halving(
        keep, bundle_any.at[1], landing, landings, early_partners, sibling, (early_send, early_recv), 8
    )
    late_sum = Halving(
        late.at[0], late.at[1], late_landing, late_landings, early_partners, sibling, (late_send, late_recv), 4
    )
    early.start()
    for copy in staging:
        copy.wait()

    lane128 = lax.broadcasted_iota(jnp.int32, (row_count, 128), 1)
    place = query_places(seq, (row_count, 128), span, patch_span, text_slots)
    aim = place + lane128 - 32
    blocks_on = (aim >> 4) - (place >> 4)
    near = (lane128 < 64) & (aim >= 0) & (aim < text_slots + patch_span * 4) & (blocks_on >= -1) & (blocks_on <= 1)
    band_ref[...] = jnp.where(near, aim, -1)
    table_acc[...] = jnp.zeros_like(table_acc)
    band_acc[...] = jnp.zeros_like(band_acc)
    lane_of_row = lax.broadcasted_iota(jnp.int32, (48, row_count), 1)
    place_of_row = jnp.where(
        lane_of_row < span, seq * span + lane_of_row, text_slots + seq * patch_span + lane_of_row - span
    )
    query_hot_ref[144:192, :] = (
        ((place_of_row >> 4) == lax.broadcasted_iota(jnp.int32, (48, row_count), 0)).astype(f32).astype(bf16)
    )
    def start_page(page):
        slot = page % 2
        for copy in page_loads(page):
            copy.wait()

        @pl.when(page < count - 1)
        def _():
            for copy in page_loads(page + 1):
                copy.start()

        bin_at = lax.broadcasted_iota(jnp.int32, (128, key_pad), 0) - 1
        key_block = lax.broadcasted_iota(jnp.int32, (128, key_pad), 1) >> 4
        half_bin = lax.broadcasted_iota(jnp.int32, (72, row_count), 0)
        for side in range(2):
            key_row = rows_ref[page, side : side + 1, :]
            query_column = columns_ref[page, :, 128 * side : 128 * side + 1]
            mask_ref[:, side * key_pad : (side + 1) * key_pad] = (
                ((key_row & 15) < (query_column & 15)).astype(f32).astype(bf16)
            )
            key_bin = key_row >> 4
            plain = jnp.where(bin_at < 64, (key_bin == bin_at).astype(f32), 0.0)
            lower = jnp.where(bin_at < 64, (key_bin - 1 == bin_at).astype(f32), 0.0)
            mine = slice(128 * side, 128 * (side + 1))
            other = slice(128 * (1 - side), 128 * (2 - side))
            change = lower - plain
            if side == 0:
                plain = jnp.where(bin_at - 71 == key_block, 1.0, plain)
            hot_ref[mine, 0:key_pad] = plain.astype(bf16)
            hot_ref[mine, (1 + side) * key_pad : (2 + side) * key_pad] = change.astype(bf16)
            hot_ref[other, (1 + side) * key_pad : (2 + side) * key_pad] = jnp.zeros((128, key_pad), bf16)
            query_bin = query_rows_ref[page, side : side + 1, 0:row_count] >> 4
            query_hot_ref[72 * side : 72 * (side + 1), :] = (71 - query_bin == half_bin).astype(f32).astype(bf16)

    def attend(page, group):
        slot = page % 2
        at = pl.ds(pl.multiple_of(group * group_width, group_width), group_width)
        own_rows = pl.ds(pl.multiple_of(page * row_count, 16), row_count)
        both_query = split_heads(query_ref[own_rows, at])
        both_back = split_heads(mixture_back_ref[own_rows, at])
        back[...] = dot_nt(both_back, value_buf[slot, :, at])
        for start in range(0, members * row_count, CHUNK):
            there = slice(start, start + CHUNK)
            here = slice(start % row_count, start % row_count + CHUNK)
            parts, total = [], None
            for block_at in range(0, key_pad, 128):
                lane = slice(block_at, block_at + 128)
                part = weights_buf[slot, group, there, lane].astype(f32)
                product = part * back[there, lane]
                total = product if total is None else total + product
                parts.append(part)
            mean = jnp.sum(total, axis=1, keepdims=True)
            for index, part in enumerate(parts):
                lane = slice(128 * index, 128 * (index + 1))
                step = (part * (back[there, lane] - mean)).astype(bf16)
                steps[there, lane] = step
                steps[there, key_pad + 128 * index : key_pad + 128 * (index + 1)] = step * mask_ref[here, lane]
                steps[there, 2 * key_pad + 128 * index : 2 * key_pad + 128 * (index + 1)] = (
                    step * mask_ref[here, key_pad + 128 * index : key_pad + 128 * (index + 1)]
                )
        query_back[own_rows, at] = (
            merge_heads(dot_nn(steps[:, 0:key_pad], key_buf[slot, :, at])) * 0.125
        ).astype(bf16)
        for kind, value in enumerate(
            (dot_tn(steps[:, 0:key_pad], both_query), dot_tn(weights_buf[slot, group], both_back))
        ):
            value = value.astype(bf16)
            for where in range(4):
                place_at = apart(where % 2, core) * 2 + apart(where // 2, across)
                outgoing[page, place_at, kind, 0:span, at] = value[where * span : (where + 1) * span]
                outgoing[page, place_at, kind, span:row_count, at] = value[
                    text_slots + where * patch_span : text_slots + (where + 1) * patch_span
                ]
        bins = dot_nt(steps[...], hot_ref[...]).astype(bf16)
        for side in range(members):
            head = members * group + side
            base = side * row_count
            both = dot_nn(query_hot_ref[...], bins[base : base + row_count])
            table_acc[head, 0:72, :] += both[0:72, 0:128]
            table_acc[head, 72:144, :] += both[72:144, 128:256]
            table_acc[head, 144:192, :] += both[144:192, 0:128]
            for first, rows_here, block, into in bands():
                source = steps[
                    base + first : base + first + rows_here, pl.ds(pl.multiple_of(block * 128, 128), 128)
                ]
                band_acc[head, into : into + rows_here, :] += source.astype(f32)

    def bands():
        before = seq - (seq + 3) // 4
        return (
            (0, span, seq, 0),
            (0, 32, before, span),
            (span - 32, 32, seq + 1, span + 32),
            (span, patch_span, 3, span + 64),
            (span, patch_span, 4, span + 64 + patch_span),
        )

    def sib_copy(page, part):
        at = slice(part * width // 2, (part + 1) * width // 2)
        return remote(
            outgoing.at[page, 2:4, :, :, at], from_sib.at[page, :, :, :, at], sib_send.at[page, part],
            sib_recv.at[page, part], *sibling,
        )

    def far_copy(page, part):
        at = slice(part * width // 2, (part + 1) * width // 2)
        return remote(
            outgoing.at[page, 1, :, :, at], from_far.at[page, :, :, at], far_send.at[page, part],
            far_recv.at[page, part], *opposite,
        )

    def pass_on(page, part):
        sib_copy(page, part).wait_recv()
        at = slice(part * width // 2, (part + 1) * width // 2)
        for kind in range(2):
            outgoing[page, 1, kind, :, at] = outgoing[page, 1, kind, :, at] + from_sib[page, 1, kind, :, at]
        far_copy(page, part).start()

    events = {
        1: [("core", 0), ("core", 1)], 2: [("core", 2), ("core", 3)], 4: [("core", 4), ("core", 5)],
        6: [("core", 6), ("core", 7)], 8: [(0, 0)], 12: [(0, 1)],
    }
    last_turn = count * groups - 1

    def step_body(turn, carry):
        page, group = turn // groups, turn % groups

        @pl.when(group == 0)
        def _():
            start_page(page)

        for at_turn, names in events.items():

            @pl.when(turn == min(at_turn, last_turn))
            def _(names=names, at_turn=at_turn):
                if at_turn == min(events):
                    keep_load.wait()
                for name in names:
                    early.take(*name)

        @pl.when(turn == min(3, last_turn))
        def _():
            for copy in later_loads:
                copy.start()

        @pl.when((group == 2) & (page > 0))
        def _():
            pass_on(page - 1, 1)

        @pl.when(group == groups - 1)
        def _():
            pass_on(page, 0)

        attend(page, group)

        for part in range(2):

            @pl.when(group == (part + 1) * groups // 2 - 1)
            def _(part=part):
                sib_copy(page, part).start()

        return carry

    lax.fori_loop(0, count * groups, step_body, 0)

    for copy in later_loads:
        copy.wait()
    flipped[...] = key_back[...].T
    lanes = 384
    rows = width // pages
    half = rows // 2

    def weight_columns(index, gradient):
        def tile(four, carry):
            tile_rows = pl.ds(pl.multiple_of(four * 4 * rows, 128), 4 * rows)
            result = dot_nn(flipped[tile_rows, :], gradient[...]).astype(bf16)
            for inner in range(4):
                page = four * 4 + inner
                first = inner * rows
                for column in range(2):
                    far = [apart((page // 2**level) % 2, bit) for level, bit in enumerate(bits)]
                    slots = [slot_of_bits(order) for order in early_orders(far, apart(column, across))]
                    at = slice(column * lanes, (column + 1) * lanes)
                    if index < 2:
                        late[core if index == 0 else 1 - core, slots[index], 0:rows, :] = result[
                            first : first + rows, at
                        ]
                    else:
                        late[core, slots[0], rows : rows + half, :] = result[first : first + half, at]
                        late[1 - core, slots[1], rows : rows + half, :] = result[first + half : first + rows, at]
            return carry

        lax.fori_loop(0, pages // 4, tile, 0)

    def project_back(gradient, matrix):
        total_back[...] = total_back[...] + dot_nt(gradient[...], matrices[matrix])

    pass_on(count - 1, 1)
    weight_columns(0, query_back)
    project_back(query_back, 0)
    sums[0, 0:16, :] = middle_sums_ref[...]
    sums[0, 10:11, :] = column_sum(query_back[...].astype(f32))

    def head_tables(head, carry):
        for plane in range(2):
            table = table_acc[head, 72 * plane : 72 * (plane + 1), :]
            lane = lax.broadcasted_iota(jnp.int32, table.shape, 1)
            table = jnp.where(lane < 72, table, 0.0)
            table = jnp.concatenate([table, jnp.zeros_like(table)], axis=1)
            sheared = pltpu.roll(table, 0, 1, stride=1, stride_axis=0)
            table_out[head, 0:1, 256 * plane : 256 * (plane + 1)] = column_sum(sheared)
        table = table_acc[head, 144:192, :]
        lane = lax.broadcasted_iota(jnp.int32, table.shape, 1)
        apart_by = lane - 72 - lax.broadcasted_iota(jnp.int32, table.shape, 0)
        in_line = (lane >= 72) & (lane < 72 + 36)
        low_tail = jnp.sum(column_sum(jnp.where(in_line & (apart_by <= -2), table, 0.0)), axis=1, keepdims=True)
        high_tail = jnp.sum(column_sum(jnp.where(in_line & (apart_by >= 2), table, 0.0)), axis=1, keepdims=True)
        band = jnp.zeros((1, 128), f32)
        for first, rows_here, block, into in bands():
            aims = band_ref[first : first + rows_here, :]
            taken = jnp.take_along_axis(band_acc[head, into : into + rows_here, :], aims & 127, axis=1)
            right = (aims >> 7) == block
            if into == span:
                right = right & (seq > 0)
            band = band + column_sum(jnp.where(right, taken, 0.0))
        lane_one = lax.broadcasted_iota(jnp.int32, (1, 128), 1)
        table_out[head, 0:1, 512:640] = (
            band + jnp.where(lane_one == 0, low_tail, 0.0) + jnp.where(lane_one == 63, high_tail, 0.0)
        )
        table_out[head, 0:1, 640:768] = jnp.zeros((1, 128), f32)
        return carry

    lax.fori_loop(0, heads, head_tables, 0)
    for head in range(heads):
        at_row = 8 + head
        sums[1, at_row : at_row + 1, :] = table_out[head, 0:1, :]

    for name in ((0, 2), (1, 0)):
        early.take(*name)
    for page in range(count):
        for part in range(2):
            far_copy(page, part).wait_recv()
        own_rows = slice(page * row_count, (page + 1) * row_count)
        for kind, target in enumerate((key_back, value_back)):
            target[own_rows, :] = (
                (outgoing[page, 0, kind].astype(f32) + from_sib[page, 0, kind].astype(f32))
                + from_far[page, kind].astype(f32)
            ).astype(bf16)
    weight_columns(1, key_back)
    weight_columns(2, value_back)
    late_sum.start()
    project_back(key_back, 1)
    project_back(value_back, 2)
    sums[0, 11:12, :] = column_sum(value_back[...].astype(f32))
    for page in range(count):
        first = page * row_count
        text_rim[page, 16 : 16 + span, :] = total_back[first : first + span, :].astype(bf16)
        patch_rim[page, 16 : 16 + patch_span, :] = total_back[first + span : first + row_count, :].astype(bf16)
    after, before = (page_at, (seq + 1) % 4), (page_at, (seq + 3) % 4)
    rim_copies = [
        remote(
            source.at[:, start : start + 16], source.at[:, stop : stop + 16], rim_send.at[index], rim_recv.at[index],
            *peer,
        )
        for index, (source, start, stop, peer) in enumerate(
            (
                (text_rim, span, 0, after), (text_rim, 16, 16 + span, before),
                (patch_rim, 16, 0, after), (patch_rim, 16, 32, before),
            )
        )
    ]
    for copy in rim_copies:
        copy.start()
    for chunk in range(4):
        late_sum.take("core", chunk)
    for name in ((0, 3), (1, 1)):
        early.take(*name)
    for copy in rim_copies:
        copy.wait()
    sums[1, 0:8, :] = jnp.zeros((8, width), f32)
    sums[1, 20:24, :] = jnp.zeros((4, width), f32)
    sums[0, 16:24, :] = jnp.zeros((8, width), f32)

    def position_tile(tile, carry):
        at = pl.ds(pl.multiple_of(tile * 256, 256), 256)
        text_taps = [jnp.zeros((1, 256), f32) for _ in range(7)]
        patch_taps = [jnp.zeros((1, 256), f32) for _ in range(9)]
        for page in range(count):
            first = page * row_count
            window = text_rim[page, :, at].astype(f32)
            window_row = lax.broadcasted_iota(jnp.int32, (span + 32, 1), 0)
            inside = ((window_row >= 16) | (seq > 0)) & ((window_row < 16 + span) | (seq < 3))
            window = jnp.where(inside, window, 0.0)
            live = seq * span + lax.broadcasted_iota(jnp.int32, (span, 1), 0) < length_ref[page]
            masked = jnp.where(live, tokens_ref[page, :, at].astype(f32), 0.0)
            total = jnp.zeros((span, 256), f32)
            for distance in range(-3, 4):
                shifted = window[16 - distance : 16 - distance + span]
                if distance == 0:
                    weight = taps_ref[1:2, at] + taps_ref[4:5, at] + taps_ref[7:8, at]
                else:
                    tap = 3 * (abs(distance) - 1) + (2 if distance > 0 else 0)
                    weight = taps_ref[tap : tap + 1, at]
                total = total + shifted * weight
                text_taps[distance + 3] = text_taps[distance + 3] + column_sum(shifted * masked)
            tokens_back_ref[page, :, at] = total_back[first : first + span, at] + jnp.where(live, total, 0.0)
            window = patch_rim[page, :, at].astype(f32)
            window_row = lax.broadcasted_iota(jnp.int32, (48, 1), 0)
            inside = ((window_row >= 16) | (seq > 0)) & ((window_row < 32) | (seq < 3))
            window = jnp.where(inside, window, 0.0)
            cell = seq * patch_span + lax.broadcasted_iota(jnp.int32, (patch_span, 1), 0)
            live = ((cell >> 3) < GRID_SIDE - 1) & ((cell & 7) < GRID_SIDE - 1)
            masked = jnp.where(live, patches_ref[page, :, at].astype(f32), 0.0)
            total = jnp.zeros((patch_span, 256), f32)
            for tap in range(9):
                distance = GRID_SIDE * (tap // 3 - 1) + tap % 3 - 1
                shifted = window[16 - distance : 32 - distance]
                total = total + shifted * taps_ref[9 + tap : 10 + tap, at]
                patch_taps[tap] = patch_taps[tap] + column_sum(shifted * masked)
            patches_back_ref[page, :, at] = total_back[first + span : first + row_count, at] + jnp.where(
                live, total, 0.0
            )
        for index, value in enumerate(text_taps):
            sums[0, 16 + index : 17 + index, at] = value
        for index, value in enumerate(patch_taps):
            if index == 0:
                sums[0, 23:24, at] = value
            else:
                sums[1, index - 1 : index, at] = value
        return carry

    early.take(2, 0)
    lax.fori_loop(0, width // 256, position_tile, 0)

    sum_partners = [opposite] + on_page
    sum_copies = [remote(sums.at[1 - core], sums_in.at[0], sum_send.at[0], sum_recv.at[0], *sibling)] + [
        remote(sums.at[core], sums_in.at[1 + index], sum_send.at[1 + index], sum_recv.at[1 + index], *partner)
        for index, partner in enumerate(sum_partners)
    ]
    last = remote(
        sums.at[core], sums_in.at[2 + levels], sum_send.at[2 + levels], sum_recv.at[2 + levels], *sibling
    )
    sum_copies[0].start()

    def sum_step(index):
        sum_copies[index].wait()
        sums[core] = sums[core] + sums_in[index]
        (sum_copies + [last])[index + 1].start()

    late_sum.take(0, 0)
    sum_step(0)
    late_sum.take(0, 1)
    sum_step(1)
    late_sum.take(1, 0)
    sum_step(2)
    for step in range(2, levels + 1):
        late_sum.take(step, 0)
        sum_step(step + 1)
    for step in range(3, levels + 1):
        early.take(step, 0)
    last.wait()
    sums_ref[core] = sums[core]
    sums_ref[1 - core] = sums_in[2 + levels]
    wide_rows = 4 * rows
    block = keep[0].astype(f32)
    low, high = block[:, 0 : lanes // 2], pltpu.roll(block, lanes // 2, 1)[:, 0 : lanes // 2]
    down_out[...] = low[0:wide_rows].astype(bf16)
    mixed_out[0:half, :] = jnp.where(core == 0, high[wide_rows:], low[wide_rows:]).astype(bf16)
    block = late[0, 0].astype(f32)
    low, high = block[:, 0 : lanes // 2], pltpu.roll(block, lanes // 2, 1)[:, 0 : lanes // 2]
    mixed_out[half:, :] = jnp.where(core == 0, high, low).astype(bf16)
    swaps = [
        remote(source, target, swap_send.at[index], swap_recv.at[index], *sibling)
        for index, (source, target) in enumerate(
            ((keep.at[0, 2 * rows : 4 * rows], up_in), (down_out, down_in), (mixed_out, mixed_in))
        )
    ]
    for copy in swaps:
        copy.start()
    early_ref[...] = keep[0]
    late_ref[...] = late[0, 0]
    for copy in swaps:
        copy.wait()
    up_in_ref[...] = up_in[...]
    down_in_ref[...] = down_in[...]
    mixed_in_ref[...] = mixed_in[...]
    early.finish()
    late_sum.finish()
    for page in range(count):
        for part in range(2):
            sib_copy(page, part).wait_send()
            far_copy(page, part).wait_send()


def backward(pages, lengths, local_values, far_values, tokens, patches):
    count, span, width = tokens.shape
    patch_span = patches.shape[1]
    row_count = span + patch_span
    total_rows = count * row_count
    bundle, weights, keys = far_values[0], far_values[1], far_values[2]
    groups, grouped_rows, key_pad = weights.shape[1:]
    heads = groups * grouped_rows // row_count
    blocks, early_rows, lanes = bundle.shape[1:]
    late_rows = 3 * width // (2 * pages)
    levels = pages.bit_length() - 1
    bf16, f32, i32 = jnp.bfloat16, jnp.float32, jnp.int32
    dma = pltpu.SemaphoreType.DMA

    def landings(rows):
        return [VMEM((blocks >> (step + 1), rows, lanes), bf16) for step in range(levels + 1)]

    early_count = 8 + 4 + 2 + (levels - 1)
    late_count = 4 + 2 + levels
    return pl.pallas_call(
        staged(functools.partial(backward_kernel, pages), 1, len(local_values)),
        out_shape=(
            jax.ShapeDtypeStruct(tokens.shape, f32),
            jax.ShapeDtypeStruct(patches.shape, f32),
            jax.ShapeDtypeStruct((early_rows, lanes), bf16),
            jax.ShapeDtypeStruct((late_rows, lanes), bf16),
            jax.ShapeDtypeStruct((2, 24, width), f32),
            jax.ShapeDtypeStruct((early_rows // 9 * 4, lanes), bf16),
            jax.ShapeDtypeStruct((early_rows // 9 * 8, lanes // 2), bf16),
            jax.ShapeDtypeStruct((early_rows // 9 + late_rows, lanes // 2), bf16),
        ),
        in_specs=[pl.BlockSpec(memory_space=pltpu.SMEM)]
        + anywhere(len(local_values) + len(far_values)),
        out_specs=tuple(in_vmem(8)),
        scratch_shapes=[
            VMEM((blocks, early_rows, lanes), bf16),
            VMEM((blocks, early_rows, lanes), bf16),
            landings(early_rows),
            VMEM((2, blocks, late_rows, lanes), bf16),
            VMEM((blocks, late_rows, lanes), bf16),
            landings(late_rows),
            VMEM((2, groups, grouped_rows, key_pad), bf16),
            VMEM((2, key_pad, width), bf16),
            VMEM((2, key_pad, width), bf16),
            VMEM((count, 4, 2, row_count, width), bf16),
            VMEM((count, 2, 2, row_count, width), bf16),
            VMEM((count, 2, row_count, width), bf16),
            VMEM((3, width, width), bf16),
            VMEM((width, total_rows), bf16),
            VMEM((total_rows, width), f32),
            VMEM((total_rows, width), bf16),
            VMEM((total_rows, width), bf16),
            VMEM((total_rows, width), bf16),
            VMEM((grouped_rows, key_pad), f32),
            VMEM((grouped_rows, 3 * key_pad), bf16),
            VMEM((row_count, 2 * key_pad), bf16),
            VMEM((256, 3 * key_pad), bf16),
            VMEM((192, row_count), bf16),
            VMEM((row_count, 128), i32),
            VMEM((heads, 192, 128), f32),
            VMEM((heads, span + 64 + 2 * patch_span, 128), f32),
            VMEM((heads, 8, width), f32),
            VMEM((count, span + 32, width), bf16),
            VMEM((count, patch_span + 32, width), bf16),
            VMEM((2, 24, width), f32),
            VMEM((3 + levels, 24, width), f32),
            VMEM((early_rows // 9 * 4, lanes), bf16),
            VMEM((early_rows // 9 * 8, lanes // 2), bf16),
            VMEM((early_rows // 9 * 8, lanes // 2), bf16),
            VMEM((early_rows // 9 + late_rows, lanes // 2), bf16),
            VMEM((early_rows // 9 + late_rows, lanes // 2), bf16),
            dma((6,)), dma((3, 2)),
            dma((early_count,)), dma((early_count,)), dma((late_count,)), dma((late_count,)),
            dma((count, 2)), dma((count, 2)), dma((count, 2)), dma((count, 2)),
            dma((4,)), dma((4,)), dma((3 + levels,)), dma((3 + levels,)), dma((3,)), dma((3,)),
        ]
        + stage_for(local_values),
        compiler_params=pltpu.CompilerParams(
            collective_id=1, has_side_effects=True, vmem_limit_bytes=KERNEL_VMEM
        ),
        cost_estimate=pl.CostEstimate(flops=12_000_000_000, bytes_accessed=40_000_000, transcendentals=0),
        name="backward",
    )(lengths, *local_values, *far_values)


def clip_lanes(sums, centre, bins):
    first, last = centre + 1 - bins // 2, centre - 1 + bins // 2
    lane = lax.broadcasted_iota(jnp.int32, sums.shape, 1)
    below = jnp.sum(jnp.where(lane < first, sums, 0.0), axis=1, keepdims=True)
    above = jnp.sum(jnp.where(lane >= last, sums, 0.0), axis=1, keepdims=True)
    moved = pltpu.roll(sums, sums.shape[1] - (first - 1), 1)
    moved = jnp.where(lane == 0, below, jnp.where(lane == bins - 1, above, moved))
    return moved[:, :bins]


def finish_kernel(staging, early_ref, late_ref, sums_ref, up_in_ref, down_in_ref, mixed_in_ref, *rest):
    carried, rest = rest[:2], rest[2:]
    *rest, carry_sem = rest
    rest, targets = rest[:-2], rest[-2:]
    (
        query_ref, key_ref, value_ref, out_ref, up_ref, down_ref, taps_ref, patch_taps_ref, line_ref, across_ref,
        upward_ref, *vector_refs,
    ) = rest
    carries = [
        pltpu.make_async_copy(source, target, carry_sem.at[index])
        for index, (source, target) in enumerate(zip(carried, targets, strict=True))
    ]
    for copy in carries:
        copy.start()
    f32 = jnp.float32
    rows, columns = query_ref.shape
    half = rows // 2
    wide_rows = 4 * rows
    first = position()[1] == 0
    for copy in staging:
        copy.wait()
    heads = line_ref.shape[0]
    block = early_ref[...].astype(f32)
    low, high = block[:, 0:columns], pltpu.roll(block, columns, 1)[:, 0:columns]
    up = jnp.where(first, block[0 : 2 * rows], up_in_ref[...].astype(f32))
    up_ref[:, 0 : 2 * columns] = up[0:rows]
    up_ref[:, 2 * columns : 4 * columns] = up[rows : 2 * rows]
    down_ref[...] = jnp.where(first, down_in_ref[...].astype(f32), high[0:wide_rows]).T
    kept = jnp.where(first, low[wide_rows:], high[wide_rows:])
    got = mixed_in_ref[0:half, :].astype(f32)
    out_ref[0:half, :] = jnp.where(first, kept, got)
    out_ref[half:rows, :] = jnp.where(first, got, kept)
    block = late_ref[...].astype(f32)
    low, high = block[:, 0:columns], pltpu.roll(block, columns, 1)[:, 0:columns]
    kept = jnp.where(first, low, high)
    got = mixed_in_ref[half:, :].astype(f32)
    query_ref[...] = jnp.where(first, kept[0:rows], got[0:rows])
    key_ref[...] = jnp.where(first, got[0:rows], kept[0:rows])
    value_ref[0:half, :] = jnp.where(first, kept[rows:], got[rows:])
    value_ref[half:rows, :] = jnp.where(first, got[rows:], kept[rows:])
    front, back = sums_ref[0], sums_ref[1]
    width = front.shape[1]
    text = [front[16 + index : 17 + index] for index in range(7)]
    order = [text[2], text[3], text[4], text[1], text[3], text[5], text[0], text[3], text[6]]
    taps_ref[...] = jnp.concatenate(order, axis=0)
    patch_taps_ref[...] = jnp.concatenate([front[23:24], back[0:8]], axis=0)
    across_ref[...] = clip_lanes(back[8:24, 0:256], 72, across_ref.shape[1])[0:heads]
    upward_ref[...] = clip_lanes(back[8:24, 256:512], 72, upward_ref.shape[1])[0:heads]
    line_ref[...] = clip_lanes(back[8:24, 512:640], 32, line_ref.shape[1])[0:heads]
    for source, target in zip((10, 11, 0, UP_BIAS, 1, 2, 3, 4, 5), vector_refs, strict=True):
        for part in range(target.shape[0] // width):
            target[pl.ds(part * width, width)] = front[source + part, :]
    for copy in carries:
        copy.wait()


def finish(values, carried, width, wide, heads, line_bins, plane_bins):
    rows, columns = values[1].shape[0] * 2 // 3, values[1].shape[1] // 2
    f32 = jnp.float32
    square = jax.ShapeDtypeStruct((rows, columns), f32)
    taps = jax.ShapeDtypeStruct((9, width), f32)
    plane = jax.ShapeDtypeStruct((heads, plane_bins), f32)
    return pl.pallas_call(
        staged(finish_kernel, 0, len(values)),
        out_shape=(
            square, square, square, square,
            jax.ShapeDtypeStruct((rows, 4 * columns), f32),
            jax.ShapeDtypeStruct((columns, 4 * rows), f32),
            taps, taps,
            jax.ShapeDtypeStruct((heads, line_bins), f32), plane, plane,
            *(jax.ShapeDtypeStruct((size,), f32) for size in (width,) * 3 + (wide,) + (width,) * 5),
            *(jax.ShapeDtypeStruct(value.shape, f32) for value in carried),
        ),
        in_specs=anywhere(len(values) + len(carried)),
        out_specs=tuple(in_vmem(22)),
        scratch_shapes=[pltpu.SemaphoreType.DMA((2,))] + stage_for(values),
        compiler_params=pltpu.CompilerParams(vmem_limit_bytes=KERNEL_VMEM),
        name="finish",
    )(*values, *carried)


def exchange(value, pages, step):
    moves = []
    for page in range(pages):
        for seq in range(4):
            on_page, on_seq = page, seq
            if (seq % 2 == step) if step < 2 else False:
                on_seq = seq ^ 2
            else:
                on_page = page ^ (1 if step < 2 else 1 << (step - 1))
            moves.append((page * 4 + seq, on_page * 4 + on_seq))
    return lax.ppermute(value, ("page", "seq"), moves)


def added(kept, got):
    return (kept.astype(jnp.float32) + got.astype(jnp.float32)).astype(jnp.bfloat16)


def bundle_sum(state, pages):
    for step in range(pages.bit_length()):
        half = state.shape[0] // 2
        state = added(state[:half], exchange(state[half:], pages, step))
    return state[0]


def bundle_parts(state, wide_rows, core):
    lanes = state.shape[1] // 2
    first = core == 0
    tail = state[wide_rows:]
    if wide_rows > 2 * tail.shape[0]:
        group = state[:wide_rows].reshape(4, wide_rows // 4, 2 * lanes)
        low = group[:2].transpose(1, 0, 2).reshape(-1, lanes)
        high = group[2:].transpose(1, 0, 2).reshape(-1, lanes)
    else:
        low, high = state[:wide_rows, :lanes], state[:wide_rows, lanes:]
    left, right = state[:wide_rows, :lanes], state[:wide_rows, lanes:]
    sent = jnp.concatenate(
        [jnp.where(first, high, left), jnp.where(first, tail[:, lanes:], tail[:, :lanes])], axis=0
    )
    got = swap(sent, "seq", 1)
    kept_tail = jnp.where(first, tail[:, :lanes], tail[:, lanes:])
    one = jnp.where(first, low, got[:wide_rows])
    two = jnp.where(first, got[:wide_rows], right)
    three = jnp.concatenate(
        [jnp.where(first, kept_tail, got[wide_rows:]), jnp.where(first, got[wide_rows:], kept_tail)], axis=0
    )
    return [value.astype(jnp.float32) for value in (one, two, three)]


def clipped(sums, centre, bins):
    first, last = centre + 1 - bins // 2, centre - 1 + bins // 2
    return jnp.concatenate(
        [
            jnp.sum(sums[..., :first], axis=-1, keepdims=True),
            sums[..., first:last],
            jnp.sum(sums[..., last:], axis=-1, keepdims=True),
        ],
        axis=-1,
    )


def grid_live(cells):
    return (cells // GRID_SIDE < GRID_SIDE - 1) & (cells % GRID_SIDE < GRID_SIDE - 1)


def grid_boxes(cells):
    return jnp.stack(
        [
            patch_pitch * (cells % GRID_SIDE) + patch_centre,
            patch_pitch * (cells // GRID_SIDE) + patch_centre,
        ]
    )


def shards(
    tokens,
    patches,
    page_length,
    box_position,
    query_weight,
    key_weight,
    value_weight,
    out_weight,
    up_weight,
    down_weight,
    conv_weight,
    patch_conv_weight,
    query_bias,
    value_bias,
    out_bias,
    up_bias,
    down_bias,
    attention_gain,
    attention_shift,
    feedforward_gain,
    feedforward_shift,
    reading_bias_table,
    horizontal_bias_table,
    vertical_bias_table,
    cotangent,
    patch_cotangent,
):
    conv_taps = conv_weight.astype(jnp.float32)
    patch_taps = patch_conv_weight.astype(jnp.float32)
    query_offset = query_bias.astype(jnp.float32)
    value_offset = value_bias.astype(jnp.float32)
    out_offset = out_bias.astype(jnp.float32)
    up_offset = up_bias.astype(jnp.float32)
    down_offset = down_bias.astype(jnp.float32)
    first_gain = attention_gain.astype(jnp.float32)
    first_shift = attention_shift.astype(jnp.float32)
    second_gain = feedforward_gain.astype(jnp.float32)
    second_shift = feedforward_shift.astype(jnp.float32)
    page_count, span_size, model_width = tokens.shape
    patch_span = patches.shape[1]
    seq_count = lax.axis_size("seq")
    slot_size = span_size * seq_count
    patch_slots = patch_span * seq_count
    row_count = span_size + patch_span
    key_count = row_count * seq_count
    head_count = reading_bias_table.shape[0]
    head_size = model_width // head_count
    line_bins = reading_bias_table.shape[1]
    plane_bins = horizontal_bias_table.shape[1]
    score_scale = head_size ** (-0.5)
    seq_index = lax.axis_index("seq")
    text_places = seq_index * span_size + jnp.arange(span_size, dtype=jnp.int32)
    local_cells = seq_index * patch_span + jnp.arange(patch_span, dtype=jnp.int32)
    text_live = text_places[None, :] < page_length[:, None]
    patch_live = grid_live(local_cells)
    text_factor = text_live[:, :, None]
    patch_factor = patch_live[None, :, None]
    masked = tokens * text_factor.astype(jnp.bfloat16)
    rimmed = with_halo(masked, (("seq", 1),), 3)
    reach = GRID_SIDE + 1
    patch_masked = patches * patch_factor.astype(jnp.bfloat16)
    patch_rimmed = with_halo(patch_masked, (("seq", 1),), reach)
    pages = lax.axis_size("page")
    (
        hidden, hidden_low, queries, mixture_low, columns, key_rows, query_rows, taps, keys, values, weights,
    ) = forward(
        pages, page_length, tokens, patches, box_position.transpose(1, 0, 2), (conv_weight.T, patch_conv_weight.T),
        (horizontal_bias_table, vertical_bias_table, reading_bias_table), (query_bias, value_bias),
        (query_weight, key_weight, value_weight),
    )
    places = jnp.stack(
        [seq_index, seq_index % 2, lax.axis_index("page"), seq_index // 2]
    ).astype(jnp.int32)
    def flat(value):
        return value.reshape(-1, value.shape[-1])

    output, patch_output, delta_first, delta_mixture, middle_sums, feedforward_bundle = middle(
        places, hidden, mixture_low, cotangent, patch_cotangent,
        (out_weight, up_weight, down_weight),
        (
            out_bias, down_bias, attention_gain, attention_shift, feedforward_gain, feedforward_shift, up_bias,
        ),
        pages,
    )
    pair_rows = weights.reshape(page_count, head_count // 2, 2 * row_count, -1)
    if in_tiles(model_width, pages):
        tokens_back, patches_back, early_state, late_state, sums, up_in, down_in, mixed_in = backward(
            pages,
            page_length,
            (
                queries, delta_mixture, columns, key_rows, query_rows, tokens, patches, taps, middle_sums,
            ),
            (
                feedforward_bundle, pair_rows, keys, values, hidden_low, delta_first, query_weight, key_weight,
                value_weight,
            ),
            tokens,
            patches,
        )
        (
            query_part, key_part, value_part, out_part, up_part, down_part, text_part, patch_part, line_part,
            across_part, upward_part, *vector_parts, tokens_gradient, patches_gradient,
        ) = finish(
            (early_state, late_state, sums, up_in, down_in, mixed_in),
            (tokens_back, patches_back), model_width, up_weight.shape[1], head_count, line_bins,
            plane_bins,
        )
        return (
            output,
            patch_output,
            tokens_gradient,
            patches_gradient,
            query_part,
            key_part,
            value_part,
            out_part,
            up_part,
            down_part.T,
            text_part.T,
            patch_part.T,
            *vector_parts,
            line_part,
            across_part,
            upward_part,
        )
    delta_first = delta_first.reshape(page_count, row_count, model_width)
    delta_mixture = delta_mixture.reshape(page_count, row_count, model_width)
    early_state = added(feedforward_bundle[0], swap(feedforward_bundle[1], "seq", 1))
    delta_mixture, early_state = lax.optimization_barrier((delta_mixture, early_state))
    delta_query_pages, delta_key_pages, delta_value_pages = [], [], []
    delta_plane, delta_line = 0.0, 0.0
    for page in range(page_count):
        delta_page_queries, delta_blocks, plane_part, line_part = backward_page(
            places,
            columns[page][:, ::128],
            key_rows[page],
            query_rows[page][:, :row_count],
            queries[page * row_count : (page + 1) * row_count],
            keys[page],
            values[page],
            delta_mixture[page],
            pair_rows[page],
        )
        got = swap(delta_blocks[2:], "seq", 1)
        chip_sum = delta_blocks[:2].astype(jnp.float32) + got.astype(jnp.float32)
        got = swap(chip_sum[1].astype(jnp.bfloat16), "seq", 2)
        whole = (chip_sum[0] + got.astype(jnp.float32)).astype(jnp.bfloat16)
        delta_query_pages.append(delta_page_queries)
        delta_key_pages.append(whole[0])
        delta_value_pages.append(whole[1])
        delta_plane = delta_plane + plane_part
        delta_line = delta_line + line_part
    delta_queries = jnp.stack(delta_query_pages)
    delta_keys = jnp.stack(delta_key_pages)
    delta_values = jnp.stack(delta_value_pages)
    delta_plane = clipped(delta_plane, 72, plane_bins)
    delta_line = clipped(delta_line, 32, line_bins)
    delta_across, delta_upward = delta_plane[0], delta_plane[1]
    delta_query_offset = row_sum(delta_queries)
    delta_value_offset = row_sum(delta_values)
    delta_hidden = (
        delta_first
        + back_dot(delta_queries, query_weight)
        + back_dot(delta_keys, key_weight)
        + back_dot(delta_values, value_weight)
    )
    delta_position = delta_hidden[:, :span_size].astype(jnp.bfloat16)
    delta_rim = with_halo(delta_position, (("seq", 1),), 3)
    delta_masked = jnp.zeros((page_count, span_size, model_width), jnp.float32)
    tap_columns = []
    for dilation in (1, 2, 3):
        for offset in (-1, 0, 1):
            column = 3 * (dilation - 1) + offset + 1
            anchor = 3 + offset * dilation
            anchor_back = 3 - offset * dilation
            delta_masked = (
                delta_masked
                + delta_rim[:, anchor_back : anchor_back + span_size, :] * conv_taps[:, column]
            )
            tap_columns.append(
                jnp.einsum(
                    "ptd,ptd->d",
                    delta_position,
                    rimmed[:, anchor : anchor + span_size, :],
                    preferred_element_type=jnp.float32,
                )
            )
    delta_taps = jnp.stack(tap_columns, axis=1)
    tokens_gradient = delta_hidden[:, :span_size] + delta_masked * text_factor.astype(jnp.float32)
    delta_patch_position = delta_hidden[:, span_size:].astype(jnp.bfloat16)
    delta_patch_rim = with_halo(delta_patch_position, (("seq", 1),), reach)
    delta_patch_masked = jnp.zeros((page_count, patch_span, model_width), jnp.float32)
    patch_columns = []
    for vertical in (-1, 0, 1):
        for horizontal in (-1, 0, 1):
            column = 3 * (vertical + 1) + horizontal + 1
            anchor = reach + vertical * GRID_SIDE + horizontal
            anchor_back = reach - vertical * GRID_SIDE - horizontal
            delta_patch_masked = (
                delta_patch_masked
                + delta_patch_rim[:, anchor_back : anchor_back + patch_span, :]
                * patch_taps[:, column]
            )
            patch_columns.append(
                jnp.einsum(
                    "ptd,ptd->d",
                    delta_patch_position,
                    patch_rimmed[:, anchor : anchor + patch_span, :],
                    preferred_element_type=jnp.float32,
                )
            )
    delta_patch_taps = jnp.stack(patch_columns, axis=1)
    patches_gradient = delta_hidden[:, span_size:] + delta_patch_masked * patch_factor.astype(
        jnp.float32
    )
    operands = [flat(value) for value in (hidden_low, delta_queries, delta_keys, delta_values)]
    tail_bundle = indexed_bundle(
        (
            ((operands[0], operands[1], None), (operands[0], operands[3], 0)),
            ((operands[0], operands[2], None), (operands[0], operands[3], 1)),
        ),
        places,
        pages,
    )
    tail_state = added(tail_bundle[0], swap(tail_bundle[1], "seq", 1))
    query_part, key_part, value_part = bundle_parts(
        bundle_sum(tail_state, pages), model_width // pages, places[1]
    )
    up_part, down_part, out_part = bundle_parts(
        bundle_sum(early_state, pages), up_weight.shape[1] // pages, places[1]
    )
    up_part = up_part.reshape(model_width // pages, -1)
    matrix_parts = (query_part, key_part, value_part, out_part, up_part, down_part)
    vector_parts = total_sum(
        (
            delta_taps,
            delta_patch_taps,
            delta_query_offset,
            delta_value_offset,
            middle_sums[OUT_BIAS],
            middle_sums[UP_BIAS : UP_BIAS + 4].reshape(-1),
            middle_sums[DOWN_BIAS],
            middle_sums[FIRST_GAIN],
            middle_sums[FIRST_SHIFT],
            middle_sums[SECOND_GAIN],
            middle_sums[SECOND_SHIFT],
            delta_line,
            delta_across,
            delta_upward,
        )
    )
    return (
        output,
        patch_output,
        tokens_gradient,
        patches_gradient,
        matrix_parts[0],
        matrix_parts[1],
        matrix_parts[2],
        matrix_parts[3],
        matrix_parts[4],
        matrix_parts[5],
        vector_parts[0],
        vector_parts[1],
        vector_parts[2],
        vector_parts[3],
        vector_parts[4],
        vector_parts[5],
        vector_parts[6],
        vector_parts[7],
        vector_parts[8],
        vector_parts[9],
        vector_parts[10],
        vector_parts[11],
        vector_parts[12],
        vector_parts[13],
    )


def solution(mesh):
    in_specs = (
        P("page", "seq", None),
        P("page", "seq", None),
        P("page"),
        P(None, "page", None),
        P(),
        P(),
        P(),
        P(),
        P(),
        P(),
        P(),
        P(),
        P(),
        P(),
        P(),
        P(),
        P(),
        P(),
        P(),
        P(),
        P(),
        P(),
        P(),
        P(),
        P("page", "seq", None),
        P("page", "seq", None),
    )
    out_specs = (
        P("page", "seq", None),
        P("page", "seq", None),
        P("page", "seq", None),
        P("page", "seq", None),
        P("page", "seq"),
        P("page", "seq"),
        P("page", "seq"),
        P("page", "seq"),
        P("page", "seq"),
        P("page", "seq"),
        P(),
        P(),
        P(),
        P(),
        P(),
        P(),
        P(),
        P(),
        P(),
        P(),
        P(),
        P(),
        P(),
        P(),
    )
    return jax.shard_map(shards, mesh=mesh, in_specs=in_specs, out_specs=out_specs, check_vma=False)
```

```python
import functools

import jax
import jax.numpy as jnp
from jax import lax
from jax.experimental import pallas as pl
from jax.experimental.pallas import tpu as pltpu
from jax.sharding import PartitionSpec as P

GRID_SIDE = 8


epsilon = 1e-05
coordinate_step = 16
masked_score = -1000000000.0
patch_pitch = 146
patch_centre = 73


def with_halo(cells, sides, width):
    for axis, dim in sides:
        count = lax.axis_size(axis)
        ends = count - 1
        head = lax.slice_in_dim(cells, 0, width, axis=dim)
        tail = lax.slice_in_dim(cells, cells.shape[dim] - width, cells.shape[dim], axis=dim)
        cells = jnp.concatenate(
            [
                lax.ppermute(tail, axis, [(i, (i + 1) % count) for i in range(ends)]),
                cells,
                lax.ppermute(head, axis, [((i + 1) % count, i) for i in range(ends)]),
            ],
            axis=dim,
        )
    return cells


def layer_norm(values, gain_vector, shift_vector):
    row_mean = jnp.mean(values, axis=-1, keepdims=True)
    centred = values - row_mean
    variance = jnp.mean(centred * centred, axis=-1, keepdims=True)
    return centred * lax.rsqrt(variance + epsilon) * gain_vector + shift_vector


def gelu_exact(values):
    return jax.nn.gelu(values, approximate=False)


def flat_dot(operand, matrix):
    front = operand.shape[:-1]
    result = jnp.dot(
        operand.reshape(-1, operand.shape[-1]), matrix, preferred_element_type=jnp.float32
    )
    return result.reshape(front + (matrix.shape[-1],))


def back_dot(operand, matrix):
    front = operand.shape[:-1]
    result = lax.dot_general(
        operand.reshape(-1, operand.shape[-1]),
        matrix,
        (((1,), (1,)), ((), ())),
        preferred_element_type=jnp.float32,
    )
    return result.reshape(front + (matrix.shape[0],))


def outer_dot(operand, gradient):
    return lax.dot_general(
        operand.reshape(-1, operand.shape[-1]),
        gradient.reshape(-1, gradient.shape[-1]),
        (((0,), (0,)), ((), ())),
        preferred_element_type=jnp.float32,
    )


def row_sum(gradient):
    return jnp.sum(gradient.astype(jnp.float32).reshape(-1, gradient.shape[-1]), axis=0)


def swap(value, axis, bit):
    count = lax.axis_size(axis)
    return lax.ppermute(value, axis, [(i, i ^ bit) for i in range(count)])


def total_sum(vectors):
    flat = jnp.concatenate([vector.reshape(-1) for vector in vectors])
    flat = jnp.pad(flat, (0, -flat.size % 1024)).reshape(-1, 128)
    for bit in (1, 2):
        flat = flat + swap(flat, "seq", bit)
    bit = 1
    while bit < lax.axis_size("page"):
        flat = flat + swap(flat, "page", bit)
        bit *= 2
    flat = flat.reshape(-1)
    result, start = [], 0
    for vector in vectors:
        result.append(flat[start : start + vector.size].reshape(vector.shape))
        start += vector.size
    return result


def query_places(seq_index, shape, span, patch_span, text_slots):
    row = lax.broadcasted_iota(jnp.int32, shape, 0)
    return jnp.where(
        row < span, seq_index * span + row, text_slots + seq_index * patch_span + row - span
    )


FIXED = 2048.0


def lookup(table_row, lanes):
    return jnp.take_along_axis(jnp.broadcast_to(table_row, lanes.shape), lanes, axis=1)


HEAD_LANES = 64


def split_heads(group):
    lane = lax.broadcasted_iota(jnp.int32, group.shape, 1) // HEAD_LANES
    zero = jnp.zeros_like(group)
    return jnp.concatenate(
        [jnp.where(lane == head, group, zero) for head in range(group.shape[1] // HEAD_LANES)], axis=0
    )


def merge_heads(rows):
    heads = rows.shape[1] // HEAD_LANES
    count = rows.shape[0] // heads
    lane = lax.broadcasted_iota(jnp.int32, (count, rows.shape[1]), 1) // HEAD_LANES
    merged = rows[:count]
    for head in range(1, heads):
        merged = jnp.where(lane == head, rows[head * count : (head + 1) * count], merged)
    return merged


def dot_nt(left, right):
    return lax.dot_general(left, right, (((1,), (1,)), ((), ())), preferred_element_type=jnp.float32)


def dot_nn(left, right):
    return lax.dot_general(left, right, (((1,), (0,)), ((), ())), preferred_element_type=jnp.float32)


def dot_tn(left, right):
    return lax.dot_general(left, right, (((0,), (0,)), ((), ())), preferred_element_type=jnp.float32)


CHUNK = 48
FORWARD_CHUNK = 48


MESH = pl.DeviceIdType.MESH


def places_of(pages):
    page = lax.axis_index("page")
    seq = lax.axis_index("seq")
    bits = []
    rest = page
    for _ in range(pages.bit_length() - 1):
        bits.append(rest % 2)
        rest = rest // 2
    return page, bits, seq, seq // 2, seq % 2


def sibling_of(seq):
    return seq + 1 - 2 * (seq % 2)


def across_of(seq):
    return seq + 2 - 4 * (seq // 2)


def remote(source, target, send, receive, page, seq):
    return pltpu.make_async_remote_copy(
        src_ref=source, dst_ref=target, send_sem=send, recv_sem=receive, device_id=(page, seq), device_id_type=MESH
    )


def column_of(row):
    square = jnp.broadcast_to(row.astype(jnp.float32), (128, 128)).T
    return square[:, 0:1].astype(jnp.int32)


def forward_kernel(
    pages,
    staging, length_ref, box_ref, text_taps_ref, patch_taps_ref, across_table_ref, upward_table_ref, line_table_ref,
    query_bias_ref, value_bias_ref, tokens_any, patches_any, query_weight_any, key_weight_any, value_weight_any,
    hidden_ref, hidden_low_ref, query_ref, mixture_ref, columns_ref, rows_ref, query_rows_ref, taps_ref, key_any,
    value_any, weights_any,
    own, matrices, key_ref, value_ref, weights_ref, arrived, text, grid, low, scores, across_ref, upward_ref,
    live_ref, line_ref, packed_ref, table_ref, vector_ref,
    load_sem, store_sem, send_sem, recv_sem,
):
    page_at, _, seq, _, _ = places_of(pages)
    count, span, width = tokens_any.shape
    patch_span = patches_any.shape[1]
    row_count = span + patch_span
    key_pad = key_ref.shape[1]
    text_slots = 4 * span
    rim = 8
    loads = [
        pltpu.make_async_copy(source, target, load_sem.at[index])
        for index, (source, target) in enumerate(
            (
                (tokens_any, own.at[:, 0:span]), (patches_any, own.at[:, span:row_count]),
                (key_weight_any, matrices.at[1]), (value_weight_any, matrices.at[2]), (query_weight_any, matrices.at[0]),
            )
        )
    ]
    for copy in loads:
        copy.start()

    def stores(page):
        return [
            pltpu.make_async_copy(source.at[page], target.at[page], store_sem.at[index, page])
            for index, (source, target) in enumerate(
                ((key_ref, key_any), (value_ref, value_any), (weights_ref, weights_any))
            )
        ]

    groups = weights_ref.shape[1]
    members = weights_ref.shape[2] // row_count
    pairs = groups * members // 2
    peers = (sibling_of(seq), across_of(seq))
    barrier = pltpu.get_barrier_semaphore()
    for peer in peers:
        pl.semaphore_signal(barrier, inc=1, device_id=(page_at, peer), device_id_type=MESH)
    pl.semaphore_wait(barrier, 2)

    def first_copies(page, side):
        return (
            remote(
                tokens_any.at[page], arrived.at[side, page, 0:span], send_sem.at[2 * side, page],
                recv_sem.at[2 * side, page], page_at, peers[side],
            ),
            remote(
                patches_any.at[page], arrived.at[side, page, span:row_count], send_sem.at[2 * side + 1, page],
                recv_sem.at[2 * side + 1, page], page_at, peers[side],
            ),
        )

    def onward_copy(page):
        return remote(
            arrived.at[1, page], arrived.at[2, page], send_sem.at[4, page], recv_sem.at[4, page], page_at, peers[0]
        )

    for page in range(count):
        for side in range(2):
            for copy in first_copies(page, side):
                copy.start()

    for copy in staging:
        copy.wait()
    table_ref[...] = jnp.zeros_like(table_ref)
    start = 0
    for source in (across_table_ref, upward_table_ref, line_table_ref):
        heads, bins = source.shape
        table_ref[0:heads, start : start + bins] = source[...].astype(jnp.float32)
        start += bins
    steps = jnp.floor(table_ref[...] * FIXED + 0.5).astype(jnp.int32)
    vector_ref[0:1, :] = query_bias_ref[...].astype(jnp.float32).reshape(1, width)
    vector_ref[1:2, :] = value_bias_ref[...].astype(jnp.float32).reshape(1, width)
    taps_ref[...] = jnp.zeros_like(taps_ref)
    taps_ref[0:9, :] = text_taps_ref[...].astype(jnp.float32)
    taps_ref[9:18, :] = patch_taps_ref[...].astype(jnp.float32)
    for pair in range(pairs):
        words = (steps[2 * pair : 2 * pair + 1] + 8192) + steps[2 * pair + 1 : 2 * pair + 2] * 65536
        packed_ref[0, pair : pair + 1, :] = words[:, 0:128]
        packed_ref[1, pair : pair + 1, :] = words[:, 128:256]
    key = lax.broadcasted_iota(jnp.int32, (row_count, key_pad), 1)
    place = query_places(seq, (row_count, key_pad), span, patch_span, text_slots)
    across_ref[...] = jnp.clip(key - place, -16, 15) + 16

    def fill(pair, carry):
        row = packed_ref[1, pl.ds(pair, 1), :]
        for at in range(0, key_pad, 128):
            line_ref[pair, :, at : at + 128] = lookup(row, across_ref[:, at : at + 128])
        return carry

    lax.fori_loop(0, pairs, fill, 0)
    text[0:rim, :] = jnp.zeros((rim, width), jnp.float32)
    text[rim + text_slots :, :] = jnp.zeros((rim, width), jnp.float32)
    grid[0:patch_span, :] = jnp.zeros((patch_span, width), jnp.float32)
    grid[patch_span * 5 :, :] = jnp.zeros((patch_span, width), jnp.float32)
    low[row_count * 4 :, :] = jnp.zeros((key_pad - row_count * 4, width), jnp.bfloat16)
    lanes = 256
    group_width = members * HEAD_LANES
    power = 1.4426950408889634 / FIXED
    for copy in first_copies(0, 1):
        copy.wait_recv()
    onward_copy(0).start()
    for copy in loads:
        copy.wait()

    def page_step(page, carry):
        length = length_ref[page]
        base = page * row_count
        cell = lax.broadcasted_iota(jnp.int32, (1, 128), 1)
        query_cell = seq * patch_span + cell
        row_cell = seq * patch_span + lax.broadcasted_iota(jnp.int32, (patch_span, 1), 0)
        for plane in range(2):
            box = box_ref[page, plane : plane + 1, :]
            patch = 146 * ((cell % GRID_SIDE) if plane == 0 else (cell // GRID_SIDE)) + 73
            own_patch = 146 * ((query_cell % GRID_SIDE) if plane == 0 else (query_cell // GRID_SIDE)) + 73
            column_patch = 146 * ((row_cell % GRID_SIDE) if plane == 0 else (row_cell // GRID_SIDE)) + 73
            rows_ref[page, plane : plane + 1, 0:text_slots] = box
            rows_ref[page, plane : plane + 1, text_slots:key_pad] = patch
            own_box = rows_ref[page, plane : plane + 1, pl.ds(pl.multiple_of(seq * span, 128), span)]
            query_rows_ref[page, plane : plane + 1, 0:span] = own_box
            query_rows_ref[page, plane : plane + 1, span:256] = own_patch
            columns_ref[page, 0:span, plane * 128 : (plane + 1) * 128] = jnp.broadcast_to(
                column_of(own_box), (span, 128)
            )
            columns_ref[page, span:row_count, plane * 128 : (plane + 1) * 128] = jnp.broadcast_to(
                column_patch, (patch_span, 128)
            )
        for plane, lanes_ref in enumerate((across_ref, upward_ref)):
            difference = rows_ref[page, plane : plane + 1, :] - columns_ref[page, :, plane * 128 : plane * 128 + 1]
            lanes_ref[...] = jnp.clip(difference >> 4, -32, 31) + (32 + 64 * plane)
        key_at = lax.broadcasted_iota(jnp.int32, live_ref.shape, 1)
        key_cell = key_at - text_slots
        live = (key_at < length) | (
            (key_cell >= 0) & ((key_cell >> 3) < GRID_SIDE - 1) & ((key_cell & 7) < GRID_SIDE - 1)
        )
        live_ref[...] = jnp.where(live, 0.0, masked_score * FIXED)
        for copy in first_copies(page, 0):
            copy.wait_recv()
        onward_copy(page).wait_recv()

        def block_of(step, start, stop, at):
            if step:
                return arrived[step - 1, page, start:stop, at].astype(jnp.float32)
            if start:
                return own[page, span:row_count, at].astype(jnp.float32)
            return own[page, 0:span, at].astype(jnp.float32)

        def slot_of(step):
            return (seq, peers[0], peers[1], sibling_of(peers[1]))[step]

        everything = slice(0, width)
        for step in range(4):
            where = slot_of(step)
            at_place = where * span + lax.broadcasted_iota(jnp.int32, (span, 1), 0)
            text[pl.ds(pl.multiple_of(rim + where * span, 8), span), :] = jnp.where(
                at_place < length, block_of(step, 0, span, everything), 0.0
            )
            at_cell = where * patch_span + lax.broadcasted_iota(jnp.int32, (patch_span, 1), 0)
            cell_live = ((at_cell >> 3) < GRID_SIDE - 1) & ((at_cell & 7) < GRID_SIDE - 1)
            grid[pl.ds(pl.multiple_of(patch_span + where * patch_span, 8), patch_span), :] = jnp.where(
                cell_live, block_of(step, span, row_count, everything), 0.0
            )
        for step in range(4):
            where = slot_of(step)

            def convolve(tile, carry):
                at = pl.ds(pl.multiple_of(tile * lanes, lanes), lanes)
                window = text[pl.ds(pl.multiple_of(where * span, 8), span + 2 * rim), at]
                centre = taps_ref[1:2, at] + taps_ref[4:5, at] + taps_ref[7:8, at]
                total = block_of(step, 0, span, at) + window[rim : rim + span] * centre
                for dilation in (1, 2, 3):
                    for offset in (-1, 1):
                        tap = 3 * (dilation - 1) + offset + 1
                        anchor = rim + offset * dilation
                        total = total + window[anchor : anchor + span] * taps_ref[tap : tap + 1, at]
                low[pl.ds(pl.multiple_of(where * span, 16), span), at] = total.astype(jnp.bfloat16)
                window = grid[pl.ds(pl.multiple_of(where * patch_span, 8), 3 * patch_span), at]
                patch_total = block_of(step, span, row_count, at)
                for vertical in (-1, 0, 1):
                    for horizontal in (-1, 0, 1):
                        tap = 9 + 3 * (vertical + 1) + horizontal + 1
                        anchor = patch_span + vertical * GRID_SIDE + horizontal
                        patch_total = patch_total + window[anchor : anchor + patch_span] * taps_ref[tap : tap + 1, at]
                low[pl.ds(pl.multiple_of(text_slots + where * patch_span, 16), patch_span), at] = (
                    patch_total.astype(jnp.bfloat16)
                )
                if step == 0:
                    for first, rows_here, value in ((0, span, total), (span, patch_span, patch_total)):
                        here = pl.ds(pl.multiple_of(base + first, 16), rows_here)
                        hidden_ref[here, at] = value
                        hidden_low_ref[here, at] = value.astype(jnp.bfloat16)
                return carry

            lax.fori_loop(0, width // lanes, convolve, 0)
        own_rows = pl.ds(pl.multiple_of(base, 16), row_count)

        key_ref[page] = dot_nn(low[...], matrices[1]).astype(jnp.bfloat16)
        value_ref[page] = (dot_nn(low[...], matrices[2]) + vector_ref[1:2, :]).astype(jnp.bfloat16)
        query_ref[own_rows, :] = (
            (dot_nn(hidden_low_ref[own_rows, :], matrices[0]) + vector_ref[0:1, :]).astype(jnp.bfloat16)
            * jnp.bfloat16(0.125)
        )

        @pl.when(page < count - 1)
        def _():
            for copy in first_copies(page + 1, 1):
                copy.wait_recv()
            onward_copy(page + 1).start()

        def attend(group, carry):
            at = pl.ds(pl.multiple_of(group * group_width, group_width), group_width)
            scores[...] = dot_nt(split_heads(query_ref[own_rows, at] * jnp.bfloat16(FIXED)), key_ref[page, :, at])
            for start, sub in ((start, sub) for start in range(0, row_count, FORWARD_CHUNK) for sub in range(members // 2)):
                pair = group * (members // 2) + sub
                plane_row = packed_ref[0, pl.ds(pair, 1), :]
                here = slice(start, start + FORWARD_CHUNK)
                packed = []
                for block_at in range(0, key_pad, 128):
                    lane = slice(block_at, block_at + 128)
                    packed.append(
                        line_ref[pair, here, lane]
                        + lookup(plane_row, across_ref[here, lane])
                        + lookup(plane_row, upward_ref[here, lane])
                    )
                for side in range(2):
                    first = (2 * sub + side) * row_count + start
                    there = slice(first, first + FORWARD_CHUNK)
                    parts, top = [], None
                    for index, word in enumerate(packed):
                        lane = slice(128 * index, 128 * (index + 1))
                        field = (word >> 16) if side else (word & 0xFFFF)
                        part = (scores[there, lane] + field.astype(jnp.float32)) + live_ref[0:1, lane]
                        top = part if top is None else jnp.maximum(top, part)
                        parts.append(part)
                    top = jnp.max(top, axis=1, keepdims=True)
                    parts = [jnp.exp2((part - top) * power) for part in parts]
                    total = parts[0]
                    for part in parts[1:]:
                        total = total + part
                    inverse = 1.0 / jnp.sum(total, axis=1, keepdims=True)
                    for index, part in enumerate(parts):
                        weights_ref[page, group, there, 128 * index : 128 * (index + 1)] = (part * inverse).astype(
                            jnp.bfloat16
                        )
            mixture_ref[own_rows, at] = merge_heads(
                dot_nn(weights_ref[page, group], value_ref[page, :, at])
            ).astype(jnp.bfloat16)
            return carry

        lax.fori_loop(0, groups, attend, 0)
        for copy in stores(page):
            copy.start()
        return carry

    lax.fori_loop(0, count, page_step, 0)
    for page in range(count):
        for side in range(2):
            for copy in first_copies(page, side):
                copy.wait_send()
        onward_copy(page).wait_send()
        for copy in stores(page):
            copy.wait()


VMEM = pltpu.VMEM
KERNEL_VMEM = 62 * 1024 * 1024


def in_vmem(count):
    return [pl.BlockSpec(memory_space=VMEM)] * count


def staged(kernel, first, count):
    def run(*refs):
        *refs, semaphore = refs
        refs, buffers = list(refs[:-count]), refs[-count:]
        copies = [
            pltpu.make_async_copy(refs[first + index], buffers[index], semaphore.at[index]) for index in range(count)
        ]
        for copy in copies:
            copy.start()
        refs[first : first + count] = buffers
        kernel(copies, *refs)

    return run


def stage_for(values):
    return [VMEM(value.shape, value.dtype) for value in values] + [pltpu.SemaphoreType.DMA((len(values),))]


def position():
    seq = lax.axis_index("seq")
    return seq, seq % 2, lax.axis_index("page"), seq // 2


def anywhere(count):
    return [pl.BlockSpec(memory_space=pl.ANY)] * count


def forward(pages, lengths, tokens, patches, box, taps, tables, biases, matrices):
    count, span, width = tokens.shape
    patch_span = patches.shape[1]
    row_count = span + patch_span
    total_rows = count * row_count
    key_pad = -(-4 * row_count // 128) * 128
    heads = tables[0].shape[0]
    pairs = heads // 2
    members = 4 if heads % 4 == 0 else 2
    groups = heads // members
    small = (box, *taps, *tables, *biases)
    bf16, f32, i32 = jnp.bfloat16, jnp.float32, jnp.int32
    own = jax.ShapeDtypeStruct((total_rows, width), bf16)
    every = jax.ShapeDtypeStruct((count, key_pad, width), bf16)
    return pl.pallas_call(
        staged(functools.partial(forward_kernel, pages), 1, len(small)),
        out_shape=(
            jax.ShapeDtypeStruct((total_rows, width), f32), own, own, own,
            jax.ShapeDtypeStruct((count, row_count, 256), i32),
            jax.ShapeDtypeStruct((count, 8, key_pad), i32),
            jax.ShapeDtypeStruct((count, 8, 256), i32),
            jax.ShapeDtypeStruct((24, width), f32),
            every, every,
            jax.ShapeDtypeStruct((count, groups, members * row_count, key_pad), bf16),
        ),
        in_specs=[pl.BlockSpec(memory_space=pltpu.SMEM)] + anywhere(len(small) + 5),
        out_specs=tuple(in_vmem(8) + anywhere(3)),
        scratch_shapes=[
            VMEM((count, row_count, width), bf16),
            VMEM((3, width, width), bf16),
            VMEM((count, key_pad, width), bf16),
            VMEM((count, key_pad, width), bf16),
            VMEM((count, groups, members * row_count, key_pad), bf16),
            VMEM((3, count, row_count, width), bf16),
            VMEM((4 * span + 16, width), f32),
            VMEM((6 * patch_span, width), f32),
            VMEM((key_pad, width), bf16),
            VMEM((members * row_count, key_pad), f32),
            VMEM((row_count, key_pad), i32),
            VMEM((row_count, key_pad), i32),
            VMEM((8, key_pad), f32),
            VMEM((pairs, row_count, key_pad), i32),
            VMEM((2, 8, 128), i32),
            VMEM((-(-heads // 8) * 8, 256), f32),
            VMEM((8, width), f32),
            pltpu.SemaphoreType.DMA((5,)),
            pltpu.SemaphoreType.DMA((3, count)),
            pltpu.SemaphoreType.DMA((5, count)),
            pltpu.SemaphoreType.DMA((5, count)),
        ]
        + stage_for(small),
        compiler_params=pltpu.CompilerParams(
            collective_id=0, has_side_effects=True, vmem_limit_bytes=KERNEL_VMEM
        ),
        cost_estimate=pl.CostEstimate(flops=8_000_000_000, bytes_accessed=25_000_000, transcendentals=3_000_000),
        name="forward",
    )(lengths, *small, tokens, patches, *matrices)


def backward_page_kernel(
    scalar_ref, columns_ref, rows_ref, query_rows_ref, query_ref, key_ref, value_ref, mixture_back_ref, weights_ref,
    query_back_ref, block_back_ref, plane_back_ref, line_back_ref,
    back, steps, mask_ref, hot_ref, query_hot_ref, band_ref,
):
    seq_index = scalar_ref[0]
    row_count, width = query_ref.shape
    key_pad = key_ref.shape[0]
    count = 4
    patch_span = GRID_SIDE * GRID_SIDE // count
    span = row_count - patch_span
    text_slots = span * count
    columns, rows = columns_ref[...], rows_ref[...]
    mask_ref[:, 0:key_pad] = ((rows[0:1, :] & 15) < (columns[:, 0:1] & 15)).astype(jnp.float32).astype(jnp.bfloat16)
    mask_ref[:, key_pad:] = ((rows[1:2, :] & 15) < (columns[:, 1:2] & 15)).astype(jnp.float32).astype(jnp.bfloat16)
    bin_at = lax.broadcasted_iota(jnp.int32, (128, key_pad), 0) - 1
    key_block = lax.broadcasted_iota(jnp.int32, (128, key_pad), 1) >> 4
    for side in range(2):
        key_bin = rows[side : side + 1, :] >> 4
        plain = (key_bin == bin_at).astype(jnp.float32)
        lower = (key_bin - 1 == bin_at).astype(jnp.float32)
        plain, lower = jnp.where(bin_at < 64, plain, 0.0), jnp.where(bin_at < 64, lower, 0.0)
        mine = slice(128 * side, 128 * (side + 1))
        other = slice(128 * (1 - side), 128 * (2 - side))
        change = lower - plain
        if side == 0:
            plain = jnp.where(bin_at - 71 == key_block, 1.0, plain)
        hot_ref[mine, 0:key_pad] = plain.astype(jnp.bfloat16)
        hot_ref[mine, (1 + side) * key_pad : (2 + side) * key_pad] = change.astype(jnp.bfloat16)
        hot_ref[other, (1 + side) * key_pad : (2 + side) * key_pad] = jnp.zeros((128, key_pad), jnp.bfloat16)
    half_bin = lax.broadcasted_iota(jnp.int32, (72, row_count), 0)
    for side in range(2):
        query_hot_ref[72 * side : 72 * (side + 1), :] = (
            (71 - (query_rows_ref[side : side + 1, :] >> 4) == half_bin).astype(jnp.float32).astype(jnp.bfloat16)
        )
    lane128 = lax.broadcasted_iota(jnp.int32, (row_count, 128), 1)
    place = query_places(seq_index, (row_count, 128), span, patch_span, text_slots)
    aim = place + lane128 - 32
    near = (lane128 < 64) & (aim >= 0) & (aim < text_slots + patch_span * count)
    apart = (aim >> 4) - (place >> 4)
    near = near & (apart >= -1) & (apart <= 1)
    band_ref[...] = jnp.where(near, aim, -1)
    pair_width = 128
    line_back_ref[...] = jnp.zeros_like(line_back_ref)
    plane_back_ref[...] = jnp.zeros_like(plane_back_ref)

    def attend(pair, carry):
        at = pl.ds(pl.multiple_of(pair * pair_width, pair_width), pair_width)
        both_query = split_heads(query_ref[:, at])
        both_back = split_heads(mixture_back_ref[:, at])
        back[...] = dot_nt(both_back, value_ref[:, at])
        for start in range(0, 2 * row_count, CHUNK):
            there = slice(start, start + CHUNK)
            here = slice(start % row_count, start % row_count + CHUNK)
            parts, total = [], None
            for block_at in range(0, key_pad, 128):
                lane = slice(block_at, block_at + 128)
                part = weights_ref[pair, there, lane].astype(jnp.float32)
                product = part * back[there, lane]
                total = product if total is None else total + product
                parts.append(part)
            mean = jnp.sum(total, axis=1, keepdims=True)
            for index, part in enumerate(parts):
                lane = slice(128 * index, 128 * (index + 1))
                step = (part * (back[there, lane] - mean)).astype(jnp.bfloat16)
                steps[there, lane] = step
                steps[there, key_pad + 128 * index : key_pad + 128 * (index + 1)] = step * mask_ref[here, lane]
                steps[there, 2 * key_pad + 128 * index : 2 * key_pad + 128 * (index + 1)] = (
                    step * mask_ref[here, key_pad + 128 * index : key_pad + 128 * (index + 1)]
                )
        query_back_ref[:, at] = (merge_heads(dot_nn(steps[:, 0:key_pad], key_ref[:, at])) * 0.125).astype(
            jnp.bfloat16
        )
        for kind, value in enumerate(
            (dot_tn(steps[:, 0:key_pad], both_query), dot_tn(weights_ref[pair], both_back))
        ):
            value = value.astype(jnp.bfloat16)
            for where in range(count):
                step_at = seq_index ^ where
                slot = (step_at & 1) * 2 + (step_at >> 1)
                block_back_ref[slot, kind, 0:span, at] = value[where * span : (where + 1) * span]
                block_back_ref[slot, kind, span:row_count, at] = value[
                    text_slots + where * patch_span : text_slots + (where + 1) * patch_span
                ]
        bins = dot_nt(steps[...], hot_ref[...])
        low_bins = bins.astype(jnp.bfloat16)
        lane_one = lax.broadcasted_iota(jnp.int32, (1, 128), 1)
        far = lane128 - 72 - (place >> 4)
        in_line = (lane128 >= 72) & (lane128 < 72 + key_pad // 16)
        for side in range(2):
            head = pl.ds(2 * pair + side, 1)
            own = slice(side * row_count, (side + 1) * row_count)
            both = dot_nn(query_hot_ref[...], low_bins[own])
            for plane in range(2):
                table = both[72 * plane : 72 * (plane + 1), 128 * plane : 128 * (plane + 1)]
                wide_lane = lax.broadcasted_iota(jnp.int32, table.shape, 1)
                table = jnp.where(wide_lane < 72, table, 0.0)
                table = jnp.concatenate([table, jnp.zeros_like(table)], axis=1)
                sheared = pltpu.roll(table, 0, 1, stride=1, stride_axis=0)
                plane_back_ref[plane, head, :] = jnp.sum(sheared, axis=0, keepdims=True)
            line_bins = bins[own, 0:128]
            low_tail = jnp.sum(jnp.where(in_line & (far <= -2), line_bins, 0.0), axis=(0, 1), keepdims=True)
            high_tail = jnp.sum(jnp.where(in_line & (far >= 2), line_bins, 0.0), axis=(0, 1), keepdims=True)
            band = jnp.zeros((1, 128), jnp.float32)
            base = side * row_count
            for first, rows_here, block in (
                (0, span, seq_index),
                (0, 32, jnp.maximum(seq_index - 1, 0)),
                (span - 32, 32, seq_index + 1),
                (span, patch_span, count - 1),
                (span, patch_span, count),
            ):
                aims = band_ref[first : first + rows_here, :]
                source = steps[
                    base + first : base + first + rows_here, pl.ds(pl.multiple_of(block * 128, 128), 128)
                ].astype(jnp.float32)
                taken = jnp.take_along_axis(source, aims & 127, axis=1)
                right = (aims >> 7) == block
                if first == 0 and rows_here == 32:
                    right = right & (seq_index > 0)
                band = band + jnp.sum(jnp.where(right, taken, 0.0), axis=0, keepdims=True)
            line_back_ref[head, :] = (
                band + jnp.where(lane_one == 0, low_tail, 0.0) + jnp.where(lane_one == 63, high_tail, 0.0)
            )
        return carry

    lax.fori_loop(0, width // pair_width, attend, 0)


def backward_page(scalars, columns, rows, query_rows, queries, keys, values, mixture_back, weights):
    row_count, width = queries.shape
    key_pad = keys.shape[0]
    heads = 2 * weights.shape[0]
    return pl.pallas_call(
        backward_page_kernel,
        out_shape=(
            jax.ShapeDtypeStruct((row_count, width), jnp.bfloat16),
            jax.ShapeDtypeStruct((4, 2, row_count, width), jnp.bfloat16),
            jax.ShapeDtypeStruct((2, heads, 256), jnp.float32),
            jax.ShapeDtypeStruct((heads, 128), jnp.float32),
        ),
        in_specs=[pl.BlockSpec(memory_space=pltpu.SMEM)] + in_vmem(8),
        out_specs=tuple(in_vmem(4)),
        scratch_shapes=[
            pltpu.VMEM((2 * row_count, key_pad), jnp.float32),
            pltpu.VMEM((2 * row_count, 3 * key_pad), jnp.bfloat16),
            pltpu.VMEM((row_count, 2 * key_pad), jnp.bfloat16),
            pltpu.VMEM((256, 3 * key_pad), jnp.bfloat16),
            pltpu.VMEM((144, row_count), jnp.bfloat16),
            pltpu.VMEM((row_count, 128), jnp.int32),
        ],
        compiler_params=pltpu.CompilerParams(vmem_limit_bytes=KERNEL_VMEM),
        cost_estimate=pl.CostEstimate(flops=3_000_000_000, bytes_accessed=6_000_000, transcendentals=1_000_000),
        name="backward_page",
    )(scalars, columns, rows, query_rows, queries, keys, values, mixture_back, weights)


def early_orders(far, side):
    return (far[1], far[0], side) + tuple(far[2:]), (far[0], far[1], side) + tuple(far[2:])


def slot_of_bits(bits):
    slot = 0
    for bit in bits:
        slot = slot * 2 + bit
    return slot


def apart(one, other):
    return (one + other) % 2


def early_slots(scalar_ref, page, column, levels):
    far = [apart((page >> level) & 1, (scalar_ref[2] >> level) & 1) for level in range(levels)]
    side = apart(column, scalar_ref[3])
    return [slot_of_bits(order) for order in early_orders(far, side)]


NORM_CHUNK = 48


def norm_rows(values):
    mean = jnp.mean(values, axis=-1, keepdims=True)
    centred = values - mean
    scale = lax.rsqrt(jnp.mean(centred * centred, axis=-1, keepdims=True) + epsilon)
    return centred * scale, scale


def norm_back(delta, unit, scale):
    return scale * (
        delta
        - jnp.mean(delta, axis=-1, keepdims=True)
        - unit * jnp.mean(delta * unit, axis=-1, keepdims=True)
    )


def column_sum(values):
    return jnp.sum(values, axis=0, keepdims=True)


OUT_BIAS, DOWN_BIAS, FIRST_GAIN, FIRST_SHIFT, SECOND_GAIN, SECOND_SHIFT = range(6)
UP_BIAS = 6


def middle_kernel(
    pages, direct,
    *rest,
):
    scalar_ref = position()
    arguments, rest = rest[:14], rest[14:]
    output_ref, patch_output_ref, first_back_ref, mixture_back_ref, sums_ref, *rest = rest
    *rest, vector_ref, load_sem, store_sem = rest
    copied, rest = rest[-14:], rest[:-14]
    hidden_ref, mixture_ref, cotangent_ref, patch_cotangent_ref, out_weight_ref, up_weight_ref, down_weight_ref = copied[:7]
    loads = [
        pltpu.make_async_copy(source, target, load_sem.at[index])
        for index, (source, target) in enumerate(zip(arguments, copied, strict=True))
    ]
    for index in (*range(7, 14), 1, 4, 0, 5, 6, 2, 3):
        loads[index].start()
    if direct:
        bundle_any, *rest, bundle_ref = rest
    else:
        normed_out_ref, up_out_ref, activated_out_ref, down_out_ref, attention_out_ref, *rest = rest
    state, unit, scale_ref, normed, activated, slope, up_back, down_back, attention_back, flipped = rest
    count, span, width = output_ref.shape
    patch_span = patch_output_ref.shape[1]
    row_count = span + patch_span
    total_rows = count * row_count
    wide = up_weight_ref.shape[1]
    lanes = width
    sums_ref[...] = jnp.zeros_like(sums_ref)

    def tile_at(tile):
        return pl.ds(pl.multiple_of(tile * lanes, lanes), lanes)

    def attention_tile(tile, carry):
        at = tile_at(tile)
        state[:, at] = hidden_ref[:, at] + (dot_nn(mixture_ref[...], out_weight_ref[:, at]) + vector_ref[2:3, at])
        return carry

    for index in (*range(7, 14), 0, 1, 4):
        loads[index].wait()
    for index, source in enumerate(copied[7:13]):
        vector_ref[2 + index : 3 + index, :] = source[...].astype(jnp.float32).reshape(1, width)
    for index in range(wide // width):
        part = copied[13][pl.ds(index * width, width)]
        vector_ref[8 + index : 9 + index, :] = part.astype(jnp.float32).reshape(1, width)
    lax.fori_loop(0, width // lanes, attention_tile, 0)

    def first_norm(chunk, carry):
        here = pl.ds(pl.multiple_of(chunk * NORM_CHUNK, 16), NORM_CHUNK)
        rows, scale = norm_rows(state[here, :])
        unit[here, :] = rows
        scale_ref[here, :] = jnp.broadcast_to(scale, (NORM_CHUNK, 128))
        rows = rows * vector_ref[4:5, :] + vector_ref[5:6, :]
        state[here, :] = rows
        normed[here, :] = rows.astype(jnp.bfloat16)
        return carry

    lax.fori_loop(0, total_rows // NORM_CHUNK, first_norm, 0)

    def up_tile(tile, carry):
        at = tile_at(tile)
        branch = dot_nn(normed[...], up_weight_ref[:, at]) + vector_ref[pl.ds(8 + tile, 1), :]
        chance = 0.5 * (1.0 + lax.erf(branch * 0.7071067811865476))
        activated[:, at] = (branch * chance).astype(jnp.bfloat16)
        slope[:, at] = chance + branch * (jnp.exp(branch * branch * -0.5) * 0.3989422804014327)
        return carry

    loads[5].wait()
    lax.fori_loop(0, wide // lanes, up_tile, 0)

    def down_tile(tile, carry):
        at = tile_at(tile)
        state[:, at] = state[:, at] + (dot_nn(activated[...], down_weight_ref[:, at]) + vector_ref[3:4, at])
        return carry

    for index in (2, 3, 6):
        loads[index].wait()
    lax.fori_loop(0, width // lanes, down_tile, 0)

    def second_norm(start, rows_here, page, out_ref, delta_ref):
        here = pl.ds(pl.multiple_of(page * row_count + start, 16), rows_here)
        there = pl.ds(0 if start == span else start, rows_here)
        rows, scale = norm_rows(state[here, :])
        out_ref[page, there, :] = rows * vector_ref[6:7, :] + vector_ref[7:8, :]
        delta = delta_ref[page, there, :].astype(jnp.float32)
        back = norm_back(delta * vector_ref[6:7, :], rows, scale)
        state[here, :] = back
        low = back.astype(jnp.bfloat16)
        down_back[here, :] = low
        for index, value in (
            (SECOND_GAIN, delta * rows), (SECOND_SHIFT, delta), (DOWN_BIAS, low.astype(jnp.float32))
        ):
            sums_ref[index : index + 1, :] += column_sum(value)

    def second_page(page, carry):
        for start in range(0, span, 32):
            second_norm(start, 32, page, output_ref, cotangent_ref)
        second_norm(span, patch_span, page, patch_output_ref, patch_cotangent_ref)
        return carry

    lax.fori_loop(0, count, second_page, 0)

    def up_back_tile(tile, carry):
        at = pl.ds(pl.multiple_of(tile * 2 * width, 2 * width), 2 * width)
        low = (dot_nt(down_back[...], down_weight_ref[at, :]) * slope[:, at]).astype(jnp.bfloat16)
        up_back[:, at] = low
        for part in range(2):
            sums_ref[pl.ds(UP_BIAS + 2 * tile + part, 1), :] = column_sum(
                low[:, part * width : (part + 1) * width].astype(jnp.float32)
            )
        return carry

    lax.fori_loop(0, wide // (2 * width), up_back_tile, 0)

    def normed_back_tile(tile, carry):
        at = tile_at(tile)
        state[:, at] = state[:, at] + dot_nt(up_back[...], up_weight_ref[at, :])
        return carry

    lax.fori_loop(0, width // lanes, normed_back_tile, 0)

    def first_back(chunk, carry):
        here = pl.ds(pl.multiple_of(chunk * NORM_CHUNK, 16), NORM_CHUNK)
        delta, rows = state[here, :], unit[here, :]
        back = norm_back(delta * vector_ref[4:5, :], rows, scale_ref[here, 0:1])
        first_back_ref[here, :] = back
        low = back.astype(jnp.bfloat16)
        attention_back[here, :] = low
        for index, value in (
            (FIRST_GAIN, delta * rows), (FIRST_SHIFT, delta), (OUT_BIAS, low.astype(jnp.float32))
        ):
            sums_ref[index : index + 1, :] += column_sum(value)
        return carry

    lax.fori_loop(0, total_rows // NORM_CHUNK, first_back, 0)

    def mixture_tile(tile, carry):
        at = tile_at(tile)
        mixture_back_ref[:, at] = dot_nt(attention_back[...], out_weight_ref[at, :]).astype(jnp.bfloat16)
        return carry

    lax.fori_loop(0, width // lanes, mixture_tile, 0)
    if not direct:
        normed_out_ref[...] = normed[...]
        up_out_ref[...] = up_back[...]
        activated_out_ref[...] = activated[...]
        down_out_ref[...] = down_back[...]
        attention_out_ref[...] = attention_back[...]
        return
    levels = pages.bit_length() - 1
    core = scalar_ref[1]
    rows = width // pages
    tall = wide // pages
    block = 384
    groups = wide // (2 * block)
    flipped[...] = normed[...].T

    def up_weight_tile(tile, carry):
        at = pl.ds(pl.multiple_of(tile * 2 * block, 2 * block), 2 * block)
        result = dot_nn(flipped[...], up_back[:, at]).astype(jnp.bfloat16)
        for part in range(2):
            column, group = (2 * tile + part) // groups, (2 * tile + part) % groups
            for page in range(pages):
                slot = early_slots(scalar_ref, page, column, levels)[0]
                bundle_ref[core, slot, pl.ds(pl.multiple_of(group * rows, 16), rows), :] = result[
                    page * rows : (page + 1) * rows, part * block : (part + 1) * block
                ]
        return carry

    lax.fori_loop(0, groups, up_weight_tile, 0)
    stores = [
        pltpu.make_async_copy(bundle_ref.at[part], bundle_any.at[part], store_sem.at[index])
        for index, part in enumerate(
            (
                (core, slice(None), slice(0, tall)), (1 - core, slice(None), slice(0, tall)),
                (slice(None), slice(None), slice(tall, tall + rows // 2)),
            )
        )
    ]
    stores[0].start()

    def down_weight_tile(four, carry):
        at = pl.ds(pl.multiple_of(four * 4 * tall, 128), 4 * tall)
        result = dot_tn(activated[:, at], down_back[...]).astype(jnp.bfloat16)
        for inner in range(4):
            for column in range(2):
                slot = early_slots(scalar_ref, 4 * four + inner, column, levels)[1]
                bundle_ref[1 - core, slot, 0:tall, :] = result[
                    inner * tall : (inner + 1) * tall, column * block : (column + 1) * block
                ]
        return carry

    lax.fori_loop(0, pages // 4, down_weight_tile, 0)
    stores[1].start()
    flipped[...] = mixture_ref[...].T
    half = rows // 2

    result = dot_nn(flipped[...], attention_back[...]).astype(jnp.bfloat16)
    for column in range(2):
        for page in range(pages):
            slots = early_slots(scalar_ref, page, column, levels)
            for order in range(2):
                first = page * rows + order * half
                bundle_ref[core if order == 0 else 1 - core, slots[order], tall : tall + half, :] = result[
                    first : first + half, column * block : (column + 1) * block
                ]
    stores[2].start()
    for copy in stores:
        copy.wait()


def in_tiles(width, pages):
    return (width // pages) % 32 == 0 and pages >= 4


def middle(places, hidden, mixture, cotangent, patch_cotangent, matrices, vectors, pages):
    count, span, width = cotangent.shape
    patch_span = patch_cotangent.shape[1]
    total_rows = hidden.shape[0]
    wide = matrices[1].shape[1]
    direct = in_tiles(width, pages)
    bf16, f32 = jnp.bfloat16, jnp.float32
    if direct:
        extra = (jax.ShapeDtypeStruct((2, 2 * pages, (wide + width // 2) // pages, 384), bf16),)
    else:
        extra = tuple(
            jax.ShapeDtypeStruct((total_rows, size), bf16) for size in (width, wide, wide, width, width)
        )
    result = pl.pallas_call(
        functools.partial(middle_kernel, pages, direct),
        out_shape=(
            jax.ShapeDtypeStruct(cotangent.shape, f32),
            jax.ShapeDtypeStruct(patch_cotangent.shape, f32),
            jax.ShapeDtypeStruct((total_rows, width), f32),
            jax.ShapeDtypeStruct((total_rows, width), bf16),
            jax.ShapeDtypeStruct((16, width), f32),
        )
        + extra,
        in_specs=anywhere(7 + len(vectors)),
        out_specs=tuple(in_vmem(5) + (anywhere(1) if direct else in_vmem(len(extra)))),
        scratch_shapes=[
            pltpu.VMEM((total_rows, width), f32),
            pltpu.VMEM((total_rows, width), f32),
            pltpu.VMEM((total_rows, 128), f32),
            pltpu.VMEM((total_rows, width), bf16),
            pltpu.VMEM((total_rows, wide), bf16),
            pltpu.VMEM((total_rows, wide), f32),
            pltpu.VMEM((total_rows, wide), bf16),
            pltpu.VMEM((total_rows, width), bf16),
            pltpu.VMEM((total_rows, width), bf16),
            pltpu.VMEM((width, total_rows), bf16),
        ]
        + [pltpu.VMEM(value.shape, value.dtype) for value in (extra if direct else ())]
        + [
            pltpu.VMEM(value.shape, value.dtype)
            for value in (hidden, mixture, cotangent, patch_cotangent, *matrices, *vectors)
        ]
        + [pltpu.VMEM((16, width), f32), pltpu.SemaphoreType.DMA((14,)), pltpu.SemaphoreType.DMA((3,))],
        compiler_params=pltpu.CompilerParams(vmem_limit_bytes=KERNEL_VMEM),
        cost_estimate=pl.CostEstimate(flops=14_000_000_000, bytes_accessed=30_000_000, transcendentals=2_600_000),
        name="middle",
    )(hidden, mixture, cotangent, patch_cotangent, *matrices, *vectors)
    first, rest = result[:5], result[5:]
    if direct:
        return first + rest
    normed, up_back, activated, down_back, attention_back = rest
    return first + (
        indexed_bundle(
            (
                ((normed, up_back, None), (mixture, attention_back, 0)),
                ((activated, down_back, None), (mixture, attention_back, 1)),
            ),
            places,
            pages,
        ),
    )


def indexed_bundle(matrices, scalars, pages):
    levels = pages.bit_length() - 1
    place = jnp.arange(2 * pages, dtype=jnp.int32)
    bits = [(place >> (levels - k)) & 1 for k in range(levels + 1)]
    halves = []
    for order, group in enumerate(matrices):
        side, near = (bits[0], bits[1]) if order == 0 else (bits[1], bits[0])
        far = near
        for level in range(1, levels):
            far = far + (bits[level + 1] << level)
        index = (far ^ scalars[2]) * 2 + (side ^ scalars[3])
        blocks = []
        for operand, gradient, part in group:
            rows = in_blocks(outer_dot(operand, gradient).astype(jnp.bfloat16), pages)
            if part is not None:
                half = rows.shape[1] // 2
                rows = rows[:, part * half : (part + 1) * half]
            blocks.append(rows)
        halves.append(jnp.concatenate(blocks, axis=1)[index])
    first, second = halves
    mine = scalars[1] == 0
    return jnp.stack([jnp.where(mine, first, second), jnp.where(mine, second, first)])


def in_blocks(matrix, pages):
    rows, columns = matrix.shape[0] // pages, matrix.shape[1] // 2
    lanes = min(columns, 384)
    blocks = matrix.reshape(pages, rows, 2, columns // lanes, lanes)
    return blocks.transpose(0, 2, 3, 1, 4).reshape(pages * 2, rows * columns // lanes, lanes)


class Halving:
    def __init__(self, keep, source, landing, landings, partners, sibling, sems, chunks):
        self.keep, self.landing, self.landings = keep, landing, landings
        total = keep.shape[0]
        unit = total // chunks
        send_sem, recv_sem = sems
        self.arrivals, self.sends, self.needs = {}, {}, {}
        used = 0
        for chunk in range(chunks):
            lo = total - (chunk + 1) * unit
            copy = remote(
                source.at[lo : lo + unit], landing.at[lo : lo + unit], send_sem.at[used], recv_sem.at[used], *sibling
            )
            self.arrivals["core", chunk] = (copy, landing, lo, unit)
            used += 1
        for step, (into, partner) in enumerate(zip(landings, partners, strict=True)):
            size = total >> (step + 1)
            piece = min(unit, size)
            for chunk in range(size // piece):
                lo = size - (chunk + 1) * piece
                copy = remote(
                    keep.at[size + lo : size + lo + piece], into.at[lo : lo + piece], send_sem.at[used],
                    recv_sem.at[used], *partner,
                )
                self.arrivals[step, chunk] = (copy, into, lo, piece)
                self.sends[step, chunk] = copy
                self.needs[step, chunk] = {
                    (source_step, block)
                    for block in range(size + lo, size + lo + piece)
                    for source_step in ("core", *range(step))
                }
                used += 1
        self.done = set()

    def start(self):
        for key, (copy, *_) in self.arrivals.items():
            if key[0] == "core":
                copy.start()

    def take(self, *key):
        copy, into, lo, count = self.arrivals[key]
        copy.wait_recv()

        def add(block, carry):
            self.keep[block] = self.keep[block] + into[block]
            return carry

        lax.fori_loop(lo, lo + count, add, 0)
        for block in range(lo, lo + count):
            self.done.add((key[0], block))
        for name in list(self.sends):
            if self.needs[name] <= self.done:
                self.sends.pop(name).start()

    def finish(self):
        for copy, *_ in self.arrivals.values():
            copy.wait_send()


def backward_kernel(
    pages,
    staging, length_ref, query_ref, mixture_back_ref, columns_ref, rows_ref, query_rows_ref, tokens_ref, patches_ref, taps_ref,
    middle_sums_ref, bundle_any, weights_any, key_any, value_any, hidden_any, first_back_any, query_weight_any,
    key_weight_any, value_weight_any,
    tokens_back_ref, patches_back_ref, early_ref, late_ref, sums_ref, up_in_ref, down_in_ref, mixed_in_ref,
    keep, landing, landings, late, late_landing, late_landings, weights_buf, key_buf, value_buf, outgoing, from_sib,
    from_far, matrices, flipped, total_back, query_back, key_back, value_back, back, steps, mask_ref, hot_ref,
    query_hot_ref, band_ref, table_acc, band_acc, table_out, text_rim, patch_rim, sums, sums_in,
    up_in, down_out, down_in, mixed_out, mixed_in,
    load_sem, page_sem, early_send, early_recv, late_send, late_recv, sib_send, sib_recv, far_send, far_recv, rim_send,
    rim_recv, sum_send, sum_recv, swap_send, swap_recv,
):
    page_at, bits, seq, across, core = places_of(pages)
    levels = len(bits)
    count, span, width = tokens_ref.shape
    patch_span = patches_ref.shape[1]
    row_count = span + patch_span
    total_rows = count * row_count
    key_pad = key_buf.shape[1]
    text_slots = 4 * span
    groups = weights_buf.shape[1]
    members = weights_buf.shape[2] // row_count
    heads = groups * members
    group_width = members * HEAD_LANES
    f32, bf16 = jnp.float32, jnp.bfloat16

    sibling = (page_at, sibling_of(seq))
    opposite = (page_at, across_of(seq))
    diagonal = (page_at, sibling_of(across_of(seq)))
    flips = [(1 - 2 * bit) * 2**level for level, bit in enumerate(bits)]
    on_page = [(page_at + flip, seq) for flip in flips]
    either = lambda first, second: first + core * (second - first)
    early_partners = [
        (page_at + either(flips[1], flips[0]), seq),
        (page_at + either(flips[0], flips[1]), seq),
        opposite,
    ] + on_page[2:]
    barrier = pltpu.get_barrier_semaphore()
    everyone = [sibling, opposite, diagonal] + on_page
    for peer in everyone:
        pl.semaphore_signal(barrier, inc=1, device_id=peer, device_id_type=MESH)

    keep_load = pltpu.make_async_copy(bundle_any.at[0], keep, load_sem.at[0])
    later_loads = [
        pltpu.make_async_copy(source, target, load_sem.at[1 + index])
        for index, (source, target) in enumerate(
            (
                (query_weight_any, matrices.at[0]), (key_weight_any, matrices.at[1]),
                (value_weight_any, matrices.at[2]), (hidden_any, key_back), (first_back_any, total_back),
            )
        )
    ]

    def page_loads(page):
        slot = page % 2
        return [
            pltpu.make_async_copy(source.at[page], target.at[slot], page_sem.at[index, slot])
            for index, (source, target) in enumerate(
                ((weights_any, weights_buf), (key_any, key_buf), (value_any, value_buf))
            )
        ]

    for copy in page_loads(0):
        copy.start()
    keep_load.start()
    pl.semaphore_wait(barrier, len(everyone))
    early = Halving(
        keep, bundle_any.at[1], landing, landings, early_partners, sibling, (early_send, early_recv), 8
    )
    late_sum = Halving(
        late.at[0], late.at[1], late_landing, late_landings, early_partners, sibling, (late_send, late_recv), 4
    )
    early.start()
    for copy in staging:
        copy.wait()

    lane128 = lax.broadcasted_iota(jnp.int32, (row_count, 128), 1)
    place = query_places(seq, (row_count, 128), span, patch_span, text_slots)
    aim = place + lane128 - 32
    blocks_on = (aim >> 4) - (place >> 4)
    near = (lane128 < 64) & (aim >= 0) & (aim < text_slots + patch_span * 4) & (blocks_on >= -1) & (blocks_on <= 1)
    band_ref[...] = jnp.where(near, aim, -1)
    table_acc[...] = jnp.zeros_like(table_acc)
    band_acc[...] = jnp.zeros_like(band_acc)
    lane_of_row = lax.broadcasted_iota(jnp.int32, (48, row_count), 1)
    place_of_row = jnp.where(
        lane_of_row < span, seq * span + lane_of_row, text_slots + seq * patch_span + lane_of_row - span
    )
    query_hot_ref[144:192, :] = (
        ((place_of_row >> 4) == lax.broadcasted_iota(jnp.int32, (48, row_count), 0)).astype(f32).astype(bf16)
    )
    def start_page(page):
        slot = page % 2
        for copy in page_loads(page):
            copy.wait()

        @pl.when(page < count - 1)
        def _():
            for copy in page_loads(page + 1):
                copy.start()

        bin_at = lax.broadcasted_iota(jnp.int32, (128, key_pad), 0) - 1
        key_block = lax.broadcasted_iota(jnp.int32, (128, key_pad), 1) >> 4
        half_bin = lax.broadcasted_iota(jnp.int32, (72, row_count), 0)
        for side in range(2):
            key_row = rows_ref[page, side : side + 1, :]
            query_column = columns_ref[page, :, 128 * side : 128 * side + 1]
            mask_ref[:, side * key_pad : (side + 1) * key_pad] = (
                ((key_row & 15) < (query_column & 15)).astype(f32).astype(bf16)
            )
            key_bin = key_row >> 4
            plain = jnp.where(bin_at < 64, (key_bin == bin_at).astype(f32), 0.0)
            lower = jnp.where(bin_at < 64, (key_bin - 1 == bin_at).astype(f32), 0.0)
            mine = slice(128 * side, 128 * (side + 1))
            other = slice(128 * (1 - side), 128 * (2 - side))
            change = lower - plain
            if side == 0:
                plain = jnp.where(bin_at - 71 == key_block, 1.0, plain)
            hot_ref[mine, 0:key_pad] = plain.astype(bf16)
            hot_ref[mine, (1 + side) * key_pad : (2 + side) * key_pad] = change.astype(bf16)
            hot_ref[other, (1 + side) * key_pad : (2 + side) * key_pad] = jnp.zeros((128, key_pad), bf16)
            query_bin = query_rows_ref[page, side : side + 1, 0:row_count] >> 4
            query_hot_ref[72 * side : 72 * (side + 1), :] = (71 - query_bin == half_bin).astype(f32).astype(bf16)

    def attend(page, group):
        slot = page % 2
        at = pl.ds(pl.multiple_of(group * group_width, group_width), group_width)
        own_rows = pl.ds(pl.multiple_of(page * row_count, 16), row_count)
        both_query = split_heads(query_ref[own_rows, at])
        both_back = split_heads(mixture_back_ref[own_rows, at])
        back[...] = dot_nt(both_back, value_buf[slot, :, at])
        for start in range(0, members * row_count, CHUNK):
            there = slice(start, start + CHUNK)
            here = slice(start % row_count, start % row_count + CHUNK)
            parts, total = [], None
            for block_at in range(0, key_pad, 128):
                lane = slice(block_at, block_at + 128)
                part = weights_buf[slot, group, there, lane].astype(f32)
                product = part * back[there, lane]
                total = product if total is None else total + product
                parts.append(part)
            mean = jnp.sum(total, axis=1, keepdims=True)
            for index, part in enumerate(parts):
                lane = slice(128 * index, 128 * (index + 1))
                step = (part * (back[there, lane] - mean)).astype(bf16)
                steps[there, lane] = step
                steps[there, key_pad + 128 * index : key_pad + 128 * (index + 1)] = step * mask_ref[here, lane]
                steps[there, 2 * key_pad + 128 * index : 2 * key_pad + 128 * (index + 1)] = (
                    step * mask_ref[here, key_pad + 128 * index : key_pad + 128 * (index + 1)]
                )
        query_back[own_rows, at] = (
            merge_heads(dot_nn(steps[:, 0:key_pad], key_buf[slot, :, at])) * 0.125
        ).astype(bf16)
        for kind, value in enumerate(
            (dot_tn(steps[:, 0:key_pad], both_query), dot_tn(weights_buf[slot, group], both_back))
        ):
            value = value.astype(bf16)
            for where in range(4):
                place_at = apart(where % 2, core) * 2 + apart(where // 2, across)
                outgoing[page, place_at, kind, 0:span, at] = value[where * span : (where + 1) * span]
                outgoing[page, place_at, kind, span:row_count, at] = value[
                    text_slots + where * patch_span : text_slots + (where + 1) * patch_span
                ]
        bins = dot_nt(steps[...], hot_ref[...]).astype(bf16)
        for side in range(members):
            head = members * group + side
            base = side * row_count
            both = dot_nn(query_hot_ref[...], bins[base : base + row_count])
            table_acc[head, 0:72, :] += both[0:72, 0:128]
            table_acc[head, 72:144, :] += both[72:144, 128:256]
            table_acc[head, 144:192, :] += both[144:192, 0:128]
            for first, rows_here, block, into in bands():
                source = steps[
                    base + first : base + first + rows_here, pl.ds(pl.multiple_of(block * 128, 128), 128)
                ]
                band_acc[head, into : into + rows_here, :] += source.astype(f32)

    def bands():
        before = seq - (seq + 3) // 4
        return (
            (0, span, seq, 0),
            (0, 32, before, span),
            (span - 32, 32, seq + 1, span + 32),
            (span, patch_span, 3, span + 64),
            (span, patch_span, 4, span + 64 + patch_span),
        )

    def sib_copy(page, part):
        at = slice(part * width // 2, (part + 1) * width // 2)
        return remote(
            outgoing.at[page, 2:4, :, :, at], from_sib.at[page, :, :, :, at], sib_send.at[page, part],
            sib_recv.at[page, part], *sibling,
        )

    def far_copy(page, part):
        at = slice(part * width // 2, (part + 1) * width // 2)
        return remote(
            outgoing.at[page, 1, :, :, at], from_far.at[page, :, :, at], far_send.at[page, part],
            far_recv.at[page, part], *opposite,
        )

    def pass_on(page, part):
        sib_copy(page, part).wait_recv()
        at = slice(part * width // 2, (part + 1) * width // 2)
        for kind in range(2):
            outgoing[page, 1, kind, :, at] = outgoing[page, 1, kind, :, at] + from_sib[page, 1, kind, :, at]
        far_copy(page, part).start()

    events = {
        1: [("core", 0), ("core", 1)], 2: [("core", 2), ("core", 3)], 4: [("core", 4), ("core", 5)],
        6: [("core", 6), ("core", 7)], 8: [(0, 0)], 12: [(0, 1)],
    }
    last_turn = count * groups - 1

    def step_body(turn, carry):
        page, group = turn // groups, turn % groups

        @pl.when(group == 0)
        def _():
            start_page(page)

        for at_turn, names in events.items():

            @pl.when(turn == min(at_turn, last_turn))
            def _(names=names, at_turn=at_turn):
                if at_turn == min(events):
                    keep_load.wait()
                for name in names:
                    early.take(*name)

        @pl.when(turn == min(3, last_turn))
        def _():
            for copy in later_loads:
                copy.start()

        @pl.when((group == 2) & (page > 0))
        def _():
            pass_on(page - 1, 1)

        @pl.when(group == groups - 1)
        def _():
            pass_on(page, 0)

        attend(page, group)

        for part in range(2):

            @pl.when(group == (part + 1) * groups // 2 - 1)
            def _(part=part):
                sib_copy(page, part).start()

        return carry

    lax.fori_loop(0, count * groups, step_body, 0)

    for copy in later_loads:
        copy.wait()
    flipped[...] = key_back[...].T
    lanes = 384
    rows = width // pages
    half = rows // 2

    def weight_columns(index, gradient):
        def tile(four, carry):
            tile_rows = pl.ds(pl.multiple_of(four * 4 * rows, 128), 4 * rows)
            result = dot_nn(flipped[tile_rows, :], gradient[...]).astype(bf16)
            for inner in range(4):
                page = four * 4 + inner
                first = inner * rows
                for column in range(2):
                    far = [apart((page // 2**level) % 2, bit) for level, bit in enumerate(bits)]
                    slots = [slot_of_bits(order) for order in early_orders(far, apart(column, across))]
                    at = slice(column * lanes, (column + 1) * lanes)
                    if index < 2:
                        late[core if index == 0 else 1 - core, slots[index], 0:rows, :] = result[
                            first : first + rows, at
                        ]
                    else:
                        late[core, slots[0], rows : rows + half, :] = result[first : first + half, at]
                        late[1 - core, slots[1], rows : rows + half, :] = result[first + half : first + rows, at]
            return carry

        lax.fori_loop(0, pages // 4, tile, 0)

    def project_back(gradient, matrix):
        total_back[...] = total_back[...] + dot_nt(gradient[...], matrices[matrix])

    pass_on(count - 1, 1)
    weight_columns(0, query_back)
    project_back(query_back, 0)
    sums[0, 0:16, :] = middle_sums_ref[...]
    sums[0, 10:11, :] = column_sum(query_back[...].astype(f32))

    def head_tables(head, carry):
        for plane in range(2):
            table = table_acc[head, 72 * plane : 72 * (plane + 1), :]
            lane = lax.broadcasted_iota(jnp.int32, table.shape, 1)
            table = jnp.where(lane < 72, table, 0.0)
            table = jnp.concatenate([table, jnp.zeros_like(table)], axis=1)
            sheared = pltpu.roll(table, 0, 1, stride=1, stride_axis=0)
            table_out[head, 0:1, 256 * plane : 256 * (plane + 1)] = column_sum(sheared)
        table = table_acc[head, 144:192, :]
        lane = lax.broadcasted_iota(jnp.int32, table.shape, 1)
        apart_by = lane - 72 - lax.broadcasted_iota(jnp.int32, table.shape, 0)
        in_line = (lane >= 72) & (lane < 72 + 36)
        low_tail = jnp.sum(column_sum(jnp.where(in_line & (apart_by <= -2), table, 0.0)), axis=1, keepdims=True)
        high_tail = jnp.sum(column_sum(jnp.where(in_line & (apart_by >= 2), table, 0.0)), axis=1, keepdims=True)
        band = jnp.zeros((1, 128), f32)
        for first, rows_here, block, into in bands():
            aims = band_ref[first : first + rows_here, :]
            taken = jnp.take_along_axis(band_acc[head, into : into + rows_here, :], aims & 127, axis=1)
            right = (aims >> 7) == block
            if into == span:
                right = right & (seq > 0)
            band = band + column_sum(jnp.where(right, taken, 0.0))
        lane_one = lax.broadcasted_iota(jnp.int32, (1, 128), 1)
        table_out[head, 0:1, 512:640] = (
            band + jnp.where(lane_one == 0, low_tail, 0.0) + jnp.where(lane_one == 63, high_tail, 0.0)
        )
        table_out[head, 0:1, 640:768] = jnp.zeros((1, 128), f32)
        return carry

    lax.fori_loop(0, heads, head_tables, 0)
    for head in range(heads):
        at_row = 8 + head
        sums[1, at_row : at_row + 1, :] = table_out[head, 0:1, :]

    for name in ((0, 2), (1, 0)):
        early.take(*name)
    for page in range(count):
        for part in range(2):
            far_copy(page, part).wait_recv()
        own_rows = slice(page * row_count, (page + 1) * row_count)
        for kind, target in enumerate((key_back, value_back)):
            target[own_rows, :] = (
                (outgoing[page, 0, kind].astype(f32) + from_sib[page, 0, kind].astype(f32))
                + from_far[page, kind].astype(f32)
            ).astype(bf16)
    weight_columns(1, key_back)
    weight_columns(2, value_back)
    late_sum.start()
    project_back(key_back, 1)
    project_back(value_back, 2)
    sums[0, 11:12, :] = column_sum(value_back[...].astype(f32))
    for page in range(count):
        first = page * row_count
        text_rim[page, 16 : 16 + span, :] = total_back[first : first + span, :].astype(bf16)
        patch_rim[page, 16 : 16 + patch_span, :] = total_back[first + span : first + row_count, :].astype(bf16)
    after, before = (page_at, (seq + 1) % 4), (page_at, (seq + 3) % 4)
    rim_copies = [
        remote(
            source.at[:, start : start + 16], source.at[:, stop : stop + 16], rim_send.at[index], rim_recv.at[index],
            *peer,
        )
        for index, (source, start, stop, peer) in enumerate(
            (
                (text_rim, span, 0, after), (text_rim, 16, 16 + span, before),
                (patch_rim, 16, 0, after), (patch_rim, 16, 32, before),
            )
        )
    ]
    for copy in rim_copies:
        copy.start()
    for chunk in range(4):
        late_sum.take("core", chunk)
    for name in ((0, 3), (1, 1)):
        early.take(*name)
    for copy in rim_copies:
        copy.wait()
    sums[1, 0:8, :] = jnp.zeros((8, width), f32)
    sums[1, 20:24, :] = jnp.zeros((4, width), f32)
    sums[0, 16:24, :] = jnp.zeros((8, width), f32)

    def position_tile(tile, carry):
        at = pl.ds(pl.multiple_of(tile * 256, 256), 256)
        text_taps = [jnp.zeros((1, 256), f32) for _ in range(7)]
        patch_taps = [jnp.zeros((1, 256), f32) for _ in range(9)]
        for page in range(count):
            first = page * row_count
            window = text_rim[page, :, at].astype(f32)
            window_row = lax.broadcasted_iota(jnp.int32, (span + 32, 1), 0)
            inside = ((window_row >= 16) | (seq > 0)) & ((window_row < 16 + span) | (seq < 3))
            window = jnp.where(inside, window, 0.0)
            live = seq * span + lax.broadcasted_iota(jnp.int32, (span, 1), 0) < length_ref[page]
            masked = jnp.where(live, tokens_ref[page, :, at].astype(f32), 0.0)
            total = jnp.zeros((span, 256), f32)
            for distance in range(-3, 4):
                shifted = window[16 - distance : 16 - distance + span]
                if distance == 0:
                    weight = taps_ref[1:2, at] + taps_ref[4:5, at] + taps_ref[7:8, at]
                else:
                    tap = 3 * (abs(distance) - 1) + (2 if distance > 0 else 0)
                    weight = taps_ref[tap : tap + 1, at]
                total = total + shifted * weight
                text_taps[distance + 3] = text_taps[distance + 3] + column_sum(shifted * masked)
            tokens_back_ref[page, :, at] = total_back[first : first + span, at] + jnp.where(live, total, 0.0)
            window = patch_rim[page, :, at].astype(f32)
            window_row = lax.broadcasted_iota(jnp.int32, (48, 1), 0)
            inside = ((window_row >= 16) | (seq > 0)) & ((window_row < 32) | (seq < 3))
            window = jnp.where(inside, window, 0.0)
            cell = seq * patch_span + lax.broadcasted_iota(jnp.int32, (patch_span, 1), 0)
            live = ((cell >> 3) < GRID_SIDE - 1) & ((cell & 7) < GRID_SIDE - 1)
            masked = jnp.where(live, patches_ref[page, :, at].astype(f32), 0.0)
            total = jnp.zeros((patch_span, 256), f32)
            for tap in range(9):
                distance = GRID_SIDE * (tap // 3 - 1) + tap % 3 - 1
                shifted = window[16 - distance : 32 - distance]
                total = total + shifted * taps_ref[9 + tap : 10 + tap, at]
                patch_taps[tap] = patch_taps[tap] + column_sum(shifted * masked)
            patches_back_ref[page, :, at] = total_back[first + span : first + row_count, at] + jnp.where(
                live, total, 0.0
            )
        for index, value in enumerate(text_taps):
            sums[0, 16 + index : 17 + index, at] = value
        for index, value in enumerate(patch_taps):
            if index == 0:
                sums[0, 23:24, at] = value
            else:
                sums[1, index - 1 : index, at] = value
        return carry

    early.take(2, 0)
    lax.fori_loop(0, width // 256, position_tile, 0)

    sum_partners = [opposite] + on_page
    sum_copies = [remote(sums.at[1 - core], sums_in.at[0], sum_send.at[0], sum_recv.at[0], *sibling)] + [
        remote(sums.at[core], sums_in.at[1 + index], sum_send.at[1 + index], sum_recv.at[1 + index], *partner)
        for index, partner in enumerate(sum_partners)
    ]
    last = remote(
        sums.at[core], sums_in.at[2 + levels], sum_send.at[2 + levels], sum_recv.at[2 + levels], *sibling
    )
    sum_copies[0].start()

    def sum_step(index):
        sum_copies[index].wait()
        sums[core] = sums[core] + sums_in[index]
        (sum_copies + [last])[index + 1].start()

    late_sum.take(0, 0)
    sum_step(0)
    late_sum.take(0, 1)
    sum_step(1)
    late_sum.take(1, 0)
    sum_step(2)
    for step in range(2, levels + 1):
        late_sum.take(step, 0)
        sum_step(step + 1)
    for step in range(3, levels + 1):
        early.take(step, 0)
    last.wait()
    sums_ref[core] = sums[core]
    sums_ref[1 - core] = sums_in[2 + levels]
    wide_rows = 4 * rows
    block = keep[0].astype(f32)
    low, high = block[:, 0 : lanes // 2], pltpu.roll(block, lanes // 2, 1)[:, 0 : lanes // 2]
    down_out[...] = low[0:wide_rows].astype(bf16)
    mixed_out[0:half, :] = jnp.where(core == 0, high[wide_rows:], low[wide_rows:]).astype(bf16)
    block = late[0, 0].astype(f32)
    low, high = block[:, 0 : lanes // 2], pltpu.roll(block, lanes // 2, 1)[:, 0 : lanes // 2]
    mixed_out[half:, :] = jnp.where(core == 0, high, low).astype(bf16)
    swaps = [
        remote(source, target, swap_send.at[index], swap_recv.at[index], *sibling)
        for index, (source, target) in enumerate(
            ((keep.at[0, 2 * rows : 4 * rows], up_in), (down_out, down_in), (mixed_out, mixed_in))
        )
    ]
    for copy in swaps:
        copy.start()
    early_ref[...] = keep[0]
    late_ref[...] = late[0, 0]
    for copy in swaps:
        copy.wait()
    up_in_ref[...] = up_in[...]
    down_in_ref[...] = down_in[...]
    mixed_in_ref[...] = mixed_in[...]
    early.finish()
    late_sum.finish()
    for page in range(count):
        for part in range(2):
            sib_copy(page, part).wait_send()
            far_copy(page, part).wait_send()


def backward(pages, lengths, local_values, far_values, tokens, patches):
    count, span, width = tokens.shape
    patch_span = patches.shape[1]
    row_count = span + patch_span
    total_rows = count * row_count
    bundle, weights, keys = far_values[0], far_values[1], far_values[2]
    groups, grouped_rows, key_pad = weights.shape[1:]
    heads = groups * grouped_rows // row_count
    blocks, early_rows, lanes = bundle.shape[1:]
    late_rows = 3 * width // (2 * pages)
    levels = pages.bit_length() - 1
    bf16, f32, i32 = jnp.bfloat16, jnp.float32, jnp.int32
    dma = pltpu.SemaphoreType.DMA

    def landings(rows):
        return [VMEM((blocks >> (step + 1), rows, lanes), bf16) for step in range(levels + 1)]

    early_count = 8 + 4 + 2 + (levels - 1)
    late_count = 4 + 2 + levels
    return pl.pallas_call(
        staged(functools.partial(backward_kernel, pages), 1, len(local_values)),
        out_shape=(
            jax.ShapeDtypeStruct(tokens.shape, f32),
            jax.ShapeDtypeStruct(patches.shape, f32),
            jax.ShapeDtypeStruct((early_rows, lanes), bf16),
            jax.ShapeDtypeStruct((late_rows, lanes), bf16),
            jax.ShapeDtypeStruct((2, 24, width), f32),
            jax.ShapeDtypeStruct((early_rows // 9 * 4, lanes), bf16),
            jax.ShapeDtypeStruct((early_rows // 9 * 8, lanes // 2), bf16),
            jax.ShapeDtypeStruct((early_rows // 9 + late_rows, lanes // 2), bf16),
        ),
        in_specs=[pl.BlockSpec(memory_space=pltpu.SMEM)]
        + anywhere(len(local_values) + len(far_values)),
        out_specs=tuple(in_vmem(8)),
        scratch_shapes=[
            VMEM((blocks, early_rows, lanes), bf16),
            VMEM((blocks, early_rows, lanes), bf16),
            landings(early_rows),
            VMEM((2, blocks, late_rows, lanes), bf16),
            VMEM((blocks, late_rows, lanes), bf16),
            landings(late_rows),
            VMEM((2, groups, grouped_rows, key_pad), bf16),
            VMEM((2, key_pad, width), bf16),
            VMEM((2, key_pad, width), bf16),
            VMEM((count, 4, 2, row_count, width), bf16),
            VMEM((count, 2, 2, row_count, width), bf16),
            VMEM((count, 2, row_count, width), bf16),
            VMEM((3, width, width), bf16),
            VMEM((width, total_rows), bf16),
            VMEM((total_rows, width), f32),
            VMEM((total_rows, width), bf16),
            VMEM((total_rows, width), bf16),
            VMEM((total_rows, width), bf16),
            VMEM((grouped_rows, key_pad), f32),
            VMEM((grouped_rows, 3 * key_pad), bf16),
            VMEM((row_count, 2 * key_pad), bf16),
            VMEM((256, 3 * key_pad), bf16),
            VMEM((192, row_count), bf16),
            VMEM((row_count, 128), i32),
            VMEM((heads, 192, 128), f32),
            VMEM((heads, span + 64 + 2 * patch_span, 128), f32),
            VMEM((heads, 8, width), f32),
            VMEM((count, span + 32, width), bf16),
            VMEM((count, patch_span + 32, width), bf16),
            VMEM((2, 24, width), f32),
            VMEM((3 + levels, 24, width), f32),
            VMEM((early_rows // 9 * 4, lanes), bf16),
            VMEM((early_rows // 9 * 8, lanes // 2), bf16),
            VMEM((early_rows // 9 * 8, lanes // 2), bf16),
            VMEM((early_rows // 9 + late_rows, lanes // 2), bf16),
            VMEM((early_rows // 9 + late_rows, lanes // 2), bf16),
            dma((6,)), dma((3, 2)),
            dma((early_count,)), dma((early_count,)), dma((late_count,)), dma((late_count,)),
            dma((count, 2)), dma((count, 2)), dma((count, 2)), dma((count, 2)),
            dma((4,)), dma((4,)), dma((3 + levels,)), dma((3 + levels,)), dma((3,)), dma((3,)),
        ]
        + stage_for(local_values),
        compiler_params=pltpu.CompilerParams(
            collective_id=1, has_side_effects=True, vmem_limit_bytes=KERNEL_VMEM
        ),
        cost_estimate=pl.CostEstimate(flops=12_000_000_000, bytes_accessed=40_000_000, transcendentals=0),
        name="backward",
    )(lengths, *local_values, *far_values)


def clip_lanes(sums, centre, bins):
    first, last = centre + 1 - bins // 2, centre - 1 + bins // 2
    lane = lax.broadcasted_iota(jnp.int32, sums.shape, 1)
    below = jnp.sum(jnp.where(lane < first, sums, 0.0), axis=1, keepdims=True)
    above = jnp.sum(jnp.where(lane >= last, sums, 0.0), axis=1, keepdims=True)
    moved = pltpu.roll(sums, sums.shape[1] - (first - 1), 1)
    moved = jnp.where(lane == 0, below, jnp.where(lane == bins - 1, above, moved))
    return moved[:, :bins]


def finish_kernel(staging, early_ref, late_ref, sums_ref, up_in_ref, down_in_ref, mixed_in_ref, *rest):
    carried, rest = rest[:2], rest[2:]
    *rest, carry_sem = rest
    rest, targets = rest[:-2], rest[-2:]
    (
        query_ref, key_ref, value_ref, out_ref, up_ref, down_ref, taps_ref, patch_taps_ref, line_ref, across_ref,
        upward_ref, *vector_refs,
    ) = rest
    carries = [
        pltpu.make_async_copy(source, target, carry_sem.at[index])
        for index, (source, target) in enumerate(zip(carried, targets, strict=True))
    ]
    for copy in carries:
        copy.start()
    f32 = jnp.float32
    rows, columns = query_ref.shape
    half = rows // 2
    wide_rows = 4 * rows
    first = position()[1] == 0
    for copy in staging:
        copy.wait()
    heads = line_ref.shape[0]
    block = early_ref[...].astype(f32)
    low, high = block[:, 0:columns], pltpu.roll(block, columns, 1)[:, 0:columns]
    up = jnp.where(first, block[0 : 2 * rows], up_in_ref[...].astype(f32))
    up_ref[:, 0 : 2 * columns] = up[0:rows]
    up_ref[:, 2 * columns : 4 * columns] = up[rows : 2 * rows]
    down_ref[...] = jnp.where(first, down_in_ref[...].astype(f32), high[0:wide_rows]).T
    kept = jnp.where(first, low[wide_rows:], high[wide_rows:])
    got = mixed_in_ref[0:half, :].astype(f32)
    out_ref[0:half, :] = jnp.where(first, kept, got)
    out_ref[half:rows, :] = jnp.where(first, got, kept)
    block = late_ref[...].astype(f32)
    low, high = block[:, 0:columns], pltpu.roll(block, columns, 1)[:, 0:columns]
    kept = jnp.where(first, low, high)
    got = mixed_in_ref[half:, :].astype(f32)
    query_ref[...] = jnp.where(first, kept[0:rows], got[0:rows])
    key_ref[...] = jnp.where(first, got[0:rows], kept[0:rows])
    value_ref[0:half, :] = jnp.where(first, kept[rows:], got[rows:])
    value_ref[half:rows, :] = jnp.where(first, got[rows:], kept[rows:])
    front, back = sums_ref[0], sums_ref[1]
    width = front.shape[1]
    text = [front[16 + index : 17 + index] for index in range(7)]
    order = [text[2], text[3], text[4], text[1], text[3], text[5], text[0], text[3], text[6]]
    taps_ref[...] = jnp.concatenate(order, axis=0)
    patch_taps_ref[...] = jnp.concatenate([front[23:24], back[0:8]], axis=0)
    across_ref[...] = clip_lanes(back[8:24, 0:256], 72, across_ref.shape[1])[0:heads]
    upward_ref[...] = clip_lanes(back[8:24, 256:512], 72, upward_ref.shape[1])[0:heads]
    line_ref[...] = clip_lanes(back[8:24, 512:640], 32, line_ref.shape[1])[0:heads]
    for source, target in zip((10, 11, 0, UP_BIAS, 1, 2, 3, 4, 5), vector_refs, strict=True):
        for part in range(target.shape[0] // width):
            target[pl.ds(part * width, width)] = front[source + part, :]
    for copy in carries:
        copy.wait()


def finish(values, carried, width, wide, heads, line_bins, plane_bins):
    rows, columns = values[1].shape[0] * 2 // 3, values[1].shape[1] // 2
    f32 = jnp.float32
    square = jax.ShapeDtypeStruct((rows, columns), f32)
    taps = jax.ShapeDtypeStruct((9, width), f32)
    plane = jax.ShapeDtypeStruct((heads, plane_bins), f32)
    return pl.pallas_call(
        staged(finish_kernel, 0, len(values)),
        out_shape=(
            square, square, square, square,
            jax.ShapeDtypeStruct((rows, 4 * columns), f32),
            jax.ShapeDtypeStruct((columns, 4 * rows), f32),
            taps, taps,
            jax.ShapeDtypeStruct((heads, line_bins), f32), plane, plane,
            *(jax.ShapeDtypeStruct((size,), f32) for size in (width,) * 3 + (wide,) + (width,) * 5),
            *(jax.ShapeDtypeStruct(value.shape, f32) for value in carried),
        ),
        in_specs=anywhere(len(values) + len(carried)),
        out_specs=tuple(in_vmem(22)),
        scratch_shapes=[pltpu.SemaphoreType.DMA((2,))] + stage_for(values),
        compiler_params=pltpu.CompilerParams(vmem_limit_bytes=KERNEL_VMEM),
        name="finish",
    )(*values, *carried)


def exchange(value, pages, step):
    moves = []
    for page in range(pages):
        for seq in range(4):
            on_page, on_seq = page, seq
            if (seq % 2 == step) if step < 2 else False:
                on_seq = seq ^ 2
            else:
                on_page = page ^ (1 if step < 2 else 1 << (step - 1))
            moves.append((page * 4 + seq, on_page * 4 + on_seq))
    return lax.ppermute(value, ("page", "seq"), moves)


def added(kept, got):
    return (kept.astype(jnp.float32) + got.astype(jnp.float32)).astype(jnp.bfloat16)


def bundle_sum(state, pages):
    for step in range(pages.bit_length()):
        half = state.shape[0] // 2
        state = added(state[:half], exchange(state[half:], pages, step))
    return state[0]


def bundle_parts(state, wide_rows, core):
    lanes = state.shape[1] // 2
    first = core == 0
    tail = state[wide_rows:]
    if wide_rows > 2 * tail.shape[0]:
        group = state[:wide_rows].reshape(4, wide_rows // 4, 2 * lanes)
        low = group[:2].transpose(1, 0, 2).reshape(-1, lanes)
        high = group[2:].transpose(1, 0, 2).reshape(-1, lanes)
    else:
        low, high = state[:wide_rows, :lanes], state[:wide_rows, lanes:]
    left, right = state[:wide_rows, :lanes], state[:wide_rows, lanes:]
    sent = jnp.concatenate(
        [jnp.where(first, high, left), jnp.where(first, tail[:, lanes:], tail[:, :lanes])], axis=0
    )
    got = swap(sent, "seq", 1)
    kept_tail = jnp.where(first, tail[:, :lanes], tail[:, lanes:])
    one = jnp.where(first, low, got[:wide_rows])
    two = jnp.where(first, got[:wide_rows], right)
    three = jnp.concatenate(
        [jnp.where(first, kept_tail, got[wide_rows:]), jnp.where(first, got[wide_rows:], kept_tail)], axis=0
    )
    return [value.astype(jnp.float32) for value in (one, two, three)]


def clipped(sums, centre, bins):
    first, last = centre + 1 - bins // 2, centre - 1 + bins // 2
    return jnp.concatenate(
        [
            jnp.sum(sums[..., :first], axis=-1, keepdims=True),
            sums[..., first:last],
            jnp.sum(sums[..., last:], axis=-1, keepdims=True),
        ],
        axis=-1,
    )


def grid_live(cells):
    return (cells // GRID_SIDE < GRID_SIDE - 1) & (cells % GRID_SIDE < GRID_SIDE - 1)


def grid_boxes(cells):
    return jnp.stack(
        [
            patch_pitch * (cells % GRID_SIDE) + patch_centre,
            patch_pitch * (cells // GRID_SIDE) + patch_centre,
        ]
    )


def shards(
    tokens,
    patches,
    page_length,
    box_position,
    query_weight,
    key_weight,
    value_weight,
    out_weight,
    up_weight,
    down_weight,
    conv_weight,
    patch_conv_weight,
    query_bias,
    value_bias,
    out_bias,
    up_bias,
    down_bias,
    attention_gain,
    attention_shift,
    feedforward_gain,
    feedforward_shift,
    reading_bias_table,
    horizontal_bias_table,
    vertical_bias_table,
    cotangent,
    patch_cotangent,
):
    conv_taps = conv_weight.astype(jnp.float32)
    patch_taps = patch_conv_weight.astype(jnp.float32)
    query_offset = query_bias.astype(jnp.float32)
    value_offset = value_bias.astype(jnp.float32)
    out_offset = out_bias.astype(jnp.float32)
    up_offset = up_bias.astype(jnp.float32)
    down_offset = down_bias.astype(jnp.float32)
    first_gain = attention_gain.astype(jnp.float32)
    first_shift = attention_shift.astype(jnp.float32)
    second_gain = feedforward_gain.astype(jnp.float32)
    second_shift = feedforward_shift.astype(jnp.float32)
    page_count, span_size, model_width = tokens.shape
    patch_span = patches.shape[1]
    seq_count = lax.axis_size("seq")
    slot_size = span_size * seq_count
    patch_slots = patch_span * seq_count
    row_count = span_size + patch_span
    key_count = row_count * seq_count
    head_count = reading_bias_table.shape[0]
    head_size = model_width // head_count
    line_bins = reading_bias_table.shape[1]
    plane_bins = horizontal_bias_table.shape[1]
    score_scale = head_size ** (-0.5)
    seq_index = lax.axis_index("seq")
    text_places = seq_index * span_size + jnp.arange(span_size, dtype=jnp.int32)
    local_cells = seq_index * patch_span + jnp.arange(patch_span, dtype=jnp.int32)
    text_live = text_places[None, :] < page_length[:, None]
    patch_live = grid_live(local_cells)
    text_factor = text_live[:, :, None]
    patch_factor = patch_live[None, :, None]
    masked = tokens * text_factor.astype(jnp.bfloat16)
    rimmed = with_halo(masked, (("seq", 1),), 3)
    reach = GRID_SIDE + 1
    patch_masked = patches * patch_factor.astype(jnp.bfloat16)
    patch_rimmed = with_halo(patch_masked, (("seq", 1),), reach)
    pages = lax.axis_size("page")
    (
        hidden, hidden_low, queries, mixture_low, columns, key_rows, query_rows, taps, keys, values, weights,
    ) = forward(
        pages, page_length, tokens, patches, box_position.transpose(1, 0, 2), (conv_weight.T, patch_conv_weight.T),
        (horizontal_bias_table, vertical_bias_table, reading_bias_table), (query_bias, value_bias),
        (query_weight, key_weight, value_weight),
    )
    places = jnp.stack(
        [seq_index, seq_index % 2, lax.axis_index("page"), seq_index // 2]
    ).astype(jnp.int32)
    def flat(value):
        return value.reshape(-1, value.shape[-1])

    output, patch_output, delta_first, delta_mixture, middle_sums, feedforward_bundle = middle(
        places, hidden, mixture_low, cotangent, patch_cotangent,
        (out_weight, up_weight, down_weight),
        (
            out_bias, down_bias, attention_gain, attention_shift, feedforward_gain, feedforward_shift, up_bias,
        ),
        pages,
    )
    pair_rows = weights.reshape(page_count, head_count // 2, 2 * row_count, -1)
    if in_tiles(model_width, pages):
        tokens_back, patches_back, early_state, late_state, sums, up_in, down_in, mixed_in = backward(
            pages,
            page_length,
            (
                queries, delta_mixture, columns, key_rows, query_rows, tokens, patches, taps, middle_sums,
            ),
            (
                feedforward_bundle, pair_rows, keys, values, hidden_low, delta_first, query_weight, key_weight,
                value_weight,
            ),
            tokens,
            patches,
        )
        (
            query_part, key_part, value_part, out_part, up_part, down_part, text_part, patch_part, line_part,
            across_part, upward_part, *vector_parts, tokens_gradient, patches_gradient,
        ) = finish(
            (early_state, late_state, sums, up_in, down_in, mixed_in),
            (tokens_back, patches_back), model_width, up_weight.shape[1], head_count, line_bins,
            plane_bins,
        )
        return (
            output,
            patch_output,
            tokens_gradient,
            patches_gradient,
            query_part,
            key_part,
            value_part,
            out_part,
            up_part,
            down_part.T,
            text_part.T,
            patch_part.T,
            *vector_parts,
            line_part,
            across_part,
            upward_part,
        )
    delta_first = delta_first.reshape(page_count, row_count, model_width)
    delta_mixture = delta_mixture.reshape(page_count, row_count, model_width)
    early_state = added(feedforward_bundle[0], swap(feedforward_bundle[1], "seq", 1))
    delta_mixture, early_state = lax.optimization_barrier((delta_mixture, early_state))
    delta_query_pages, delta_key_pages, delta_value_pages = [], [], []
    delta_plane, delta_line = 0.0, 0.0
    for page in range(page_count):
        delta_page_queries, delta_blocks, plane_part, line_part = backward_page(
            places,
            columns[page][:, ::128],
            key_rows[page],
            query_rows[page][:, :row_count],
            queries[page * row_count : (page + 1) * row_count],
            keys[page],
            values[page],
            delta_mixture[page],
            pair_rows[page],
        )
        got = swap(delta_blocks[2:], "seq", 1)
        chip_sum = delta_blocks[:2].astype(jnp.float32) + got.astype(jnp.float32)
        got = swap(chip_sum[1].astype(jnp.bfloat16), "seq", 2)
        whole = (chip_sum[0] + got.astype(jnp.float32)).astype(jnp.bfloat16)
        delta_query_pages.append(delta_page_queries)
        delta_key_pages.append(whole[0])
        delta_value_pages.append(whole[1])
        delta_plane = delta_plane + plane_part
        delta_line = delta_line + line_part
    delta_queries = jnp.stack(delta_query_pages)
    delta_keys = jnp.stack(delta_key_pages)
    delta_values = jnp.stack(delta_value_pages)
    delta_plane = clipped(delta_plane, 72, plane_bins)
    delta_line = clipped(delta_line, 32, line_bins)
    delta_across, delta_upward = delta_plane[0], delta_plane[1]
    delta_query_offset = row_sum(delta_queries)
    delta_value_offset = row_sum(delta_values)
    delta_hidden = (
        delta_first
        + back_dot(delta_queries, query_weight)
        + back_dot(delta_keys, key_weight)
        + back_dot(delta_values, value_weight)
    )
    delta_position = delta_hidden[:, :span_size].astype(jnp.bfloat16)
    delta_rim = with_halo(delta_position, (("seq", 1),), 3)
    delta_masked = jnp.zeros((page_count, span_size, model_width), jnp.float32)
    tap_columns = []
    for dilation in (1, 2, 3):
        for offset in (-1, 0, 1):
            column = 3 * (dilation - 1) + offset + 1
            anchor = 3 + offset * dilation
            anchor_back = 3 - offset * dilation
            delta_masked = (
                delta_masked
                + delta_rim[:, anchor_back : anchor_back + span_size, :] * conv_taps[:, column]
            )
            tap_columns.append(
                jnp.einsum(
                    "ptd,ptd->d",
                    delta_position,
                    rimmed[:, anchor : anchor + span_size, :],
                    preferred_element_type=jnp.float32,
                )
            )
    delta_taps = jnp.stack(tap_columns, axis=1)
    tokens_gradient = delta_hidden[:, :span_size] + delta_masked * text_factor.astype(jnp.float32)
    delta_patch_position = delta_hidden[:, span_size:].astype(jnp.bfloat16)
    delta_patch_rim = with_halo(delta_patch_position, (("seq", 1),), reach)
    delta_patch_masked = jnp.zeros((page_count, patch_span, model_width), jnp.float32)
    patch_columns = []
    for vertical in (-1, 0, 1):
        for horizontal in (-1, 0, 1):
            column = 3 * (vertical + 1) + horizontal + 1
            anchor = reach + vertical * GRID_SIDE + horizontal
            anchor_back = reach - vertical * GRID_SIDE - horizontal
            delta_patch_masked = (
                delta_patch_masked
                + delta_patch_rim[:, anchor_back : anchor_back + patch_span, :]
                * patch_taps[:, column]
            )
            patch_columns.append(
                jnp.einsum(
                    "ptd,ptd->d",
                    delta_patch_position,
                    patch_rimmed[:, anchor : anchor + patch_span, :],
                    preferred_element_type=jnp.float32,
                )
            )
    delta_patch_taps = jnp.stack(patch_columns, axis=1)
    patches_gradient = delta_hidden[:, span_size:] + delta_patch_masked * patch_factor.astype(
        jnp.float32
    )
    operands = [flat(value) for value in (hidden_low, delta_queries, delta_keys, delta_values)]
    tail_bundle = indexed_bundle(
        (
            ((operands[0], operands[1], None), (operands[0], operands[3], 0)),
            ((operands[0], operands[2], None), (operands[0], operands[3], 1)),
        ),
        places,
        pages,
    )
    tail_state = added(tail_bundle[0], swap(tail_bundle[1], "seq", 1))
    query_part, key_part, value_part = bundle_parts(
        bundle_sum(tail_state, pages), model_width // pages, places[1]
    )
    up_part, down_part, out_part = bundle_parts(
        bundle_sum(early_state, pages), up_weight.shape[1] // pages, places[1]
    )
    up_part = up_part.reshape(model_width // pages, -1)
    matrix_parts = (query_part, key_part, value_part, out_part, up_part, down_part)
    vector_parts = total_sum(
        (
            delta_taps,
            delta_patch_taps,
            delta_query_offset,
            delta_value_offset,
            middle_sums[OUT_BIAS],
            middle_sums[UP_BIAS : UP_BIAS + 4].reshape(-1),
            middle_sums[DOWN_BIAS],
            middle_sums[FIRST_GAIN],
            middle_sums[FIRST_SHIFT],
            middle_sums[SECOND_GAIN],
            middle_sums[SECOND_SHIFT],
            delta_line,
            delta_across,
            delta_upward,
        )
    )
    return (
        output,
        patch_output,
        tokens_gradient,
        patches_gradient,
        matrix_parts[0],
        matrix_parts[1],
        matrix_parts[2],
        matrix_parts[3],
        matrix_parts[4],
        matrix_parts[5],
        vector_parts[0],
        vector_parts[1],
        vector_parts[2],
        vector_parts[3],
        vector_parts[4],
        vector_parts[5],
        vector_parts[6],
        vector_parts[7],
        vector_parts[8],
        vector_parts[9],
        vector_parts[10],
        vector_parts[11],
        vector_parts[12],
        vector_parts[13],
    )


def solution(mesh):
    in_specs = (
        P("page", "seq", None),
        P("page", "seq", None),
        P("page"),
        P(None, "page", None),
        P(),
        P(),
        P(),
        P(),
        P(),
        P(),
        P(),
        P(),
        P(),
        P(),
        P(),
        P(),
        P(),
        P(),
        P(),
        P(),
        P(),
        P(),
        P(),
        P(),
        P("page", "seq", None),
        P("page", "seq", None),
    )
    out_specs = (
        P("page", "seq", None),
        P("page", "seq", None),
        P("page", "seq", None),
        P("page", "seq", None),
        P("page", "seq"),
        P("page", "seq"),
        P("page", "seq"),
        P("page", "seq"),
        P("page", "seq"),
        P("page", "seq"),
        P(),
        P(),
        P(),
        P(),
        P(),
        P(),
        P(),
        P(),
        P(),
        P(),
        P(),
        P(),
        P(),
        P(),
    )
    return jax.shard_map(shards, mesh=mesh, in_specs=in_specs, out_specs=out_specs, check_vma=False)
```
